32 devices in a mesh: seq: 4 (over z), batch: 8 (over y, x, core).
Axes of the slice: x: 2, y: 2, z: 4, core: 2. Of those that a mesh axis runs over, the one named last changes fastest.
Arguments:
- inputs: float32 [8, 1024, 1024], P('batch', 'seq'), may hold values from -6 to 6
- targets: int32 [8, 1024], P('batch', 'seq'), may hold values from 0 to 267734, as said below
- neighbours: int32 [8, 1024, 1024], P('batch', 'seq'), may hold values from 0 to 16367, as said below
- neighbour_scores: float32 [8, 1024, 1024], P('batch', 'seq'), may hold values from -10 to 10
- loglik_grad: float32 [8, 1024], P('batch', 'seq'), may hold values from -6 to 6
- first_gain: float32 [1024], replicated, may hold values from 0.5 to 1.5
- first_shift: float32 [1024], replicated, may hold values from -1 to 1
- query_weight: bfloat16 [1024, 1024], replicated, may hold values from -0.1875 to 0.1875
- query_bias: float32 [1024], replicated, may hold values from -1 to 1
- key_weight: bfloat16 [1024, 1024], replicated, may hold values from -0.1875 to 0.1875
- value_weight: bfloat16 [1024, 1024], replicated, may hold values from -0.1875 to 0.1875
- value_bias: float32 [1024], replicated, may hold values from -1 to 1
- out_weight: bfloat16 [1024, 1024], replicated, may hold values from -0.75 to 0.75
- out_bias: float32 [1024], replicated, may hold values from -1 to 1
- second_gain: float32 [1024], replicated, may hold values from 0.5 to 1.5
- second_shift: float32 [1024], replicated, may hold values from -1 to 1
- inner_weight: bfloat16 [1024, 4096], replicated, may hold values from -0.1875 to 0.1875
- inner_bias: float32 [4096], replicated, may hold values from -1.5 to 1.5
- outer_weight: bfloat16 [4096, 1024], replicated, may hold values from -0.09375 to 0.09375
- outer_bias: float32 [1024], replicated, may hold values from -1 to 1
- final_gain: float32 [1024], replicated, may hold values from 0.5 to 1.5
- final_shift: float32 [1024], replicated, may hold values from -1 to 1
- head_table: bfloat16 [20000, 1024], P('batch'), may hold values from -0.375 to 0.375
- cluster_weight: bfloat16 [1024, 2], replicated, may hold values from -0.375 to 0.375
- middle_map: bfloat16 [1024, 256], replicated, may hold values from -0.1875 to 0.1875
- middle_table: bfloat16 [40000, 256], P('batch'), may hold values from -0.75 to 0.75
- tail_map: bfloat16 [1024, 64], replicated, may hold values from -0.1875 to 0.1875
- tail_table: bfloat16 [207736, 64], P('batch'), may hold values from -1.5 to 1.5
Outputs:
- loglik: float32 [8, 1024], P('batch', 'seq')
- input_grad: float32 [8, 1024, 1024], P('batch', 'seq')
- first_gain_grad: float32 [1024], P('batch')
- first_shift_grad: float32 [1024], P('batch')
- query_weight_grad: float32 [1024, 1024], P('batch')
- query_bias_grad: float32 [1024], P('batch')
- key_weight_grad: float32 [1024, 1024], P('batch')
- value_weight_grad: float32 [1024, 1024], P('batch')
- value_bias_grad: float32 [1024], P('batch')
- out_weight_grad: float32 [1024, 1024], P('batch')
- out_bias_grad: float32 [1024], P('batch')
- second_gain_grad: float32 [1024], P('batch')
- second_shift_grad: float32 [1024], P('batch')
- inner_weight_grad: float32 [1024, 4096], P('batch')
- inner_bias_grad: float32 [4096], P('batch')
- outer_weight_grad: float32 [4096, 1024], P('batch')
- outer_bias_grad: float32 [1024], P('batch')
- final_gain_grad: float32 [1024], P('batch')
- final_shift_grad: float32 [1024], P('batch')
- head_table_grad: float32 [20000, 1024], P('batch')
- cluster_weight_grad: float32 [1024, 2], P('batch')
- middle_map_grad: float32 [1024, 256], P('batch')
- middle_table_grad: float32 [40000, 256], P('batch')
- tail_map_grad: float32 [1024, 64], P('batch')
- tail_table_grad: float32 [207736, 64], P('batch')
The draws below stay inside these ranges and needn't reach their ends.
Inputs may be any that keep to these rules, and one draw needn't show every extreme that they name: `targets`: target words; those from 20000 to 59999 form the middle band, higher ones the tail band. `neighbours`: 0 marks a neighbour whose word is the token's target.
All inputs are finite; a program needn't handle non-finite values.
Results may differ from the reference program's by a relative error of at most 0.033.
Values may be sent and summed in bfloat16 or wider, within the bound.
No kernel may reach another device: no remote copies, remote signals or barrier semaphores. Data moves between devices by JAX's collectives and lax.ppermute only.
A program may use at most 256 MiB of HBM per device.

```python
import math
import jax
import jax.numpy as jnp
from jax import lax

D = 1024
HEADS = 16
HEAD_DIM = 64
FF = 4096
MID_DIM = 256
TAIL_DIM = 64
HEAD_WORDS = 20000
MID_WORDS = 40000
TAIL_WORDS = 207735
NEIGHB = 1024
TAIL_ROWS = 207736
LEN = 1024
SEQS = 8
VOCAB = 267735


def target_words(key):
    band_key, head_key, middle_key, tail_key, place_key = jax.random.split(key, 5)
    grid_shape = (SEQS, LEN)
    band_choice = jax.random.randint(band_key, grid_shape, 0, 4)
    head_ids = jax.random.randint(head_key, grid_shape, 0, HEAD_WORDS)
    middle_ids = HEAD_WORDS + jax.random.randint(middle_key, grid_shape, 0, MID_WORDS)
    tail_ids = HEAD_WORDS + MID_WORDS + jax.random.randint(tail_key, grid_shape, 0, TAIL_WORDS)
    word_ids = jnp.where(band_choice == 0, head_ids, jnp.where(band_choice == 1, middle_ids, tail_ids))
    flattened = word_ids.reshape(-1)
    position = jax.random.randint(place_key, (), 0, SEQS * LEN)
    flattened = flattened.at[position].set(VOCAB - 1)
    flattened = flattened.at[(position + 1) % (SEQS * LEN)].set(0)
    return flattened.reshape(grid_shape).astype(jnp.int32)


def draw_targets(key, part):
    word_ids = target_words(key)
    return word_ids


def draw_neighbours(key, part):
    key = jax.random.fold_in(key, 11)
    other_key, token_key, entry_key, place_key = jax.random.split(key, 4)
    grid_shape = (SEQS, LEN, NEIGHB)
    largest = min(16367, VOCAB - 1)
    others = jax.random.randint(other_key, grid_shape, 1, largest + 1)
    token_hit = jax.random.randint(token_key, (SEQS, LEN, 1), 0, 8) == 0
    entry_hit = jax.random.randint(entry_key, grid_shape, 0, max(NEIGHB // 4, 1)) == 0
    chosen = jnp.where(token_hit & entry_hit, 0, others)
    flattened = chosen.reshape(-1)
    position = jax.random.randint(place_key, (), 0, SEQS * LEN * NEIGHB)
    flattened = flattened.at[position].set(largest)
    flattened = flattened.at[(position + 1) % (SEQS * LEN * NEIGHB)].set(0)
    return flattened.reshape(grid_shape).astype(jnp.int32)


def block_levels(stream_key, shape, shards, low, high):
    loudness = 1.0
    for dim, blocks in shards:
        steps = jax.random.uniform(jax.random.fold_in(jax.random.fold_in(stream_key, 6), dim), (blocks,), jnp.float32, low / len(shards), high / len(shards))
        loudness = loudness * jnp.repeat(jnp.exp(steps), shape[dim] // blocks).reshape((-1,) + (1,) * (len(shape) - 1 - dim))
    return loudness


def noise(key, shape, width, limit, cuts=(), kind=jnp.bfloat16):
    loudness = block_levels(key, shape, cuts, -0.22, 0.18) if cuts else 1.0
    values = jax.random.normal(key, shape, jnp.float32) * width * loudness
    return jnp.minimum(jnp.maximum(values, -limit), limit).astype(kind)


def setup_inputs(seed: int = 0) -> dict:
    arg_keys = jax.random.split(jax.random.key(seed), 29)
    return {
        "inputs": noise(arg_keys[0], (SEQS, LEN, D), 1.0, 6.0, ((0, 8), (1, 4)), jnp.float32),
        "targets": draw_targets(jax.random.fold_in(arg_keys[28], 71), 0),
        "neighbours": draw_neighbours(jax.random.fold_in(arg_keys[28], 71), 0),
        "neighbour_scores": noise(arg_keys[3], (SEQS, LEN, NEIGHB), 2.0, 10.0, ((0, 8), (1, 4)), jnp.float32),
        "loglik_grad": noise(arg_keys[4], (SEQS, LEN), 1.0, 6.0, ((0, 8), (1, 4)), jnp.float32),
        "first_gain": jnp.clip(1.0 + 0.1 * jax.random.normal(arg_keys[5], (D,), jnp.float32), 0.5, 1.5),
        "first_shift": noise(arg_keys[6], (D,), 0.2, 1.0, (), jnp.float32),
        "query_weight": noise(arg_keys[7], (D, D), D ** -0.5, 0.1875),
        "query_bias": noise(arg_keys[8], (D,), 0.2, 1.0, (), jnp.float32),
        "key_weight": noise(arg_keys[9], (D, D), D ** -0.5, 0.1875),
        "value_weight": noise(arg_keys[10], (D, D), D ** -0.5, 0.1875),
        "value_bias": noise(arg_keys[11], (D,), 0.2, 1.0, (), jnp.float32),
        "out_weight": noise(arg_keys[12], (D, D), (D // 16) ** -0.5, 0.75),
        "out_bias": noise(arg_keys[13], (D,), 0.2, 1.0, (), jnp.float32),
        "second_gain": jnp.clip(1.0 + 0.1 * jax.random.normal(arg_keys[14], (D,), jnp.float32), 0.5, 1.5),
        "second_shift": noise(arg_keys[15], (D,), 0.2, 1.0, (), jnp.float32),
        "inner_weight": noise(arg_keys[16], (D, FF), D ** -0.5, 0.1875),
        "inner_bias": noise(arg_keys[17], (FF,), 0.3, 1.5, (), jnp.float32),
        "outer_weight": noise(arg_keys[18], (FF, D), FF ** -0.5, 0.09375),
        "outer_bias": noise(arg_keys[19], (D,), 0.2, 1.0, (), jnp.float32),
        "final_gain": jnp.clip(1.0 + 0.1 * jax.random.normal(arg_keys[20], (D,), jnp.float32), 0.5, 1.5),
        "final_shift": noise(arg_keys[21], (D,), 0.2, 1.0, (), jnp.float32),
        "head_table": noise(arg_keys[22], (HEAD_WORDS, D), (D // 4) ** -0.5, 0.375, ((0, 8),)),
        "cluster_weight": noise(arg_keys[23], (D, 2), (D // 4) ** -0.5, 0.375),
        "middle_map": noise(arg_keys[24], (D, MID_DIM), D ** -0.5, 0.1875),
        "middle_table": noise(arg_keys[25], (MID_WORDS, MID_DIM), (MID_DIM // 4) ** -0.5, 0.75, ((0, 8),)),
        "tail_map": noise(arg_keys[26], (D, TAIL_DIM), D ** -0.5, 0.1875),
        "tail_table": noise(arg_keys[27], (TAIL_ROWS, TAIL_DIM), (TAIL_DIM // 4) ** -0.5, 1.5, ((0, 8),)),
    }


@jax.custom_vjp
def low(v):
    return lax.optimization_barrier(v.astype(jnp.bfloat16)).astype(jnp.float32)

@jax.custom_vjp
def low_back(v):
    return v

def low_keep(v):
    return (low(v), None)

def low_pass(kept, grad):
    return (grad,)

def back_keep(v):
    return (v, None)

def back_low(kept, grad):
    return (low(grad),)
low.defvjp(low_keep, low_pass)
low_back.defvjp(back_keep, back_low)
HIGHEST = lax.Precision.HIGHEST
NEG_FILL = -1e+30
EPSILON = 1e-05

def product(former, latter):
    return jnp.dot(former, latter, precision=HIGHEST)

def layer_norm(values, gain_vector, shift_vector):
    average = lax.optimization_barrier(jnp.mean(values, -1, keepdims=True))
    centred = values - average
    spread = lax.optimization_barrier(jnp.mean(centred * centred, -1, keepdims=True))
    return centred * lax.rsqrt(spread + EPSILON) * gain_vector + shift_vector

def log_total(logits):
    top_value = lax.optimization_barrier(jnp.max(logits, -1, keepdims=True))
    return top_value[:, 0] + jnp.log(lax.optimization_barrier(jnp.sum(jnp.exp(logits - top_value), -1)))

def pick_column(logits, column):
    clipped = jnp.clip(column, 0, logits.shape[1] - 1).astype(jnp.int32)
    return jnp.take_along_axis(logits, clipped[:, None], axis=1)[:, 0]

def attend(queries, key_rows, value_rows):
    length = queries.shape[0]
    block_size = math.gcd(length, 512)
    scale = HEAD_DIM ** (-0.5)
    key_pos = jnp.arange(length, dtype=jnp.int32)

    def one_block(inputs):
        query_block, block_start = inputs
        raw_scores = jnp.einsum('qhd,khd->hqk', query_block, key_rows, precision=HIGHEST) * scale
        scores = low_back(raw_scores)
        query_pos = block_start + jnp.arange(block_size, dtype=jnp.int32)
        allowed = (key_pos[None, :] <= query_pos[:, None])[None]
        masked = jnp.where(allowed, scores, NEG_FILL)
        top_value = lax.optimization_barrier(jnp.max(masked, -1, keepdims=True))
        exponent = jnp.where(allowed, jnp.exp(masked - top_value), 0.0)
        probs = exponent / lax.optimization_barrier(jnp.sum(exponent, -1, keepdims=True))
        return jnp.einsum('hqk,khd->qhd', low(probs), value_rows, precision=HIGHEST)
    starts = jnp.arange(length // block_size, dtype=jnp.int32) * block_size
    blocks = queries.reshape(length // block_size, block_size, HEADS, HEAD_DIM)
    result = lax.map(jax.checkpoint(one_block), (blocks, starts))
    return result.reshape(length, HEADS * HEAD_DIM)

def sequence_loss(params, tokens, token_ids, knn_prob):
    first_gain, first_shift, query_weight, query_bias, key_weight, value_weight, value_bias, out_weight, out_bias, second_gain, second_shift, inner_weight, inner_bias, outer_weight, outer_bias, final_gain, final_shift, head_table, cluster_weight, middle_map, middle_table, tail_map, tail_table = params
    used_tail = tail_table[:TAIL_WORDS]
    length = tokens.shape[0]
    normed_low = low(layer_norm(tokens, first_gain, first_shift))
    queries = low(low_back(product(normed_low, query_weight) + query_bias)).reshape(length, HEADS, HEAD_DIM)
    key_rows = low(low_back(product(normed_low, key_weight))).reshape(length, HEADS, HEAD_DIM)
    value_rows = low(low_back(product(normed_low, value_weight) + value_bias)).reshape(length, HEADS, HEAD_DIM)
    attended_low = low(low_back(attend(queries, key_rows, value_rows)))
    mixed = tokens + low_back(product(attended_low, out_weight)) + out_bias
    second_low = low(layer_norm(mixed, second_gain, second_shift))
    before = low_back(product(second_low, inner_weight) + inner_bias)
    hidden_low = low(jax.nn.gelu(before))
    final = mixed + low_back(product(hidden_low, outer_weight)) + outer_bias
    state_low = low(layer_norm(final, final_gain, final_shift))
    middle_low = low(low_back(product(state_low, middle_map)))
    tail_low = low(low_back(product(state_low, tail_map)))
    clusters = product(state_low, cluster_weight)
    block_size = math.gcd(length, 128)
    block_count = length // block_size

    def word_block(inputs):
        state_rows, middle_rows, tail_rows, cluster_rows, block_ids, block_knn = inputs
        head_logits = low_back(product(state_rows, head_table.T))
        middle_logits = low_back(product(middle_rows, middle_table.T))
        tail_logits = low_back(product(tail_rows, used_tail.T))
        head_total = log_total(jnp.concatenate([head_logits, cluster_rows], -1))
        middle_total = log_total(middle_logits)
        tail_total = log_total(tail_logits)
        in_head = block_ids < HEAD_WORDS
        in_middle = (block_ids >= HEAD_WORDS) & (block_ids < HEAD_WORDS + MID_WORDS)
        head_pick = pick_column(head_logits, block_ids)
        middle_pick = pick_column(middle_logits, block_ids - HEAD_WORDS)
        tail_pick = pick_column(tail_logits, block_ids - HEAD_WORDS - MID_WORDS)
        model_logp = jnp.where(in_head, head_pick - head_total, jnp.where(in_middle, cluster_rows[:, 0] - head_total + middle_pick - middle_total, cluster_rows[:, 1] - head_total + tail_pick - tail_total))
        return model_logp + jnp.log(0.75 + 0.25 * block_knn * jnp.exp(-model_logp))
    inputs = (state_low.reshape(block_count, block_size, -1), middle_low.reshape(block_count, block_size, -1), tail_low.reshape(block_count, block_size, -1), clusters.reshape(block_count, block_size, 2), token_ids.reshape(block_count, block_size), knn_prob.reshape(block_count, block_size))
    return lax.map(jax.checkpoint(word_block), inputs).reshape(length)

def reference(inputs, targets, neighbours, neighbour_scores, loglik_grad, first_gain, first_shift, query_weight, query_bias, key_weight, value_weight, value_bias, out_weight, out_bias, second_gain, second_shift, inner_weight, inner_bias, outer_weight, outer_bias, final_gain, final_shift, head_table, cluster_weight, middle_map, middle_table, tail_map, tail_table):
    params = tuple((element.astype(jnp.float32) for element in (first_gain, first_shift, query_weight, query_bias, key_weight, value_weight, value_bias, out_weight, out_bias, second_gain, second_shift, inner_weight, inner_bias, outer_weight, outer_bias, final_gain, final_shift, head_table, cluster_weight, middle_map, middle_table, tail_map, tail_table)))
    top_score = lax.optimization_barrier(jnp.max(neighbour_scores, -1, keepdims=True))
    exponent = jnp.exp(neighbour_scores - top_score)
    shares = exponent / lax.optimization_barrier(jnp.sum(exponent, -1, keepdims=True))
    knn_prob = lax.optimization_barrier(jnp.sum(jnp.where(neighbours == 0, shares, 0.0), -1))

    def forward(weights, tokens):

        def one_sequence(inputs_one):
            seq_tokens, seq_ids, seq_knn = inputs_one
            return sequence_loss(weights, seq_tokens, seq_ids, seq_knn)
        return lax.map(jax.checkpoint(one_sequence), (tokens, targets, knn_prob))
    loglik, pullback = jax.vjp(forward, params, inputs.astype(jnp.float32))
    grads, input_grad = pullback(loglik_grad.astype(jnp.float32))
    return (loglik, input_grad, grads[0], grads[1], grads[2], grads[3], grads[4], grads[5], grads[6], grads[7], grads[8], grads[9], grads[10], grads[11], grads[12], grads[13], grads[14], grads[15], grads[16], grads[17], grads[18], grads[19], grads[20], grads[21], grads[22])
```

```python
import functools
import math

import jax
import jax.numpy as jnp
from jax import lax
from jax.experimental import pallas as pl
from jax.experimental.pallas import tpu as pltpu
from jax.sharding import PartitionSpec as P

HEADS = 16
HEAD_WORDS = 20000
MID_WORDS = 40000
TAIL_WORDS = 207735


NEG_FILL = -1e30
EPSILON = 1e-05
BLOCK = 256
SAFE = 1e30
VMEM_BYTES = 56 << 20
ONCE = dict(pipeline_mode=pl.Buffered(1))


def layer_norm(values, gain_vector, shift_vector):
    average = jnp.mean(values, -1, keepdims=True)
    centred = values - average
    spread = jnp.mean(centred * centred, -1, keepdims=True)
    return centred * lax.rsqrt(spread + EPSILON) * gain_vector + shift_vector


def norm_back(values, gain_vector, shift_vector, upstream):
    unused, pullback = jax.vjp(layer_norm, values, gain_vector, shift_vector)
    return pullback(upstream)


def gelu_back(before, upstream):
    unused, pullback = jax.vjp(jax.nn.gelu, before)
    return pullback(upstream)[0]


def product(former, latter):
    return jnp.dot(former, latter, preferred_element_type=jnp.float32)


def product_tn(former, latter):
    return lax.dot_general(
        former, latter, (((0,), (0,)), ((), ())), preferred_element_type=jnp.float32
    )


def product_nt(former, latter):
    return lax.dot_general(
        former, latter, (((1,), (1,)), ((), ())), preferred_element_type=jnp.float32
    )


def lowered(values):
    return values.astype(jnp.bfloat16)


def round_up(count, unit):
    return -(-count // unit) * unit


def thirds(values):
    high = lowered(values)
    rest = values - high.astype(jnp.float32)
    middle = lowered(rest)
    return [high, middle, lowered(rest - middle.astype(jnp.float32))]


def attend_kernel(start_ref, query_ref, key_ref, value_ref, out_ref):
    rows, keys = query_ref.shape[0], key_ref.shape[0]
    half = query_ref.shape[1] // 2
    query_pos = start_ref[0] + lax.broadcasted_iota(jnp.int32, (rows, keys), 0)
    allowed = lax.broadcasted_iota(jnp.int32, (rows, keys), 1) <= query_pos
    for part in range(2):
        cols = slice(part * half, part * half + half)
        scores = product_nt(query_ref[:, cols], key_ref[:, cols]) * half**-0.5
        scores = jnp.where(allowed, scores, NEG_FILL)
        weights = jnp.exp(scores - jnp.max(scores, 1, keepdims=True))
        weights = weights / jnp.sum(weights, 1, keepdims=True)
        out_ref[:, cols] = lowered(product(lowered(weights), value_ref[:, cols]))


def attend(start, queries, keys, values):
    rows, features = queries.shape
    width = 2 * features // HEADS
    own = pl.BlockSpec((rows, width), lambda i, s: (0, i))
    whole = pl.BlockSpec((keys.shape[0], width), lambda i, s: (0, i))
    return pl.pallas_call(
        attend_kernel,
        grid_spec=pltpu.PrefetchScalarGridSpec(
            num_scalar_prefetch=1,
            grid=(features // width,),
            in_specs=[own, whole, whole],
            out_specs=own,
        ),
        out_shape=jax.ShapeDtypeStruct((rows, features), jnp.bfloat16),
        compiler_params=pltpu.CompilerParams(vmem_limit_bytes=VMEM_BYTES),
        cost_estimate=pl.CostEstimate(
            flops=4 * rows * keys.shape[0] * features,
            bytes_accessed=4 * (rows + keys.shape[0]) * features,
            transcendentals=rows * keys.shape[0] * HEADS,
        ),
        name="attend",
    )(start, queries, keys, values)


def attend_back_kernel(
    start_ref, query_ref, key_ref, value_ref, up_ref, query_grad_ref, key_grad_ref, value_grad_ref
):
    rows, keys = query_ref.shape[0], key_ref.shape[0]
    half = query_ref.shape[1] // 2
    scale = half**-0.5
    query_pos = start_ref[0] + lax.broadcasted_iota(jnp.int32, (keys, rows), 1)
    allowed = lax.broadcasted_iota(jnp.int32, (keys, rows), 0) <= query_pos
    for part in range(2):
        cols = slice(part * half, part * half + half)
        query, key, value, up = (
            ref[:, cols] for ref in (query_ref, key_ref, value_ref, up_ref)
        )
        scores = jnp.where(allowed, product_nt(key, query) * scale, NEG_FILL)
        probs = jnp.exp(scores - jnp.max(scores, 0, keepdims=True))
        probs = probs / jnp.sum(probs, 0, keepdims=True)
        prob_grad = product_nt(value, up)
        delta = jnp.sum(probs * prob_grad, 0, keepdims=True)
        score_grad = lowered(probs * (prob_grad - delta))
        value_grad_ref[:, cols] = lowered(product(lowered(probs), up))
        key_grad_ref[:, cols] = lowered(product(score_grad, query) * scale)
        query_grad_ref[:, cols] = lowered(product_tn(score_grad, key) * scale)


def attend_back(start, queries, keys, values, upstream):
    rows, features = queries.shape
    count = keys.shape[0]
    width = 2 * features // HEADS
    own = pl.BlockSpec((rows, width), lambda i, s: (0, i))
    whole = pl.BlockSpec((count, width), lambda i, s: (0, i))
    return pl.pallas_call(
        attend_back_kernel,
        grid_spec=pltpu.PrefetchScalarGridSpec(
            num_scalar_prefetch=1,
            grid=(features // width,),
            in_specs=[own, whole, whole, own],
            out_specs=[own, whole, whole],
        ),
        out_shape=[
            jax.ShapeDtypeStruct((rows, features), jnp.bfloat16),
            jax.ShapeDtypeStruct((count, features), jnp.bfloat16),
            jax.ShapeDtypeStruct((count, features), jnp.bfloat16),
        ],
        compiler_params=pltpu.CompilerParams(vmem_limit_bytes=VMEM_BYTES),
        cost_estimate=pl.CostEstimate(
            flops=10 * rows * count * features,
            bytes_accessed=6 * (rows + count) * features,
            transcendentals=rows * count * HEADS,
        ),
        name="attend_back",
    )(start, queries, keys, values, upstream)


def pick_kernel(by_slot, index_ref, rows_ref, out_ref):
    count = rows_ref.shape[0]
    total = jnp.zeros(out_ref.shape, jnp.float32)
    base = pl.program_id(0) * BLOCK
    for at in range(0, count, BLOCK):
        if by_slot:
            place = base + lax.broadcasted_iota(jnp.int32, (BLOCK, BLOCK), 0)
            hit = index_ref[:, at : at + BLOCK] == place
        else:
            place = at + lax.broadcasted_iota(jnp.int32, (BLOCK, BLOCK), 1)
            hit = index_ref[...] == place
        onehot = lowered(jnp.where(hit, 1.0, 0.0))
        total = total + product(onehot, rows_ref[at : at + BLOCK, :])
    out_ref[...] = total.astype(out_ref.dtype)


def pick_rows(index, rows, out_count, by_slot, kind):
    count, width = rows.shape
    if by_slot:
        index = index.reshape(1, -1)
        index_spec = pl.BlockSpec(index.shape, lambda i: (0, 0))
    else:
        index = index.reshape(-1, 1)
        index_spec = pl.BlockSpec((BLOCK, 1), lambda i: (i, 0))
    return pl.pallas_call(
        functools.partial(pick_kernel, by_slot),
        grid=(out_count // BLOCK,),
        in_specs=[index_spec, pl.BlockSpec(rows.shape, lambda i: (0, 0), **ONCE)],
        out_specs=pl.BlockSpec((BLOCK, width), lambda i: (i, 0)),
        out_shape=jax.ShapeDtypeStruct((out_count, width), kind),
        compiler_params=pltpu.CompilerParams(vmem_limit_bytes=VMEM_BYTES),
        cost_estimate=pl.CostEstimate(
            flops=2 * out_count * count * max(width, 256),
            bytes_accessed=rows.size * 2 + out_count * width * 4,
            transcendentals=0,
        ),
        name="pick_rows",
    )(index, rows)


def band_kernel(chunk, per, words, sum_column, span_ref, rows_ref, table_ref, stat_ref, out_ref, mix_ref):
    step_id = pl.program_id(0)
    count, width = mix_ref.shape
    chunk_count = table_ref.shape[0] // chunk
    group_count = chunk_count // per
    active = (step_id >= span_ref[0]) & (step_id < span_ref[1])

    def put_stats(top, total):
        lane = lax.broadcasted_iota(jnp.int32, (count, 128), 1)
        both = jnp.where(lane == 0, top, jnp.where(lane == 1, total, 0.0))
        stat_ref[...] = both.T[:8, :]

    def logits_at(at, rows):
        return product_nt(rows, table_ref[pl.ds(at, chunk), :])

    def beyond(at, shape):
        return at + lax.broadcasted_iota(jnp.int32, shape, 1) >= words

    def run(rows, top):
        mix_ref[...] = jnp.zeros(mix_ref.shape, jnp.float32)

        def visit(group, total):
            for inner in range(per):
                at = (group * per + inner) * chunk
                checked = isinstance(at, int) and at + chunk > words
                if not isinstance(at, int):
                    at = pl.multiple_of(at, chunk)
                weights = jnp.exp(logits_at(at, rows) - top)
                if checked:
                    weights = jnp.where(beyond(at, weights.shape), 0.0, weights)
                if sum_column is None:
                    for lane in range(0, chunk, 128):
                        total = total + weights[:, lane : lane + 128]
                mix_ref[...] += product(lowered(weights), table_ref[pl.ds(at, chunk), :])
            return total

        lanes = jnp.zeros((count, 128), jnp.float32)
        lanes = visit(0, lanes) if group_count == 1 else lax.fori_loop(0, group_count, visit, lanes)
        if sum_column is None:
            return jnp.sum(lanes, 1, keepdims=True)
        return mix_ref[:, sum_column : sum_column + 1]

    @pl.when(active)
    def _():
        rows = rows_ref[...]
        first = product_nt(rows, table_ref[pl.ds(0, 128), :])
        top = jnp.max(first, 1, keepdims=True)
        total = run(rows, top)
        put_stats(top, total)

        @pl.when(jnp.logical_not(jnp.max(jnp.where(total < SAFE, 0.0, 1.0)) < 0.5))
        def _():
            def largest(index, top):
                at = pl.multiple_of(index * chunk, chunk)
                logits = logits_at(at, rows)
                if sum_column is None:
                    logits = jnp.where(beyond(at, logits.shape), NEG_FILL, logits)
                return jnp.maximum(top, jnp.max(logits, 1, keepdims=True))

            exact = lax.fori_loop(0, chunk_count, largest, jnp.full((count, 1), NEG_FILL))
            put_stats(exact, run(rows, exact))

        out_ref[...] = lowered(mix_ref[...])

    @pl.when(jnp.logical_not(active))
    def _():
        put_stats(jnp.full((count, 1), NEG_FILL), jnp.zeros((count, 1), jnp.float32))
        out_ref[...] = jnp.zeros(out_ref.shape, jnp.bfloat16)


def band_forward(span, rows, table, words, chunk, sum_column, share):
    count, width = rows.shape[0], table.shape[1]
    chunk_count = table.shape[0] // chunk
    per = chunk_count if chunk_count <= 4 else 4
    assert chunk_count % per == 0 and words >= 128
    return pl.pallas_call(
        functools.partial(band_kernel, chunk, per, words, sum_column),
        grid_spec=pltpu.PrefetchScalarGridSpec(
            num_scalar_prefetch=1,
            grid=(count // BLOCK,),
            in_specs=[
                pl.BlockSpec((BLOCK, width), lambda i, s: (i, 0)),
                pl.BlockSpec(table.shape, lambda i, s: (0, 0), **ONCE),
            ],
            out_specs=[
                pl.BlockSpec((8, BLOCK), lambda i, s: (0, i)),
                pl.BlockSpec((BLOCK, width), lambda i, s: (i, 0)),
            ],
            scratch_shapes=[pltpu.VMEM((BLOCK, width), jnp.float32)],
        ),
        out_shape=[
            jax.ShapeDtypeStruct((8, count), jnp.float32),
            jax.ShapeDtypeStruct((count, width), jnp.bfloat16),
        ],
        compiler_params=pltpu.CompilerParams(vmem_limit_bytes=VMEM_BYTES),
        cost_estimate=pl.CostEstimate(
            flops=int(share * 4 * count * table.shape[0] * max(width, 256)),
            bytes_accessed=table.size * 2 + count * width * 6,
            transcendentals=int(share * count * table.shape[0]),
        ),
        name="band_forward",
    )(span, rows, table)


def head_grad_kernel(chunk, lists, base_ref, table_ref, *refs):
    out_ref, sum_ref = refs[2 * lists :]
    words = table_ref.shape[0]
    base = base_ref[0] + pl.program_id(0) * words
    sum_ref[...] = jnp.zeros(sum_ref.shape, jnp.float32)
    for rows_ref, fact_ref in zip(refs[0 : 2 * lists : 2], refs[1 : 2 * lists : 2]):
        piece = min(rows_ref.shape[0], 1024)

        def visit(step, unused, rows_ref=rows_ref, fact_ref=fact_ref, piece=piece):
            at = pl.multiple_of(step * piece, piece)
            rows = rows_ref[pl.ds(at, piece), :]
            weight = fact_ref[0:1, pl.ds(at, piece)]
            total = fact_ref[1:2, pl.ds(at, piece)]
            ids = fact_ref[2:3, pl.ds(at, piece)].astype(jnp.int32)
            for start in range(0, words, chunk):
                probs = jnp.exp(product_nt(table_ref[start : start + chunk, :], rows) - total)
                word = base + start + lax.broadcasted_iota(jnp.int32, (chunk, 1), 0)
                grads = weight * (jnp.where(word == ids, 1.0, 0.0) - probs)
                sum_ref[start : start + chunk, :] += product(lowered(grads), rows)
            return unused

        lax.fori_loop(0, rows_ref.shape[0] // piece, visit, 0)
    out_ref[...] = lowered(sum_ref[...])


def head_grad(table, part, part_words, first_word, lists):
    width = table.shape[1]
    word_block = math.gcd(part_words, 640)
    steps = part_words // word_block
    chunk = word_block // 2 if word_block % 32 == 0 else word_block
    specs = []
    for rows, facts in lists:
        specs.append(pl.BlockSpec(rows.shape, lambda i, s: (0, 0), **ONCE))
        specs.append(pl.BlockSpec(facts.shape, lambda i, s: (0, 0), **ONCE))
    count = sum(rows.shape[0] for rows, facts in lists)
    scalars = jnp.stack([first_word + part * part_words, part * steps]).astype(jnp.int32)
    return pl.pallas_call(
        functools.partial(head_grad_kernel, chunk, len(lists)),
        grid_spec=pltpu.PrefetchScalarGridSpec(
            num_scalar_prefetch=1,
            grid=(steps,),
            in_specs=[pl.BlockSpec((word_block, width), lambda i, s: (s[1] + i, 0))] + specs,
            out_specs=pl.BlockSpec((word_block, width), lambda i, s: (i, 0)),
            scratch_shapes=[pltpu.VMEM((word_block, width), jnp.float32)],
        ),
        out_shape=jax.ShapeDtypeStruct((part_words, width), jnp.bfloat16),
        compiler_params=pltpu.CompilerParams(vmem_limit_bytes=VMEM_BYTES),
        cost_estimate=pl.CostEstimate(
            flops=4 * count * part_words * width,
            bytes_accessed=(count + part_words) * width * 2,
            transcendentals=count * part_words,
        ),
        name="head_grad",
    )(scalars, table, *[value for pair in lists for value in pair])


def band_grad_kernel(chunk, most, plan_ref, table_ref, rows_ref, fact_ref, out_ref, sum_ref):
    words = table_ref.shape[0]
    step_id = pl.program_id(0)
    base = plan_ref[most + 1] + step_id * words
    sum_ref[...] = jnp.zeros(sum_ref.shape, jnp.float32)

    def block_at(position):
        return pl.multiple_of(plan_ref[position] * BLOCK, BLOCK)

    def spread(starts):
        rows = [rows_ref[pl.ds(start, BLOCK), :] for start in starts]
        facts = [fact_ref[:, pl.ds(start, BLOCK)] for start in starts]
        rows = rows[0] if len(rows) == 1 else jnp.concatenate(rows, 0)
        facts = facts[0] if len(facts) == 1 else jnp.concatenate(facts, 1)
        weight, total = facts[0:1], facts[1:2]
        for start in range(0, words, chunk):
            probs = jnp.exp(product_nt(table_ref[start : start + chunk, :], rows) - total)
            sum_ref[start : start + chunk, :] -= product(lowered(weight * probs), rows)

    count = plan_ref[0]

    def pair(step, unused):
        spread([block_at(1 + 2 * step), block_at(2 + 2 * step)])
        return unused

    lax.fori_loop(0, count // 2, pair, 0)

    @pl.when(count % 2 == 1)
    def _():
        spread([block_at(count)])

    line = most + 2 + step_id * (most + 1)

    def hits(step, unused):
        at = block_at(line + 1 + step)
        rows = rows_ref[pl.ds(at, BLOCK), :]
        weight = fact_ref[0:1, pl.ds(at, BLOCK)]
        ids = fact_ref[2:3, pl.ds(at, BLOCK)].astype(jnp.int32)
        for start in range(0, words, chunk):
            word = base + start + lax.broadcasted_iota(jnp.int32, (chunk, 1), 0)
            chosen = lowered(jnp.where(word == ids, weight, 0.0))
            sum_ref[start : start + chunk, :] += product(chosen, rows)
        return unused

    lax.fori_loop(0, plan_ref[line], hits, 0)
    out_ref[...] = sum_ref[:, : out_ref.shape[1]].astype(out_ref.dtype)


def listed(flags):
    size = flags.shape[-1]
    order = jnp.cumsum(flags.astype(jnp.int32), -1)
    chosen = (order[..., None, :] == jnp.arange(1, size + 1)[:, None]) & flags[..., None, :]
    places = jnp.sum(jnp.where(chosen, jnp.arange(size), 0), -1)
    return jnp.concatenate([order[..., -1:], places], -1).astype(jnp.int32)


def band_grad(table, rows, facts, active, lowest, highest, part, part_words, first_word, width, chunk):
    count, full = rows.shape[0], table.shape[1]
    word_block = chunk
    steps = part_words // word_block
    most = count // BLOCK
    first = first_word + part * part_words
    low = first + jnp.arange(steps, dtype=jnp.int32)[:, None] * word_block
    step_hits = active[None, :] & (lowest[None, :] < low + word_block) & (highest[None, :] >= low)
    plan = jnp.concatenate(
        [
            listed(active),
            first.reshape(1).astype(jnp.int32),
            listed(step_hits).reshape(-1),
            (part * steps).reshape(1).astype(jnp.int32),
        ]
    )
    last = plan.shape[0] - 1
    return pl.pallas_call(
        functools.partial(band_grad_kernel, chunk // 2 if chunk > 832 else chunk, most),
        grid_spec=pltpu.PrefetchScalarGridSpec(
            num_scalar_prefetch=1,
            grid=(steps,),
            in_specs=[
                pl.BlockSpec((word_block, full), lambda i, s: (s[last] + i, 0)),
                pl.BlockSpec((count, full), lambda i, s: (0, 0), **ONCE),
                pl.BlockSpec(facts.shape, lambda i, s: (0, 0), **ONCE),
            ],
            out_specs=pl.BlockSpec((word_block, width), lambda i, s: (i, 0)),
            scratch_shapes=[pltpu.VMEM((word_block, full), jnp.float32)],
        ),
        out_shape=jax.ShapeDtypeStruct((part_words, width), jnp.bfloat16),
        compiler_params=pltpu.CompilerParams(vmem_limit_bytes=VMEM_BYTES),
        cost_estimate=pl.CostEstimate(
            flops=2 * count * part_words * 256,
            bytes_accessed=count * full * 2 + part_words * full * 4,
            transcendentals=count * part_words // 2,
        ),
        name="band_grad",
    )(plan, table, rows, facts)


def settle_kernel(
    member_ref,
    everyone_ref,
    fact_ref,
    head_mix_ref,
    middle_mix_ref,
    tail_mix_ref,
    head_hit_ref,
    middle_hit_ref,
    tail_hit_ref,
    term_ref,
    line_ref,
    slot_ref,
):
    step = pl.program_id(0)
    devices, _, slots = everyone_ref.shape
    tail_width = 64
    here = pl.ds(pl.multiple_of(step * BLOCK, BLOCK), BLOCK)

    def merged(read):
        lines = [read(device) for device in range(devices)]
        top = functools.reduce(jnp.maximum, [line[0] for line in lines])
        return top, sum(line[1] * jnp.exp(line[0] - top) for line in lines)

    head_top, head_sum = merged(
        lambda d: (everyone_ref[d, 0:1, here], everyone_ref[d, 1:2, here])
    )
    target = sum(everyone_ref[d, 2:3, here] for d in range(devices))
    slot_top, slot_sum = merged(lambda d: (everyone_ref[d, 3:4, :], everyone_ref[d, 4:5, :]))
    used = slot_sum > 0.0
    slot_total = jnp.where(used, slot_top + jnp.log(jnp.where(used, slot_sum, 1.0)), 0.0)
    member = member_ref[0]
    own_slot_top = jnp.where(used, everyone_ref[member, 3:4, :], 0.0)
    own_head_top = everyone_ref[member, 0:1, here]

    facts = fact_ref[...]
    slot, share, cotangent, first_cluster, second_cluster, band, word = (
        facts[index : index + 1] for index in range(7)
    )

    def as_columns(lines):
        square = jnp.concatenate(
            lines + [jnp.zeros((128 - len(lines), BLOCK), jnp.float32)], 0
        )
        return square.T

    def three(line):
        return [part.astype(jnp.float32) for part in thirds(line)]

    slot_column = as_columns([slot])[:, 0:1].astype(jnp.int32)
    hot = lowered(
        jnp.where(lax.broadcasted_iota(jnp.int32, (BLOCK, slots), 1) == slot_column, 1.0, 0.0)
    )
    lines = three(slot_total) + three(own_slot_top) + [jnp.zeros((10, slots), jnp.float32)]
    on_tokens = product_nt(lowered(jnp.concatenate(lines, 0)), hot)
    band_total = on_tokens[0:1] + on_tokens[1:2] + on_tokens[2:3]
    own_band_top = on_tokens[3:4] + on_tokens[4:5] + on_tokens[5:6]

    cluster_top = jnp.maximum(head_top, jnp.maximum(first_cluster, second_cluster))
    head_total = cluster_top + jnp.log(
        head_sum * jnp.exp(head_top - cluster_top)
        + jnp.exp(first_cluster - cluster_top)
        + jnp.exp(second_cluster - cluster_top)
    )
    in_head = band < 0.5
    cluster = jnp.where(band < 1.5, first_cluster, second_cluster)
    model_logp = target - head_total + jnp.where(in_head, 0.0, cluster - band_total)
    ratio = 0.25 * share * jnp.exp(-model_logp)
    weight = cotangent * 0.75 / (0.75 + ratio)
    head_scale = weight * jnp.exp(own_head_top - head_total)
    band_scale = weight * jnp.where(in_head, 0.0, jnp.exp(own_band_top - band_total))
    columns = as_columns([weight, head_scale, band_scale])
    weight_column, head_column, band_column = (columns[:, i : i + 1] for i in range(3))
    width = head_mix_ref.shape[1]
    term_ref[:, :width] = lowered(
        weight_column * head_hit_ref[...].astype(jnp.float32)
        - head_column * head_mix_ref[...].astype(jnp.float32)
    )
    narrow = tail_mix_ref.shape[1]
    kept = lax.broadcasted_iota(jnp.int32, (BLOCK, narrow), 1) < tail_width

    def widened(values):
        values = jnp.where(kept, values, 0.0)
        more = middle_mix_ref.shape[1] - narrow
        return jnp.concatenate([values, jnp.zeros((BLOCK, more), jnp.float32)], 1)

    band_mix = product(hot, middle_mix_ref[...]) + widened(product(hot, tail_mix_ref[...]))
    band_hit = middle_hit_ref[...].astype(jnp.float32) + widened(
        tail_hit_ref[...].astype(jnp.float32)
    )
    term_ref[:, width:] = lowered(weight_column * band_hit - band_column * band_mix)
    line_ref[...] = jnp.concatenate(
        [
            model_logp + jnp.log(0.75 + ratio),
            weight,
            head_total,
            word,
            jnp.zeros((4, BLOCK), jnp.float32),
        ],
        0,
    )

    @pl.when(step == 0)
    def _():
        slot_ref[...] = jnp.concatenate(
            [jnp.zeros((8, slots), jnp.float32), slot_total, jnp.zeros((7, slots), jnp.float32)], 0
        )

    sent = three(weight) + three(word) + [jnp.zeros((10, BLOCK), jnp.float32)]
    slot_ref[0:8, :] += product(lowered(jnp.concatenate(sent, 0)), hot)[0:8]


def settle(member, everyone, facts, head_mix, middle_mix, tail_mix, hits):
    count, width = head_mix.shape
    slots = middle_mix.shape[0]
    full = width + middle_mix.shape[1]

    def tokens(values):
        return pl.BlockSpec((BLOCK, values.shape[1]), lambda i, s: (i, 0))

    def whole(values):
        return pl.BlockSpec(values.shape, lambda i, s: (0,) * values.ndim, **ONCE)

    lines = pl.BlockSpec((8, BLOCK), lambda i, s: (0, i))
    return pl.pallas_call(
        settle_kernel,
        grid_spec=pltpu.PrefetchScalarGridSpec(
            num_scalar_prefetch=1,
            grid=(count // BLOCK,),
            in_specs=[whole(everyone), lines, tokens(head_mix), whole(middle_mix), whole(tail_mix)]
            + [tokens(hit) for hit in hits],
            out_specs=[
                pl.BlockSpec((BLOCK, full), lambda i, s: (i, 0)),
                lines,
                pl.BlockSpec((16, slots), lambda i, s: (0, 0)),
            ],
        ),
        out_shape=[
            jax.ShapeDtypeStruct((count, full), jnp.bfloat16),
            jax.ShapeDtypeStruct((8, count), jnp.float32),
            jax.ShapeDtypeStruct((16, slots), jnp.float32),
        ],
        compiler_params=pltpu.CompilerParams(vmem_limit_bytes=VMEM_BYTES),
        cost_estimate=pl.CostEstimate(
            flops=2 * count * slots * 1024,
            bytes_accessed=count * width * 12 + slots * full,
            transcendentals=slots * 64,
        ),
        name="settle",
    )(member.reshape(1).astype(jnp.int32), everyone, facts, head_mix, middle_mix, tail_mix, *hits)


def line_pieces(value, both=True):
    size = lax.axis_size("seq")
    before, behind = [value], [value]
    for step in range(1, size):
        before.append(
            lax.ppermute(before[-1], "seq", [(d, d + 1) for d in range(step - 1, size - 1)])
        )
        if both:
            behind.append(
                lax.ppermute(behind[-1], "seq", [(d, d - 1) for d in range(1, size - step + 1)])
            )
    return before, behind


def line_gather(value):
    size, place = lax.axis_size("seq"), lax.axis_index("seq")
    before, behind = line_pieces(value)
    return [value] + [
        jnp.where(place + k < size, behind[k], before[size - k]) for k in range(1, size)
    ]


def in_order(pieces):
    size, place = lax.axis_size("seq"), lax.axis_index("seq")
    joined = jnp.zeros((size,) + pieces[0].shape, pieces[0].dtype)
    for k, piece in enumerate(pieces):
        joined = lax.dynamic_update_index_in_dim(joined, piece, lax.rem(place + k, size), 0)
    return joined.reshape((-1,) + pieces[0].shape[1:])


def line_scatter(values, forward=True):
    size, place = lax.axis_size("seq"), lax.axis_index("seq")
    parts = values.reshape((size, -1) + values.shape[1:])

    def part(index):
        index = jnp.clip(index, 0, size - 1)
        return lax.dynamic_index_in_dim(parts, index, 0, False).astype(jnp.float32)

    ahead, back = 0.0, 0.0
    for step in range(1, size):
        if forward:
            sent = lowered(part(place + size - step) + ahead)
            ahead = lax.ppermute(sent, "seq", [(d, d + 1) for d in range(step)]).astype(jnp.float32)
        sent = lowered(part(place - size + step) + back)
        back = lax.ppermute(
            sent, "seq", [(d, d - 1) for d in range(size - step, size)]
        ).astype(jnp.float32)
    return part(place) + ahead + back


def line_sum(values):
    return in_order(line_gather(lowered(line_scatter(values)))).astype(jnp.float32)


def word_pad(rows, biggest, splits):
    chunk = min(biggest, round_up(rows, 128))
    chunks = -(-rows // chunk)
    if chunks > 4:
        chunks = round_up(chunks, 4)
    return chunk, chunks * chunk


def on_device(
    inputs,
    targets,
    neighbours,
    neighbour_scores,
    loglik_grad,
    first_gain,
    first_shift,
    query_weight,
    query_bias,
    key_weight,
    value_weight,
    value_bias,
    out_weight,
    out_bias,
    second_gain,
    second_shift,
    inner_weight,
    inner_bias,
    outer_weight,
    outer_bias,
    final_gain,
    final_shift,
    head_table,
    cluster_weight,
    middle_map,
    middle_table,
    tail_map,
    tail_table,
):
    nb = lax.axis_size("batch")
    nz = lax.axis_size("seq")
    member = lax.axis_index("batch")
    place = lax.axis_index("seq")
    tokens = inputs[0]
    own_ids = targets[0]
    token_count, feature_count = tokens.shape
    group_count = token_count * nb
    slot_count = group_count + BLOCK
    query_start = (place * token_count).reshape(1)

    normed_low = lowered(layer_norm(tokens, first_gain, first_shift))
    earlier, unused = line_pieces(normed_low, False)
    normed_parts = jnp.zeros((nz,) + normed_low.shape, jnp.bfloat16)
    for step in range(nz - 1, -1, -1):
        normed_parts = lax.dynamic_update_index_in_dim(
            normed_parts, earlier[step], jnp.maximum(place - step, 0), 0
        )
    normed_all = normed_parts.reshape(-1, feature_count)
    top_score = jnp.max(neighbour_scores[0], -1, keepdims=True)
    exponent = jnp.exp(neighbour_scores[0] - top_score)
    knn_prob = jnp.sum(jnp.where(neighbours[0] == 0, exponent, 0.0), -1) / jnp.sum(exponent, -1)
    early = jnp.stack([own_ids.astype(jnp.float32), knn_prob, loglik_grad[0]])
    early = lax.all_gather(early, "batch", axis=1, tiled=True)
    all_ids = early[0].astype(jnp.int32)
    all_knn, all_up = early[1], early[2]
    in_head = all_ids < HEAD_WORDS
    in_middle = (all_ids >= HEAD_WORDS) & (all_ids < HEAD_WORDS + MID_WORDS)
    in_tail = all_ids >= HEAD_WORDS + MID_WORDS
    order = jnp.arange(group_count, dtype=jnp.int32)
    ahead = (all_ids[None, :] < all_ids[:, None]) | (
        (all_ids[None, :] == all_ids[:, None]) & (order[None, :] < order[:, None])
    )
    rank = jnp.sum(ahead.astype(jnp.int32), -1)
    head_size = jnp.sum(in_head.astype(jnp.int32))
    middle_size = jnp.sum(in_middle.astype(jnp.int32))
    tail_size = group_count - head_size - middle_size
    middle_blocks = (middle_size + BLOCK - 1) // BLOCK
    tail_blocks = (tail_size + BLOCK - 1) // BLOCK
    slot = jnp.where(
        in_head,
        -1,
        rank - head_size + jnp.where(in_tail, middle_blocks * BLOCK - middle_size, 0),
    )
    zero_span = jnp.zeros((1,), jnp.int32)
    head_span = jnp.array([0, group_count // BLOCK], jnp.int32)
    middle_span = jnp.stack([0 * middle_blocks, middle_blocks]).astype(jnp.int32)
    tail_span = jnp.stack([middle_blocks, middle_blocks + tail_blocks]).astype(jnp.int32)
    slot_order = jnp.arange(slot_count, dtype=jnp.int32)
    slot_middle = slot_order < middle_size
    slot_tail = (slot_order >= middle_blocks * BLOCK) & (
        slot_order < middle_blocks * BLOCK + tail_size
    )
    slot_used = slot_middle | slot_tail
    band_id = all_ids - jnp.where(in_tail, HEAD_WORDS + MID_WORDS, HEAD_WORDS)

    tables = (head_table, middle_table, tail_table)
    sizes = tuple(table.shape[0] for table in tables)
    head_chunk, head_padded = word_pad(sizes[0], 1280, nz)
    middle_chunk, middle_padded = word_pad(sizes[1], 1280, nz)
    tail_chunk, tail_padded = word_pad(sizes[2], 1664, nz)
    tail_width = tail_table.shape[1]
    head_pad = jnp.pad(head_table, ((0, head_padded - sizes[0]), (0, 0)))
    middle_pad = jnp.pad(middle_table, ((0, middle_padded - sizes[1]), (0, 0)))
    tail_word = jnp.arange(tail_padded, dtype=jnp.int32)
    tail_bias = jnp.where(tail_word < jnp.minimum(TAIL_WORDS - member * sizes[2], sizes[2]), 0.0, NEG_FILL)
    tail_pad = jnp.concatenate(
        [
            jnp.pad(tail_table, ((0, tail_padded - sizes[2]), (0, 0))),
            jnp.ones((tail_padded, 1), jnp.bfloat16),
            lowered(tail_bias)[:, None],
            jnp.zeros((tail_padded, 126 - tail_width), jnp.bfloat16),
        ],
        1,
    )
    locals_ = (
        all_ids - member * sizes[0],
        all_ids - HEAD_WORDS - member * sizes[1],
        all_ids - HEAD_WORDS - MID_WORDS - member * sizes[2],
    )
    owned = tuple(
        inside & (local >= 0) & (local < size)
        for inside, local, size in zip((in_head, in_middle, in_tail), locals_, sizes)
    )
    hit_rows = tuple(
        jnp.where(
            own[:, None],
            jnp.take(table, jnp.clip(local, 0, size - 1), axis=0, mode="clip"),
            jnp.bfloat16(0),
        )
        for own, table, local, size in zip(owned, (head_pad, middle_pad, tail_pad), locals_, sizes)
    )

    queries = lowered(product(normed_low, query_weight) + query_bias)
    key_rows = lowered(product(normed_all, key_weight))
    value_rows = lowered(product(normed_all, value_weight) + value_bias)
    attended_low = attend(query_start, queries, key_rows, value_rows)
    mixed = tokens + product(attended_low, out_weight) + out_bias
    second_low = lowered(layer_norm(mixed, second_gain, second_shift))
    before = product(second_low, inner_weight) + inner_bias
    hidden_low = lowered(jax.nn.gelu(before))
    final = mixed + product(hidden_low, outer_weight) + outer_bias
    state_low = lowered(layer_norm(final, final_gain, final_shift))
    all_states = lax.all_gather(state_low, "batch", axis=0, tiled=True)

    middle_width = middle_map.shape[1]
    maps = jnp.pad(jnp.concatenate([middle_map, tail_map], 1), ((0, 0), (0, 128 - tail_width)))
    one_column = (jnp.arange(middle_width + 128) == middle_width + tail_width + 1).astype(jnp.float32)
    band_low = lowered(product(all_states, maps) + one_column)
    middle_low, tail_low = band_low[:, :middle_width], band_low[:, middle_width:]
    cluster_lines = product_nt(
        jnp.pad(cluster_weight.T, ((0, 6), (0, 0))), all_states
    )
    slot_full = pick_rows(slot, band_low, slot_count, True, jnp.bfloat16)
    first_tail = middle_blocks * BLOCK
    in_tail_slot = slot_order >= first_tail
    slot_low = jnp.where(
        in_tail_slot[:, None],
        jnp.pad(slot_full[:, middle_width:], ((0, 0), (0, middle_width - 128))),
        slot_full[:, :middle_width],
    )
    tail_stats, tail_mix = band_forward(
        tail_span, slot_low, tail_pad, tail_padded, tail_chunk, tail_width, 0.5
    )
    middle_stats, middle_mix = band_forward(
        middle_span, slot_low, middle_pad, sizes[1], middle_chunk, None, 0.25
    )
    head_stats, head_mix = band_forward(
        head_span, all_states, head_pad, sizes[0], head_chunk, None, 1.0
    )
    inner_lane = jnp.arange(128) < tail_width
    target_part = (
        jnp.sum(hit_rows[0].astype(jnp.float32) * all_states.astype(jnp.float32), -1)
        + jnp.sum(hit_rows[1].astype(jnp.float32) * middle_low.astype(jnp.float32), -1)
        + jnp.sum(
            jnp.where(inner_lane, hit_rows[2].astype(jnp.float32), 0.0)
            * tail_low.astype(jnp.float32),
            -1,
        )
    )
    slot_stats = jnp.where(in_tail_slot[None, :], tail_stats[:2], middle_stats[:2])
    extra = ((0, 0), (0, BLOCK))
    stats = jnp.concatenate(
        [
            jnp.pad(jnp.concatenate([head_stats[:2], target_part[None]], 0), extra),
            slot_stats,
            jnp.zeros((3, slot_count), jnp.float32),
        ],
        0,
    )
    everyone = lax.all_gather(stats, "batch")

    token_facts = jnp.concatenate(
        [
            slot.astype(jnp.float32)[None],
            early[1:3],
            cluster_lines[:2],
            jnp.where(in_head, 0.0, jnp.where(in_middle, 1.0, 2.0))[None],
            early[0:1],
            jnp.zeros((1, group_count), jnp.float32),
        ],
        0,
    )
    terms, lines, slot_lines = settle(
        member, everyone, token_facts, head_mix, middle_mix, tail_mix, hit_rows
    )
    own_terms = lax.psum_scatter(terms, "batch", scatter_dimension=0, tiled=True).astype(jnp.float32)

    def own_part(values):
        return lax.dynamic_slice_in_dim(values, member * token_count, token_count, 0)

    loglik = own_part(lines[0])

    split = 2 * nz * group_count * feature_count <= 24 << 20
    kind = jnp.where(slot_middle, 1.0, jnp.where(slot_tail, 2.0, 0.0))
    slot_facts = jnp.stack(
        [
            jnp.sum(slot_lines[0:3], 0),
            slot_lines[8],
            jnp.sum(slot_lines[3:6], 0),
            kind,
        ]
    )
    head_facts = jnp.concatenate([lines[1:4], jnp.zeros((1, group_count), jnp.float32)], 0)
    if split:
        piece = slot_count // nb
        slot_piece = lax.dynamic_slice_in_dim(slot_low, member * piece, piece, 0)
        other_states = jnp.concatenate(line_gather(state_low)[1:], 0)
        other_states = lax.all_gather(other_states, "batch", axis=0, tiled=True)
        other_slots = jnp.concatenate(line_gather(slot_piece)[1:], 0)
        other_slots = lax.all_gather(other_slots, "batch", axis=0, tiled=True)
        other_slots = (
            other_slots.reshape(nb, nz - 1, piece, middle_width)
            .transpose(1, 0, 2, 3)
            .reshape(-1, middle_width)
        )
        rows_all = jnp.concatenate([slot_low, other_slots], 0)
        fact_pieces = line_gather(jnp.concatenate([slot_facts, head_facts], 1))
        facts = jnp.concatenate([value[:, :slot_count] for value in fact_pieces], 1)
        other_facts = (
            jnp.stack([value[:, slot_count:] for value in fact_pieces[1:]], 1)
            .reshape(4, nz - 1, nb, token_count)
            .transpose(0, 2, 1, 3)
            .reshape(4, -1)
        )
        lists = [(all_states, head_facts), (other_states, other_facts)]
        part, parts = place, nz
    else:
        rows_all, facts, lists = slot_low, slot_facts, [(all_states, head_facts)]
        part, parts = 0 * place, 1
    head_part = head_grad(head_pad, part, head_padded // parts, member * sizes[0], lists)
    block_facts = facts[2:4].reshape(2, -1, BLOCK)
    block_kind = jnp.max(block_facts[1], -1)
    filled = block_facts[1] > 0
    lowest = jnp.min(jnp.where(filled, block_facts[0], 1e9), -1).astype(jnp.int32)
    highest = jnp.max(jnp.where(filled, block_facts[0], -1e9), -1).astype(jnp.int32)
    facts = jnp.concatenate(
        [facts[:2], jnp.where(facts[3:4] > 0, facts[2:3], -1e9), jnp.zeros_like(facts[:1])], 0
    )
    table_parts = [head_part]
    for band, table, padded, start, width, chunk in (
        (1, middle_pad, middle_padded, HEAD_WORDS, middle_width, middle_chunk),
        (2, tail_pad, tail_padded, HEAD_WORDS + MID_WORDS, tail_width, tail_chunk),
    ):
        part_words = padded // parts
        table_parts.append(
            band_grad(
                table,
                rows_all,
                facts,
                block_kind == band,
                lowest,
                highest,
                part,
                part_words,
                start + member * sizes[band],
                width,
                math.gcd(part_words, chunk),
            )
        )
    if split:
        table_sums = [in_order(line_gather(value)) for value in table_parts]
    else:
        table_sums = [lax.psum(value, "seq") for value in table_parts]
    head_table_grad, middle_table_grad, tail_table_grad = (
        value[:size].astype(jnp.float32) for value, size in zip(table_sums, sizes)
    )

    own_middle = own_part(in_middle)
    own_tail = own_part(in_tail)
    own_lines = lax.dynamic_slice_in_dim(lines, member * token_count, token_count, 1)
    own_weights, own_total = own_lines[1], own_lines[2]
    own_clusters = product(state_low, cluster_weight)
    band_state = own_terms[:, feature_count:]
    middle_state = lowered(jnp.where(own_middle[:, None], band_state, 0.0))
    tail_state = lowered(jnp.where(own_tail[:, None], band_state[:, :tail_width], 0.0))
    cluster_hit = jnp.stack([own_middle, own_tail], -1).astype(jnp.float32)
    cluster_grad = own_weights[:, None] * (
        cluster_hit - jnp.exp(own_clusters - own_total[:, None])
    )
    state_grad = (
        own_terms[:, :feature_count]
        + product_nt(middle_state, middle_map)
        + product_nt(tail_state, tail_map)
        + product_nt(cluster_grad, cluster_weight.astype(jnp.float32))
    )
    middle_map_grad = product_tn(state_low, middle_state)
    tail_map_rows = product_tn(tail_state, state_low)
    cluster_rows = product_tn(cluster_grad, state_low.astype(jnp.float32))
    final_grad, final_gain_grad, final_shift_grad = norm_back(
        final, final_gain, final_shift, state_grad
    )
    final_low = lowered(final_grad)
    outer_weight_grad = product_tn(hidden_low, final_low)
    outer_bias_grad = jnp.sum(final_grad, 0)
    outer_part = lax.psum_scatter(
        lowered(outer_weight_grad), "batch", scatter_dimension=0, tiled=True
    )
    before_grad = lowered(gelu_back(before, product_nt(final_low, outer_weight)))
    inner_weight_grad = product_tn(second_low, before_grad)
    inner_bias_grad = jnp.sum(before_grad.astype(jnp.float32), 0)
    inner_part = lax.psum_scatter(
        lowered(inner_weight_grad), "batch", scatter_dimension=0, tiled=True
    )
    second_in_grad, second_gain_grad, second_shift_grad = norm_back(
        mixed, second_gain, second_shift, product_nt(before_grad, inner_weight)
    )
    mixed_grad = final_grad + second_in_grad
    mixed_low = lowered(mixed_grad)
    out_weight_grad = product_tn(attended_low, mixed_low)
    out_bias_grad = jnp.sum(mixed_grad, 0)
    attended_grad = lowered(product_nt(mixed_low, out_weight))
    query_low, key_low, value_low = attend_back(
        query_start, queries, key_rows, value_rows, attended_grad
    )
    query_weight_grad = product_tn(normed_low, query_low)
    key_weight_grad = product_tn(normed_all, key_low)
    value_weight_grad = product_tn(normed_all, value_low)
    query_bias_grad = jnp.sum(query_low.astype(jnp.float32), 0)
    value_bias_grad = jnp.sum(value_low.astype(jnp.float32), 0)
    spread = product_nt(key_low, key_weight) + product_nt(value_low, value_weight)
    query_spread = product_nt(query_low, query_weight)
    first_shift_grad = jnp.sum(spread, 0) + jnp.sum(query_spread, 0)
    all_centred = (normed_all.astype(jnp.float32) - first_shift) / first_gain
    own_average = jnp.mean(tokens, -1, keepdims=True)
    own_spread = jnp.mean((tokens - own_average) ** 2, -1, keepdims=True)
    own_centred = (tokens - own_average) * lax.rsqrt(own_spread + EPSILON)
    first_gain_grad = jnp.sum(all_centred * spread, 0) + jnp.sum(own_centred * query_spread, 0)
    normed_grad = query_spread + line_scatter(lowered(spread), False)
    first_in_grad, unused, unused = norm_back(tokens, first_gain, first_shift, normed_grad)
    input_grad = mixed_grad + first_in_grad

    bias_rows = inner_bias_grad.shape[0] // feature_count
    inner_bias_rows = (
        inner_bias_grad.reshape(nb, bias_rows, -1).transpose(1, 0, 2).reshape(bias_rows, -1)
    )
    vectors = [
        first_gain_grad,
        first_shift_grad,
        query_bias_grad,
        value_bias_grad,
        out_bias_grad,
        second_gain_grad,
        second_shift_grad,
        outer_bias_grad,
        final_gain_grad,
        final_shift_grad,
    ]
    rows = [tail_map_rows, cluster_rows, inner_bias_rows] + [value[None] for value in vectors]
    edges = [0]
    for row in rows:
        edges.append(edges[-1] + row.shape[0])
    row_count = round_up(edges[-1], 128)
    rows.append(jnp.zeros((row_count - edges[-1], feature_count), jnp.float32))
    columns = [
        query_weight_grad,
        key_weight_grad,
        value_weight_grad,
        out_weight_grad,
        middle_map_grad,
        jnp.concatenate(rows, 0).T,
    ]
    rest_part = lax.psum_scatter(
        jnp.concatenate([lowered(column) for column in columns], 1),
        "batch",
        scatter_dimension=0,
        tiled=True,
    )
    outer_sum = line_sum(outer_part)
    inner_sum = line_sum(inner_part)
    rest_sum = lax.psum(rest_part, "seq").astype(jnp.float32)
    cut = [rest_sum[:, i * feature_count : (i + 1) * feature_count] for i in range(4)]
    middle_map_sum = rest_sum[:, 4 * feature_count : 4 * feature_count + middle_width]
    row_sum = rest_sum[:, 4 * feature_count + middle_width :].T
    tail_map_sum, cluster_sum, inner_bias_sum = (
        row_sum[low:high] for low, high in zip(edges[:3], edges[1:4])
    )
    lines = [row_sum[index] for index in range(edges[3], edges[3] + len(vectors))]
    return (
        loglik.reshape(1, token_count),
        input_grad.reshape(1, token_count, feature_count),
        lines[0],
        lines[1],
        cut[0],
        lines[2],
        cut[1],
        cut[2],
        lines[3],
        cut[3],
        lines[4],
        lines[5],
        lines[6],
        inner_sum,
        inner_bias_sum.reshape(-1),
        outer_sum,
        lines[7],
        lines[8],
        lines[9],
        head_table_grad,
        cluster_sum.T,
        middle_map_sum,
        middle_table_grad,
        tail_map_sum.T,
        tail_table_grad,
    )


def solution(mesh):
    return jax.shard_map(
        on_device,
        mesh=mesh,
        in_specs=(
            P("batch", "seq", None),
            P("batch", "seq"),
            P("batch", "seq", None),
            P("batch", "seq", None),
            P("batch", "seq"),
            P(),
            P(),
            P(),
            P(),
            P(),
            P(),
            P(),
            P(),
            P(),
            P(),
            P(),
            P(),
            P(),
            P(),
            P(),
            P(),
            P(),
            P("batch", None),
            P(),
            P(),
            P("batch", None),
            P(),
            P("batch", None),
        ),
        out_specs=(
            P("batch", "seq"),
            P("batch", "seq", None),
            P("batch"),
            P("batch"),
            P("batch", None),
            P("batch"),
            P("batch", None),
            P("batch", None),
            P("batch"),
            P("batch", None),
            P("batch"),
            P("batch"),
            P("batch"),
            P("batch", None),
            P("batch"),
            P("batch", None),
            P("batch"),
            P("batch"),
            P("batch"),
            P("batch", None),
            P("batch", None),
            P("batch", None),
            P("batch", None),
            P("batch", None),
            P("batch", None),
        ),
        check_vma=False,
    )
```

```python
import functools
import math

import jax
import jax.numpy as jnp
from jax import lax
from jax.experimental import pallas as pl
from jax.experimental.pallas import tpu as pltpu
from jax.sharding import PartitionSpec as P

HEADS = 16
HEAD_WORDS = 20000
MID_WORDS = 40000
TAIL_WORDS = 207735


NEG_FILL = -1e30
EPSILON = 1e-05
BLOCK = 256
SAFE = 1e30
VMEM_BYTES = 56 << 20
ONCE = dict(pipeline_mode=pl.Buffered(1))


def layer_norm(values, gain_vector, shift_vector):
    average = jnp.mean(values, -1, keepdims=True)
    centred = values - average
    spread = jnp.mean(centred * centred, -1, keepdims=True)
    return centred * lax.rsqrt(spread + EPSILON) * gain_vector + shift_vector


def norm_back(values, gain_vector, shift_vector, upstream):
    unused, pullback = jax.vjp(layer_norm, values, gain_vector, shift_vector)
    return pullback(upstream)


def gelu_back(before, upstream):
    unused, pullback = jax.vjp(jax.nn.gelu, before)
    return pullback(upstream)[0]


def product(former, latter):
    return jnp.dot(former, latter, preferred_element_type=jnp.float32)


def product_tn(former, latter):
    return lax.dot_general(
        former, latter, (((0,), (0,)), ((), ())), preferred_element_type=jnp.float32
    )


def product_nt(former, latter):
    return lax.dot_general(
        former, latter, (((1,), (1,)), ((), ())), preferred_element_type=jnp.float32
    )


def lowered(values):
    return values.astype(jnp.bfloat16)


def round_up(count, unit):
    return -(-count // unit) * unit


def thirds(values):
    high = lowered(values)
    rest = values - high.astype(jnp.float32)
    middle = lowered(rest)
    return [high, middle, lowered(rest - middle.astype(jnp.float32))]


def attend_kernel(start_ref, query_ref, key_ref, value_ref, out_ref):
    rows, keys = query_ref.shape[0], key_ref.shape[0]
    half = query_ref.shape[1] // 2
    query_pos = start_ref[0] + lax.broadcasted_iota(jnp.int32, (rows, keys), 0)
    allowed = lax.broadcasted_iota(jnp.int32, (rows, keys), 1) <= query_pos
    for part in range(2):
        cols = slice(part * half, part * half + half)
        scores = product_nt(query_ref[:, cols], key_ref[:, cols]) * half**-0.5
        scores = jnp.where(allowed, scores, NEG_FILL)
        weights = jnp.exp(scores - jnp.max(scores, 1, keepdims=True))
        weights = weights / jnp.sum(weights, 1, keepdims=True)
        out_ref[:, cols] = lowered(product(lowered(weights), value_ref[:, cols]))


def attend(start, queries, keys, values):
    rows, features = queries.shape
    width = 2 * features // HEADS
    own = pl.BlockSpec((rows, width), lambda i, s: (0, i))
    whole = pl.BlockSpec((keys.shape[0], width), lambda i, s: (0, i))
    return pl.pallas_call(
        attend_kernel,
        grid_spec=pltpu.PrefetchScalarGridSpec(
            num_scalar_prefetch=1,
            grid=(features // width,),
            in_specs=[own, whole, whole],
            out_specs=own,
        ),
        out_shape=jax.ShapeDtypeStruct((rows, features), jnp.bfloat16),
        compiler_params=pltpu.CompilerParams(vmem_limit_bytes=VMEM_BYTES),
        cost_estimate=pl.CostEstimate(
            flops=4 * rows * keys.shape[0] * features,
            bytes_accessed=4 * (rows + keys.shape[0]) * features,
            transcendentals=rows * keys.shape[0] * HEADS,
        ),
        name="attend",
    )(start, queries, keys, values)


def attend_back_kernel(
    start_ref, query_ref, key_ref, value_ref, up_ref, query_grad_ref, key_grad_ref, value_grad_ref
):
    rows, keys = query_ref.shape[0], key_ref.shape[0]
    half = query_ref.shape[1] // 2
    scale = half**-0.5
    query_pos = start_ref[0] + lax.broadcasted_iota(jnp.int32, (keys, rows), 1)
    allowed = lax.broadcasted_iota(jnp.int32, (keys, rows), 0) <= query_pos
    for part in range(2):
        cols = slice(part * half, part * half + half)
        query, key, value, up = (
            ref[:, cols] for ref in (query_ref, key_ref, value_ref, up_ref)
        )
        scores = jnp.where(allowed, product_nt(key, query) * scale, NEG_FILL)
        probs = jnp.exp(scores - jnp.max(scores, 0, keepdims=True))
        probs = probs / jnp.sum(probs, 0, keepdims=True)
        prob_grad = product_nt(value, up)
        delta = jnp.sum(probs * prob_grad, 0, keepdims=True)
        score_grad = lowered(probs * (prob_grad - delta))
        value_grad_ref[:, cols] = lowered(product(lowered(probs), up))
        key_grad_ref[:, cols] = lowered(product(score_grad, query) * scale)
        query_grad_ref[:, cols] = lowered(product_tn(score_grad, key) * scale)


def attend_back(start, queries, keys, values, upstream):
    rows, features = queries.shape
    count = keys.shape[0]
    width = 2 * features // HEADS
    own = pl.BlockSpec((rows, width), lambda i, s: (0, i))
    whole = pl.BlockSpec((count, width), lambda i, s: (0, i))
    return pl.pallas_call(
        attend_back_kernel,
        grid_spec=pltpu.PrefetchScalarGridSpec(
            num_scalar_prefetch=1,
            grid=(features // width,),
            in_specs=[own, whole, whole, own],
            out_specs=[own, whole, whole],
        ),
        out_shape=[
            jax.ShapeDtypeStruct((rows, features), jnp.bfloat16),
            jax.ShapeDtypeStruct((count, features), jnp.bfloat16),
            jax.ShapeDtypeStruct((count, features), jnp.bfloat16),
        ],
        compiler_params=pltpu.CompilerParams(vmem_limit_bytes=VMEM_BYTES),
        cost_estimate=pl.CostEstimate(
            flops=10 * rows * count * features,
            bytes_accessed=6 * (rows + count) * features,
            transcendentals=rows * count * HEADS,
        ),
        name="attend_back",
    )(start, queries, keys, values, upstream)


def pick_kernel(by_slot, index_ref, rows_ref, out_ref):
    count = rows_ref.shape[0]
    total = jnp.zeros(out_ref.shape, jnp.float32)
    base = pl.program_id(0) * BLOCK
    for at in range(0, count, BLOCK):
        if by_slot:
            place = base + lax.broadcasted_iota(jnp.int32, (BLOCK, BLOCK), 0)
            hit = index_ref[:, at : at + BLOCK] == place
        else:
            place = at + lax.broadcasted_iota(jnp.int32, (BLOCK, BLOCK), 1)
            hit = index_ref[...] == place
        onehot = lowered(jnp.where(hit, 1.0, 0.0))
        total = total + product(onehot, rows_ref[at : at + BLOCK, :])
    out_ref[...] = total.astype(out_ref.dtype)


def pick_rows(index, rows, out_count, by_slot, kind):
    count, width = rows.shape
    if by_slot:
        index = index.reshape(1, -1)
        index_spec = pl.BlockSpec(index.shape, lambda i: (0, 0))
    else:
        index = index.reshape(-1, 1)
        index_spec = pl.BlockSpec((BLOCK, 1), lambda i: (i, 0))
    return pl.pallas_call(
        functools.partial(pick_kernel, by_slot),
        grid=(out_count // BLOCK,),
        in_specs=[index_spec, pl.BlockSpec(rows.shape, lambda i: (0, 0), **ONCE)],
        out_specs=pl.BlockSpec((BLOCK, width), lambda i: (i, 0)),
        out_shape=jax.ShapeDtypeStruct((out_count, width), kind),
        compiler_params=pltpu.CompilerParams(vmem_limit_bytes=VMEM_BYTES),
        cost_estimate=pl.CostEstimate(
            flops=2 * out_count * count * max(width, 256),
            bytes_accessed=rows.size * 2 + out_count * width * 4,
            transcendentals=0,
        ),
        name="pick_rows",
    )(index, rows)


def band_kernel(chunk, per, words, sum_column, span_ref, rows_ref, table_ref, stat_ref, out_ref, mix_ref):
    step_id = pl.program_id(0)
    count, width = mix_ref.shape
    chunk_count = table_ref.shape[0] // chunk
    group_count = chunk_count // per
    active = (step_id >= span_ref[0]) & (step_id < span_ref[1])

    def put_stats(top, total):
        lane = lax.broadcasted_iota(jnp.int32, (count, 128), 1)
        both = jnp.where(lane == 0, top, jnp.where(lane == 1, total, 0.0))
        stat_ref[...] = both.T[:8, :]

    def logits_at(at, rows):
        return product_nt(rows, table_ref[pl.ds(at, chunk), :])

    def beyond(at, shape):
        return at + lax.broadcasted_iota(jnp.int32, shape, 1) >= words

    def run(rows, top):
        mix_ref[...] = jnp.zeros(mix_ref.shape, jnp.float32)

        def visit(group, total):
            for inner in range(per):
                at = (group * per + inner) * chunk
                checked = isinstance(at, int) and at + chunk > words
                if not isinstance(at, int):
                    at = pl.multiple_of(at, chunk)
                weights = jnp.exp(logits_at(at, rows) - top)
                if checked:
                    weights = jnp.where(beyond(at, weights.shape), 0.0, weights)
                if sum_column is None:
                    for lane in range(0, chunk, 128):
                        total = total + weights[:, lane : lane + 128]
                mix_ref[...] += product(lowered(weights), table_ref[pl.ds(at, chunk), :])
            return total

        lanes = jnp.zeros((count, 128), jnp.float32)
        lanes = visit(0, lanes) if group_count == 1 else lax.fori_loop(0, group_count, visit, lanes)
        if sum_column is None:
            return jnp.sum(lanes, 1, keepdims=True)
        return mix_ref[:, sum_column : sum_column + 1]

    @pl.when(active)
    def _():
        rows = rows_ref[...]
        first = product_nt(rows, table_ref[pl.ds(0, 128), :])
        top = jnp.max(first, 1, keepdims=True)
        total = run(rows, top)
        put_stats(top, total)

        @pl.when(jnp.logical_not(jnp.max(jnp.where(total < SAFE, 0.0, 1.0)) < 0.5))
        def _():
            def largest(index, top):
                at = pl.multiple_of(index * chunk, chunk)
                logits = logits_at(at, rows)
                if sum_column is None:
                    logits = jnp.where(beyond(at, logits.shape), NEG_FILL, logits)
                return jnp.maximum(top, jnp.max(logits, 1, keepdims=True))

            exact = lax.fori_loop(0, chunk_count, largest, jnp.full((count, 1), NEG_FILL))
            put_stats(exact, run(rows, exact))

        out_ref[...] = lowered(mix_ref[...])

    @pl.when(jnp.logical_not(active))
    def _():
        put_stats(jnp.full((count, 1), NEG_FILL), jnp.zeros((count, 1), jnp.float32))
        out_ref[...] = jnp.zeros(out_ref.shape, jnp.bfloat16)


def band_forward(span, rows, table, words, chunk, sum_column, share):
    count, width = rows.shape[0], table.shape[1]
    chunk_count = table.shape[0] // chunk
    per = chunk_count if chunk_count <= 4 else 4
    assert chunk_count % per == 0 and words >= 128
    return pl.pallas_call(
        functools.partial(band_kernel, chunk, per, words, sum_column),
        grid_spec=pltpu.PrefetchScalarGridSpec(
            num_scalar_prefetch=1,
            grid=(count // BLOCK,),
            in_specs=[
                pl.BlockSpec((BLOCK, width), lambda i, s: (i, 0)),
                pl.BlockSpec(table.shape, lambda i, s: (0, 0), **ONCE),
            ],
            out_specs=[
                pl.BlockSpec((8, BLOCK), lambda i, s: (0, i)),
                pl.BlockSpec((BLOCK, width), lambda i, s: (i, 0)),
            ],
            scratch_shapes=[pltpu.VMEM((BLOCK, width), jnp.float32)],
        ),
        out_shape=[
            jax.ShapeDtypeStruct((8, count), jnp.float32),
            jax.ShapeDtypeStruct((count, width), jnp.bfloat16),
        ],
        compiler_params=pltpu.CompilerParams(vmem_limit_bytes=VMEM_BYTES),
        cost_estimate=pl.CostEstimate(
            flops=int(share * 4 * count * table.shape[0] * max(width, 256)),
            bytes_accessed=table.size * 2 + count * width * 6,
            transcendentals=int(share * count * table.shape[0]),
        ),
        name="band_forward",
    )(span, rows, table)


def head_grad_kernel(chunk, lists, base_ref, table_ref, *refs):
    out_ref, sum_ref = refs[2 * lists :]
    words = table_ref.shape[0]
    base = base_ref[0] + pl.program_id(0) * words
    sum_ref[...] = jnp.zeros(sum_ref.shape, jnp.float32)
    for rows_ref, fact_ref in zip(refs[0 : 2 * lists : 2], refs[1 : 2 * lists : 2]):
        piece = min(rows_ref.shape[0], 1024)

        def visit(step, unused, rows_ref=rows_ref, fact_ref=fact_ref, piece=piece):
            at = pl.multiple_of(step * piece, piece)
            rows = rows_ref[pl.ds(at, piece), :]
            weight = fact_ref[0:1, pl.ds(at, piece)]
            total = fact_ref[1:2, pl.ds(at, piece)]
            ids = fact_ref[2:3, pl.ds(at, piece)].astype(jnp.int32)
            for start in range(0, words, chunk):
                probs = jnp.exp(product_nt(table_ref[start : start + chunk, :], rows) - total)
                word = base + start + lax.broadcasted_iota(jnp.int32, (chunk, 1), 0)
                grads = weight * (jnp.where(word == ids, 1.0, 0.0) - probs)
                sum_ref[start : start + chunk, :] += product(lowered(grads), rows)
            return unused

        lax.fori_loop(0, rows_ref.shape[0] // piece, visit, 0)
    out_ref[...] = lowered(sum_ref[...])


def head_grad(table, part, part_words, first_word, lists):
    width = table.shape[1]
    word_block = math.gcd(part_words, 640)
    steps = part_words // word_block
    chunk = word_block // 2 if word_block % 32 == 0 else word_block
    specs = []
    for rows, facts in lists:
        specs.append(pl.BlockSpec(rows.shape, lambda i, s: (0, 0), **ONCE))
        specs.append(pl.BlockSpec(facts.shape, lambda i, s: (0, 0), **ONCE))
    count = sum(rows.shape[0] for rows, facts in lists)
    scalars = jnp.stack([first_word + part * part_words, part * steps]).astype(jnp.int32)
    return pl.pallas_call(
        functools.partial(head_grad_kernel, chunk, len(lists)),
        grid_spec=pltpu.PrefetchScalarGridSpec(
            num_scalar_prefetch=1,
            grid=(steps,),
            in_specs=[pl.BlockSpec((word_block, width), lambda i, s: (s[1] + i, 0))] + specs,
            out_specs=pl.BlockSpec((word_block, width), lambda i, s: (i, 0)),
            scratch_shapes=[pltpu.VMEM((word_block, width), jnp.float32)],
        ),
        out_shape=jax.ShapeDtypeStruct((part_words, width), jnp.bfloat16),
        compiler_params=pltpu.CompilerParams(vmem_limit_bytes=VMEM_BYTES),
        cost_estimate=pl.CostEstimate(
            flops=4 * count * part_words * width,
            bytes_accessed=(count + part_words) * width * 2,
            transcendentals=count * part_words,
        ),
        name="head_grad",
    )(scalars, table, *[value for pair in lists for value in pair])


def band_grad_kernel(chunk, most, across, plan_ref, table_ref, rows_ref, fact_ref, out_ref, sum_ref):
    words = table_ref.shape[0]
    step_id = pl.program_id(0)
    base = plan_ref[most + 1] + step_id * words
    sum_ref[...] = jnp.zeros(sum_ref.shape, jnp.float32)

    def block_at(position):
        return pl.multiple_of(plan_ref[position] * BLOCK, BLOCK)

    def spread(starts):
        rows = [rows_ref[pl.ds(start, BLOCK), :] for start in starts]
        facts = [fact_ref[:, pl.ds(start, BLOCK)] for start in starts]
        rows = rows[0] if len(rows) == 1 else jnp.concatenate(rows, 0)
        facts = facts[0] if len(facts) == 1 else jnp.concatenate(facts, 1)
        weight, total = facts[0:1], facts[1:2]
        for start in range(0, words, chunk):
            probs = jnp.exp(product_nt(table_ref[start : start + chunk, :], rows) - total)
            sum_ref[start : start + chunk, :] -= product(lowered(weight * probs), rows)

    count = plan_ref[0]

    def pair(step, unused):
        spread([block_at(1 + 2 * step), block_at(2 + 2 * step)])
        return unused

    lax.fori_loop(0, count // 2, pair, 0)

    @pl.when(count % 2 == 1)
    def _():
        spread([block_at(count)])

    line = most + 2 + step_id * (most + 1)

    def hits(step, unused):
        at = block_at(line + 1 + step)
        rows = rows_ref[pl.ds(at, BLOCK), :]
        weight = fact_ref[0:1, pl.ds(at, BLOCK)]
        ids = fact_ref[2:3, pl.ds(at, BLOCK)].astype(jnp.int32)
        for start in range(0, words, chunk):
            word = base + start + lax.broadcasted_iota(jnp.int32, (chunk, 1), 0)
            chosen = lowered(jnp.where(word == ids, weight, 0.0))
            sum_ref[start : start + chunk, :] += product(chosen, rows)
        return unused

    lax.fori_loop(0, plan_ref[line], hits, 0)
    if across:
        out_ref[...] = sum_ref[...].T[: out_ref.shape[0], :].astype(out_ref.dtype)
    else:
        out_ref[...] = sum_ref[...].astype(out_ref.dtype)


def listed(flags):
    size = flags.shape[-1]
    order = jnp.cumsum(flags.astype(jnp.int32), -1)
    chosen = (order[..., None, :] == jnp.arange(1, size + 1)[:, None]) & flags[..., None, :]
    places = jnp.sum(jnp.where(chosen, jnp.arange(size), 0), -1)
    return jnp.concatenate([order[..., -1:], places], -1).astype(jnp.int32)


def band_grad(
    table, rows, facts, active, lowest, highest, part, part_words, first_word, chunk, result, across
):
    count, full = rows.shape[0], table.shape[1]
    word_block = chunk
    steps = part_words // word_block
    most = count // BLOCK
    first = first_word + part * part_words
    low = first + jnp.arange(steps, dtype=jnp.int32)[:, None] * word_block
    step_hits = active[None, :] & (lowest[None, :] < low + word_block) & (highest[None, :] >= low)
    plan = jnp.concatenate(
        [
            listed(active),
            first.reshape(1).astype(jnp.int32),
            listed(step_hits).reshape(-1),
            (part * steps).reshape(1).astype(jnp.int32),
        ]
    )
    last = plan.shape[0] - 1
    return pl.pallas_call(
        functools.partial(band_grad_kernel, chunk // 2 if chunk > 832 else chunk, most, across),
        grid_spec=pltpu.PrefetchScalarGridSpec(
            num_scalar_prefetch=1,
            grid=(steps,),
            in_specs=[
                pl.BlockSpec((word_block, full), lambda i, s: (s[last] + i, 0)),
                pl.BlockSpec((count, full), lambda i, s: (0, 0), **ONCE),
                pl.BlockSpec(facts.shape, lambda i, s: (0, 0), **ONCE),
            ],
            out_specs=(
                pl.BlockSpec((result.shape[0], word_block), lambda i, s: (0, i))
                if across
                else pl.BlockSpec((word_block, full), lambda i, s: (i, 0))
            ),
            scratch_shapes=[pltpu.VMEM((word_block, full), jnp.float32)],
        ),
        out_shape=result,
        compiler_params=pltpu.CompilerParams(vmem_limit_bytes=VMEM_BYTES),
        cost_estimate=pl.CostEstimate(
            flops=2 * count * part_words * 256,
            bytes_accessed=count * full * 2 + part_words * full * 4,
            transcendentals=count * part_words // 2,
        ),
        name="band_grad",
    )(plan, table, rows, facts)


def settle_kernel(
    member_ref,
    everyone_ref,
    fact_ref,
    head_mix_ref,
    middle_mix_ref,
    tail_mix_ref,
    head_hit_ref,
    middle_hit_ref,
    tail_hit_ref,
    term_ref,
    line_ref,
    slot_ref,
):
    step = pl.program_id(0)
    devices, _, slots = everyone_ref.shape
    tail_width = 64
    here = pl.ds(pl.multiple_of(step * BLOCK, BLOCK), BLOCK)

    def merged(read):
        lines = [read(device) for device in range(devices)]
        top = functools.reduce(jnp.maximum, [line[0] for line in lines])
        return top, sum(line[1] * jnp.exp(line[0] - top) for line in lines)

    head_top, head_sum = merged(
        lambda d: (everyone_ref[d, 0:1, here], everyone_ref[d, 1:2, here])
    )
    target = sum(everyone_ref[d, 2:3, here] for d in range(devices))
    slot_top, slot_sum = merged(lambda d: (everyone_ref[d, 3:4, :], everyone_ref[d, 4:5, :]))
    used = slot_sum > 0.0
    slot_total = jnp.where(used, slot_top + jnp.log(jnp.where(used, slot_sum, 1.0)), 0.0)
    member = member_ref[0]
    own_slot_top = jnp.where(used, everyone_ref[member, 3:4, :], 0.0)
    own_head_top = everyone_ref[member, 0:1, here]

    facts = fact_ref[...]
    slot, share, cotangent, first_cluster, second_cluster, band, word = (
        facts[index : index + 1] for index in range(7)
    )

    def as_columns(lines):
        square = jnp.concatenate(
            lines + [jnp.zeros((128 - len(lines), BLOCK), jnp.float32)], 0
        )
        return square.T

    def three(line):
        return [part.astype(jnp.float32) for part in thirds(line)]

    slot_column = as_columns([slot])[:, 0:1].astype(jnp.int32)
    hot = lowered(
        jnp.where(lax.broadcasted_iota(jnp.int32, (BLOCK, slots), 1) == slot_column, 1.0, 0.0)
    )
    lines = three(slot_total) + three(own_slot_top) + [jnp.zeros((10, slots), jnp.float32)]
    on_tokens = product_nt(lowered(jnp.concatenate(lines, 0)), hot)
    band_total = on_tokens[0:1] + on_tokens[1:2] + on_tokens[2:3]
    own_band_top = on_tokens[3:4] + on_tokens[4:5] + on_tokens[5:6]

    cluster_top = jnp.maximum(head_top, jnp.maximum(first_cluster, second_cluster))
    head_total = cluster_top + jnp.log(
        head_sum * jnp.exp(head_top - cluster_top)
        + jnp.exp(first_cluster - cluster_top)
        + jnp.exp(second_cluster - cluster_top)
    )
    in_head = band < 0.5
    cluster = jnp.where(band < 1.5, first_cluster, second_cluster)
    model_logp = target - head_total + jnp.where(in_head, 0.0, cluster - band_total)
    ratio = 0.25 * share * jnp.exp(-model_logp)
    weight = cotangent * 0.75 / (0.75 + ratio)
    head_scale = weight * jnp.exp(own_head_top - head_total)
    band_scale = weight * jnp.where(in_head, 0.0, jnp.exp(own_band_top - band_total))
    columns = as_columns([weight, head_scale, band_scale])
    weight_column, head_column, band_column = (columns[:, i : i + 1] for i in range(3))
    width = head_mix_ref.shape[1]
    term_ref[:, :width] = lowered(
        weight_column * head_hit_ref[...].astype(jnp.float32)
        - head_column * head_mix_ref[...].astype(jnp.float32)
    )
    narrow = tail_mix_ref.shape[1]
    kept = lax.broadcasted_iota(jnp.int32, (BLOCK, narrow), 1) < tail_width

    def widened(values):
        values = jnp.where(kept, values, 0.0)
        more = middle_mix_ref.shape[1] - narrow
        return jnp.concatenate([values, jnp.zeros((BLOCK, more), jnp.float32)], 1)

    band_mix = product(hot, middle_mix_ref[...]) + widened(product(hot, tail_mix_ref[...]))
    band_hit = middle_hit_ref[...].astype(jnp.float32) + widened(
        tail_hit_ref[...].astype(jnp.float32)
    )
    term_ref[:, width:] = lowered(weight_column * band_hit - band_column * band_mix)
    line_ref[...] = jnp.concatenate(
        [
            model_logp + jnp.log(0.75 + ratio),
            weight,
            head_total,
            word,
            jnp.zeros((4, BLOCK), jnp.float32),
        ],
        0,
    )

    @pl.when(step == 0)
    def _():
        slot_ref[...] = jnp.concatenate(
            [jnp.zeros((8, slots), jnp.float32), slot_total, jnp.zeros((7, slots), jnp.float32)], 0
        )

    sent = three(weight) + three(word) + [jnp.zeros((10, BLOCK), jnp.float32)]
    slot_ref[0:8, :] += product(lowered(jnp.concatenate(sent, 0)), hot)[0:8]


def settle(member, everyone, facts, head_mix, middle_mix, tail_mix, hits):
    count, width = head_mix.shape
    slots = middle_mix.shape[0]
    full = width + middle_mix.shape[1]

    def tokens(values):
        return pl.BlockSpec((BLOCK, values.shape[1]), lambda i, s: (i, 0))

    def whole(values):
        return pl.BlockSpec(values.shape, lambda i, s: (0,) * values.ndim, **ONCE)

    lines = pl.BlockSpec((8, BLOCK), lambda i, s: (0, i))
    return pl.pallas_call(
        settle_kernel,
        grid_spec=pltpu.PrefetchScalarGridSpec(
            num_scalar_prefetch=1,
            grid=(count // BLOCK,),
            in_specs=[whole(everyone), lines, tokens(head_mix), whole(middle_mix), whole(tail_mix)]
            + [tokens(hit) for hit in hits],
            out_specs=[
                pl.BlockSpec((BLOCK, full), lambda i, s: (i, 0)),
                lines,
                pl.BlockSpec((16, slots), lambda i, s: (0, 0)),
            ],
        ),
        out_shape=[
            jax.ShapeDtypeStruct((count, full), jnp.bfloat16),
            jax.ShapeDtypeStruct((8, count), jnp.float32),
            jax.ShapeDtypeStruct((16, slots), jnp.float32),
        ],
        compiler_params=pltpu.CompilerParams(vmem_limit_bytes=VMEM_BYTES),
        cost_estimate=pl.CostEstimate(
            flops=2 * count * slots * 1024,
            bytes_accessed=count * width * 12 + slots * full,
            transcendentals=slots * 64,
        ),
        name="settle",
    )(member.reshape(1).astype(jnp.int32), everyone, facts, head_mix, middle_mix, tail_mix, *hits)


def line_gather(value, direct):
    size, place = lax.axis_size("seq"), lax.axis_index("seq")
    if direct:
        return [value] + [
            lax.ppermute(value, "seq", [(d, (d - k) % size) for d in range(size)])
            for k in range(1, size)
        ]
    before, behind = [value], [value]
    for step in range(1, size):
        before.append(
            lax.ppermute(before[-1], "seq", [(d, d + 1) for d in range(step - 1, size - 1)])
        )
        behind.append(
            lax.ppermute(behind[-1], "seq", [(d, d - 1) for d in range(1, size - step + 1)])
        )
    return [value] + [
        jnp.where(place + k < size, behind[k], before[size - k]) for k in range(1, size)
    ]


def earlier_joined(value):
    size, place = lax.axis_size("seq"), lax.axis_index("seq")
    joined = jnp.zeros((size,) + value.shape, value.dtype)
    for step in range(size - 1, -1, -1):
        piece = value
        if step:
            piece = lax.ppermute(value, "seq", [(d, d + step) for d in range(size - step)])
        joined = lax.dynamic_update_index_in_dim(joined, piece, jnp.maximum(place - step, 0), 0)
    return joined.reshape((-1,) + value.shape[1:])


def in_order(pieces):
    size, place = lax.axis_size("seq"), lax.axis_index("seq")
    joined = jnp.zeros((size,) + pieces[0].shape, pieces[0].dtype)
    for k, piece in enumerate(pieces):
        joined = lax.dynamic_update_index_in_dim(joined, piece, lax.rem(place + k, size), 0)
    return joined.reshape((-1,) + pieces[0].shape[1:])


def line_scatter(values, behind=True):
    size, place = lax.axis_size("seq"), lax.axis_index("seq")
    parts = values.reshape((size, -1) + values.shape[1:])

    def part(index):
        return lax.dynamic_index_in_dim(parts, lax.rem(index, size), 0, False)

    total = part(place).astype(jnp.float32)
    for k in range(1, size):
        pairs = [(d, (d - k) % size) for d in range(0 if behind else k, size)]
        total = total + lax.ppermute(part(place + size - k), "seq", pairs).astype(jnp.float32)
    return total


def line_sum(values):
    return in_order(line_gather(lowered(line_scatter(values)), True)).astype(jnp.float32)


def turn_kernel(rows_ref, out_ref):
    out_ref[...] = rows_ref[...].astype(jnp.float32).T.astype(out_ref.dtype)


def turned(rows, kind):
    return pl.pallas_call(
        turn_kernel, out_shape=jax.ShapeDtypeStruct(rows.shape[::-1], kind), name="turned"
    )(rows)


def word_pad(rows, biggest, splits):
    chunk = min(biggest, round_up(rows, 128))
    chunks = -(-rows // chunk)
    if chunks > 4:
        chunks = round_up(chunks, 4)
    return chunk, chunks * chunk


def on_device(
    inputs,
    targets,
    neighbours,
    neighbour_scores,
    loglik_grad,
    first_gain,
    first_shift,
    query_weight,
    query_bias,
    key_weight,
    value_weight,
    value_bias,
    out_weight,
    out_bias,
    second_gain,
    second_shift,
    inner_weight,
    inner_bias,
    outer_weight,
    outer_bias,
    final_gain,
    final_shift,
    head_table,
    cluster_weight,
    middle_map,
    middle_table,
    tail_map,
    tail_table,
):
    nb = lax.axis_size("batch")
    nz = lax.axis_size("seq")
    member = lax.axis_index("batch")
    place = lax.axis_index("seq")
    tokens = inputs[0]
    own_ids = targets[0]
    token_count, feature_count = tokens.shape
    group_count = token_count * nb
    slot_count = group_count + BLOCK
    query_start = (place * token_count).reshape(1)

    normed_low = lowered(layer_norm(tokens, first_gain, first_shift))
    normed_all = earlier_joined(normed_low)
    top_score = jnp.max(neighbour_scores[0], -1, keepdims=True)
    exponent = jnp.exp(neighbour_scores[0] - top_score)
    knn_prob = jnp.sum(jnp.where(neighbours[0] == 0, exponent, 0.0), -1) / jnp.sum(exponent, -1)
    early = jnp.stack([own_ids.astype(jnp.float32), knn_prob, loglik_grad[0]])
    early = lax.all_gather(early, "batch", axis=1, tiled=True)
    all_ids = early[0].astype(jnp.int32)
    all_knn, all_up = early[1], early[2]
    in_head = all_ids < HEAD_WORDS
    in_middle = (all_ids >= HEAD_WORDS) & (all_ids < HEAD_WORDS + MID_WORDS)
    in_tail = all_ids >= HEAD_WORDS + MID_WORDS
    order = jnp.arange(group_count, dtype=jnp.int32)
    ahead = (all_ids[None, :] < all_ids[:, None]) | (
        (all_ids[None, :] == all_ids[:, None]) & (order[None, :] < order[:, None])
    )
    rank = jnp.sum(ahead.astype(jnp.int32), -1)
    head_size = jnp.sum(in_head.astype(jnp.int32))
    middle_size = jnp.sum(in_middle.astype(jnp.int32))
    tail_size = group_count - head_size - middle_size
    middle_blocks = (middle_size + BLOCK - 1) // BLOCK
    tail_blocks = (tail_size + BLOCK - 1) // BLOCK
    slot = jnp.where(
        in_head,
        -1,
        rank - head_size + jnp.where(in_tail, middle_blocks * BLOCK - middle_size, 0),
    )
    zero_span = jnp.zeros((1,), jnp.int32)
    head_span = jnp.array([0, group_count // BLOCK], jnp.int32)
    middle_span = jnp.stack([0 * middle_blocks, middle_blocks]).astype(jnp.int32)
    tail_span = jnp.stack([middle_blocks, middle_blocks + tail_blocks]).astype(jnp.int32)
    slot_order = jnp.arange(slot_count, dtype=jnp.int32)
    slot_middle = slot_order < middle_size
    slot_tail = (slot_order >= middle_blocks * BLOCK) & (
        slot_order < middle_blocks * BLOCK + tail_size
    )
    slot_used = slot_middle | slot_tail
    band_id = all_ids - jnp.where(in_tail, HEAD_WORDS + MID_WORDS, HEAD_WORDS)

    tables = (head_table, middle_table, tail_table)
    sizes = tuple(table.shape[0] for table in tables)
    head_chunk, head_padded = word_pad(sizes[0], 1280, nz)
    middle_chunk, middle_padded = word_pad(sizes[1], 1280, nz)
    tail_chunk, tail_padded = word_pad(sizes[2], 1664, nz)
    tail_width = tail_table.shape[1]
    head_pad = jnp.pad(head_table, ((0, head_padded - sizes[0]), (0, 0)))
    middle_pad = jnp.pad(middle_table, ((0, middle_padded - sizes[1]), (0, 0)))
    tail_word = jnp.arange(tail_padded, dtype=jnp.int32)
    tail_bias = jnp.where(tail_word < jnp.minimum(TAIL_WORDS - member * sizes[2], sizes[2]), 0.0, NEG_FILL)
    tail_pad = jnp.concatenate(
        [
            jnp.pad(tail_table.T, ((0, 0), (0, tail_padded - sizes[2]))),
            jnp.ones((1, tail_padded), jnp.bfloat16),
            lowered(tail_bias)[None, :],
            jnp.zeros((126 - tail_width, tail_padded), jnp.bfloat16),
        ],
        0,
    ).T
    locals_ = (
        all_ids - member * sizes[0],
        all_ids - HEAD_WORDS - member * sizes[1],
        all_ids - HEAD_WORDS - MID_WORDS - member * sizes[2],
    )
    owned = tuple(
        inside & (local >= 0) & (local < size)
        for inside, local, size in zip((in_head, in_middle, in_tail), locals_, sizes)
    )
    hit_rows = tuple(
        jnp.where(
            own[:, None],
            jnp.take(table, jnp.clip(local, 0, size - 1), axis=0, mode="clip"),
            jnp.bfloat16(0),
        )
        for own, table, local, size in zip(owned, (head_pad, middle_pad, tail_pad), locals_, sizes)
    )

    queries = lowered(product(normed_low, query_weight) + query_bias)
    key_rows = lowered(product(normed_all, key_weight))
    value_rows = lowered(product(normed_all, value_weight) + value_bias)
    attended_low = attend(query_start, queries, key_rows, value_rows)
    mixed = tokens + product(attended_low, out_weight) + out_bias
    second_low = lowered(layer_norm(mixed, second_gain, second_shift))
    before = product(second_low, inner_weight) + inner_bias
    hidden_low = lowered(jax.nn.gelu(before))
    final = mixed + product(hidden_low, outer_weight) + outer_bias
    state_low = lowered(layer_norm(final, final_gain, final_shift))
    all_states = lax.all_gather(state_low, "batch", axis=0, tiled=True)
    split = 2 * nz * group_count * feature_count <= 24 << 20
    if split:
        other_states = jnp.concatenate(line_gather(state_low, True)[1:], 0)
        all_states, other_states = lax.optimization_barrier((all_states, other_states))
        other_states = lax.all_gather(other_states, "batch", axis=0, tiled=True)

    middle_width = middle_map.shape[1]
    maps = jnp.pad(jnp.concatenate([middle_map, tail_map], 1), ((0, 0), (0, 128 - tail_width)))
    one_column = (jnp.arange(middle_width + 128) == middle_width + tail_width + 1).astype(jnp.float32)
    band_low = lowered(product(all_states, maps) + one_column)
    middle_low, tail_low = band_low[:, :middle_width], band_low[:, middle_width:]
    cluster_lines = product_nt(
        jnp.pad(cluster_weight.T, ((0, 6), (0, 0))), all_states
    )
    slot_full = pick_rows(slot, band_low, slot_count, True, jnp.bfloat16)
    first_tail = middle_blocks * BLOCK
    in_tail_slot = slot_order >= first_tail
    slot_low = jnp.where(
        in_tail_slot[:, None],
        jnp.pad(slot_full[:, middle_width:], ((0, 0), (0, middle_width - 128))),
        slot_full[:, :middle_width],
    )
    if split:
        piece = slot_count // nb
        slot_piece = lax.dynamic_slice_in_dim(slot_low, member * piece, piece, 0)
        other_slots = jnp.concatenate(line_gather(slot_piece, True)[1:], 0)
    tail_stats, tail_mix = band_forward(
        tail_span, slot_low, tail_pad, tail_padded, tail_chunk, tail_width, 0.5
    )
    middle_stats, middle_mix = band_forward(
        middle_span, slot_low, middle_pad, sizes[1], middle_chunk, None, 0.25
    )
    if split:
        all_states, other_states, other_slots, tail_stats, middle_stats = lax.optimization_barrier(
            (all_states, other_states, other_slots, tail_stats, middle_stats)
        )
        other_slots = lax.all_gather(other_slots, "batch", axis=0, tiled=True)
    head_stats, head_mix = band_forward(
        head_span, all_states, head_pad, sizes[0], head_chunk, None, 1.0
    )
    inner_lane = jnp.arange(128) < tail_width
    target_part = (
        jnp.sum(hit_rows[0].astype(jnp.float32) * all_states.astype(jnp.float32), -1)
        + jnp.sum(hit_rows[1].astype(jnp.float32) * middle_low.astype(jnp.float32), -1)
        + jnp.sum(
            jnp.where(inner_lane, hit_rows[2].astype(jnp.float32), 0.0)
            * tail_low.astype(jnp.float32),
            -1,
        )
    )
    slot_stats = jnp.where(in_tail_slot[None, :], tail_stats[:2], middle_stats[:2])
    extra = ((0, 0), (0, BLOCK))
    stats = jnp.concatenate(
        [
            jnp.pad(jnp.concatenate([head_stats[:2], target_part[None]], 0), extra),
            slot_stats,
            jnp.zeros((3, slot_count), jnp.float32),
        ],
        0,
    )
    if split:
        stats, other_states, other_slots = lax.optimization_barrier(
            (stats, other_states, other_slots)
        )
    everyone = lax.all_gather(stats, "batch")

    token_facts = jnp.concatenate(
        [
            slot.astype(jnp.float32)[None],
            early[1:3],
            cluster_lines[:2],
            jnp.where(in_head, 0.0, jnp.where(in_middle, 1.0, 2.0))[None],
            early[0:1],
            jnp.zeros((1, group_count), jnp.float32),
        ],
        0,
    )
    terms, lines, slot_lines = settle(
        member, everyone, token_facts, head_mix, middle_mix, tail_mix, hit_rows
    )
    own_terms = lax.psum_scatter(terms, "batch", scatter_dimension=0, tiled=True).astype(jnp.float32)

    def own_part(values):
        return lax.dynamic_slice_in_dim(values, member * token_count, token_count, 0)

    loglik = own_part(lines[0])

    kind = jnp.where(slot_middle, 1.0, jnp.where(slot_tail, 2.0, 0.0))
    slot_facts = jnp.stack(
        [
            jnp.sum(slot_lines[0:3], 0),
            slot_lines[8],
            jnp.sum(slot_lines[3:6], 0),
            kind,
        ]
    )
    head_facts = jnp.concatenate([lines[1:4], jnp.zeros((1, group_count), jnp.float32)], 0)
    if split:
        other_slots = (
            other_slots.reshape(nb, nz - 1, piece, middle_width)
            .transpose(1, 0, 2, 3)
            .reshape(-1, middle_width)
        )
        rows_all = jnp.concatenate([slot_low, other_slots], 0)
        fact_pieces = line_gather(jnp.concatenate([slot_facts, head_facts], 1), True)
        facts = jnp.concatenate([value[:, :slot_count] for value in fact_pieces], 1)
        other_facts = (
            jnp.stack([value[:, slot_count:] for value in fact_pieces[1:]], 1)
            .reshape(4, nz - 1, nb, token_count)
            .transpose(0, 2, 1, 3)
            .reshape(4, -1)
        )
        lists = [(all_states, head_facts), (other_states, other_facts)]
        part, parts = place, nz
    else:
        rows_all, facts, lists = slot_low, slot_facts, [(all_states, head_facts)]
        part, parts = 0 * place, 1
    head_part = head_grad(head_pad, part, head_padded // parts, member * sizes[0], lists)
    block_facts = facts[2:4].reshape(2, -1, BLOCK)
    block_kind = jnp.max(block_facts[1], -1)
    filled = block_facts[1] > 0
    lowest = jnp.min(jnp.where(filled, block_facts[0], 1e9), -1).astype(jnp.int32)
    highest = jnp.max(jnp.where(filled, block_facts[0], -1e9), -1).astype(jnp.int32)
    facts = jnp.concatenate(
        [facts[:2], jnp.where(facts[3:4] > 0, facts[2:3], -1e9), jnp.zeros_like(facts[:1])], 0
    )
    tail_part = band_grad(
        tail_pad,
        rows_all,
        facts,
        block_kind == 2,
        lowest,
        highest,
        part,
        tail_padded // parts,
        HEAD_WORDS + MID_WORDS + member * sizes[2],
        math.gcd(tail_padded // parts, tail_chunk),
        jax.ShapeDtypeStruct((tail_width, tail_padded // parts), jnp.bfloat16),
        True,
    )
    if split:
        head_pieces = line_gather(head_part, True)
        own_terms, tail_part, head_pieces[1] = lax.optimization_barrier(
            (own_terms, tail_part, head_pieces[1])
        )
        tail_pieces = line_gather(tail_part[None], True)
    else:
        own_terms, tail_part = lax.optimization_barrier((own_terms, tail_part))

    own_middle = own_part(in_middle)
    own_tail = own_part(in_tail)
    own_lines = lax.dynamic_slice_in_dim(lines, member * token_count, token_count, 1)
    own_weights, own_total = own_lines[1], own_lines[2]
    own_clusters = product(state_low, cluster_weight)
    band_state = own_terms[:, feature_count:]
    middle_state = lowered(jnp.where(own_middle[:, None], band_state, 0.0))
    tail_state = lowered(jnp.where(own_tail[:, None], band_state[:, :tail_width], 0.0))
    cluster_hit = jnp.stack([own_middle, own_tail], -1).astype(jnp.float32)
    cluster_grad = own_weights[:, None] * (
        cluster_hit - jnp.exp(own_clusters - own_total[:, None])
    )
    state_grad = (
        own_terms[:, :feature_count]
        + product_nt(middle_state, middle_map)
        + product_nt(tail_state, tail_map)
        + product_nt(cluster_grad, cluster_weight.astype(jnp.float32))
    )
    middle_map_grad = product_tn(state_low, middle_state)
    tail_map_rows = product_tn(tail_state, state_low)
    cluster_rows = product_tn(cluster_grad, state_low.astype(jnp.float32))
    final_grad, final_gain_grad, final_shift_grad = norm_back(
        final, final_gain, final_shift, state_grad
    )
    final_low = lowered(final_grad)
    outer_weight_grad = product_tn(hidden_low, final_low)
    outer_bias_grad = jnp.sum(final_grad, 0)
    outer_part = lax.psum_scatter(
        lowered(outer_weight_grad), "batch", scatter_dimension=0, tiled=True
    )
    before_grad = lowered(gelu_back(before, product_nt(final_low, outer_weight)))
    inner_weight_grad = product_tn(second_low, before_grad)
    inner_bias_grad = jnp.sum(before_grad.astype(jnp.float32), 0)
    inner_part = lax.psum_scatter(
        lowered(inner_weight_grad), "batch", scatter_dimension=0, tiled=True
    )
    second_in_grad, second_gain_grad, second_shift_grad = norm_back(
        mixed, second_gain, second_shift, product_nt(before_grad, inner_weight)
    )
    mixed_grad = final_grad + second_in_grad
    mixed_low = lowered(mixed_grad)
    out_weight_grad = product_tn(attended_low, mixed_low)
    out_bias_grad = jnp.sum(mixed_grad, 0)
    attended_grad = lowered(product_nt(mixed_low, out_weight))
    if split:
        attended_grad, head_pieces[-1] = lax.optimization_barrier((attended_grad, head_pieces[-1]))
    query_low, key_low, value_low = attend_back(
        query_start, queries, key_rows, value_rows, attended_grad
    )
    if split:
        query_low, *head_pieces = lax.optimization_barrier((query_low, *head_pieces))
    query_weight_grad = product_tn(normed_low, query_low)
    key_weight_grad = product_tn(normed_all, key_low)
    value_weight_grad = product_tn(normed_all, value_low)
    query_bias_grad = jnp.sum(query_low.astype(jnp.float32), 0)
    value_bias_grad = jnp.sum(value_low.astype(jnp.float32), 0)
    spread = product_nt(key_low, key_weight) + product_nt(value_low, value_weight)
    query_spread = product_nt(query_low, query_weight)
    first_shift_grad = jnp.sum(spread, 0) + jnp.sum(query_spread, 0)
    all_centred = (normed_all.astype(jnp.float32) - first_shift) / first_gain
    own_average = jnp.mean(tokens, -1, keepdims=True)
    own_spread = jnp.mean((tokens - own_average) ** 2, -1, keepdims=True)
    own_centred = (tokens - own_average) * lax.rsqrt(own_spread + EPSILON)
    first_gain_grad = jnp.sum(all_centred * spread, 0) + jnp.sum(own_centred * query_spread, 0)
    normed_grad = query_spread + line_scatter(lowered(spread), False)
    first_in_grad, unused, unused = norm_back(tokens, first_gain, first_shift, normed_grad)
    input_grad = mixed_grad + first_in_grad

    bias_rows = inner_bias_grad.shape[0] // feature_count
    inner_bias_rows = (
        inner_bias_grad.reshape(nb, bias_rows, -1).transpose(1, 0, 2).reshape(bias_rows, -1)
    )
    vectors = [
        first_gain_grad,
        first_shift_grad,
        query_bias_grad,
        value_bias_grad,
        out_bias_grad,
        second_gain_grad,
        second_shift_grad,
        outer_bias_grad,
        final_gain_grad,
        final_shift_grad,
    ]
    rows = [tail_map_rows, cluster_rows, inner_bias_rows] + [value[None] for value in vectors]
    edges = [0]
    for row in rows:
        edges.append(edges[-1] + row.shape[0])
    row_count = round_up(edges[-1], 128)
    rows.append(jnp.zeros((row_count - edges[-1], feature_count), jnp.float32))
    columns = [
        query_weight_grad,
        key_weight_grad,
        value_weight_grad,
        out_weight_grad,
        middle_map_grad,
        turned(jnp.concatenate(rows, 0), jnp.bfloat16),
    ]
    rest = jnp.concatenate([lowered(column) for column in columns], 1)
    rest, facts = lax.optimization_barrier((rest, facts))
    if split:
        rest, tail_pieces[1], tail_pieces[-1] = lax.optimization_barrier(
            (rest, tail_pieces[1], tail_pieces[-1])
        )
    rest_part = lax.psum_scatter(rest, "batch", scatter_dimension=0, tiled=True)
    middle_result = jax.ShapeDtypeStruct(
        (sizes[1], middle_width) if split else (middle_padded, middle_width),
        jnp.float32 if split else jnp.bfloat16,
    )
    middle_part = band_grad(
        middle_pad,
        rows_all,
        facts,
        block_kind == 1,
        lowest,
        highest,
        0 * place,
        middle_padded,
        HEAD_WORDS + member * sizes[1],
        middle_chunk,
        middle_result,
        False,
    )
    if split:
        middle_table_grad = middle_part
        head_table_grad = in_order(head_pieces)
        tail_sum = in_order(tail_pieces)
        tail_sum = tail_sum.transpose(1, 0, 2).reshape(tail_width, -1)
    else:
        middle_table_grad = lax.psum(middle_part, "seq")[: sizes[1]].astype(jnp.float32)
        head_table_grad = lax.psum(head_part, "seq")
        tail_sum = lax.psum(tail_part, "seq")
    head_table_grad = head_table_grad[: sizes[0]].astype(jnp.float32)
    tail_table_grad = tail_sum[:, : sizes[2]].astype(jnp.float32).T
    outer_sum = line_sum(outer_part)
    inner_sum = line_sum(inner_part)
    rest_low = lax.psum(rest_part, "seq")
    rest_sum = rest_low[:, : 4 * feature_count + middle_width].astype(jnp.float32)
    cut = [rest_sum[:, i * feature_count : (i + 1) * feature_count] for i in range(4)]
    middle_map_sum = rest_sum[:, 4 * feature_count : 4 * feature_count + middle_width]
    row_sum = turned(rest_low[:, 4 * feature_count + middle_width :], jnp.float32)
    tail_map_sum, cluster_sum, inner_bias_sum = (
        row_sum[low:high] for low, high in zip(edges[:3], edges[1:4])
    )
    lines = [row_sum[index] for index in range(edges[3], edges[3] + len(vectors))]
    return (
        loglik.reshape(1, token_count),
        input_grad.reshape(1, token_count, feature_count),
        lines[0],
        lines[1],
        cut[0],
        lines[2],
        cut[1],
        cut[2],
        lines[3],
        cut[3],
        lines[4],
        lines[5],
        lines[6],
        inner_sum,
        inner_bias_sum.reshape(-1),
        outer_sum,
        lines[7],
        lines[8],
        lines[9],
        head_table_grad,
        cluster_sum.T,
        middle_map_sum,
        middle_table_grad,
        tail_map_sum.T,
        tail_table_grad,
    )


def solution(mesh):
    return jax.shard_map(
        on_device,
        mesh=mesh,
        in_specs=(
            P("batch", "seq", None),
            P("batch", "seq"),
            P("batch", "seq", None),
            P("batch", "seq", None),
            P("batch", "seq"),
            P(),
            P(),
            P(),
            P(),
            P(),
            P(),
            P(),
            P(),
            P(),
            P(),
            P(),
            P(),
            P(),
            P(),
            P(),
            P(),
            P(),
            P("batch", None),
            P(),
            P(),
            P("batch", None),
            P(),
            P("batch", None),
        ),
        out_specs=(
            P("batch", "seq"),
            P("batch", "seq", None),
            P("batch"),
            P("batch"),
            P("batch", None),
            P("batch"),
            P("batch", None),
            P("batch", None),
            P("batch"),
            P("batch", None),
            P("batch"),
            P("batch"),
            P("batch"),
            P("batch", None),
            P("batch"),
            P("batch", None),
            P("batch"),
            P("batch"),
            P("batch"),
            P("batch", None),
            P("batch", None),
            P("batch", None),
            P("batch", None),
            P("batch", None),
            P("batch", None),
        ),
        check_vma=False,
    )
```

```python
import functools
import math

import jax
import jax.numpy as jnp
from jax import lax
from jax.experimental import pallas as pl
from jax.experimental.pallas import tpu as pltpu
from jax.sharding import PartitionSpec as P

HEADS = 16
HEAD_WORDS = 20000
MID_WORDS = 40000
TAIL_WORDS = 207735


NEG_FILL = -1e30
EPSILON = 1e-05
BLOCK = 256
SAFE = 1e30
VMEM_BYTES = 56 << 20
ONCE = dict(pipeline_mode=pl.Buffered(1))


def layer_norm(values, gain_vector, shift_vector):
    average = jnp.mean(values, -1, keepdims=True)
    centred = values - average
    spread = jnp.mean(centred * centred, -1, keepdims=True)
    return centred * lax.rsqrt(spread + EPSILON) * gain_vector + shift_vector


def norm_back(values, gain_vector, shift_vector, upstream):
    unused, pullback = jax.vjp(layer_norm, values, gain_vector, shift_vector)
    return pullback(upstream)


def gelu_back(before, upstream):
    unused, pullback = jax.vjp(jax.nn.gelu, before)
    return pullback(upstream)[0]


def product(former, latter):
    return jnp.dot(former, latter, preferred_element_type=jnp.float32)


def product_tn(former, latter):
    return lax.dot_general(
        former, latter, (((0,), (0,)), ((), ())), preferred_element_type=jnp.float32
    )


def product_nt(former, latter):
    return lax.dot_general(
        former, latter, (((1,), (1,)), ((), ())), preferred_element_type=jnp.float32
    )


def lowered(values):
    return values.astype(jnp.bfloat16)


def round_up(count, unit):
    return -(-count // unit) * unit


def thirds(values):
    high = lowered(values)
    rest = values - high.astype(jnp.float32)
    middle = lowered(rest)
    return [high, middle, lowered(rest - middle.astype(jnp.float32))]


def attend_kernel(start_ref, query_ref, key_ref, value_ref, out_ref):
    rows, keys = query_ref.shape[0], key_ref.shape[0]
    half = query_ref.shape[1] // 2
    query_pos = start_ref[0] + lax.broadcasted_iota(jnp.int32, (rows, keys), 0)
    allowed = lax.broadcasted_iota(jnp.int32, (rows, keys), 1) <= query_pos
    for part in range(2):
        cols = slice(part * half, part * half + half)
        scores = product_nt(query_ref[:, cols], key_ref[:, cols]) * half**-0.5
        scores = jnp.where(allowed, scores, NEG_FILL)
        weights = jnp.exp(scores - jnp.max(scores, 1, keepdims=True))
        weights = weights / jnp.sum(weights, 1, keepdims=True)
        out_ref[:, cols] = lowered(product(lowered(weights), value_ref[:, cols]))


def attend(start, queries, keys, values):
    rows, features = queries.shape
    width = 2 * features // HEADS
    own = pl.BlockSpec((rows, width), lambda i, s: (0, i))
    whole = pl.BlockSpec((keys.shape[0], width), lambda i, s: (0, i))
    return pl.pallas_call(
        attend_kernel,
        grid_spec=pltpu.PrefetchScalarGridSpec(
            num_scalar_prefetch=1,
            grid=(features // width,),
            in_specs=[own, whole, whole],
            out_specs=own,
        ),
        out_shape=jax.ShapeDtypeStruct((rows, features), jnp.bfloat16),
        compiler_params=pltpu.CompilerParams(vmem_limit_bytes=VMEM_BYTES),
        cost_estimate=pl.CostEstimate(
            flops=4 * rows * keys.shape[0] * features,
            bytes_accessed=4 * (rows + keys.shape[0]) * features,
            transcendentals=rows * keys.shape[0] * HEADS,
        ),
        name="attend",
    )(start, queries, keys, values)


def attend_back_kernel(
    start_ref, query_ref, key_ref, value_ref, up_ref, query_grad_ref, key_grad_ref, value_grad_ref
):
    rows, keys = query_ref.shape[0], key_ref.shape[0]
    half = query_ref.shape[1] // 2
    scale = half**-0.5
    query_pos = start_ref[0] + lax.broadcasted_iota(jnp.int32, (keys, rows), 1)
    allowed = lax.broadcasted_iota(jnp.int32, (keys, rows), 0) <= query_pos
    for part in range(2):
        cols = slice(part * half, part * half + half)
        query, key, value, up = (
            ref[:, cols] for ref in (query_ref, key_ref, value_ref, up_ref)
        )
        scores = jnp.where(allowed, product_nt(key, query) * scale, NEG_FILL)
        probs = jnp.exp(scores - jnp.max(scores, 0, keepdims=True))
        probs = probs / jnp.sum(probs, 0, keepdims=True)
        prob_grad = product_nt(value, up)
        delta = jnp.sum(probs * prob_grad, 0, keepdims=True)
        score_grad = lowered(probs * (prob_grad - delta))
        value_grad_ref[:, cols] = lowered(product(lowered(probs), up))
        key_grad_ref[:, cols] = lowered(product(score_grad, query) * scale)
        query_grad_ref[:, cols] = lowered(product_tn(score_grad, key) * scale)


def attend_back(start, queries, keys, values, upstream):
    rows, features = queries.shape
    count = keys.shape[0]
    width = 2 * features // HEADS
    own = pl.BlockSpec((rows, width), lambda i, s: (0, i))
    whole = pl.BlockSpec((count, width), lambda i, s: (0, i))
    return pl.pallas_call(
        attend_back_kernel,
        grid_spec=pltpu.PrefetchScalarGridSpec(
            num_scalar_prefetch=1,
            grid=(features // width,),
            in_specs=[own, whole, whole, own],
            out_specs=[own, whole, whole],
        ),
        out_shape=[
            jax.ShapeDtypeStruct((rows, features), jnp.bfloat16),
            jax.ShapeDtypeStruct((count, features), jnp.bfloat16),
            jax.ShapeDtypeStruct((count, features), jnp.bfloat16),
        ],
        compiler_params=pltpu.CompilerParams(vmem_limit_bytes=VMEM_BYTES),
        cost_estimate=pl.CostEstimate(
            flops=10 * rows * count * features,
            bytes_accessed=6 * (rows + count) * features,
            transcendentals=rows * count * HEADS,
        ),
        name="attend_back",
    )(start, queries, keys, values, upstream)


def pick_kernel(by_slot, index_ref, rows_ref, out_ref):
    count = rows_ref.shape[0]
    total = jnp.zeros(out_ref.shape, jnp.float32)
    base = pl.program_id(0) * BLOCK
    for at in range(0, count, BLOCK):
        if by_slot:
            place = base + lax.broadcasted_iota(jnp.int32, (BLOCK, BLOCK), 0)
            hit = index_ref[:, at : at + BLOCK] == place
        else:
            place = at + lax.broadcasted_iota(jnp.int32, (BLOCK, BLOCK), 1)
            hit = index_ref[...] == place
        onehot = lowered(jnp.where(hit, 1.0, 0.0))
        total = total + product(onehot, rows_ref[at : at + BLOCK, :])
    out_ref[...] = total.astype(out_ref.dtype)


def pick_rows(index, rows, out_count, by_slot, kind):
    count, width = rows.shape
    if by_slot:
        index = index.reshape(1, -1)
        index_spec = pl.BlockSpec(index.shape, lambda i: (0, 0))
    else:
        index = index.reshape(-1, 1)
        index_spec = pl.BlockSpec((BLOCK, 1), lambda i: (i, 0))
    return pl.pallas_call(
        functools.partial(pick_kernel, by_slot),
        grid=(out_count // BLOCK,),
        in_specs=[index_spec, pl.BlockSpec(rows.shape, lambda i: (0, 0), **ONCE)],
        out_specs=pl.BlockSpec((BLOCK, width), lambda i: (i, 0)),
        out_shape=jax.ShapeDtypeStruct((out_count, width), kind),
        compiler_params=pltpu.CompilerParams(vmem_limit_bytes=VMEM_BYTES),
        cost_estimate=pl.CostEstimate(
            flops=2 * out_count * count * max(width, 256),
            bytes_accessed=rows.size * 2 + out_count * width * 4,
            transcendentals=0,
        ),
        name="pick_rows",
    )(index, rows)


def band_kernel(chunk, per, words, sum_column, span_ref, rows_ref, table_ref, stat_ref, out_ref, mix_ref):
    step_id = pl.program_id(0)
    count, width = mix_ref.shape
    chunk_count = table_ref.shape[0] // chunk
    group_count = chunk_count // per
    active = (step_id >= span_ref[0]) & (step_id < span_ref[1])

    def put_stats(top, total):
        lane = lax.broadcasted_iota(jnp.int32, (count, 128), 1)
        both = jnp.where(lane == 0, top, jnp.where(lane == 1, total, 0.0))
        stat_ref[...] = both.T[:8, :]

    def logits_at(at, rows):
        return product_nt(rows, table_ref[pl.ds(at, chunk), :])

    def beyond(at, shape):
        return at + lax.broadcasted_iota(jnp.int32, shape, 1) >= words

    def run(rows, top):
        mix_ref[...] = jnp.zeros(mix_ref.shape, jnp.float32)

        def visit(group, total):
            for inner in range(per):
                at = (group * per + inner) * chunk
                checked = isinstance(at, int) and at + chunk > words
                if not isinstance(at, int):
                    at = pl.multiple_of(at, chunk)
                weights = jnp.exp(logits_at(at, rows) - top)
                if checked:
                    weights = jnp.where(beyond(at, weights.shape), 0.0, weights)
                if sum_column is None:
                    for lane in range(0, chunk, 128):
                        total = total + weights[:, lane : lane + 128]
                mix_ref[...] += product(lowered(weights), table_ref[pl.ds(at, chunk), :])
            return total

        lanes = jnp.zeros((count, 128), jnp.float32)
        lanes = visit(0, lanes) if group_count == 1 else lax.fori_loop(0, group_count, visit, lanes)
        if sum_column is None:
            return jnp.sum(lanes, 1, keepdims=True)
        return mix_ref[:, sum_column : sum_column + 1]

    @pl.when(active)
    def _():
        rows = rows_ref[...]
        first = product_nt(rows, table_ref[pl.ds(0, 128), :])
        top = jnp.max(first, 1, keepdims=True)
        total = run(rows, top)
        put_stats(top, total)

        @pl.when(jnp.logical_not(jnp.max(jnp.where(total < SAFE, 0.0, 1.0)) < 0.5))
        def _():
            def largest(index, top):
                at = pl.multiple_of(index * chunk, chunk)
                logits = logits_at(at, rows)
                if sum_column is None:
                    logits = jnp.where(beyond(at, logits.shape), NEG_FILL, logits)
                return jnp.maximum(top, jnp.max(logits, 1, keepdims=True))

            exact = lax.fori_loop(0, chunk_count, largest, jnp.full((count, 1), NEG_FILL))
            put_stats(exact, run(rows, exact))

        out_ref[...] = lowered(mix_ref[...])

    @pl.when(jnp.logical_not(active))
    def _():
        put_stats(jnp.full((count, 1), NEG_FILL), jnp.zeros((count, 1), jnp.float32))
        out_ref[...] = jnp.zeros(out_ref.shape, jnp.bfloat16)


def band_forward(span, rows, table, words, chunk, sum_column, share):
    count, width = rows.shape[0], table.shape[1]
    chunk_count = table.shape[0] // chunk
    per = chunk_count if chunk_count <= 4 else 4
    assert chunk_count % per == 0 and words >= 128
    return pl.pallas_call(
        functools.partial(band_kernel, chunk, per, words, sum_column),
        grid_spec=pltpu.PrefetchScalarGridSpec(
            num_scalar_prefetch=1,
            grid=(count // BLOCK,),
            in_specs=[
                pl.BlockSpec((BLOCK, width), lambda i, s: (i, 0)),
                pl.BlockSpec(table.shape, lambda i, s: (0, 0), **ONCE),
            ],
            out_specs=[
                pl.BlockSpec((8, BLOCK), lambda i, s: (0, i)),
                pl.BlockSpec((BLOCK, width), lambda i, s: (i, 0)),
            ],
            scratch_shapes=[pltpu.VMEM((BLOCK, width), jnp.float32)],
        ),
        out_shape=[
            jax.ShapeDtypeStruct((8, count), jnp.float32),
            jax.ShapeDtypeStruct((count, width), jnp.bfloat16),
        ],
        compiler_params=pltpu.CompilerParams(vmem_limit_bytes=VMEM_BYTES),
        cost_estimate=pl.CostEstimate(
            flops=int(share * 4 * count * table.shape[0] * max(width, 256)),
            bytes_accessed=table.size * 2 + count * width * 6,
            transcendentals=int(share * count * table.shape[0]),
        ),
        name="band_forward",
    )(span, rows, table)


def head_grad_kernel(chunk, lists, base_ref, table_ref, *refs):
    out_ref, sum_ref = refs[2 * lists :]
    words = table_ref.shape[0]
    base = base_ref[0] + pl.program_id(0) * words
    sum_ref[...] = jnp.zeros(sum_ref.shape, jnp.float32)
    for rows_ref, fact_ref in zip(refs[0 : 2 * lists : 2], refs[1 : 2 * lists : 2]):
        piece = min(rows_ref.shape[0], 1024)

        def visit(step, unused, rows_ref=rows_ref, fact_ref=fact_ref, piece=piece):
            at = pl.multiple_of(step * piece, piece)
            rows = rows_ref[pl.ds(at, piece), :]
            weight = fact_ref[0:1, pl.ds(at, piece)]
            total = fact_ref[1:2, pl.ds(at, piece)]
            ids = fact_ref[2:3, pl.ds(at, piece)].astype(jnp.int32)
            for start in range(0, words, chunk):
                probs = jnp.exp(product_nt(table_ref[start : start + chunk, :], rows) - total)
                word = base + start + lax.broadcasted_iota(jnp.int32, (chunk, 1), 0)
                grads = weight * (jnp.where(word == ids, 1.0, 0.0) - probs)
                sum_ref[start : start + chunk, :] += product(lowered(grads), rows)
            return unused

        lax.fori_loop(0, rows_ref.shape[0] // piece, visit, 0)
    out_ref[...] = lowered(sum_ref[...])


def head_grad(table, part, part_words, first_word, lists):
    width = table.shape[1]
    word_block = math.gcd(part_words, 640)
    steps = part_words // word_block
    chunk = word_block // 2 if word_block % 32 == 0 else word_block
    specs = []
    for rows, facts in lists:
        specs.append(pl.BlockSpec(rows.shape, lambda i, s: (0, 0), **ONCE))
        specs.append(pl.BlockSpec(facts.shape, lambda i, s: (0, 0), **ONCE))
    count = sum(rows.shape[0] for rows, facts in lists)
    scalars = jnp.stack([first_word + part * part_words, part * steps]).astype(jnp.int32)
    return pl.pallas_call(
        functools.partial(head_grad_kernel, chunk, len(lists)),
        grid_spec=pltpu.PrefetchScalarGridSpec(
            num_scalar_prefetch=1,
            grid=(steps,),
            in_specs=[pl.BlockSpec((word_block, width), lambda i, s: (s[1] + i, 0))] + specs,
            out_specs=pl.BlockSpec((word_block, width), lambda i, s: (i, 0)),
            scratch_shapes=[pltpu.VMEM((word_block, width), jnp.float32)],
        ),
        out_shape=jax.ShapeDtypeStruct((part_words, width), jnp.bfloat16),
        compiler_params=pltpu.CompilerParams(vmem_limit_bytes=VMEM_BYTES),
        cost_estimate=pl.CostEstimate(
            flops=4 * count * part_words * width,
            bytes_accessed=(count + part_words) * width * 2,
            transcendentals=count * part_words,
        ),
        name="head_grad",
    )(scalars, table, *[value for pair in lists for value in pair])


def band_grad_kernel(chunk, most, across, plan_ref, table_ref, rows_ref, fact_ref, out_ref, sum_ref):
    words = table_ref.shape[0]
    step_id = pl.program_id(0)
    base = plan_ref[most + 1] + step_id * words
    sum_ref[...] = jnp.zeros(sum_ref.shape, jnp.float32)

    def block_at(position):
        return pl.multiple_of(plan_ref[position] * BLOCK, BLOCK)

    def spread(starts):
        rows = [rows_ref[pl.ds(start, BLOCK), :] for start in starts]
        facts = [fact_ref[:, pl.ds(start, BLOCK)] for start in starts]
        rows = rows[0] if len(rows) == 1 else jnp.concatenate(rows, 0)
        facts = facts[0] if len(facts) == 1 else jnp.concatenate(facts, 1)
        weight, total = facts[0:1], facts[1:2]
        for start in range(0, words, chunk):
            probs = jnp.exp(product_nt(table_ref[start : start + chunk, :], rows) - total)
            sum_ref[start : start + chunk, :] -= product(lowered(weight * probs), rows)

    count = plan_ref[0]

    def pair(step, unused):
        spread([block_at(1 + 2 * step), block_at(2 + 2 * step)])
        return unused

    lax.fori_loop(0, count // 2, pair, 0)

    @pl.when(count % 2 == 1)
    def _():
        spread([block_at(count)])

    line = most + 2 + step_id * (most + 1)

    def hits(step, unused):
        at = block_at(line + 1 + step)
        rows = rows_ref[pl.ds(at, BLOCK), :]
        weight = fact_ref[0:1, pl.ds(at, BLOCK)]
        ids = fact_ref[2:3, pl.ds(at, BLOCK)].astype(jnp.int32)
        for start in range(0, words, chunk):
            word = base + start + lax.broadcasted_iota(jnp.int32, (chunk, 1), 0)
            chosen = lowered(jnp.where(word == ids, weight, 0.0))
            sum_ref[start : start + chunk, :] += product(chosen, rows)
        return unused

    lax.fori_loop(0, plan_ref[line], hits, 0)
    if across:
        out_ref[...] = sum_ref[...].T[: out_ref.shape[0], :].astype(out_ref.dtype)
    else:
        out_ref[...] = sum_ref[...].astype(out_ref.dtype)


def listed(flags):
    size = flags.shape[-1]
    order = jnp.cumsum(flags.astype(jnp.int32), -1)
    chosen = (order[..., None, :] == jnp.arange(1, size + 1)[:, None]) & flags[..., None, :]
    places = jnp.sum(jnp.where(chosen, jnp.arange(size), 0), -1)
    return jnp.concatenate([order[..., -1:], places], -1).astype(jnp.int32)


def band_grad(
    table, rows, facts, active, lowest, highest, part, part_words, first_word, chunk, result, across
):
    count, full = rows.shape[0], table.shape[1]
    word_block = chunk
    steps = part_words // word_block
    most = count // BLOCK
    first = first_word + part * part_words
    low = first + jnp.arange(steps, dtype=jnp.int32)[:, None] * word_block
    step_hits = active[None, :] & (lowest[None, :] < low + word_block) & (highest[None, :] >= low)
    plan = jnp.concatenate(
        [
            listed(active),
            first.reshape(1).astype(jnp.int32),
            listed(step_hits).reshape(-1),
            (part * steps).reshape(1).astype(jnp.int32),
        ]
    )
    last = plan.shape[0] - 1
    return pl.pallas_call(
        functools.partial(band_grad_kernel, chunk // 2 if chunk > 832 else chunk, most, across),
        grid_spec=pltpu.PrefetchScalarGridSpec(
            num_scalar_prefetch=1,
            grid=(steps,),
            in_specs=[
                pl.BlockSpec((word_block, full), lambda i, s: (s[last] + i, 0)),
                pl.BlockSpec((count, full), lambda i, s: (0, 0), **ONCE),
                pl.BlockSpec(facts.shape, lambda i, s: (0, 0), **ONCE),
            ],
            out_specs=(
                pl.BlockSpec((result.shape[0], word_block), lambda i, s: (0, i))
                if across
                else pl.BlockSpec((word_block, full), lambda i, s: (i, 0))
            ),
            scratch_shapes=[pltpu.VMEM((word_block, full), jnp.float32)],
        ),
        out_shape=result,
        compiler_params=pltpu.CompilerParams(vmem_limit_bytes=VMEM_BYTES),
        cost_estimate=pl.CostEstimate(
            flops=2 * count * part_words * 256,
            bytes_accessed=count * full * 2 + part_words * full * 4,
            transcendentals=count * part_words // 2,
        ),
        name="band_grad",
    )(plan, table, rows, facts)


def settle_kernel(
    member_ref,
    everyone_ref,
    fact_ref,
    head_mix_ref,
    middle_mix_ref,
    tail_mix_ref,
    head_hit_ref,
    middle_hit_ref,
    tail_hit_ref,
    term_ref,
    line_ref,
    slot_ref,
):
    step = pl.program_id(0)
    devices, _, slots = everyone_ref.shape
    tail_width = 64
    here = pl.ds(pl.multiple_of(step * BLOCK, BLOCK), BLOCK)

    def merged(read):
        lines = [read(device) for device in range(devices)]
        top = functools.reduce(jnp.maximum, [line[0] for line in lines])
        return top, sum(line[1] * jnp.exp(line[0] - top) for line in lines)

    head_top, head_sum = merged(
        lambda d: (everyone_ref[d, 0:1, here], everyone_ref[d, 1:2, here])
    )
    target = sum(everyone_ref[d, 2:3, here] for d in range(devices))
    slot_top, slot_sum = merged(lambda d: (everyone_ref[d, 3:4, :], everyone_ref[d, 4:5, :]))
    used = slot_sum > 0.0
    slot_total = jnp.where(used, slot_top + jnp.log(jnp.where(used, slot_sum, 1.0)), 0.0)
    member = member_ref[0]
    own_slot_top = jnp.where(used, everyone_ref[member, 3:4, :], 0.0)
    own_head_top = everyone_ref[member, 0:1, here]

    facts = fact_ref[...]
    slot, share, cotangent, first_cluster, second_cluster, band, word = (
        facts[index : index + 1] for index in range(7)
    )

    def as_columns(lines):
        square = jnp.concatenate(
            lines + [jnp.zeros((128 - len(lines), BLOCK), jnp.float32)], 0
        )
        return square.T

    def three(line):
        return [part.astype(jnp.float32) for part in thirds(line)]

    slot_column = as_columns([slot])[:, 0:1].astype(jnp.int32)
    hot = lowered(
        jnp.where(lax.broadcasted_iota(jnp.int32, (BLOCK, slots), 1) == slot_column, 1.0, 0.0)
    )
    lines = three(slot_total) + three(own_slot_top) + [jnp.zeros((10, slots), jnp.float32)]
    on_tokens = product_nt(lowered(jnp.concatenate(lines, 0)), hot)
    band_total = on_tokens[0:1] + on_tokens[1:2] + on_tokens[2:3]
    own_band_top = on_tokens[3:4] + on_tokens[4:5] + on_tokens[5:6]

    cluster_top = jnp.maximum(head_top, jnp.maximum(first_cluster, second_cluster))
    head_total = cluster_top + jnp.log(
        head_sum * jnp.exp(head_top - cluster_top)
        + jnp.exp(first_cluster - cluster_top)
        + jnp.exp(second_cluster - cluster_top)
    )
    in_head = band < 0.5
    cluster = jnp.where(band < 1.5, first_cluster, second_cluster)
    model_logp = target - head_total + jnp.where(in_head, 0.0, cluster - band_total)
    ratio = 0.25 * share * jnp.exp(-model_logp)
    weight = cotangent * 0.75 / (0.75 + ratio)
    head_scale = weight * jnp.exp(own_head_top - head_total)
    band_scale = weight * jnp.where(in_head, 0.0, jnp.exp(own_band_top - band_total))
    columns = as_columns([weight, head_scale, band_scale])
    weight_column, head_column, band_column = (columns[:, i : i + 1] for i in range(3))
    width = head_mix_ref.shape[1]
    term_ref[:, :width] = lowered(
        weight_column * head_hit_ref[...].astype(jnp.float32)
        - head_column * head_mix_ref[...].astype(jnp.float32)
    )
    narrow = tail_mix_ref.shape[1]
    kept = lax.broadcasted_iota(jnp.int32, (BLOCK, narrow), 1) < tail_width

    def widened(values):
        values = jnp.where(kept, values, 0.0)
        more = middle_mix_ref.shape[1] - narrow
        return jnp.concatenate([values, jnp.zeros((BLOCK, more), jnp.float32)], 1)

    band_mix = product(hot, middle_mix_ref[...]) + widened(product(hot, tail_mix_ref[...]))
    band_hit = middle_hit_ref[...].astype(jnp.float32) + widened(
        tail_hit_ref[...].astype(jnp.float32)
    )
    term_ref[:, width:] = lowered(weight_column * band_hit - band_column * band_mix)
    line_ref[...] = jnp.concatenate(
        [
            model_logp + jnp.log(0.75 + ratio),
            weight,
            head_total,
            word,
            jnp.zeros((4, BLOCK), jnp.float32),
        ],
        0,
    )

    @pl.when(step == 0)
    def _():
        slot_ref[...] = jnp.concatenate(
            [jnp.zeros((8, slots), jnp.float32), slot_total, jnp.zeros((7, slots), jnp.float32)], 0
        )

    sent = three(weight) + three(word) + [jnp.zeros((10, BLOCK), jnp.float32)]
    slot_ref[0:8, :] += product(lowered(jnp.concatenate(sent, 0)), hot)[0:8]


def settle(member, everyone, facts, head_mix, middle_mix, tail_mix, hits):
    count, width = head_mix.shape
    slots = middle_mix.shape[0]
    full = width + middle_mix.shape[1]

    def tokens(values):
        return pl.BlockSpec((BLOCK, values.shape[1]), lambda i, s: (i, 0))

    def whole(values):
        return pl.BlockSpec(values.shape, lambda i, s: (0,) * values.ndim, **ONCE)

    lines = pl.BlockSpec((8, BLOCK), lambda i, s: (0, i))
    return pl.pallas_call(
        settle_kernel,
        grid_spec=pltpu.PrefetchScalarGridSpec(
            num_scalar_prefetch=1,
            grid=(count // BLOCK,),
            in_specs=[whole(everyone), lines, tokens(head_mix), whole(middle_mix), whole(tail_mix)]
            + [tokens(hit) for hit in hits],
            out_specs=[
                pl.BlockSpec((BLOCK, full), lambda i, s: (i, 0)),
                lines,
                pl.BlockSpec((16, slots), lambda i, s: (0, 0)),
            ],
        ),
        out_shape=[
            jax.ShapeDtypeStruct((count, full), jnp.bfloat16),
            jax.ShapeDtypeStruct((8, count), jnp.float32),
            jax.ShapeDtypeStruct((16, slots), jnp.float32),
        ],
        compiler_params=pltpu.CompilerParams(vmem_limit_bytes=VMEM_BYTES),
        cost_estimate=pl.CostEstimate(
            flops=2 * count * slots * 1024,
            bytes_accessed=count * width * 12 + slots * full,
            transcendentals=slots * 64,
        ),
        name="settle",
    )(member.reshape(1).astype(jnp.int32), everyone, facts, head_mix, middle_mix, tail_mix, *hits)


def line_turns(value):
    size = lax.axis_size("seq")
    return [value] + [
        lax.ppermute(value, "seq", [(d, (d - k) % size) for d in range(size)])
        for k in range(1, size)
    ]


def line_step(before, behind, step):
    size = lax.axis_size("seq")
    return (
        lax.ppermute(before, "seq", [(d, d + 1) for d in range(step - 1, size - 1)]),
        lax.ppermute(behind, "seq", [(d, d - 1) for d in range(1, size - step + 1)]),
    )


def line_steps(value):
    found = [(value, value)]

    def advance(*others):
        step = len(found)
        if step == lax.axis_size("seq"):
            return others
        moved = line_step(*found[-1], step)
        moved, others = lax.optimization_barrier((moved, others))
        found.append(moved)
        return others

    return found, advance


def line_ordered(found, axis):
    size, place = lax.axis_size("seq"), lax.axis_index("seq")
    ordered = []
    for source in range(size):
        value = found[0][0]
        for step in range(1, size):
            if source + step < size:
                value = jnp.where(place == source + step, found[step][0], value)
            if source - step >= 0:
                value = jnp.where(place == source - step, found[step][1], value)
        ordered.append(value)
    return jnp.concatenate(ordered, axis)


def earlier_joined(value):
    size, place = lax.axis_size("seq"), lax.axis_index("seq")
    joined = jnp.zeros((size,) + value.shape, value.dtype)
    for step in range(size - 1, -1, -1):
        piece = value
        if step:
            piece = lax.ppermute(value, "seq", [(d, d + step) for d in range(size - step)])
        joined = lax.dynamic_update_index_in_dim(joined, piece, jnp.maximum(place - step, 0), 0)
    return joined.reshape((-1,) + value.shape[1:])


def in_order(pieces):
    size, place = lax.axis_size("seq"), lax.axis_index("seq")
    joined = jnp.zeros((size,) + pieces[0].shape, pieces[0].dtype)
    for k, piece in enumerate(pieces):
        joined = lax.dynamic_update_index_in_dim(joined, piece, lax.rem(place + k, size), 0)
    return joined.reshape((-1,) + pieces[0].shape[1:])


def line_scatter(values, behind=True):
    size, place = lax.axis_size("seq"), lax.axis_index("seq")
    parts = values.reshape((size, -1) + values.shape[1:])

    def part(index):
        return lax.dynamic_index_in_dim(parts, lax.rem(index, size), 0, False)

    total = part(place).astype(jnp.float32)
    for k in range(1, size):
        pairs = [(d, (d - k) % size) for d in range(0 if behind else k, size)]
        total = total + lax.ppermute(part(place + size - k), "seq", pairs).astype(jnp.float32)
    return total


def turn_kernel(rows_ref, out_ref):
    out_ref[...] = rows_ref[...].astype(jnp.float32).T.astype(out_ref.dtype)


def turned(rows, kind):
    return pl.pallas_call(
        turn_kernel, out_shape=jax.ShapeDtypeStruct(rows.shape[::-1], kind), name="turned"
    )(rows)


def word_pad(rows, biggest, splits):
    chunk = min(biggest, round_up(rows, 128))
    chunks = -(-rows // chunk)
    if chunks > 4:
        chunks = round_up(chunks, 4)
    return chunk, chunks * chunk


def on_device(
    inputs,
    targets,
    neighbours,
    neighbour_scores,
    loglik_grad,
    first_gain,
    first_shift,
    query_weight,
    query_bias,
    key_weight,
    value_weight,
    value_bias,
    out_weight,
    out_bias,
    second_gain,
    second_shift,
    inner_weight,
    inner_bias,
    outer_weight,
    outer_bias,
    final_gain,
    final_shift,
    head_table,
    cluster_weight,
    middle_map,
    middle_table,
    tail_map,
    tail_table,
):
    nb = lax.axis_size("batch")
    nz = lax.axis_size("seq")
    member = lax.axis_index("batch")
    place = lax.axis_index("seq")
    tokens = inputs[0]
    own_ids = targets[0]
    token_count, feature_count = tokens.shape
    group_count = token_count * nb
    slot_count = group_count + BLOCK
    query_start = (place * token_count).reshape(1)

    normed_low = lowered(layer_norm(tokens, first_gain, first_shift))
    normed_all = earlier_joined(normed_low)
    top_score = jnp.max(neighbour_scores[0], -1, keepdims=True)
    exponent = jnp.exp(neighbour_scores[0] - top_score)
    knn_prob = jnp.sum(jnp.where(neighbours[0] == 0, exponent, 0.0), -1) / jnp.sum(exponent, -1)
    early = jnp.stack([own_ids.astype(jnp.float32), knn_prob, loglik_grad[0]])
    early = lax.all_gather(early, "batch", axis=1, tiled=True)
    all_ids = early[0].astype(jnp.int32)
    all_knn, all_up = early[1], early[2]
    in_head = all_ids < HEAD_WORDS
    in_middle = (all_ids >= HEAD_WORDS) & (all_ids < HEAD_WORDS + MID_WORDS)
    in_tail = all_ids >= HEAD_WORDS + MID_WORDS
    order = jnp.arange(group_count, dtype=jnp.int32)
    ahead = (all_ids[None, :] < all_ids[:, None]) | (
        (all_ids[None, :] == all_ids[:, None]) & (order[None, :] < order[:, None])
    )
    rank = jnp.sum(ahead.astype(jnp.int32), -1)
    head_size = jnp.sum(in_head.astype(jnp.int32))
    middle_size = jnp.sum(in_middle.astype(jnp.int32))
    tail_size = group_count - head_size - middle_size
    middle_blocks = (middle_size + BLOCK - 1) // BLOCK
    tail_blocks = (tail_size + BLOCK - 1) // BLOCK
    slot = jnp.where(
        in_head,
        -1,
        rank - head_size + jnp.where(in_tail, middle_blocks * BLOCK - middle_size, 0),
    )
    zero_span = jnp.zeros((1,), jnp.int32)
    head_span = jnp.array([0, group_count // BLOCK], jnp.int32)
    middle_span = jnp.stack([0 * middle_blocks, middle_blocks]).astype(jnp.int32)
    tail_span = jnp.stack([middle_blocks, middle_blocks + tail_blocks]).astype(jnp.int32)
    slot_order = jnp.arange(slot_count, dtype=jnp.int32)
    slot_middle = slot_order < middle_size
    slot_tail = (slot_order >= middle_blocks * BLOCK) & (
        slot_order < middle_blocks * BLOCK + tail_size
    )
    slot_used = slot_middle | slot_tail
    band_id = all_ids - jnp.where(in_tail, HEAD_WORDS + MID_WORDS, HEAD_WORDS)

    tables = (head_table, middle_table, tail_table)
    sizes = tuple(table.shape[0] for table in tables)
    head_chunk, head_padded = word_pad(sizes[0], 1280, nz)
    middle_chunk, middle_padded = word_pad(sizes[1], 1280, nz)
    tail_chunk, tail_padded = word_pad(sizes[2], 1664, nz)
    tail_width = tail_table.shape[1]
    head_pad = jnp.pad(head_table, ((0, head_padded - sizes[0]), (0, 0)))
    middle_pad = jnp.pad(middle_table, ((0, middle_padded - sizes[1]), (0, 0)))
    tail_word = jnp.arange(tail_padded, dtype=jnp.int32)
    tail_bias = jnp.where(tail_word < jnp.minimum(TAIL_WORDS - member * sizes[2], sizes[2]), 0.0, NEG_FILL)
    tail_pad = jnp.concatenate(
        [
            jnp.pad(tail_table.T, ((0, 0), (0, tail_padded - sizes[2]))),
            jnp.ones((1, tail_padded), jnp.bfloat16),
            lowered(tail_bias)[None, :],
            jnp.zeros((126 - tail_width, tail_padded), jnp.bfloat16),
        ],
        0,
    ).T
    locals_ = (
        all_ids - member * sizes[0],
        all_ids - HEAD_WORDS - member * sizes[1],
        all_ids - HEAD_WORDS - MID_WORDS - member * sizes[2],
    )
    owned = tuple(
        inside & (local >= 0) & (local < size)
        for inside, local, size in zip((in_head, in_middle, in_tail), locals_, sizes)
    )
    hit_rows = tuple(
        jnp.where(
            own[:, None],
            jnp.take(table, jnp.clip(local, 0, size - 1), axis=0, mode="clip"),
            jnp.bfloat16(0),
        )
        for own, table, local, size in zip(owned, (head_pad, middle_pad, tail_pad), locals_, sizes)
    )

    queries = lowered(product(normed_low, query_weight) + query_bias)
    key_rows = lowered(product(normed_all, key_weight))
    value_rows = lowered(product(normed_all, value_weight) + value_bias)
    attended_low = attend(query_start, queries, key_rows, value_rows)
    mixed = tokens + product(attended_low, out_weight) + out_bias
    second_low = lowered(layer_norm(mixed, second_gain, second_shift))
    before = product(second_low, inner_weight) + inner_bias
    hidden_low = lowered(jax.nn.gelu(before))
    final = mixed + product(hidden_low, outer_weight) + outer_bias
    state_low = lowered(layer_norm(final, final_gain, final_shift))
    all_states = lax.all_gather(state_low, "batch", axis=0, tiled=True)
    split = 2 * nz * group_count * feature_count <= 24 << 20
    if split:
        other_states = jnp.concatenate(line_turns(state_low)[1:], 0)
        all_states, other_states, head_pad, middle_pad, tail_pad, hit_rows, slot, early = (
            lax.optimization_barrier(
                (all_states, other_states, head_pad, middle_pad, tail_pad, hit_rows, slot, early)
            )
        )
        other_states = lax.all_gather(other_states, "batch", axis=0, tiled=True)

    middle_width = middle_map.shape[1]
    maps = jnp.pad(jnp.concatenate([middle_map, tail_map], 1), ((0, 0), (0, 128 - tail_width)))
    one_column = (jnp.arange(middle_width + 128) == middle_width + tail_width + 1).astype(jnp.float32)
    band_low = lowered(product(all_states, maps) + one_column)
    middle_low, tail_low = band_low[:, :middle_width], band_low[:, middle_width:]
    cluster_lines = product_nt(
        jnp.pad(cluster_weight.T, ((0, 6), (0, 0))), all_states
    )
    slot_full = pick_rows(slot, band_low, slot_count, True, jnp.bfloat16)
    first_tail = middle_blocks * BLOCK
    in_tail_slot = slot_order >= first_tail
    slot_low = jnp.where(
        in_tail_slot[:, None],
        jnp.pad(slot_full[:, middle_width:], ((0, 0), (0, middle_width - 128))),
        slot_full[:, :middle_width],
    )
    if split:
        piece = slot_count // nb
        slot_piece = lax.dynamic_slice_in_dim(slot_low, member * piece, piece, 0)
        other_slots = jnp.concatenate(line_turns(slot_piece)[1:], 0)
    tail_stats, tail_mix = band_forward(
        tail_span, slot_low, tail_pad, tail_padded, tail_chunk, tail_width, 0.5
    )
    middle_stats, middle_mix = band_forward(
        middle_span, slot_low, middle_pad, sizes[1], middle_chunk, None, 0.25
    )
    if split:
        all_states, other_states, other_slots, tail_stats, middle_stats = lax.optimization_barrier(
            (all_states, other_states, other_slots, tail_stats, middle_stats)
        )
        other_slots = lax.all_gather(other_slots, "batch", axis=0, tiled=True)
    head_stats, head_mix = band_forward(
        head_span, all_states, head_pad, sizes[0], head_chunk, None, 1.0
    )
    inner_lane = jnp.arange(128) < tail_width
    target_part = (
        jnp.sum(hit_rows[0].astype(jnp.float32) * all_states.astype(jnp.float32), -1)
        + jnp.sum(hit_rows[1].astype(jnp.float32) * middle_low.astype(jnp.float32), -1)
        + jnp.sum(
            jnp.where(inner_lane, hit_rows[2].astype(jnp.float32), 0.0)
            * tail_low.astype(jnp.float32),
            -1,
        )
    )
    slot_stats = jnp.where(in_tail_slot[None, :], tail_stats[:2], middle_stats[:2])
    extra = ((0, 0), (0, BLOCK))
    stats = jnp.concatenate(
        [
            jnp.pad(jnp.concatenate([head_stats[:2], target_part[None]], 0), extra),
            slot_stats,
            jnp.zeros((3, slot_count), jnp.float32),
        ],
        0,
    )
    if split:
        stats, other_states, other_slots = lax.optimization_barrier(
            (stats, other_states, other_slots)
        )
    everyone = lax.all_gather(stats, "batch")

    token_facts = jnp.concatenate(
        [
            slot.astype(jnp.float32)[None],
            early[1:3],
            cluster_lines[:2],
            jnp.where(in_head, 0.0, jnp.where(in_middle, 1.0, 2.0))[None],
            early[0:1],
            jnp.zeros((1, group_count), jnp.float32),
        ],
        0,
    )
    terms, lines, slot_lines = settle(
        member, everyone, token_facts, head_mix, middle_mix, tail_mix, hit_rows
    )
    own_terms = lax.psum_scatter(terms, "batch", scatter_dimension=0, tiled=True).astype(jnp.float32)

    def own_part(values):
        return lax.dynamic_slice_in_dim(values, member * token_count, token_count, 0)

    loglik = own_part(lines[0])

    kind = jnp.where(slot_middle, 1.0, jnp.where(slot_tail, 2.0, 0.0))
    slot_facts = jnp.stack(
        [
            jnp.sum(slot_lines[0:3], 0),
            slot_lines[8],
            jnp.sum(slot_lines[3:6], 0),
            kind,
        ]
    )
    head_facts = jnp.concatenate([lines[1:4], jnp.zeros((1, group_count), jnp.float32)], 0)
    if split:
        other_slots = (
            other_slots.reshape(nb, nz - 1, piece, middle_width)
            .transpose(1, 0, 2, 3)
            .reshape(-1, middle_width)
        )
        rows_all = jnp.concatenate([slot_low, other_slots], 0)
        fact_pieces = line_turns(jnp.concatenate([slot_facts, head_facts], 1))
        facts = jnp.concatenate([value[:, :slot_count] for value in fact_pieces], 1)
        other_facts = (
            jnp.stack([value[:, slot_count:] for value in fact_pieces[1:]], 1)
            .reshape(4, nz - 1, nb, token_count)
            .transpose(0, 2, 1, 3)
            .reshape(4, -1)
        )
        lists = [(all_states, head_facts), (other_states, other_facts)]
        part, parts = place, nz
    else:
        rows_all, facts, lists = slot_low, slot_facts, [(all_states, head_facts)]
        part, parts = 0 * place, 1
    head_part = head_grad(head_pad, part, head_padded // parts, member * sizes[0], lists)
    block_facts = facts[2:4].reshape(2, -1, BLOCK)
    block_kind = jnp.max(block_facts[1], -1)
    filled = block_facts[1] > 0
    lowest = jnp.min(jnp.where(filled, block_facts[0], 1e9), -1).astype(jnp.int32)
    highest = jnp.max(jnp.where(filled, block_facts[0], -1e9), -1).astype(jnp.int32)
    facts = jnp.concatenate(
        [facts[:2], jnp.where(facts[3:4] > 0, facts[2:3], -1e9), jnp.zeros_like(facts[:1])], 0
    )
    tail_part = band_grad(
        tail_pad,
        rows_all,
        facts,
        block_kind == 2,
        lowest,
        highest,
        part,
        tail_padded // parts,
        HEAD_WORDS + MID_WORDS + member * sizes[2],
        math.gcd(tail_padded // parts, tail_chunk),
        jax.ShapeDtypeStruct((tail_width, tail_padded // parts), jnp.bfloat16),
        True,
    )
    if split:
        head_found, head_advance = line_steps(head_part)
        own_terms, tail_part = head_advance(own_terms, tail_part)
        tail_found, tail_advance = line_steps(tail_part)
    else:
        own_terms, tail_part = lax.optimization_barrier((own_terms, tail_part))

    own_middle = own_part(in_middle)
    own_tail = own_part(in_tail)
    own_lines = lax.dynamic_slice_in_dim(lines, member * token_count, token_count, 1)
    own_weights, own_total = own_lines[1], own_lines[2]
    own_clusters = product(state_low, cluster_weight)
    band_state = own_terms[:, feature_count:]
    middle_state = lowered(jnp.where(own_middle[:, None], band_state, 0.0))
    tail_state = lowered(jnp.where(own_tail[:, None], band_state[:, :tail_width], 0.0))
    cluster_hit = jnp.stack([own_middle, own_tail], -1).astype(jnp.float32)
    cluster_grad = own_weights[:, None] * (
        cluster_hit - jnp.exp(own_clusters - own_total[:, None])
    )
    state_grad = (
        own_terms[:, :feature_count]
        + product_nt(middle_state, middle_map)
        + product_nt(tail_state, tail_map)
        + product_nt(cluster_grad, cluster_weight.astype(jnp.float32))
    )
    middle_map_grad = product_tn(state_low, middle_state)
    tail_map_rows = product_tn(tail_state, state_low)
    cluster_rows = product_tn(cluster_grad, state_low.astype(jnp.float32))
    final_grad, final_gain_grad, final_shift_grad = norm_back(
        final, final_gain, final_shift, state_grad
    )
    final_low = lowered(final_grad)
    outer_weight_grad = product_tn(hidden_low, final_low)
    outer_bias_grad = jnp.sum(final_grad, 0)
    outer_part = lax.psum_scatter(
        lowered(outer_weight_grad), "batch", scatter_dimension=0, tiled=True
    )
    before_grad = lowered(gelu_back(before, product_nt(final_low, outer_weight)))
    inner_weight_grad = product_tn(second_low, before_grad)
    inner_bias_grad = jnp.sum(before_grad.astype(jnp.float32), 0)
    inner_part = lax.psum_scatter(
        lowered(inner_weight_grad), "batch", scatter_dimension=0, tiled=True
    )
    second_in_grad, second_gain_grad, second_shift_grad = norm_back(
        mixed, second_gain, second_shift, product_nt(before_grad, inner_weight)
    )
    mixed_grad = final_grad + second_in_grad
    mixed_low = lowered(mixed_grad)
    out_weight_grad = product_tn(attended_low, mixed_low)
    out_bias_grad = jnp.sum(mixed_grad, 0)
    attended_grad = lowered(product_nt(mixed_low, out_weight))
    if split:
        (attended_grad,) = head_advance(attended_grad)
    query_low, key_low, value_low = attend_back(
        query_start, queries, key_rows, value_rows, attended_grad
    )
    if split:
        for unused in range(nz - 3):
            (query_low,) = head_advance(query_low)
        (query_low,) = tail_advance(query_low)
    query_weight_grad = product_tn(normed_low, query_low)
    key_weight_grad = product_tn(normed_all, key_low)
    value_weight_grad = product_tn(normed_all, value_low)
    query_bias_grad = jnp.sum(query_low.astype(jnp.float32), 0)
    value_bias_grad = jnp.sum(value_low.astype(jnp.float32), 0)
    spread = product_nt(key_low, key_weight) + product_nt(value_low, value_weight)
    query_spread = product_nt(query_low, query_weight)
    first_shift_grad = jnp.sum(spread, 0) + jnp.sum(query_spread, 0)
    all_centred = (normed_all.astype(jnp.float32) - first_shift) / first_gain
    own_average = jnp.mean(tokens, -1, keepdims=True)
    own_spread = jnp.mean((tokens - own_average) ** 2, -1, keepdims=True)
    own_centred = (tokens - own_average) * lax.rsqrt(own_spread + EPSILON)
    first_gain_grad = jnp.sum(all_centred * spread, 0) + jnp.sum(own_centred * query_spread, 0)
    normed_grad = query_spread + line_scatter(lowered(spread), False)
    first_in_grad, unused, unused = norm_back(tokens, first_gain, first_shift, normed_grad)
    input_grad = mixed_grad + first_in_grad

    bias_rows = inner_bias_grad.shape[0] // feature_count
    inner_bias_rows = (
        inner_bias_grad.reshape(nb, bias_rows, -1).transpose(1, 0, 2).reshape(bias_rows, -1)
    )
    vectors = [
        first_gain_grad,
        first_shift_grad,
        query_bias_grad,
        value_bias_grad,
        out_bias_grad,
        second_gain_grad,
        second_shift_grad,
        outer_bias_grad,
        final_gain_grad,
        final_shift_grad,
    ]
    rows = [tail_map_rows, cluster_rows, inner_bias_rows] + [value[None] for value in vectors]
    edges = [0]
    for row in rows:
        edges.append(edges[-1] + row.shape[0])
    row_count = round_up(edges[-1], 128)
    rows.append(jnp.zeros((row_count - edges[-1], feature_count), jnp.float32))
    columns = [
        query_weight_grad,
        key_weight_grad,
        value_weight_grad,
        out_weight_grad,
        middle_map_grad,
        turned(jnp.concatenate(rows, 0), jnp.bfloat16),
    ]
    rest = jnp.concatenate([lowered(column) for column in columns], 1)
    rest, facts, inner_part = lax.optimization_barrier((rest, facts, inner_part))
    if split:
        rest, facts = tail_advance(rest, facts)
    rest_part = lax.psum_scatter(rest, "batch", scatter_dimension=0, tiled=True)
    middle_result = jax.ShapeDtypeStruct(
        (sizes[1], middle_width) if split else (middle_padded, middle_width),
        jnp.float32 if split else jnp.bfloat16,
    )
    middle_part = band_grad(
        middle_pad,
        rows_all,
        facts,
        block_kind == 1,
        lowest,
        highest,
        0 * place,
        middle_padded,
        HEAD_WORDS + member * sizes[1],
        middle_chunk,
        middle_result,
        False,
    )
    if split:
        middle_table_grad = middle_part
        for unused in range(nz - 3):
            (middle_table_grad,) = tail_advance(middle_table_grad)
        head_table_grad = line_ordered(head_found, 0)
        tail_sum = line_ordered(tail_found, 1)
    else:
        middle_table_grad = lax.psum(middle_part, "seq")[: sizes[1]].astype(jnp.float32)
        head_table_grad = lax.psum(head_part, "seq")
        tail_sum = lax.psum(tail_part, "seq")
    head_table_grad = head_table_grad[: sizes[0]].astype(jnp.float32)
    tail_table_grad = tail_sum[:, : sizes[2]].astype(jnp.float32).T
    inner_low = lowered(line_scatter(inner_part))
    inner_low, outer_part, middle_table_grad = lax.optimization_barrier(
        (inner_low, outer_part, middle_table_grad)
    )
    inner_pieces = line_turns(inner_low)
    outer_low = lowered(line_scatter(outer_part))
    rest_part, outer_low, inner_pieces = lax.optimization_barrier(
        (rest_part, outer_low, inner_pieces)
    )
    inner_sum = in_order(inner_pieces).astype(jnp.float32)
    outer_sum = in_order(line_turns(outer_low)).astype(jnp.float32)
    rest_low = lax.psum(rest_part, "seq")
    rest_sum = rest_low[:, : 4 * feature_count + middle_width].astype(jnp.float32)
    cut = [rest_sum[:, i * feature_count : (i + 1) * feature_count] for i in range(4)]
    middle_map_sum = rest_sum[:, 4 * feature_count : 4 * feature_count + middle_width]
    row_sum = turned(rest_low[:, 4 * feature_count + middle_width :], jnp.float32)
    tail_map_sum, cluster_sum, inner_bias_sum = (
        row_sum[low:high] for low, high in zip(edges[:3], edges[1:4])
    )
    lines = [row_sum[index] for index in range(edges[3], edges[3] + len(vectors))]
    return (
        loglik.reshape(1, token_count),
        input_grad.reshape(1, token_count, feature_count),
        lines[0],
        lines[1],
        cut[0],
        lines[2],
        cut[1],
        cut[2],
        lines[3],
        cut[3],
        lines[4],
        lines[5],
        lines[6],
        inner_sum,
        inner_bias_sum.reshape(-1),
        outer_sum,
        lines[7],
        lines[8],
        lines[9],
        head_table_grad,
        cluster_sum.T,
        middle_map_sum,
        middle_table_grad,
        tail_map_sum.T,
        tail_table_grad,
    )


def solution(mesh):
    return jax.shard_map(
        on_device,
        mesh=mesh,
        in_specs=(
            P("batch", "seq", None),
            P("batch", "seq"),
            P("batch", "seq", None),
            P("batch", "seq", None),
            P("batch", "seq"),
            P(),
            P(),
            P(),
            P(),
            P(),
            P(),
            P(),
            P(),
            P(),
            P(),
            P(),
            P(),
            P(),
            P(),
            P(),
            P(),
            P(),
            P("batch", None),
            P(),
            P(),
            P("batch", None),
            P(),
            P("batch", None),
        ),
        out_specs=(
            P("batch", "seq"),
            P("batch", "seq", None),
            P("batch"),
            P("batch"),
            P("batch", None),
            P("batch"),
            P("batch", None),
            P("batch", None),
            P("batch"),
            P("batch", None),
            P("batch"),
            P("batch"),
            P("batch"),
            P("batch", None),
            P("batch"),
            P("batch", None),
            P("batch"),
            P("batch"),
            P("batch"),
            P("batch", None),
            P("batch", None),
            P("batch", None),
            P("batch", None),
            P("batch", None),
            P("batch", None),
        ),
        check_vma=False,
    )
```

```python
import functools
import math

import jax
import jax.numpy as jnp
from jax import lax
from jax.experimental import pallas as pl
from jax.experimental.pallas import tpu as pltpu
from jax.sharding import PartitionSpec as P

HEADS = 16
HEAD_WORDS = 20000
MID_WORDS = 40000
TAIL_WORDS = 207735


NEG_FILL = -1e30
EPSILON = 1e-05
BLOCK = 256
SAFE = 1e30
VMEM_BYTES = 56 << 20
ONCE = dict(pipeline_mode=pl.Buffered(1))


def layer_norm(values, gain_vector, shift_vector):
    average = jnp.mean(values, -1, keepdims=True)
    centred = values - average
    spread = jnp.mean(centred * centred, -1, keepdims=True)
    return centred * lax.rsqrt(spread + EPSILON) * gain_vector + shift_vector


def norm_back(values, gain_vector, shift_vector, upstream):
    unused, pullback = jax.vjp(layer_norm, values, gain_vector, shift_vector)
    return pullback(upstream)


def gelu_back(before, upstream):
    unused, pullback = jax.vjp(jax.nn.gelu, before)
    return pullback(upstream)[0]


def product(former, latter):
    return jnp.dot(former, latter, preferred_element_type=jnp.float32)


def product_tn(former, latter):
    return lax.dot_general(
        former, latter, (((0,), (0,)), ((), ())), preferred_element_type=jnp.float32
    )


def product_nt(former, latter):
    return lax.dot_general(
        former, latter, (((1,), (1,)), ((), ())), preferred_element_type=jnp.float32
    )


def lowered(values):
    return values.astype(jnp.bfloat16)


def round_up(count, unit):
    return -(-count // unit) * unit


def thirds(values):
    high = lowered(values)
    rest = values - high.astype(jnp.float32)
    middle = lowered(rest)
    return [high, middle, lowered(rest - middle.astype(jnp.float32))]


def attend_kernel(start_ref, query_ref, key_ref, value_ref, out_ref):
    rows, keys = query_ref.shape[0], key_ref.shape[0]
    half = query_ref.shape[1] // 2
    query_pos = start_ref[0] + lax.broadcasted_iota(jnp.int32, (rows, keys), 0)
    allowed = lax.broadcasted_iota(jnp.int32, (rows, keys), 1) <= query_pos
    for part in range(2):
        cols = slice(part * half, part * half + half)
        scores = product_nt(query_ref[:, cols], key_ref[:, cols]) * half**-0.5
        scores = jnp.where(allowed, scores, NEG_FILL)
        weights = jnp.exp(scores - jnp.max(scores, 1, keepdims=True))
        weights = weights / jnp.sum(weights, 1, keepdims=True)
        out_ref[:, cols] = lowered(product(lowered(weights), value_ref[:, cols]))


def attend(start, queries, keys, values):
    rows, features = queries.shape
    width = 2 * features // HEADS
    own = pl.BlockSpec((rows, width), lambda i, s: (0, i))
    whole = pl.BlockSpec((keys.shape[0], width), lambda i, s: (0, i))
    return pl.pallas_call(
        attend_kernel,
        grid_spec=pltpu.PrefetchScalarGridSpec(
            num_scalar_prefetch=1,
            grid=(features // width,),
            in_specs=[own, whole, whole],
            out_specs=own,
        ),
        out_shape=jax.ShapeDtypeStruct((rows, features), jnp.bfloat16),
        compiler_params=pltpu.CompilerParams(vmem_limit_bytes=VMEM_BYTES),
        cost_estimate=pl.CostEstimate(
            flops=4 * rows * keys.shape[0] * features,
            bytes_accessed=4 * (rows + keys.shape[0]) * features,
            transcendentals=rows * keys.shape[0] * HEADS,
        ),
        name="attend",
    )(start, queries, keys, values)


def attend_back_kernel(
    start_ref, query_ref, key_ref, value_ref, up_ref, query_grad_ref, key_grad_ref, value_grad_ref
):
    rows, keys = query_ref.shape[0], key_ref.shape[0]
    half = query_ref.shape[1] // 2
    scale = half**-0.5
    query_pos = start_ref[0] + lax.broadcasted_iota(jnp.int32, (keys, rows), 1)
    allowed = lax.broadcasted_iota(jnp.int32, (keys, rows), 0) <= query_pos
    for part in range(2):
        cols = slice(part * half, part * half + half)
        query, key, value, up = (
            ref[:, cols] for ref in (query_ref, key_ref, value_ref, up_ref)
        )
        scores = jnp.where(allowed, product_nt(key, query) * scale, NEG_FILL)
        probs = jnp.exp(scores - jnp.max(scores, 0, keepdims=True))
        probs = probs / jnp.sum(probs, 0, keepdims=True)
        prob_grad = product_nt(value, up)
        delta = jnp.sum(probs * prob_grad, 0, keepdims=True)
        score_grad = lowered(probs * (prob_grad - delta))
        value_grad_ref[:, cols] = lowered(product(lowered(probs), up))
        key_grad_ref[:, cols] = lowered(product(score_grad, query) * scale)
        query_grad_ref[:, cols] = lowered(product_tn(score_grad, key) * scale)


def attend_back(start, queries, keys, values, upstream):
    rows, features = queries.shape
    count = keys.shape[0]
    width = 2 * features // HEADS
    own = pl.BlockSpec((rows, width), lambda i, s: (0, i))
    whole = pl.BlockSpec((count, width), lambda i, s: (0, i))
    return pl.pallas_call(
        attend_back_kernel,
        grid_spec=pltpu.PrefetchScalarGridSpec(
            num_scalar_prefetch=1,
            grid=(features // width,),
            in_specs=[own, whole, whole, own],
            out_specs=[own, whole, whole],
        ),
        out_shape=[
            jax.ShapeDtypeStruct((rows, features), jnp.bfloat16),
            jax.ShapeDtypeStruct((count, features), jnp.bfloat16),
            jax.ShapeDtypeStruct((count, features), jnp.bfloat16),
        ],
        compiler_params=pltpu.CompilerParams(vmem_limit_bytes=VMEM_BYTES),
        cost_estimate=pl.CostEstimate(
            flops=10 * rows * count * features,
            bytes_accessed=6 * (rows + count) * features,
            transcendentals=rows * count * HEADS,
        ),
        name="attend_back",
    )(start, queries, keys, values, upstream)


def pick_kernel(by_slot, index_ref, rows_ref, out_ref):
    count = rows_ref.shape[0]
    total = jnp.zeros(out_ref.shape, jnp.float32)
    base = pl.program_id(0) * BLOCK
    for at in range(0, count, BLOCK):
        if by_slot:
            place = base + lax.broadcasted_iota(jnp.int32, (BLOCK, BLOCK), 0)
            hit = index_ref[:, at : at + BLOCK] == place
        else:
            place = at + lax.broadcasted_iota(jnp.int32, (BLOCK, BLOCK), 1)
            hit = index_ref[...] == place
        onehot = lowered(jnp.where(hit, 1.0, 0.0))
        total = total + product(onehot, rows_ref[at : at + BLOCK, :])
    out_ref[...] = total.astype(out_ref.dtype)


def pick_rows(index, rows, out_count, by_slot, kind):
    count, width = rows.shape
    if by_slot:
        index = index.reshape(1, -1)
        index_spec = pl.BlockSpec(index.shape, lambda i: (0, 0))
    else:
        index = index.reshape(-1, 1)
        index_spec = pl.BlockSpec((BLOCK, 1), lambda i: (i, 0))
    return pl.pallas_call(
        functools.partial(pick_kernel, by_slot),
        grid=(out_count // BLOCK,),
        in_specs=[index_spec, pl.BlockSpec(rows.shape, lambda i: (0, 0), **ONCE)],
        out_specs=pl.BlockSpec((BLOCK, width), lambda i: (i, 0)),
        out_shape=jax.ShapeDtypeStruct((out_count, width), kind),
        compiler_params=pltpu.CompilerParams(vmem_limit_bytes=VMEM_BYTES),
        cost_estimate=pl.CostEstimate(
            flops=2 * out_count * count * max(width, 256),
            bytes_accessed=rows.size * 2 + out_count * width * 4,
            transcendentals=0,
        ),
        name="pick_rows",
    )(index, rows)


def band_kernel(chunk, per, words, sum_column, span_ref, rows_ref, table_ref, stat_ref, out_ref, mix_ref):
    step_id = pl.program_id(0)
    count, width = mix_ref.shape
    chunk_count = table_ref.shape[0] // chunk
    group_count = chunk_count // per
    active = (step_id >= span_ref[0]) & (step_id < span_ref[1])

    def put_stats(top, total):
        lane = lax.broadcasted_iota(jnp.int32, (count, 128), 1)
        both = jnp.where(lane == 0, top, jnp.where(lane == 1, total, 0.0))
        stat_ref[...] = both.T[:8, :]

    def logits_at(at, rows):
        return product_nt(rows, table_ref[pl.ds(at, chunk), :])

    def beyond(at, shape):
        return at + lax.broadcasted_iota(jnp.int32, shape, 1) >= words

    def run(rows, top):
        mix_ref[...] = jnp.zeros(mix_ref.shape, jnp.float32)

        def visit(group, total):
            for inner in range(per):
                at = (group * per + inner) * chunk
                checked = isinstance(at, int) and at + chunk > words
                if not isinstance(at, int):
                    at = pl.multiple_of(at, chunk)
                weights = jnp.exp(logits_at(at, rows) - top)
                if checked:
                    weights = jnp.where(beyond(at, weights.shape), 0.0, weights)
                if sum_column is None:
                    for lane in range(0, chunk, 128):
                        total = total + weights[:, lane : lane + 128]
                mix_ref[...] += product(lowered(weights), table_ref[pl.ds(at, chunk), :])
            return total

        lanes = jnp.zeros((count, 128), jnp.float32)
        lanes = visit(0, lanes) if group_count == 1 else lax.fori_loop(0, group_count, visit, lanes)
        if sum_column is None:
            return jnp.sum(lanes, 1, keepdims=True)
        return mix_ref[:, sum_column : sum_column + 1]

    @pl.when(active)
    def _():
        rows = rows_ref[...]
        first = product_nt(rows, table_ref[pl.ds(0, 128), :])
        top = jnp.max(first, 1, keepdims=True)
        total = run(rows, top)
        put_stats(top, total)

        @pl.when(jnp.logical_not(jnp.max(jnp.where(total < SAFE, 0.0, 1.0)) < 0.5))
        def _():
            def largest(index, top):
                at = pl.multiple_of(index * chunk, chunk)
                logits = logits_at(at, rows)
                if sum_column is None:
                    logits = jnp.where(beyond(at, logits.shape), NEG_FILL, logits)
                return jnp.maximum(top, jnp.max(logits, 1, keepdims=True))

            exact = lax.fori_loop(0, chunk_count, largest, jnp.full((count, 1), NEG_FILL))
            put_stats(exact, run(rows, exact))

        out_ref[...] = lowered(mix_ref[...])

    @pl.when(jnp.logical_not(active))
    def _():
        put_stats(jnp.full((count, 1), NEG_FILL), jnp.zeros((count, 1), jnp.float32))
        out_ref[...] = jnp.zeros(out_ref.shape, jnp.bfloat16)


def band_forward(span, rows, table, words, chunk, sum_column, share):
    count, width = rows.shape[0], table.shape[1]
    chunk_count = table.shape[0] // chunk
    per = chunk_count if chunk_count <= 4 else 4
    assert chunk_count % per == 0 and words >= 128
    return pl.pallas_call(
        functools.partial(band_kernel, chunk, per, words, sum_column),
        grid_spec=pltpu.PrefetchScalarGridSpec(
            num_scalar_prefetch=1,
            grid=(count // BLOCK,),
            in_specs=[
                pl.BlockSpec((BLOCK, width), lambda i, s: (i, 0)),
                pl.BlockSpec(table.shape, lambda i, s: (0, 0), **ONCE),
            ],
            out_specs=[
                pl.BlockSpec((8, BLOCK), lambda i, s: (0, i)),
                pl.BlockSpec((BLOCK, width), lambda i, s: (i, 0)),
            ],
            scratch_shapes=[pltpu.VMEM((BLOCK, width), jnp.float32)],
        ),
        out_shape=[
            jax.ShapeDtypeStruct((8, count), jnp.float32),
            jax.ShapeDtypeStruct((count, width), jnp.bfloat16),
        ],
        compiler_params=pltpu.CompilerParams(vmem_limit_bytes=VMEM_BYTES),
        cost_estimate=pl.CostEstimate(
            flops=int(share * 4 * count * table.shape[0] * max(width, 256)),
            bytes_accessed=table.size * 2 + count * width * 6,
            transcendentals=int(share * count * table.shape[0]),
        ),
        name="band_forward",
    )(span, rows, table)


def head_grad_kernel(chunk, lists, base_ref, table_ref, *refs):
    out_ref, sum_ref = refs[2 * lists :]
    words = table_ref.shape[0]
    base = base_ref[0] + pl.program_id(0) * words
    sum_ref[...] = jnp.zeros(sum_ref.shape, jnp.float32)
    for rows_ref, fact_ref in zip(refs[0 : 2 * lists : 2], refs[1 : 2 * lists : 2]):
        piece = min(rows_ref.shape[0], 1024)

        def visit(step, unused, rows_ref=rows_ref, fact_ref=fact_ref, piece=piece):
            at = pl.multiple_of(step * piece, piece)
            rows = rows_ref[pl.ds(at, piece), :]
            weight = fact_ref[0:1, pl.ds(at, piece)]
            total = fact_ref[1:2, pl.ds(at, piece)]
            ids = fact_ref[2:3, pl.ds(at, piece)].astype(jnp.int32)
            for start in range(0, words, chunk):
                probs = jnp.exp(product_nt(table_ref[start : start + chunk, :], rows) - total)
                word = base + start + lax.broadcasted_iota(jnp.int32, (chunk, 1), 0)
                grads = weight * (jnp.where(word == ids, 1.0, 0.0) - probs)
                sum_ref[start : start + chunk, :] += product(lowered(grads), rows)
            return unused

        lax.fori_loop(0, rows_ref.shape[0] // piece, visit, 0)
    out_ref[...] = lowered(sum_ref[...])


def head_grad(table, part, part_words, first_word, lists):
    width = table.shape[1]
    word_block = math.gcd(part_words, 640)
    steps = part_words // word_block
    chunk = word_block // 2 if word_block % 32 == 0 else word_block
    specs = []
    for rows, facts in lists:
        specs.append(pl.BlockSpec(rows.shape, lambda i, s: (0, 0), **ONCE))
        specs.append(pl.BlockSpec(facts.shape, lambda i, s: (0, 0), **ONCE))
    count = sum(rows.shape[0] for rows, facts in lists)
    scalars = jnp.stack([first_word + part * part_words, part * steps]).astype(jnp.int32)
    return pl.pallas_call(
        functools.partial(head_grad_kernel, chunk, len(lists)),
        grid_spec=pltpu.PrefetchScalarGridSpec(
            num_scalar_prefetch=1,
            grid=(steps,),
            in_specs=[pl.BlockSpec((word_block, width), lambda i, s: (s[1] + i, 0))] + specs,
            out_specs=pl.BlockSpec((word_block, width), lambda i, s: (i, 0)),
            scratch_shapes=[pltpu.VMEM((word_block, width), jnp.float32)],
        ),
        out_shape=jax.ShapeDtypeStruct((part_words, width), jnp.bfloat16),
        compiler_params=pltpu.CompilerParams(vmem_limit_bytes=VMEM_BYTES),
        cost_estimate=pl.CostEstimate(
            flops=4 * count * part_words * width,
            bytes_accessed=(count + part_words) * width * 2,
            transcendentals=count * part_words,
        ),
        name="head_grad",
    )(scalars, table, *[value for pair in lists for value in pair])


def band_grad_kernel(chunk, most, across, plan_ref, table_ref, rows_ref, fact_ref, out_ref, sum_ref):
    words = table_ref.shape[0]
    step_id = pl.program_id(0)
    base = plan_ref[most + 1] + step_id * words
    sum_ref[...] = jnp.zeros(sum_ref.shape, jnp.float32)

    def block_at(position):
        return pl.multiple_of(plan_ref[position] * BLOCK, BLOCK)

    def spread(starts):
        rows = [rows_ref[pl.ds(start, BLOCK), :] for start in starts]
        facts = [fact_ref[:, pl.ds(start, BLOCK)] for start in starts]
        rows = rows[0] if len(rows) == 1 else jnp.concatenate(rows, 0)
        facts = facts[0] if len(facts) == 1 else jnp.concatenate(facts, 1)
        weight, total = facts[0:1], facts[1:2]
        for start in range(0, words, chunk):
            probs = jnp.exp(product_nt(table_ref[start : start + chunk, :], rows) - total)
            sum_ref[start : start + chunk, :] -= product(lowered(weight * probs), rows)

    count = plan_ref[0]

    def pair(step, unused):
        spread([block_at(1 + 2 * step), block_at(2 + 2 * step)])
        return unused

    lax.fori_loop(0, count // 2, pair, 0)

    @pl.when(count % 2 == 1)
    def _():
        spread([block_at(count)])

    line = most + 2 + step_id * (most + 1)

    def hits(step, unused):
        at = block_at(line + 1 + step)
        rows = rows_ref[pl.ds(at, BLOCK), :]
        weight = fact_ref[0:1, pl.ds(at, BLOCK)]
        ids = fact_ref[2:3, pl.ds(at, BLOCK)].astype(jnp.int32)
        for start in range(0, words, chunk):
            word = base + start + lax.broadcasted_iota(jnp.int32, (chunk, 1), 0)
            chosen = lowered(jnp.where(word == ids, weight, 0.0))
            sum_ref[start : start + chunk, :] += product(chosen, rows)
        return unused

    lax.fori_loop(0, plan_ref[line], hits, 0)
    if across:
        out_ref[...] = sum_ref[...].T[: out_ref.shape[0], :].astype(out_ref.dtype)
    else:
        out_ref[...] = sum_ref[...].astype(out_ref.dtype)


def listed(flags):
    size = flags.shape[-1]
    order = jnp.cumsum(flags.astype(jnp.int32), -1)
    chosen = (order[..., None, :] == jnp.arange(1, size + 1)[:, None]) & flags[..., None, :]
    places = jnp.sum(jnp.where(chosen, jnp.arange(size), 0), -1)
    return jnp.concatenate([order[..., -1:], places], -1).astype(jnp.int32)


def band_grad(
    table, rows, facts, active, lowest, highest, part, part_words, first_word, chunk, result, across
):
    count, full = rows.shape[0], table.shape[1]
    word_block = chunk
    steps = part_words // word_block
    most = count // BLOCK
    first = first_word + part * part_words
    low = first + jnp.arange(steps, dtype=jnp.int32)[:, None] * word_block
    step_hits = active[None, :] & (lowest[None, :] < low + word_block) & (highest[None, :] >= low)
    plan = jnp.concatenate(
        [
            listed(active),
            first.reshape(1).astype(jnp.int32),
            listed(step_hits).reshape(-1),
            (part * steps).reshape(1).astype(jnp.int32),
        ]
    )
    last = plan.shape[0] - 1
    return pl.pallas_call(
        functools.partial(band_grad_kernel, chunk // 2 if chunk > 832 else chunk, most, across),
        grid_spec=pltpu.PrefetchScalarGridSpec(
            num_scalar_prefetch=1,
            grid=(steps,),
            in_specs=[
                pl.BlockSpec((word_block, full), lambda i, s: (s[last] + i, 0)),
                pl.BlockSpec((count, full), lambda i, s: (0, 0), **ONCE),
                pl.BlockSpec(facts.shape, lambda i, s: (0, 0), **ONCE),
            ],
            out_specs=(
                pl.BlockSpec((result.shape[0], word_block), lambda i, s: (0, i))
                if across
                else pl.BlockSpec((word_block, full), lambda i, s: (i, 0))
            ),
            scratch_shapes=[pltpu.VMEM((word_block, full), jnp.float32)],
        ),
        out_shape=result,
        compiler_params=pltpu.CompilerParams(vmem_limit_bytes=VMEM_BYTES),
        cost_estimate=pl.CostEstimate(
            flops=2 * count * part_words * 256,
            bytes_accessed=count * full * 2 + part_words * full * 4,
            transcendentals=count * part_words // 2,
        ),
        name="band_grad",
    )(plan, table, rows, facts)


def settle_kernel(
    member_ref,
    everyone_ref,
    fact_ref,
    head_mix_ref,
    middle_mix_ref,
    tail_mix_ref,
    head_hit_ref,
    middle_hit_ref,
    tail_hit_ref,
    term_ref,
    line_ref,
    slot_ref,
):
    step = pl.program_id(0)
    devices, _, slots = everyone_ref.shape
    tail_width = 64
    here = pl.ds(pl.multiple_of(step * BLOCK, BLOCK), BLOCK)

    def merged(read):
        lines = [read(device) for device in range(devices)]
        top = functools.reduce(jnp.maximum, [line[0] for line in lines])
        return top, sum(line[1] * jnp.exp(line[0] - top) for line in lines)

    head_top, head_sum = merged(
        lambda d: (everyone_ref[d, 0:1, here], everyone_ref[d, 1:2, here])
    )
    target = sum(everyone_ref[d, 2:3, here] for d in range(devices))
    slot_top, slot_sum = merged(lambda d: (everyone_ref[d, 3:4, :], everyone_ref[d, 4:5, :]))
    used = slot_sum > 0.0
    slot_total = jnp.where(used, slot_top + jnp.log(jnp.where(used, slot_sum, 1.0)), 0.0)
    member = member_ref[0]
    own_slot_top = jnp.where(used, everyone_ref[member, 3:4, :], 0.0)
    own_head_top = everyone_ref[member, 0:1, here]

    facts = fact_ref[...]
    slot, share, cotangent, first_cluster, second_cluster, band, word = (
        facts[index : index + 1] for index in range(7)
    )

    def as_columns(lines):
        square = jnp.concatenate(
            lines + [jnp.zeros((128 - len(lines), BLOCK), jnp.float32)], 0
        )
        return square.T

    def three(line):
        return [part.astype(jnp.float32) for part in thirds(line)]

    slot_column = as_columns([slot])[:, 0:1].astype(jnp.int32)
    hot = lowered(
        jnp.where(lax.broadcasted_iota(jnp.int32, (BLOCK, slots), 1) == slot_column, 1.0, 0.0)
    )
    lines = three(slot_total) + three(own_slot_top) + [jnp.zeros((10, slots), jnp.float32)]
    on_tokens = product_nt(lowered(jnp.concatenate(lines, 0)), hot)
    band_total = on_tokens[0:1] + on_tokens[1:2] + on_tokens[2:3]
    own_band_top = on_tokens[3:4] + on_tokens[4:5] + on_tokens[5:6]

    cluster_top = jnp.maximum(head_top, jnp.maximum(first_cluster, second_cluster))
    head_total = cluster_top + jnp.log(
        head_sum * jnp.exp(head_top - cluster_top)
        + jnp.exp(first_cluster - cluster_top)
        + jnp.exp(second_cluster - cluster_top)
    )
    in_head = band < 0.5
    cluster = jnp.where(band < 1.5, first_cluster, second_cluster)
    model_logp = target - head_total + jnp.where(in_head, 0.0, cluster - band_total)
    ratio = 0.25 * share * jnp.exp(-model_logp)
    weight = cotangent * 0.75 / (0.75 + ratio)
    head_scale = weight * jnp.exp(own_head_top - head_total)
    band_scale = weight * jnp.where(in_head, 0.0, jnp.exp(own_band_top - band_total))
    columns = as_columns([weight, head_scale, band_scale])
    weight_column, head_column, band_column = (columns[:, i : i + 1] for i in range(3))
    width = head_mix_ref.shape[1]
    term_ref[:, :width] = lowered(
        weight_column * head_hit_ref[...].astype(jnp.float32)
        - head_column * head_mix_ref[...].astype(jnp.float32)
    )
    narrow = tail_mix_ref.shape[1]
    kept = lax.broadcasted_iota(jnp.int32, (BLOCK, narrow), 1) < tail_width

    def widened(values):
        values = jnp.where(kept, values, 0.0)
        more = middle_mix_ref.shape[1] - narrow
        return jnp.concatenate([values, jnp.zeros((BLOCK, more), jnp.float32)], 1)

    band_mix = product(hot, middle_mix_ref[...]) + widened(product(hot, tail_mix_ref[...]))
    band_hit = middle_hit_ref[...].astype(jnp.float32) + widened(
        tail_hit_ref[...].astype(jnp.float32)
    )
    term_ref[:, width:] = lowered(weight_column * band_hit - band_column * band_mix)
    line_ref[...] = jnp.concatenate(
        [
            model_logp + jnp.log(0.75 + ratio),
            weight,
            head_total,
            word,
            jnp.zeros((4, BLOCK), jnp.float32),
        ],
        0,
    )

    @pl.when(step == 0)
    def _():
        slot_ref[...] = jnp.concatenate(
            [jnp.zeros((8, slots), jnp.float32), slot_total, jnp.zeros((7, slots), jnp.float32)], 0
        )

    sent = three(weight) + three(word) + [jnp.zeros((10, BLOCK), jnp.float32)]
    slot_ref[0:8, :] += product(lowered(jnp.concatenate(sent, 0)), hot)[0:8]


def settle(member, everyone, facts, head_mix, middle_mix, tail_mix, hits):
    count, width = head_mix.shape
    slots = middle_mix.shape[0]
    full = width + middle_mix.shape[1]

    def tokens(values):
        return pl.BlockSpec((BLOCK, values.shape[1]), lambda i, s: (i, 0))

    def whole(values):
        return pl.BlockSpec(values.shape, lambda i, s: (0,) * values.ndim, **ONCE)

    lines = pl.BlockSpec((8, BLOCK), lambda i, s: (0, i))
    return pl.pallas_call(
        settle_kernel,
        grid_spec=pltpu.PrefetchScalarGridSpec(
            num_scalar_prefetch=1,
            grid=(count // BLOCK,),
            in_specs=[whole(everyone), lines, tokens(head_mix), whole(middle_mix), whole(tail_mix)]
            + [tokens(hit) for hit in hits],
            out_specs=[
                pl.BlockSpec((BLOCK, full), lambda i, s: (i, 0)),
                lines,
                pl.BlockSpec((16, slots), lambda i, s: (0, 0)),
            ],
        ),
        out_shape=[
            jax.ShapeDtypeStruct((count, full), jnp.bfloat16),
            jax.ShapeDtypeStruct((8, count), jnp.float32),
            jax.ShapeDtypeStruct((16, slots), jnp.float32),
        ],
        compiler_params=pltpu.CompilerParams(vmem_limit_bytes=VMEM_BYTES),
        cost_estimate=pl.CostEstimate(
            flops=2 * count * slots * 1024,
            bytes_accessed=count * width * 12 + slots * full,
            transcendentals=slots * 64,
        ),
        name="settle",
    )(member.reshape(1).astype(jnp.int32), everyone, facts, head_mix, middle_mix, tail_mix, *hits)


def line_turns(value):
    size = lax.axis_size("seq")
    return [value] + [
        lax.ppermute(value, "seq", [(d, (d - k) % size) for d in range(size)])
        for k in range(1, size)
    ]


def line_step(before, behind, step):
    size = lax.axis_size("seq")
    return (
        lax.ppermute(before, "seq", [(d, d + 1) for d in range(step - 1, size - 1)]),
        lax.ppermute(behind, "seq", [(d, d - 1) for d in range(1, size - step + 1)]),
    )


def line_steps(value):
    found = [(value, value)]

    def advance(*others):
        step = len(found)
        if step == lax.axis_size("seq"):
            return others
        moved = line_step(*found[-1], step)
        moved, others = lax.optimization_barrier((moved, others))
        found.append(moved)
        return others

    return found, advance


def line_ordered(found, axis):
    size, place = lax.axis_size("seq"), lax.axis_index("seq")
    ordered = []
    for source in range(size):
        value = found[0][0]
        for step in range(1, size):
            if source + step < size:
                value = jnp.where(place == source + step, found[step][0], value)
            if source - step >= 0:
                value = jnp.where(place == source - step, found[step][1], value)
        ordered.append(value)
    return jnp.concatenate(ordered, axis)


def earlier_joined(value):
    size, place = lax.axis_size("seq"), lax.axis_index("seq")
    joined = jnp.zeros((size,) + value.shape, value.dtype)
    for step in range(size - 1, -1, -1):
        piece = value
        if step:
            piece = lax.ppermute(value, "seq", [(d, d + step) for d in range(size - step)])
        joined = lax.dynamic_update_index_in_dim(joined, piece, jnp.maximum(place - step, 0), 0)
    return joined.reshape((-1,) + value.shape[1:])


def in_order(pieces):
    size, place = lax.axis_size("seq"), lax.axis_index("seq")
    joined = jnp.zeros((size,) + pieces[0].shape, pieces[0].dtype)
    for k, piece in enumerate(pieces):
        joined = lax.dynamic_update_index_in_dim(joined, piece, lax.rem(place + k, size), 0)
    return joined.reshape((-1,) + pieces[0].shape[1:])


def line_scatter(values, behind=True):
    size, place = lax.axis_size("seq"), lax.axis_index("seq")
    parts = values.reshape((size, -1) + values.shape[1:])

    def part(index):
        return lax.dynamic_index_in_dim(parts, lax.rem(index, size), 0, False)

    total = part(place).astype(jnp.float32)
    for k in range(1, size):
        pairs = [(d, (d - k) % size) for d in range(0 if behind else k, size)]
        total = total + lax.ppermute(part(place + size - k), "seq", pairs).astype(jnp.float32)
    return total


def turn_kernel(rows_ref, out_ref):
    out_ref[...] = rows_ref[...].astype(jnp.float32).T.astype(out_ref.dtype)


def turned(rows, kind):
    return pl.pallas_call(
        turn_kernel, out_shape=jax.ShapeDtypeStruct(rows.shape[::-1], kind), name="turned"
    )(rows)


def word_pad(rows, biggest, splits):
    chunk = min(biggest, round_up(rows, 128))
    chunks = -(-rows // chunk)
    if chunks > 4:
        chunks = round_up(chunks, 4)
    return chunk, chunks * chunk


def on_device(
    inputs,
    targets,
    neighbours,
    neighbour_scores,
    loglik_grad,
    first_gain,
    first_shift,
    query_weight,
    query_bias,
    key_weight,
    value_weight,
    value_bias,
    out_weight,
    out_bias,
    second_gain,
    second_shift,
    inner_weight,
    inner_bias,
    outer_weight,
    outer_bias,
    final_gain,
    final_shift,
    head_table,
    cluster_weight,
    middle_map,
    middle_table,
    tail_map,
    tail_table,
):
    nb = lax.axis_size("batch")
    nz = lax.axis_size("seq")
    member = lax.axis_index("batch")
    place = lax.axis_index("seq")
    tokens = inputs[0]
    own_ids = targets[0]
    token_count, feature_count = tokens.shape
    group_count = token_count * nb
    slot_count = group_count + BLOCK
    query_start = (place * token_count).reshape(1)

    normed_low = lowered(layer_norm(tokens, first_gain, first_shift))
    normed_all = earlier_joined(normed_low)
    top_score = jnp.max(neighbour_scores[0], -1, keepdims=True)
    exponent = jnp.exp(neighbour_scores[0] - top_score)
    knn_prob = jnp.sum(jnp.where(neighbours[0] == 0, exponent, 0.0), -1) / jnp.sum(exponent, -1)
    early = jnp.stack([own_ids.astype(jnp.float32), knn_prob, loglik_grad[0]])
    early = lax.all_gather(early, "batch", axis=1, tiled=True)
    all_ids = early[0].astype(jnp.int32)
    all_knn, all_up = early[1], early[2]
    in_head = all_ids < HEAD_WORDS
    in_middle = (all_ids >= HEAD_WORDS) & (all_ids < HEAD_WORDS + MID_WORDS)
    in_tail = all_ids >= HEAD_WORDS + MID_WORDS
    order = jnp.arange(group_count, dtype=jnp.int32)
    ahead = (all_ids[None, :] < all_ids[:, None]) | (
        (all_ids[None, :] == all_ids[:, None]) & (order[None, :] < order[:, None])
    )
    rank = jnp.sum(ahead.astype(jnp.int32), -1)
    head_size = jnp.sum(in_head.astype(jnp.int32))
    middle_size = jnp.sum(in_middle.astype(jnp.int32))
    tail_size = group_count - head_size - middle_size
    middle_blocks = (middle_size + BLOCK - 1) // BLOCK
    tail_blocks = (tail_size + BLOCK - 1) // BLOCK
    slot = jnp.where(
        in_head,
        -1,
        rank - head_size + jnp.where(in_tail, middle_blocks * BLOCK - middle_size, 0),
    )
    zero_span = jnp.zeros((1,), jnp.int32)
    head_span = jnp.array([0, group_count // BLOCK], jnp.int32)
    middle_span = jnp.stack([0 * middle_blocks, middle_blocks]).astype(jnp.int32)
    tail_span = jnp.stack([middle_blocks, middle_blocks + tail_blocks]).astype(jnp.int32)
    slot_order = jnp.arange(slot_count, dtype=jnp.int32)
    slot_middle = slot_order < middle_size
    slot_tail = (slot_order >= middle_blocks * BLOCK) & (
        slot_order < middle_blocks * BLOCK + tail_size
    )
    slot_used = slot_middle | slot_tail
    band_id = all_ids - jnp.where(in_tail, HEAD_WORDS + MID_WORDS, HEAD_WORDS)

    tables = (head_table, middle_table, tail_table)
    sizes = tuple(table.shape[0] for table in tables)
    head_chunk, head_padded = word_pad(sizes[0], 1280, nz)
    middle_chunk, middle_padded = word_pad(sizes[1], 1280, nz)
    tail_chunk, tail_padded = word_pad(sizes[2], 1664, nz)
    tail_width = tail_table.shape[1]
    head_pad = jnp.pad(head_table, ((0, head_padded - sizes[0]), (0, 0)))
    middle_pad = jnp.pad(middle_table, ((0, middle_padded - sizes[1]), (0, 0)))
    tail_word = jnp.arange(tail_padded, dtype=jnp.int32)
    tail_bias = jnp.where(tail_word < jnp.minimum(TAIL_WORDS - member * sizes[2], sizes[2]), 0.0, NEG_FILL)
    tail_pad = jnp.concatenate(
        [
            jnp.pad(tail_table.T, ((0, 0), (0, tail_padded - sizes[2]))),
            jnp.ones((1, tail_padded), jnp.bfloat16),
            lowered(tail_bias)[None, :],
            jnp.zeros((126 - tail_width, tail_padded), jnp.bfloat16),
        ],
        0,
    ).T
    locals_ = (
        all_ids - member * sizes[0],
        all_ids - HEAD_WORDS - member * sizes[1],
        all_ids - HEAD_WORDS - MID_WORDS - member * sizes[2],
    )
    owned = tuple(
        inside & (local >= 0) & (local < size)
        for inside, local, size in zip((in_head, in_middle, in_tail), locals_, sizes)
    )
    hit_rows = tuple(
        jnp.where(
            own[:, None],
            jnp.take(table, jnp.clip(local, 0, size - 1), axis=0, mode="clip"),
            jnp.bfloat16(0),
        )
        for own, table, local, size in zip(owned, (head_pad, middle_pad, tail_pad), locals_, sizes)
    )

    queries = lowered(product(normed_low, query_weight) + query_bias)
    key_rows = lowered(product(normed_all, key_weight))
    value_rows = lowered(product(normed_all, value_weight) + value_bias)
    attended_low = attend(query_start, queries, key_rows, value_rows)
    mixed = tokens + product(attended_low, out_weight) + out_bias
    second_low = lowered(layer_norm(mixed, second_gain, second_shift))
    before = product(second_low, inner_weight) + inner_bias
    hidden_low = lowered(jax.nn.gelu(before))
    final = mixed + product(hidden_low, outer_weight) + outer_bias
    state_low = lowered(layer_norm(final, final_gain, final_shift))
    all_states = lax.all_gather(state_low, "batch", axis=0, tiled=True)
    split = 2 * nz * group_count * feature_count <= 24 << 20
    if split:
        block_states = lax.all_gather(state_low, "seq", axis=0, tiled=True)
    all_states, head_pad, middle_pad, tail_pad, hit_rows, slot, early = lax.optimization_barrier(
        (all_states, head_pad, middle_pad, tail_pad, hit_rows, slot, early)
    )

    middle_width = middle_map.shape[1]
    maps = jnp.pad(jnp.concatenate([middle_map, tail_map], 1), ((0, 0), (0, 128 - tail_width)))
    one_column = (jnp.arange(middle_width + 128) == middle_width + tail_width + 1).astype(jnp.float32)
    band_low = lowered(product(all_states, maps) + one_column)
    middle_low, tail_low = band_low[:, :middle_width], band_low[:, middle_width:]
    cluster_lines = product_nt(
        jnp.pad(cluster_weight.T, ((0, 6), (0, 0))), all_states
    )
    slot_full = pick_rows(slot, band_low, slot_count, True, jnp.bfloat16)
    first_tail = middle_blocks * BLOCK
    in_tail_slot = slot_order >= first_tail
    slot_low = jnp.where(
        in_tail_slot[:, None],
        jnp.pad(slot_full[:, middle_width:], ((0, 0), (0, middle_width - 128))),
        slot_full[:, :middle_width],
    )
    if split:
        piece = slot_count // nb
        slot_piece = lax.dynamic_slice_in_dim(slot_low, member * piece, piece, 0)
        other_slots = jnp.concatenate(line_turns(slot_piece)[1:], 0)
        slot_low, block_states = lax.optimization_barrier((slot_low, block_states))
        other_states = lax.dynamic_slice_in_dim(
            jnp.concatenate([block_states, block_states], 0),
            (place + 1) * token_count,
            (nz - 1) * token_count,
            0,
        )
        other_states = lax.all_gather(other_states, "batch", axis=0, tiled=True)
    tail_stats, tail_mix = band_forward(
        tail_span, slot_low, tail_pad, tail_padded, tail_chunk, tail_width, 0.5
    )
    middle_stats, middle_mix = band_forward(
        middle_span, slot_low, middle_pad, sizes[1], middle_chunk, None, 0.25
    )
    head_stats, head_mix = band_forward(
        head_span, all_states, head_pad, sizes[0], head_chunk, None, 1.0
    )
    inner_lane = jnp.arange(128) < tail_width
    target_part = (
        jnp.sum(hit_rows[0].astype(jnp.float32) * all_states.astype(jnp.float32), -1)
        + jnp.sum(hit_rows[1].astype(jnp.float32) * middle_low.astype(jnp.float32), -1)
        + jnp.sum(
            jnp.where(inner_lane, hit_rows[2].astype(jnp.float32), 0.0)
            * tail_low.astype(jnp.float32),
            -1,
        )
    )
    slot_stats = jnp.where(in_tail_slot[None, :], tail_stats[:2], middle_stats[:2])
    extra = ((0, 0), (0, BLOCK))
    stats = jnp.concatenate(
        [
            jnp.pad(jnp.concatenate([head_stats[:2], target_part[None]], 0), extra),
            slot_stats,
            jnp.zeros((3, slot_count), jnp.float32),
        ],
        0,
    )
    if split:
        stats, other_states, other_slots = lax.optimization_barrier(
            (stats, other_states, other_slots)
        )
        other_slots = lax.all_gather(other_slots, "batch", axis=0, tiled=True)
    everyone = lax.all_gather(stats, "batch")

    token_facts = jnp.concatenate(
        [
            slot.astype(jnp.float32)[None],
            early[1:3],
            cluster_lines[:2],
            jnp.where(in_head, 0.0, jnp.where(in_middle, 1.0, 2.0))[None],
            early[0:1],
            jnp.zeros((1, group_count), jnp.float32),
        ],
        0,
    )
    terms, lines, slot_lines = settle(
        member, everyone, token_facts, head_mix, middle_mix, tail_mix, hit_rows
    )
    own_terms = lax.psum_scatter(terms, "batch", scatter_dimension=0, tiled=True).astype(jnp.float32)

    def own_part(values):
        return lax.dynamic_slice_in_dim(values, member * token_count, token_count, 0)

    loglik = own_part(lines[0])

    kind = jnp.where(slot_middle, 1.0, jnp.where(slot_tail, 2.0, 0.0))
    slot_facts = jnp.stack(
        [
            jnp.sum(slot_lines[0:3], 0),
            slot_lines[8],
            jnp.sum(slot_lines[3:6], 0),
            kind,
        ]
    )
    head_facts = jnp.concatenate([lines[1:4], jnp.zeros((1, group_count), jnp.float32)], 0)
    if split:
        other_slots = (
            other_slots.reshape(nb, nz - 1, piece, middle_width)
            .transpose(1, 0, 2, 3)
            .reshape(-1, middle_width)
        )
        rows_all = jnp.concatenate([slot_low, other_slots], 0)
        fact_pieces = line_turns(jnp.concatenate([slot_facts, head_facts], 1))
        facts = jnp.concatenate([value[:, :slot_count] for value in fact_pieces], 1)
        other_facts = (
            jnp.stack([value[:, slot_count:] for value in fact_pieces[1:]], 1)
            .reshape(4, nz - 1, nb, token_count)
            .transpose(0, 2, 1, 3)
            .reshape(4, -1)
        )
        lists = [(all_states, head_facts), (other_states, other_facts)]
        part, parts = place, nz
    else:
        rows_all, facts, lists = slot_low, slot_facts, [(all_states, head_facts)]
        part, parts = 0 * place, 1
    head_part = head_grad(head_pad, part, head_padded // parts, member * sizes[0], lists)
    block_facts = facts[2:4].reshape(2, -1, BLOCK)
    block_kind = jnp.max(block_facts[1], -1)
    filled = block_facts[1] > 0
    lowest = jnp.min(jnp.where(filled, block_facts[0], 1e9), -1).astype(jnp.int32)
    highest = jnp.max(jnp.where(filled, block_facts[0], -1e9), -1).astype(jnp.int32)
    facts = jnp.concatenate(
        [facts[:2], jnp.where(facts[3:4] > 0, facts[2:3], -1e9), jnp.zeros_like(facts[:1])], 0
    )
    middle_result = jax.ShapeDtypeStruct(
        (sizes[1], middle_width) if split else (middle_padded, middle_width),
        jnp.float32 if split else jnp.bfloat16,
    )
    middle_part = band_grad(
        middle_pad,
        rows_all,
        facts,
        block_kind == 1,
        lowest,
        highest,
        0 * place,
        middle_padded,
        HEAD_WORDS + member * sizes[1],
        middle_chunk,
        middle_result,
        False,
    )
    if split:
        head_found, head_advance = line_steps(head_part)
        own_terms, middle_part = head_advance(own_terms, middle_part)
    else:
        own_terms, middle_part = lax.optimization_barrier((own_terms, middle_part))

    own_middle = own_part(in_middle)
    own_tail = own_part(in_tail)
    own_lines = lax.dynamic_slice_in_dim(lines, member * token_count, token_count, 1)
    own_weights, own_total = own_lines[1], own_lines[2]
    own_clusters = product(state_low, cluster_weight)
    band_state = own_terms[:, feature_count:]
    middle_state = lowered(jnp.where(own_middle[:, None], band_state, 0.0))
    tail_state = lowered(jnp.where(own_tail[:, None], band_state[:, :tail_width], 0.0))
    cluster_hit = jnp.stack([own_middle, own_tail], -1).astype(jnp.float32)
    cluster_grad = own_weights[:, None] * (
        cluster_hit - jnp.exp(own_clusters - own_total[:, None])
    )
    state_grad = (
        own_terms[:, :feature_count]
        + product_nt(middle_state, middle_map)
        + product_nt(tail_state, tail_map)
        + product_nt(cluster_grad, cluster_weight.astype(jnp.float32))
    )
    middle_map_grad = product_tn(state_low, middle_state)
    tail_map_rows = product_tn(tail_state, state_low)
    cluster_rows = product_tn(cluster_grad, state_low.astype(jnp.float32))
    final_grad, final_gain_grad, final_shift_grad = norm_back(
        final, final_gain, final_shift, state_grad
    )
    final_low = lowered(final_grad)
    outer_weight_grad = product_tn(hidden_low, final_low)
    outer_bias_grad = jnp.sum(final_grad, 0)
    outer_part = lax.psum_scatter(
        lowered(outer_weight_grad), "batch", scatter_dimension=0, tiled=True
    )
    before_grad = lowered(gelu_back(before, product_nt(final_low, outer_weight)))
    inner_weight_grad = product_tn(second_low, before_grad)
    inner_bias_grad = jnp.sum(before_grad.astype(jnp.float32), 0)
    inner_part = lax.psum_scatter(
        lowered(inner_weight_grad), "batch", scatter_dimension=0, tiled=True
    )
    second_in_grad, second_gain_grad, second_shift_grad = norm_back(
        mixed, second_gain, second_shift, product_nt(before_grad, inner_weight)
    )
    mixed_grad = final_grad + second_in_grad
    mixed_low = lowered(mixed_grad)
    out_weight_grad = product_tn(attended_low, mixed_low)
    out_bias_grad = jnp.sum(mixed_grad, 0)
    attended_grad = lowered(product_nt(mixed_low, out_weight))
    if split:
        (attended_grad,) = head_advance(attended_grad)
    query_low, key_low, value_low = attend_back(
        query_start, queries, key_rows, value_rows, attended_grad
    )
    if split:
        for unused in range(nz - 3):
            query_low, key_low, value_low = head_advance(query_low, key_low, value_low)
    query_weight_grad = product_tn(normed_low, query_low)
    key_weight_grad = product_tn(normed_all, key_low)
    value_weight_grad = product_tn(normed_all, value_low)
    query_bias_grad = jnp.sum(query_low.astype(jnp.float32), 0)
    value_bias_grad = jnp.sum(value_low.astype(jnp.float32), 0)
    spread = product_nt(key_low, key_weight) + product_nt(value_low, value_weight)
    query_spread = product_nt(query_low, query_weight)
    first_shift_grad = jnp.sum(spread, 0) + jnp.sum(query_spread, 0)
    all_centred = (normed_all.astype(jnp.float32) - first_shift) / first_gain
    own_average = jnp.mean(tokens, -1, keepdims=True)
    own_spread = jnp.mean((tokens - own_average) ** 2, -1, keepdims=True)
    own_centred = (tokens - own_average) * lax.rsqrt(own_spread + EPSILON)
    first_gain_grad = jnp.sum(all_centred * spread, 0) + jnp.sum(own_centred * query_spread, 0)
    bias_rows = inner_bias_grad.shape[0] // feature_count
    inner_bias_rows = (
        inner_bias_grad.reshape(nb, bias_rows, -1).transpose(1, 0, 2).reshape(bias_rows, -1)
    )
    vectors = [
        first_gain_grad,
        first_shift_grad,
        query_bias_grad,
        value_bias_grad,
        out_bias_grad,
        second_gain_grad,
        second_shift_grad,
        outer_bias_grad,
        final_gain_grad,
        final_shift_grad,
    ]
    rows = [tail_map_rows, cluster_rows, inner_bias_rows] + [value[None] for value in vectors]
    edges = [0]
    for row in rows:
        edges.append(edges[-1] + row.shape[0])
    row_count = round_up(edges[-1], 128)
    rows.append(jnp.zeros((row_count - edges[-1], feature_count), jnp.float32))
    columns = [
        query_weight_grad,
        key_weight_grad,
        value_weight_grad,
        out_weight_grad,
        middle_map_grad,
        turned(jnp.concatenate(rows, 0), jnp.bfloat16),
    ]
    rest = jnp.concatenate([lowered(column) for column in columns], 1)
    inner_low = lowered(line_scatter(inner_part))
    spread_low = lowered(spread)
    rest, facts, inner_low, spread_low = lax.optimization_barrier(
        (rest, facts, inner_low, spread_low)
    )
    rest_part = lax.psum_scatter(rest, "batch", scatter_dimension=0, tiled=True)
    inner_pieces = line_turns(inner_low)

    def tail_gradient(part, parts):
        return band_grad(
            tail_pad,
            rows_all,
            facts,
            block_kind == 2,
            lowest,
            highest,
            part,
            tail_padded // parts,
            HEAD_WORDS + MID_WORDS + member * sizes[2],
            math.gcd(tail_padded // parts, tail_chunk),
            jax.ShapeDtypeStruct((tail_width, tail_padded // parts), jnp.bfloat16),
            True,
        )

    if split:
        middle_table_grad = middle_part
        head_table_grad = line_ordered(head_found, 0)
        first_tail = tail_gradient(2 * place, 2 * nz)
        first_tail, facts, inner_pieces, outer_part = lax.optimization_barrier(
            (first_tail, facts, inner_pieces, outer_part)
        )
        first_found, first_advance = line_steps(first_tail)
        second_tail = tail_gradient(2 * place + 1, 2 * nz)
        outer_low = lowered(line_scatter(outer_part))
        second_tail, outer_low = first_advance(second_tail, outer_low)
        second_found, second_advance = line_steps(second_tail)
        for unused in range(nz - 1):
            first_advance()
            second_advance()
        halves = [
            line_ordered(found, 0).reshape(nz, tail_width, -1)
            for found in (first_found, second_found)
        ]
        tail_sum = jnp.stack(halves, 1).transpose(2, 0, 1, 3).reshape(tail_width, -1)
    else:
        outer_low = lowered(line_scatter(outer_part))
        middle_table_grad = lax.psum(middle_part, "seq")[: sizes[1]].astype(jnp.float32)
        head_table_grad = lax.psum(head_part, "seq")
        tail_sum = lax.psum(tail_gradient(part, parts), "seq")
    head_table_grad = head_table_grad[: sizes[0]].astype(jnp.float32)
    tail_table_grad = tail_sum[:, : sizes[2]].astype(jnp.float32).T
    normed_grad = query_spread + line_scatter(spread_low, False)
    first_in_grad, unused, unused = norm_back(tokens, first_gain, first_shift, normed_grad)
    input_grad = mixed_grad + first_in_grad

    inner_sum = in_order(inner_pieces).astype(jnp.float32)
    outer_sum = in_order(line_turns(outer_low)).astype(jnp.float32)
    rest_low = lax.psum(rest_part, "seq")
    rest_sum = rest_low[:, : 4 * feature_count + middle_width].astype(jnp.float32)
    cut = [rest_sum[:, i * feature_count : (i + 1) * feature_count] for i in range(4)]
    middle_map_sum = rest_sum[:, 4 * feature_count : 4 * feature_count + middle_width]
    row_sum = turned(rest_low[:, 4 * feature_count + middle_width :], jnp.float32)
    tail_map_sum, cluster_sum, inner_bias_sum = (
        row_sum[low:high] for low, high in zip(edges[:3], edges[1:4])
    )
    lines = [row_sum[index] for index in range(edges[3], edges[3] + len(vectors))]
    return (
        loglik.reshape(1, token_count),
        input_grad.reshape(1, token_count, feature_count),
        lines[0],
        lines[1],
        cut[0],
        lines[2],
        cut[1],
        cut[2],
        lines[3],
        cut[3],
        lines[4],
        lines[5],
        lines[6],
        inner_sum,
        inner_bias_sum.reshape(-1),
        outer_sum,
        lines[7],
        lines[8],
        lines[9],
        head_table_grad,
        cluster_sum.T,
        middle_map_sum,
        middle_table_grad,
        tail_map_sum.T,
        tail_table_grad,
    )


def solution(mesh):
    return jax.shard_map(
        on_device,
        mesh=mesh,
        in_specs=(
            P("batch", "seq", None),
            P("batch", "seq"),
            P("batch", "seq", None),
            P("batch", "seq", None),
            P("batch", "seq"),
            P(),
            P(),
            P(),
            P(),
            P(),
            P(),
            P(),
            P(),
            P(),
            P(),
            P(),
            P(),
            P(),
            P(),
            P(),
            P(),
            P(),
            P("batch", None),
            P(),
            P(),
            P("batch", None),
            P(),
            P("batch", None),
        ),
        out_specs=(
            P("batch", "seq"),
            P("batch", "seq", None),
            P("batch"),
            P("batch"),
            P("batch", None),
            P("batch"),
            P("batch", None),
            P("batch", None),
            P("batch"),
            P("batch", None),
            P("batch"),
            P("batch"),
            P("batch"),
            P("batch", None),
            P("batch"),
            P("batch", None),
            P("batch"),
            P("batch"),
            P("batch"),
            P("batch", None),
            P("batch", None),
            P("batch", None),
            P("batch", None),
            P("batch", None),
            P("batch", None),
        ),
        check_vma=False,
    )
```

```python
import functools
import math

import jax
import jax.numpy as jnp
from jax import lax
from jax.experimental import pallas as pl
from jax.experimental.pallas import tpu as pltpu
from jax.sharding import PartitionSpec as P

HEADS = 16
HEAD_WORDS = 20000
MID_WORDS = 40000
TAIL_WORDS = 207735


NEG_FILL = -1e30
EPSILON = 1e-05
BLOCK = 256
SAFE = 1e30
VMEM_BYTES = 56 << 20
ONCE = dict(pipeline_mode=pl.Buffered(1))


def layer_norm(values, gain_vector, shift_vector):
    average = jnp.mean(values, -1, keepdims=True)
    centred = values - average
    spread = jnp.mean(centred * centred, -1, keepdims=True)
    return centred * lax.rsqrt(spread + EPSILON) * gain_vector + shift_vector


def norm_back(values, gain_vector, shift_vector, upstream):
    unused, pullback = jax.vjp(layer_norm, values, gain_vector, shift_vector)
    return pullback(upstream)


def gelu_back(before, upstream):
    unused, pullback = jax.vjp(jax.nn.gelu, before)
    return pullback(upstream)[0]


def product(former, latter):
    return jnp.dot(former, latter, preferred_element_type=jnp.float32)


def product_tn(former, latter):
    return lax.dot_general(
        former, latter, (((0,), (0,)), ((), ())), preferred_element_type=jnp.float32
    )


def product_nt(former, latter):
    return lax.dot_general(
        former, latter, (((1,), (1,)), ((), ())), preferred_element_type=jnp.float32
    )


def lowered(values):
    return values.astype(jnp.bfloat16)


def round_up(count, unit):
    return -(-count // unit) * unit


def thirds(values):
    high = lowered(values)
    rest = values - high.astype(jnp.float32)
    middle = lowered(rest)
    return [high, middle, lowered(rest - middle.astype(jnp.float32))]


def attend_kernel(start_ref, query_ref, key_ref, value_ref, out_ref):
    rows, keys = query_ref.shape[0], key_ref.shape[0]
    half = query_ref.shape[1] // 2
    query_pos = start_ref[0] + lax.broadcasted_iota(jnp.int32, (rows, keys), 0)
    allowed = lax.broadcasted_iota(jnp.int32, (rows, keys), 1) <= query_pos
    for part in range(2):
        cols = slice(part * half, part * half + half)
        scores = product_nt(query_ref[:, cols], key_ref[:, cols]) * half**-0.5
        scores = jnp.where(allowed, scores, NEG_FILL)
        weights = jnp.exp(scores - jnp.max(scores, 1, keepdims=True))
        weights = weights / jnp.sum(weights, 1, keepdims=True)
        out_ref[:, cols] = lowered(product(lowered(weights), value_ref[:, cols]))


def attend(start, queries, keys, values):
    rows, features = queries.shape
    width = 2 * features // HEADS
    own = pl.BlockSpec((rows, width), lambda i, s: (0, i))
    whole = pl.BlockSpec((keys.shape[0], width), lambda i, s: (0, i))
    return pl.pallas_call(
        attend_kernel,
        grid_spec=pltpu.PrefetchScalarGridSpec(
            num_scalar_prefetch=1,
            grid=(features // width,),
            in_specs=[own, whole, whole],
            out_specs=own,
        ),
        out_shape=jax.ShapeDtypeStruct((rows, features), jnp.bfloat16),
        compiler_params=pltpu.CompilerParams(vmem_limit_bytes=VMEM_BYTES),
        cost_estimate=pl.CostEstimate(
            flops=4 * rows * keys.shape[0] * features,
            bytes_accessed=4 * (rows + keys.shape[0]) * features,
            transcendentals=rows * keys.shape[0] * HEADS,
        ),
        name="attend",
    )(start, queries, keys, values)


def attend_back_kernel(
    start_ref, query_ref, key_ref, value_ref, up_ref, query_grad_ref, key_grad_ref, value_grad_ref
):
    rows, keys = query_ref.shape[0], key_ref.shape[0]
    half = query_ref.shape[1] // 2
    scale = half**-0.5
    query_pos = start_ref[0] + lax.broadcasted_iota(jnp.int32, (keys, rows), 1)
    allowed = lax.broadcasted_iota(jnp.int32, (keys, rows), 0) <= query_pos
    for part in range(2):
        cols = slice(part * half, part * half + half)
        query, key, value, up = (
            ref[:, cols] for ref in (query_ref, key_ref, value_ref, up_ref)
        )
        scores = jnp.where(allowed, product_nt(key, query) * scale, NEG_FILL)
        probs = jnp.exp(scores - jnp.max(scores, 0, keepdims=True))
        probs = probs / jnp.sum(probs, 0, keepdims=True)
        prob_grad = product_nt(value, up)
        delta = jnp.sum(probs * prob_grad, 0, keepdims=True)
        score_grad = lowered(probs * (prob_grad - delta))
        value_grad_ref[:, cols] = lowered(product(lowered(probs), up))
        key_grad_ref[:, cols] = lowered(product(score_grad, query) * scale)
        query_grad_ref[:, cols] = lowered(product_tn(score_grad, key) * scale)


def attend_back(start, queries, keys, values, upstream):
    rows, features = queries.shape
    count = keys.shape[0]
    width = 2 * features // HEADS
    own = pl.BlockSpec((rows, width), lambda i, s: (0, i))
    whole = pl.BlockSpec((count, width), lambda i, s: (0, i))
    return pl.pallas_call(
        attend_back_kernel,
        grid_spec=pltpu.PrefetchScalarGridSpec(
            num_scalar_prefetch=1,
            grid=(features // width,),
            in_specs=[own, whole, whole, own],
            out_specs=[own, whole, whole],
        ),
        out_shape=[
            jax.ShapeDtypeStruct((rows, features), jnp.bfloat16),
            jax.ShapeDtypeStruct((count, features), jnp.bfloat16),
            jax.ShapeDtypeStruct((count, features), jnp.bfloat16),
        ],
        compiler_params=pltpu.CompilerParams(vmem_limit_bytes=VMEM_BYTES),
        cost_estimate=pl.CostEstimate(
            flops=10 * rows * count * features,
            bytes_accessed=6 * (rows + count) * features,
            transcendentals=rows * count * HEADS,
        ),
        name="attend_back",
    )(start, queries, keys, values, upstream)


def pick_kernel(by_slot, index_ref, rows_ref, out_ref):
    count = rows_ref.shape[0]
    total = jnp.zeros(out_ref.shape, jnp.float32)
    base = pl.program_id(0) * BLOCK
    for at in range(0, count, BLOCK):
        if by_slot:
            place = base + lax.broadcasted_iota(jnp.int32, (BLOCK, BLOCK), 0)
            hit = index_ref[:, at : at + BLOCK] == place
        else:
            place = at + lax.broadcasted_iota(jnp.int32, (BLOCK, BLOCK), 1)
            hit = index_ref[...] == place
        onehot = lowered(jnp.where(hit, 1.0, 0.0))
        total = total + product(onehot, rows_ref[at : at + BLOCK, :])
    out_ref[...] = total.astype(out_ref.dtype)


def pick_rows(index, rows, out_count, by_slot, kind):
    count, width = rows.shape
    if by_slot:
        index = index.reshape(1, -1)
        index_spec = pl.BlockSpec(index.shape, lambda i: (0, 0))
    else:
        index = index.reshape(-1, 1)
        index_spec = pl.BlockSpec((BLOCK, 1), lambda i: (i, 0))
    return pl.pallas_call(
        functools.partial(pick_kernel, by_slot),
        grid=(out_count // BLOCK,),
        in_specs=[index_spec, pl.BlockSpec(rows.shape, lambda i: (0, 0), **ONCE)],
        out_specs=pl.BlockSpec((BLOCK, width), lambda i: (i, 0)),
        out_shape=jax.ShapeDtypeStruct((out_count, width), kind),
        compiler_params=pltpu.CompilerParams(vmem_limit_bytes=VMEM_BYTES),
        cost_estimate=pl.CostEstimate(
            flops=2 * out_count * count * max(width, 256),
            bytes_accessed=rows.size * 2 + out_count * width * 4,
            transcendentals=0,
        ),
        name="pick_rows",
    )(index, rows)


def band_kernel(chunk, per, words, sum_column, span_ref, rows_ref, table_ref, stat_ref, out_ref, mix_ref):
    step_id = pl.program_id(0)
    count, width = mix_ref.shape
    chunk_count = table_ref.shape[0] // chunk
    group_count = chunk_count // per
    active = (step_id >= span_ref[0]) & (step_id < span_ref[1])

    def put_stats(top, total):
        lane = lax.broadcasted_iota(jnp.int32, (count, 128), 1)
        both = jnp.where(lane == 0, top, jnp.where(lane == 1, total, 0.0))
        stat_ref[...] = both.T[:8, :]

    def logits_at(at, rows):
        return product_nt(rows, table_ref[pl.ds(at, chunk), :])

    def beyond(at, shape):
        return at + lax.broadcasted_iota(jnp.int32, shape, 1) >= words

    def run(rows, top):
        mix_ref[...] = jnp.zeros(mix_ref.shape, jnp.float32)

        def visit(group, total):
            for inner in range(per):
                at = (group * per + inner) * chunk
                checked = isinstance(at, int) and at + chunk > words
                if not isinstance(at, int):
                    at = pl.multiple_of(at, chunk)
                weights = jnp.exp(logits_at(at, rows) - top)
                if checked:
                    weights = jnp.where(beyond(at, weights.shape), 0.0, weights)
                if sum_column is None:
                    for lane in range(0, chunk, 128):
                        total = total + weights[:, lane : lane + 128]
                mix_ref[...] += product(lowered(weights), table_ref[pl.ds(at, chunk), :])
            return total

        lanes = jnp.zeros((count, 128), jnp.float32)
        lanes = visit(0, lanes) if group_count == 1 else lax.fori_loop(0, group_count, visit, lanes)
        if sum_column is None:
            return jnp.sum(lanes, 1, keepdims=True)
        return mix_ref[:, sum_column : sum_column + 1]

    @pl.when(active)
    def _():
        rows = rows_ref[...]
        first = product_nt(rows, table_ref[pl.ds(0, 128), :])
        top = jnp.max(first, 1, keepdims=True)
        total = run(rows, top)
        put_stats(top, total)

        @pl.when(jnp.logical_not(jnp.max(jnp.where(total < SAFE, 0.0, 1.0)) < 0.5))
        def _():
            def largest(index, top):
                at = pl.multiple_of(index * chunk, chunk)
                logits = logits_at(at, rows)
                if sum_column is None:
                    logits = jnp.where(beyond(at, logits.shape), NEG_FILL, logits)
                return jnp.maximum(top, jnp.max(logits, 1, keepdims=True))

            exact = lax.fori_loop(0, chunk_count, largest, jnp.full((count, 1), NEG_FILL))
            put_stats(exact, run(rows, exact))

        out_ref[...] = lowered(mix_ref[...])

    @pl.when(jnp.logical_not(active))
    def _():
        put_stats(jnp.full((count, 1), NEG_FILL), jnp.zeros((count, 1), jnp.float32))
        out_ref[...] = jnp.zeros(out_ref.shape, jnp.bfloat16)


def band_forward(span, rows, table, words, chunk, sum_column, share):
    count, width = rows.shape[0], table.shape[1]
    chunk_count = table.shape[0] // chunk
    per = chunk_count if chunk_count <= 4 else 4
    assert chunk_count % per == 0 and words >= 128
    return pl.pallas_call(
        functools.partial(band_kernel, chunk, per, words, sum_column),
        grid_spec=pltpu.PrefetchScalarGridSpec(
            num_scalar_prefetch=1,
            grid=(count // BLOCK,),
            in_specs=[
                pl.BlockSpec((BLOCK, width), lambda i, s: (i, 0)),
                pl.BlockSpec(table.shape, lambda i, s: (0, 0), **ONCE),
            ],
            out_specs=[
                pl.BlockSpec((8, BLOCK), lambda i, s: (0, i)),
                pl.BlockSpec((BLOCK, width), lambda i, s: (i, 0)),
            ],
            scratch_shapes=[pltpu.VMEM((BLOCK, width), jnp.float32)],
        ),
        out_shape=[
            jax.ShapeDtypeStruct((8, count), jnp.float32),
            jax.ShapeDtypeStruct((count, width), jnp.bfloat16),
        ],
        compiler_params=pltpu.CompilerParams(vmem_limit_bytes=VMEM_BYTES),
        cost_estimate=pl.CostEstimate(
            flops=int(share * 4 * count * table.shape[0] * max(width, 256)),
            bytes_accessed=table.size * 2 + count * width * 6,
            transcendentals=int(share * count * table.shape[0]),
        ),
        name="band_forward",
    )(span, rows, table)


def head_grad_kernel(chunk, lists, base_ref, table_ref, *refs):
    out_ref, sum_ref = refs[2 * lists :]
    words = table_ref.shape[0]
    base = base_ref[0] + pl.program_id(0) * words
    sum_ref[...] = jnp.zeros(sum_ref.shape, jnp.float32)
    for rows_ref, fact_ref in zip(refs[0 : 2 * lists : 2], refs[1 : 2 * lists : 2]):
        piece = min(rows_ref.shape[0], 1024)

        def visit(step, unused, rows_ref=rows_ref, fact_ref=fact_ref, piece=piece):
            at = pl.multiple_of(step * piece, piece)
            rows = rows_ref[pl.ds(at, piece), :]
            weight = fact_ref[0:1, pl.ds(at, piece)]
            total = fact_ref[1:2, pl.ds(at, piece)]
            ids = fact_ref[2:3, pl.ds(at, piece)].astype(jnp.int32)
            for start in range(0, words, chunk):
                probs = jnp.exp(product_nt(table_ref[start : start + chunk, :], rows) - total)
                word = base + start + lax.broadcasted_iota(jnp.int32, (chunk, 1), 0)
                grads = weight * (jnp.where(word == ids, 1.0, 0.0) - probs)
                sum_ref[start : start + chunk, :] += product(lowered(grads), rows)
            return unused

        lax.fori_loop(0, rows_ref.shape[0] // piece, visit, 0)
    out_ref[...] = lowered(sum_ref[...])


def head_grad(table, part, part_words, first_word, lists):
    width = table.shape[1]
    word_block = math.gcd(part_words, 640)
    steps = part_words // word_block
    chunk = word_block // 2 if word_block % 32 == 0 else word_block
    specs = []
    for rows, facts in lists:
        specs.append(pl.BlockSpec(rows.shape, lambda i, s: (0, 0), **ONCE))
        specs.append(pl.BlockSpec(facts.shape, lambda i, s: (0, 0), **ONCE))
    count = sum(rows.shape[0] for rows, facts in lists)
    scalars = jnp.stack([first_word + part * part_words, part * steps]).astype(jnp.int32)
    return pl.pallas_call(
        functools.partial(head_grad_kernel, chunk, len(lists)),
        grid_spec=pltpu.PrefetchScalarGridSpec(
            num_scalar_prefetch=1,
            grid=(steps,),
            in_specs=[pl.BlockSpec((word_block, width), lambda i, s: (s[1] + i, 0))] + specs,
            out_specs=pl.BlockSpec((word_block, width), lambda i, s: (i, 0)),
            scratch_shapes=[pltpu.VMEM((word_block, width), jnp.float32)],
        ),
        out_shape=jax.ShapeDtypeStruct((part_words, width), jnp.bfloat16),
        compiler_params=pltpu.CompilerParams(vmem_limit_bytes=VMEM_BYTES),
        cost_estimate=pl.CostEstimate(
            flops=4 * count * part_words * width,
            bytes_accessed=(count + part_words) * width * 2,
            transcendentals=count * part_words,
        ),
        name="head_grad",
    )(scalars, table, *[value for pair in lists for value in pair])


def band_grad_kernel(chunk, most, across, plan_ref, table_ref, rows_ref, fact_ref, out_ref, sum_ref):
    words = table_ref.shape[0]
    step_id = pl.program_id(0)
    base = plan_ref[most + 1] + step_id * words
    sum_ref[...] = jnp.zeros(sum_ref.shape, jnp.float32)

    def block_at(position):
        return pl.multiple_of(plan_ref[position] * BLOCK, BLOCK)

    def spread(starts):
        rows = [rows_ref[pl.ds(start, BLOCK), :] for start in starts]
        facts = [fact_ref[:, pl.ds(start, BLOCK)] for start in starts]
        rows = rows[0] if len(rows) == 1 else jnp.concatenate(rows, 0)
        facts = facts[0] if len(facts) == 1 else jnp.concatenate(facts, 1)
        weight, total = facts[0:1], facts[1:2]
        for start in range(0, words, chunk):
            probs = jnp.exp(product_nt(table_ref[start : start + chunk, :], rows) - total)
            sum_ref[start : start + chunk, :] -= product(lowered(weight * probs), rows)

    count = plan_ref[0]

    def pair(step, unused):
        spread([block_at(1 + 2 * step), block_at(2 + 2 * step)])
        return unused

    lax.fori_loop(0, count // 2, pair, 0)

    @pl.when(count % 2 == 1)
    def _():
        spread([block_at(count)])

    line = most + 2 + step_id * (most + 1)

    def hits(step, unused):
        at = block_at(line + 1 + step)
        rows = rows_ref[pl.ds(at, BLOCK), :]
        weight = fact_ref[0:1, pl.ds(at, BLOCK)]
        ids = fact_ref[2:3, pl.ds(at, BLOCK)].astype(jnp.int32)
        for start in range(0, words, chunk):
            word = base + start + lax.broadcasted_iota(jnp.int32, (chunk, 1), 0)
            chosen = lowered(jnp.where(word == ids, weight, 0.0))
            sum_ref[start : start + chunk, :] += product(chosen, rows)
        return unused

    lax.fori_loop(0, plan_ref[line], hits, 0)
    if across:
        out_ref[...] = sum_ref[...].T[: out_ref.shape[0], :].astype(out_ref.dtype)
    else:
        out_ref[...] = sum_ref[...].astype(out_ref.dtype)


def listed(flags):
    size = flags.shape[-1]
    order = jnp.cumsum(flags.astype(jnp.int32), -1)
    chosen = (order[..., None, :] == jnp.arange(1, size + 1)[:, None]) & flags[..., None, :]
    places = jnp.sum(jnp.where(chosen, jnp.arange(size), 0), -1)
    return jnp.concatenate([order[..., -1:], places], -1).astype(jnp.int32)


def band_grad(
    table, rows, facts, active, lowest, highest, part, part_words, first_word, chunk, result, across
):
    count, full = rows.shape[0], table.shape[1]
    word_block = chunk
    steps = part_words // word_block
    most = count // BLOCK
    first = first_word + part * part_words
    low = first + jnp.arange(steps, dtype=jnp.int32)[:, None] * word_block
    step_hits = active[None, :] & (lowest[None, :] < low + word_block) & (highest[None, :] >= low)
    plan = jnp.concatenate(
        [
            listed(active),
            first.reshape(1).astype(jnp.int32),
            listed(step_hits).reshape(-1),
            (part * steps).reshape(1).astype(jnp.int32),
        ]
    )
    last = plan.shape[0] - 1
    return pl.pallas_call(
        functools.partial(band_grad_kernel, chunk // 2 if chunk > 832 else chunk, most, across),
        grid_spec=pltpu.PrefetchScalarGridSpec(
            num_scalar_prefetch=1,
            grid=(steps,),
            in_specs=[
                pl.BlockSpec((word_block, full), lambda i, s: (s[last] + i, 0)),
                pl.BlockSpec((count, full), lambda i, s: (0, 0), **ONCE),
                pl.BlockSpec(facts.shape, lambda i, s: (0, 0), **ONCE),
            ],
            out_specs=(
                pl.BlockSpec((result.shape[0], word_block), lambda i, s: (0, i))
                if across
                else pl.BlockSpec((word_block, full), lambda i, s: (i, 0))
            ),
            scratch_shapes=[pltpu.VMEM((word_block, full), jnp.float32)],
        ),
        out_shape=result,
        compiler_params=pltpu.CompilerParams(vmem_limit_bytes=VMEM_BYTES),
        cost_estimate=pl.CostEstimate(
            flops=2 * count * part_words * 256,
            bytes_accessed=count * full * 2 + part_words * full * 4,
            transcendentals=count * part_words // 2,
        ),
        name="band_grad",
    )(plan, table, rows, facts)


def settle_kernel(
    member_ref,
    everyone_ref,
    fact_ref,
    head_mix_ref,
    middle_mix_ref,
    tail_mix_ref,
    head_hit_ref,
    middle_hit_ref,
    tail_hit_ref,
    term_ref,
    line_ref,
    slot_ref,
):
    step = pl.program_id(0)
    devices, _, slots = everyone_ref.shape
    tail_width = 64
    here = pl.ds(pl.multiple_of(step * BLOCK, BLOCK), BLOCK)

    def merged(read):
        lines = [read(device) for device in range(devices)]
        top = functools.reduce(jnp.maximum, [line[0] for line in lines])
        return top, sum(line[1] * jnp.exp(line[0] - top) for line in lines)

    head_top, head_sum = merged(
        lambda d: (everyone_ref[d, 0:1, here], everyone_ref[d, 1:2, here])
    )
    target = sum(everyone_ref[d, 2:3, here] for d in range(devices))
    slot_top, slot_sum = merged(lambda d: (everyone_ref[d, 3:4, :], everyone_ref[d, 4:5, :]))
    used = slot_sum > 0.0
    slot_total = jnp.where(used, slot_top + jnp.log(jnp.where(used, slot_sum, 1.0)), 0.0)
    member = member_ref[0]
    own_slot_top = jnp.where(used, everyone_ref[member, 3:4, :], 0.0)
    own_head_top = everyone_ref[member, 0:1, here]

    facts = fact_ref[...]
    slot, share, cotangent, first_cluster, second_cluster, band, word = (
        facts[index : index + 1] for index in range(7)
    )

    def as_columns(lines):
        square = jnp.concatenate(
            lines + [jnp.zeros((128 - len(lines), BLOCK), jnp.float32)], 0
        )
        return square.T

    def three(line):
        return [part.astype(jnp.float32) for part in thirds(line)]

    slot_column = as_columns([slot])[:, 0:1].astype(jnp.int32)
    hot = lowered(
        jnp.where(lax.broadcasted_iota(jnp.int32, (BLOCK, slots), 1) == slot_column, 1.0, 0.0)
    )
    lines = three(slot_total) + three(own_slot_top) + [jnp.zeros((10, slots), jnp.float32)]
    on_tokens = product_nt(lowered(jnp.concatenate(lines, 0)), hot)
    band_total = on_tokens[0:1] + on_tokens[1:2] + on_tokens[2:3]
    own_band_top = on_tokens[3:4] + on_tokens[4:5] + on_tokens[5:6]

    cluster_top = jnp.maximum(head_top, jnp.maximum(first_cluster, second_cluster))
    head_total = cluster_top + jnp.log(
        head_sum * jnp.exp(head_top - cluster_top)
        + jnp.exp(first_cluster - cluster_top)
        + jnp.exp(second_cluster - cluster_top)
    )
    in_head = band < 0.5
    cluster = jnp.where(band < 1.5, first_cluster, second_cluster)
    model_logp = target - head_total + jnp.where(in_head, 0.0, cluster - band_total)
    ratio = 0.25 * share * jnp.exp(-model_logp)
    weight = cotangent * 0.75 / (0.75 + ratio)
    head_scale = weight * jnp.exp(own_head_top - head_total)
    band_scale = weight * jnp.where(in_head, 0.0, jnp.exp(own_band_top - band_total))
    columns = as_columns([weight, head_scale, band_scale])
    weight_column, head_column, band_column = (columns[:, i : i + 1] for i in range(3))
    width = head_mix_ref.shape[1]
    term_ref[:, :width] = lowered(
        weight_column * head_hit_ref[...].astype(jnp.float32)
        - head_column * head_mix_ref[...].astype(jnp.float32)
    )
    narrow = tail_mix_ref.shape[1]
    kept = lax.broadcasted_iota(jnp.int32, (BLOCK, narrow), 1) < tail_width

    def widened(values):
        values = jnp.where(kept, values, 0.0)
        more = middle_mix_ref.shape[1] - narrow
        return jnp.concatenate([values, jnp.zeros((BLOCK, more), jnp.float32)], 1)

    band_mix = product(hot, middle_mix_ref[...]) + widened(product(hot, tail_mix_ref[...]))
    band_hit = middle_hit_ref[...].astype(jnp.float32) + widened(
        tail_hit_ref[...].astype(jnp.float32)
    )
    term_ref[:, width:] = lowered(weight_column * band_hit - band_column * band_mix)
    line_ref[...] = jnp.concatenate(
        [
            model_logp + jnp.log(0.75 + ratio),
            weight,
            head_total,
            word,
            jnp.zeros((4, BLOCK), jnp.float32),
        ],
        0,
    )

    @pl.when(step == 0)
    def _():
        slot_ref[...] = jnp.concatenate(
            [jnp.zeros((8, slots), jnp.float32), slot_total, jnp.zeros((7, slots), jnp.float32)], 0
        )

    sent = three(weight) + three(word) + [jnp.zeros((10, BLOCK), jnp.float32)]
    slot_ref[0:8, :] += product(lowered(jnp.concatenate(sent, 0)), hot)[0:8]


def settle(member, everyone, facts, head_mix, middle_mix, tail_mix, hits):
    count, width = head_mix.shape
    slots = middle_mix.shape[0]
    full = width + middle_mix.shape[1]

    def tokens(values):
        return pl.BlockSpec((BLOCK, values.shape[1]), lambda i, s: (i, 0))

    def whole(values):
        return pl.BlockSpec(values.shape, lambda i, s: (0,) * values.ndim, **ONCE)

    lines = pl.BlockSpec((8, BLOCK), lambda i, s: (0, i))
    return pl.pallas_call(
        settle_kernel,
        grid_spec=pltpu.PrefetchScalarGridSpec(
            num_scalar_prefetch=1,
            grid=(count // BLOCK,),
            in_specs=[whole(everyone), lines, tokens(head_mix), whole(middle_mix), whole(tail_mix)]
            + [tokens(hit) for hit in hits],
            out_specs=[
                pl.BlockSpec((BLOCK, full), lambda i, s: (i, 0)),
                lines,
                pl.BlockSpec((16, slots), lambda i, s: (0, 0)),
            ],
        ),
        out_shape=[
            jax.ShapeDtypeStruct((count, full), jnp.bfloat16),
            jax.ShapeDtypeStruct((8, count), jnp.float32),
            jax.ShapeDtypeStruct((16, slots), jnp.float32),
        ],
        compiler_params=pltpu.CompilerParams(vmem_limit_bytes=VMEM_BYTES),
        cost_estimate=pl.CostEstimate(
            flops=2 * count * slots * 1024,
            bytes_accessed=count * width * 12 + slots * full,
            transcendentals=slots * 64,
        ),
        name="settle",
    )(member.reshape(1).astype(jnp.int32), everyone, facts, head_mix, middle_mix, tail_mix, *hits)


def line_turns(value):
    size = lax.axis_size("seq")
    return [value] + [
        lax.ppermute(value, "seq", [(d, (d - k) % size) for d in range(size)])
        for k in range(1, size)
    ]


def line_step(before, behind, step):
    size = lax.axis_size("seq")
    return (
        lax.ppermute(before, "seq", [(d, d + 1) for d in range(step - 1, size - 1)]),
        lax.ppermute(behind, "seq", [(d, d - 1) for d in range(1, size - step + 1)]),
    )


def line_steps(value):
    found = [(value, value)]

    def advance(*others):
        step = len(found)
        if step == lax.axis_size("seq"):
            return others
        moved = line_step(*found[-1], step)
        moved, others = lax.optimization_barrier((moved, others))
        found.append(moved)
        return others

    return found, advance


def line_ordered(found):
    size, place = lax.axis_size("seq"), lax.axis_index("seq")
    ordered = []
    for source in range(size):
        value = found[0][0]
        for step in range(1, size):
            if source + step < size:
                value = jnp.where(place == source + step, found[step][0], value)
            if source - step >= 0:
                value = jnp.where(place == source - step, found[step][1], value)
        ordered.append(value)
    return ordered


def earlier_joined(value):
    size, place = lax.axis_size("seq"), lax.axis_index("seq")
    joined = jnp.zeros((size,) + value.shape, value.dtype)
    for step in range(size - 1, -1, -1):
        piece = value
        if step:
            piece = lax.ppermute(value, "seq", [(d, d + step) for d in range(size - step)])
        joined = lax.dynamic_update_index_in_dim(joined, piece, jnp.maximum(place - step, 0), 0)
    return joined.reshape((-1,) + value.shape[1:])


def in_order(pieces):
    size, place = lax.axis_size("seq"), lax.axis_index("seq")
    joined = jnp.zeros((size,) + pieces[0].shape, pieces[0].dtype)
    for k, piece in enumerate(pieces):
        joined = lax.dynamic_update_index_in_dim(joined, piece, lax.rem(place + k, size), 0)
    return joined.reshape((-1,) + pieces[0].shape[1:])


def line_scatter(values, behind=True):
    size, place = lax.axis_size("seq"), lax.axis_index("seq")
    parts = values.reshape((size, -1) + values.shape[1:])

    def part(index):
        return lax.dynamic_index_in_dim(parts, lax.rem(index, size), 0, False)

    total = part(place).astype(jnp.float32)
    for k in range(1, size):
        pairs = [(d, (d - k) % size) for d in range(0 if behind else k, size)]
        total = total + lax.ppermute(part(place + size - k), "seq", pairs).astype(jnp.float32)
    return total


def batch_halves(values, bit):
    member, size = lax.axis_index("batch"), lax.axis_size("batch")
    blocks, bits_left = values
    axis = bits_left.index(bit)
    mine = (member >> bit) & 1
    got = lax.ppermute(
        lax.dynamic_index_in_dim(blocks, 1 - mine, axis, False),
        "batch",
        [(d, d ^ (1 << bit)) for d in range(size)],
    )
    kept = lax.dynamic_index_in_dim(blocks, mine, axis, False)
    total = lowered(kept.astype(jnp.float32) + got.astype(jnp.float32))
    return total, bits_left[:axis] + bits_left[axis + 1 :]


def batch_blocks(values):
    size = lax.axis_size("batch")
    bits = size.bit_length() - 1
    assert size == 1 << bits
    return values.reshape((2,) * bits + (-1,) + values.shape[1:]), list(range(bits - 1, -1, -1))


def turn_kernel(rows_ref, out_ref):
    out_ref[...] = rows_ref[...].astype(jnp.float32).T.astype(out_ref.dtype)


def turned(rows, kind):
    return pl.pallas_call(
        turn_kernel, out_shape=jax.ShapeDtypeStruct(rows.shape[::-1], kind), name="turned"
    )(rows)


def word_pad(rows, biggest, splits):
    chunk = min(biggest, round_up(rows, 128))
    chunks = -(-rows // chunk)
    if chunks > 4:
        chunks = round_up(chunks, 4)
    return chunk, chunks * chunk


def on_device(
    inputs,
    targets,
    neighbours,
    neighbour_scores,
    loglik_grad,
    first_gain,
    first_shift,
    query_weight,
    query_bias,
    key_weight,
    value_weight,
    value_bias,
    out_weight,
    out_bias,
    second_gain,
    second_shift,
    inner_weight,
    inner_bias,
    outer_weight,
    outer_bias,
    final_gain,
    final_shift,
    head_table,
    cluster_weight,
    middle_map,
    middle_table,
    tail_map,
    tail_table,
):
    nb = lax.axis_size("batch")
    nz = lax.axis_size("seq")
    member = lax.axis_index("batch")
    place = lax.axis_index("seq")
    tokens = inputs[0]
    own_ids = targets[0]
    token_count, feature_count = tokens.shape
    group_count = token_count * nb
    slot_count = group_count + BLOCK
    query_start = (place * token_count).reshape(1)

    normed_low = lowered(layer_norm(tokens, first_gain, first_shift))
    normed_all = earlier_joined(normed_low)
    top_score = jnp.max(neighbour_scores[0], -1, keepdims=True)
    exponent = jnp.exp(neighbour_scores[0] - top_score)
    knn_prob = jnp.sum(jnp.where(neighbours[0] == 0, exponent, 0.0), -1) / jnp.sum(exponent, -1)
    early = jnp.stack([own_ids.astype(jnp.float32), knn_prob, loglik_grad[0]])
    early = lax.all_gather(early, "batch", axis=1, tiled=True)
    all_ids = early[0].astype(jnp.int32)
    all_knn, all_up = early[1], early[2]
    in_head = all_ids < HEAD_WORDS
    in_middle = (all_ids >= HEAD_WORDS) & (all_ids < HEAD_WORDS + MID_WORDS)
    in_tail = all_ids >= HEAD_WORDS + MID_WORDS
    order = jnp.arange(group_count, dtype=jnp.int32)
    ahead = (all_ids[None, :] < all_ids[:, None]) | (
        (all_ids[None, :] == all_ids[:, None]) & (order[None, :] < order[:, None])
    )
    rank = jnp.sum(ahead.astype(jnp.int32), -1)
    head_size = jnp.sum(in_head.astype(jnp.int32))
    middle_size = jnp.sum(in_middle.astype(jnp.int32))
    tail_size = group_count - head_size - middle_size
    middle_blocks = (middle_size + BLOCK - 1) // BLOCK
    tail_blocks = (tail_size + BLOCK - 1) // BLOCK
    slot = jnp.where(
        in_head,
        -1,
        rank - head_size + jnp.where(in_tail, middle_blocks * BLOCK - middle_size, 0),
    )
    zero_span = jnp.zeros((1,), jnp.int32)
    head_span = jnp.array([0, group_count // BLOCK], jnp.int32)
    middle_span = jnp.stack([0 * middle_blocks, middle_blocks]).astype(jnp.int32)
    tail_span = jnp.stack([middle_blocks, middle_blocks + tail_blocks]).astype(jnp.int32)
    slot_order = jnp.arange(slot_count, dtype=jnp.int32)
    slot_middle = slot_order < middle_size
    slot_tail = (slot_order >= middle_blocks * BLOCK) & (
        slot_order < middle_blocks * BLOCK + tail_size
    )
    slot_used = slot_middle | slot_tail
    band_id = all_ids - jnp.where(in_tail, HEAD_WORDS + MID_WORDS, HEAD_WORDS)

    tables = (head_table, middle_table, tail_table)
    sizes = tuple(table.shape[0] for table in tables)
    head_chunk, head_padded = word_pad(sizes[0], 1280, nz)
    middle_chunk, middle_padded = word_pad(sizes[1], 1280, nz)
    tail_chunk, tail_padded = word_pad(sizes[2], 1664, nz)
    tail_width = tail_table.shape[1]
    head_pad = jnp.pad(head_table, ((0, head_padded - sizes[0]), (0, 0)))
    middle_pad = jnp.pad(middle_table, ((0, middle_padded - sizes[1]), (0, 0)))
    tail_word = jnp.arange(tail_padded, dtype=jnp.int32)
    tail_bias = jnp.where(tail_word < jnp.minimum(TAIL_WORDS - member * sizes[2], sizes[2]), 0.0, NEG_FILL)
    tail_pad = jnp.concatenate(
        [
            jnp.pad(tail_table.T, ((0, 0), (0, tail_padded - sizes[2]))),
            jnp.ones((1, tail_padded), jnp.bfloat16),
            lowered(tail_bias)[None, :],
            jnp.zeros((126 - tail_width, tail_padded), jnp.bfloat16),
        ],
        0,
    ).T
    locals_ = (
        all_ids - member * sizes[0],
        all_ids - HEAD_WORDS - member * sizes[1],
        all_ids - HEAD_WORDS - MID_WORDS - member * sizes[2],
    )
    owned = tuple(
        inside & (local >= 0) & (local < size)
        for inside, local, size in zip((in_head, in_middle, in_tail), locals_, sizes)
    )
    hit_rows = tuple(
        jnp.where(
            own[:, None],
            jnp.take(table, jnp.clip(local, 0, size - 1), axis=0, mode="clip"),
            jnp.bfloat16(0),
        )
        for own, table, local, size in zip(owned, (head_pad, middle_pad, tail_pad), locals_, sizes)
    )

    queries = lowered(product(normed_low, query_weight) + query_bias)
    key_rows = lowered(product(normed_all, key_weight))
    value_rows = lowered(product(normed_all, value_weight) + value_bias)
    attended_low = attend(query_start, queries, key_rows, value_rows)
    mixed = tokens + product(attended_low, out_weight) + out_bias
    second_low = lowered(layer_norm(mixed, second_gain, second_shift))
    before = product(second_low, inner_weight) + inner_bias
    hidden_low = lowered(jax.nn.gelu(before))
    final = mixed + product(hidden_low, outer_weight) + outer_bias
    state_low = lowered(layer_norm(final, final_gain, final_shift))
    all_states = lax.all_gather(state_low, "batch", axis=0, tiled=True)
    split = 2 * nz * group_count * feature_count <= 24 << 20
    if split:
        block_states = lax.all_gather(state_low, "seq", axis=0, tiled=True)
    all_states, head_pad, middle_pad, tail_pad, tail_hits, slot, early = lax.optimization_barrier(
        (all_states, head_pad, middle_pad, tail_pad, hit_rows[2], slot, early)
    )
    hit_rows = hit_rows[:2] + (tail_hits,)

    middle_width = middle_map.shape[1]
    maps = jnp.pad(jnp.concatenate([middle_map, tail_map], 1), ((0, 0), (0, 128 - tail_width)))
    one_column = (jnp.arange(middle_width + 128) == middle_width + tail_width + 1).astype(jnp.float32)
    band_low = lowered(product(all_states, maps) + one_column)
    middle_low, tail_low = band_low[:, :middle_width], band_low[:, middle_width:]
    cluster_lines = product_nt(
        jnp.pad(cluster_weight.T, ((0, 6), (0, 0))), all_states
    )
    slot_full = pick_rows(slot, band_low, slot_count, True, jnp.bfloat16)
    first_tail = middle_blocks * BLOCK
    in_tail_slot = slot_order >= first_tail
    slot_low = jnp.where(
        in_tail_slot[:, None],
        jnp.pad(slot_full[:, middle_width:], ((0, 0), (0, middle_width - 128))),
        slot_full[:, :middle_width],
    )
    if split:
        piece = slot_count // nb
        slot_piece = lax.dynamic_slice_in_dim(slot_low, member * piece, piece, 0)
        other_slots = jnp.concatenate(line_turns(slot_piece)[1:], 0)
        slot_low, block_states, hit_rows = lax.optimization_barrier(
            (slot_low, block_states, hit_rows)
        )
        other_states = lax.dynamic_slice_in_dim(
            jnp.concatenate([block_states, block_states], 0),
            (place + 1) * token_count,
            (nz - 1) * token_count,
            0,
        )
        other_states = lax.all_gather(other_states, "batch", axis=0, tiled=True)
    tail_stats, tail_mix = band_forward(
        tail_span, slot_low, tail_pad, tail_padded, tail_chunk, tail_width, 0.5
    )
    middle_stats, middle_mix = band_forward(
        middle_span, slot_low, middle_pad, sizes[1], middle_chunk, None, 0.25
    )
    head_stats, head_mix = band_forward(
        head_span, all_states, head_pad, sizes[0], head_chunk, None, 1.0
    )
    inner_lane = jnp.arange(128) < tail_width
    target_part = (
        jnp.sum(hit_rows[0].astype(jnp.float32) * all_states.astype(jnp.float32), -1)
        + jnp.sum(hit_rows[1].astype(jnp.float32) * middle_low.astype(jnp.float32), -1)
        + jnp.sum(
            jnp.where(inner_lane, hit_rows[2].astype(jnp.float32), 0.0)
            * tail_low.astype(jnp.float32),
            -1,
        )
    )
    slot_stats = jnp.where(in_tail_slot[None, :], tail_stats[:2], middle_stats[:2])
    extra = ((0, 0), (0, BLOCK))
    stats = jnp.concatenate(
        [
            jnp.pad(jnp.concatenate([head_stats[:2], target_part[None]], 0), extra),
            slot_stats,
            jnp.zeros((3, slot_count), jnp.float32),
        ],
        0,
    )
    if split:
        stats, other_states, other_slots = lax.optimization_barrier(
            (stats, other_states, other_slots)
        )
        other_slots = lax.all_gather(other_slots, "batch", axis=0, tiled=True)
    everyone = lax.all_gather(stats, "batch")

    token_facts = jnp.concatenate(
        [
            slot.astype(jnp.float32)[None],
            early[1:3],
            cluster_lines[:2],
            jnp.where(in_head, 0.0, jnp.where(in_middle, 1.0, 2.0))[None],
            early[0:1],
            jnp.zeros((1, group_count), jnp.float32),
        ],
        0,
    )
    terms, lines, slot_lines = settle(
        member, everyone, token_facts, head_mix, middle_mix, tail_mix, hit_rows
    )
    own_terms = lax.psum_scatter(terms, "batch", scatter_dimension=0, tiled=True).astype(jnp.float32)

    def own_part(values):
        return lax.dynamic_slice_in_dim(values, member * token_count, token_count, 0)

    loglik = own_part(lines[0])

    kind = jnp.where(slot_middle, 1.0, jnp.where(slot_tail, 2.0, 0.0))
    slot_facts = jnp.stack(
        [
            jnp.sum(slot_lines[0:3], 0),
            slot_lines[8],
            jnp.sum(slot_lines[3:6], 0),
            kind,
        ]
    )
    head_facts = jnp.concatenate([lines[1:4], jnp.zeros((1, group_count), jnp.float32)], 0)
    if split:
        other_slots = (
            other_slots.reshape(nb, nz - 1, piece, middle_width)
            .transpose(1, 0, 2, 3)
            .reshape(-1, middle_width)
        )
        rows_all = jnp.concatenate([slot_low, other_slots], 0)
        fact_pieces = line_turns(jnp.concatenate([slot_facts, head_facts], 1))
        facts = jnp.concatenate([value[:, :slot_count] for value in fact_pieces], 1)
        other_facts = (
            jnp.stack([value[:, slot_count:] for value in fact_pieces[1:]], 1)
            .reshape(4, nz - 1, nb, token_count)
            .transpose(0, 2, 1, 3)
            .reshape(4, -1)
        )
        lists = [(all_states, head_facts), (other_states, other_facts)]
        part, parts = place, nz
    else:
        rows_all, facts, lists = slot_low, slot_facts, [(all_states, head_facts)]
        part, parts = 0 * place, 1
    head_part = head_grad(head_pad, part, head_padded // parts, member * sizes[0], lists)
    block_facts = facts[2:4].reshape(2, -1, BLOCK)
    block_kind = jnp.max(block_facts[1], -1)
    filled = block_facts[1] > 0
    lowest = jnp.min(jnp.where(filled, block_facts[0], 1e9), -1).astype(jnp.int32)
    highest = jnp.max(jnp.where(filled, block_facts[0], -1e9), -1).astype(jnp.int32)
    facts = jnp.concatenate(
        [facts[:2], jnp.where(facts[3:4] > 0, facts[2:3], -1e9), jnp.zeros_like(facts[:1])], 0
    )
    own_terms, head_part = lax.optimization_barrier((own_terms, head_part))
    if split:
        head_found, head_advance = line_steps(head_part)

    own_middle = own_part(in_middle)
    own_tail = own_part(in_tail)
    own_lines = lax.dynamic_slice_in_dim(lines, member * token_count, token_count, 1)
    own_weights, own_total = own_lines[1], own_lines[2]
    own_clusters = product(state_low, cluster_weight)
    band_state = own_terms[:, feature_count:]
    middle_state = lowered(jnp.where(own_middle[:, None], band_state, 0.0))
    tail_state = lowered(jnp.where(own_tail[:, None], band_state[:, :tail_width], 0.0))
    cluster_hit = jnp.stack([own_middle, own_tail], -1).astype(jnp.float32)
    cluster_grad = own_weights[:, None] * (
        cluster_hit - jnp.exp(own_clusters - own_total[:, None])
    )
    state_grad = (
        own_terms[:, :feature_count]
        + product_nt(middle_state, middle_map)
        + product_nt(tail_state, tail_map)
        + product_nt(cluster_grad, cluster_weight.astype(jnp.float32))
    )
    middle_map_grad = product_tn(state_low, middle_state)
    tail_map_rows = product_tn(tail_state, state_low)
    cluster_rows = product_tn(cluster_grad, state_low.astype(jnp.float32))
    final_grad, final_gain_grad, final_shift_grad = norm_back(
        final, final_gain, final_shift, state_grad
    )
    final_low = lowered(final_grad)
    outer_weight_grad = product_tn(hidden_low, final_low)
    outer_bias_grad = jnp.sum(final_grad, 0)
    outer_part = lax.psum_scatter(
        lowered(outer_weight_grad), "batch", scatter_dimension=0, tiled=True
    )
    before_grad = lowered(gelu_back(before, product_nt(final_low, outer_weight)))
    inner_weight_grad = product_tn(second_low, before_grad)
    inner_bias_grad = jnp.sum(before_grad.astype(jnp.float32), 0)
    inner_part = lax.psum_scatter(
        lowered(inner_weight_grad), "batch", scatter_dimension=0, tiled=True
    )
    second_in_grad, second_gain_grad, second_shift_grad = norm_back(
        mixed, second_gain, second_shift, product_nt(before_grad, inner_weight)
    )
    mixed_grad = final_grad + second_in_grad
    mixed_low = lowered(mixed_grad)
    out_weight_grad = product_tn(attended_low, mixed_low)
    out_bias_grad = jnp.sum(mixed_grad, 0)
    attended_grad = lowered(product_nt(mixed_low, out_weight))
    if split:
        (attended_grad,) = head_advance(attended_grad)
    query_low, key_low, value_low = attend_back(
        query_start, queries, key_rows, value_rows, attended_grad
    )
    if split:
        query_low, key_low, value_low = head_advance(query_low, key_low, value_low)
    query_weight_grad = product_tn(normed_low, query_low)
    key_weight_grad = product_tn(normed_all, key_low)
    value_weight_grad = product_tn(normed_all, value_low)
    query_bias_grad = jnp.sum(query_low.astype(jnp.float32), 0)
    value_bias_grad = jnp.sum(value_low.astype(jnp.float32), 0)
    spread = product_nt(key_low, key_weight) + product_nt(value_low, value_weight)
    query_spread = product_nt(query_low, query_weight)
    first_shift_grad = jnp.sum(spread, 0) + jnp.sum(query_spread, 0)
    all_centred = (normed_all.astype(jnp.float32) - first_shift) / first_gain
    own_average = jnp.mean(tokens, -1, keepdims=True)
    own_spread = jnp.mean((tokens - own_average) ** 2, -1, keepdims=True)
    own_centred = (tokens - own_average) * lax.rsqrt(own_spread + EPSILON)
    first_gain_grad = jnp.sum(all_centred * spread, 0) + jnp.sum(own_centred * query_spread, 0)
    bias_rows = inner_bias_grad.shape[0] // feature_count
    inner_bias_rows = (
        inner_bias_grad.reshape(nb, bias_rows, -1).transpose(1, 0, 2).reshape(bias_rows, -1)
    )
    vectors = [
        first_gain_grad,
        first_shift_grad,
        query_bias_grad,
        value_bias_grad,
        out_bias_grad,
        second_gain_grad,
        second_shift_grad,
        outer_bias_grad,
        final_gain_grad,
        final_shift_grad,
    ]
    rows = [tail_map_rows, cluster_rows, inner_bias_rows] + [value[None] for value in vectors]
    edges = [0]
    for row in rows:
        edges.append(edges[-1] + row.shape[0])
    row_count = round_up(edges[-1], 128)
    rows.append(jnp.zeros((row_count - edges[-1], feature_count), jnp.float32))
    columns = [
        query_weight_grad,
        key_weight_grad,
        value_weight_grad,
        out_weight_grad,
        middle_map_grad,
        turned(jnp.concatenate(rows, 0), jnp.bfloat16),
    ]
    spread_low = lowered(spread)
    rests = [
        jnp.concatenate([lowered(column) for column in group], 1)
        for group in (columns[:2], columns[2:])
    ]
    rests, facts, spread_low = lax.optimization_barrier((rests, facts, spread_low))
    rests = [batch_halves(batch_blocks(value), 0) for value in rests]
    bits = rests[0][1]
    values, facts = lax.optimization_barrier(([value for value, left in rests], facts))
    rests = [(value, bits) for value in values]
    orders = (bits, bits[::-1])
    inner_low = lowered(line_scatter(inner_part))

    def tail_gradient(part, parts):
        return band_grad(
            tail_pad,
            rows_all,
            facts,
            block_kind == 2,
            lowest,
            highest,
            part,
            tail_padded // parts,
            HEAD_WORDS + MID_WORDS + member * sizes[2],
            math.gcd(tail_padded // parts, tail_chunk),
            jax.ShapeDtypeStruct((tail_width, tail_padded // parts), jnp.bfloat16),
            True,
        )

    first_tail = tail_gradient(2 * part, 2 * parts)
    for step in range(len(bits)):
        rests = [batch_halves(value, order[step]) for value, order in zip(rests, orders)]
        if step == 0:
            values = [value for value, left in rests]
            if split:
                for unused in range(nz - 3):
                    (first_tail,) = head_advance(first_tail)
            values, first_tail, facts = lax.optimization_barrier((values, first_tail, facts))
            rests = [(value, left) for value, (unused, left) in zip(values, rests)]
    rest_parts, facts = lax.optimization_barrier(([value for value, left in rests], facts))
    rest_lows = [lax.psum(value, "seq") for value in rest_parts]
    second_tail = tail_gradient(2 * part + 1, 2 * parts)
    if split:
        first_found, first_advance = line_steps(first_tail)
        second_tail, inner_low, outer_part, facts, spread_low = first_advance(
            second_tail, inner_low, outer_part, facts, spread_low
        )
    inner_pieces = line_turns(inner_low)
    outer_low = lowered(line_scatter(outer_part))
    middle_result = jax.ShapeDtypeStruct(
        (sizes[1], middle_width) if split else (middle_padded, middle_width),
        jnp.float32 if split else jnp.bfloat16,
    )
    middle_part = band_grad(
        middle_pad,
        rows_all,
        facts,
        block_kind == 1,
        lowest,
        highest,
        0 * place,
        middle_padded,
        HEAD_WORDS + member * sizes[1],
        middle_chunk,
        middle_result,
        False,
    )
    if split:
        second_found, second_advance = line_steps(second_tail)
        middle_part, outer_low, inner_pieces, rest_lows = second_advance(
            middle_part, outer_low, inner_pieces, rest_lows
        )
        for unused in range(nz - 1):
            first_advance()
            second_advance()
        middle_table_grad = middle_part
        head_table_grad = jnp.concatenate(line_ordered(head_found), 0)
        tail_sum = [
            value
            for pair in zip(line_ordered(first_found), line_ordered(second_found))
            for value in pair
        ]
        tail_sum = jnp.concatenate(tail_sum, 1)
    else:
        middle_table_grad = lax.psum(middle_part, "seq")[: sizes[1]].astype(jnp.float32)
        head_table_grad = lax.psum(head_part, "seq")
        tail_sum = lax.psum(jnp.concatenate([first_tail, second_tail], 1), "seq")
    head_table_grad = head_table_grad[: sizes[0]].astype(jnp.float32)
    tail_table_grad = tail_sum[:, : sizes[2]].astype(jnp.float32).T
    normed_grad = query_spread + line_scatter(spread_low, False)
    first_in_grad, unused, unused = norm_back(tokens, first_gain, first_shift, normed_grad)
    input_grad = mixed_grad + first_in_grad

    inner_sum = in_order(inner_pieces).astype(jnp.float32)
    outer_sum = in_order(line_turns(outer_low)).astype(jnp.float32)
    edge = 2 * feature_count
    cut = [
        low[:, start : start + feature_count].astype(jnp.float32)
        for low in rest_lows
        for start in (0, feature_count)
    ]
    middle_map_sum = rest_lows[1][:, edge : edge + middle_width].astype(jnp.float32)
    row_sum = turned(rest_lows[1][:, edge + middle_width :], jnp.float32)
    tail_map_sum, cluster_sum, inner_bias_sum = (
        row_sum[low:high] for low, high in zip(edges[:3], edges[1:4])
    )
    lines = [row_sum[index] for index in range(edges[3], edges[3] + len(vectors))]
    return (
        loglik.reshape(1, token_count),
        input_grad.reshape(1, token_count, feature_count),
        lines[0],
        lines[1],
        cut[0],
        lines[2],
        cut[1],
        cut[2],
        lines[3],
        cut[3],
        lines[4],
        lines[5],
        lines[6],
        inner_sum,
        inner_bias_sum.reshape(-1),
        outer_sum,
        lines[7],
        lines[8],
        lines[9],
        head_table_grad,
        cluster_sum.T,
        middle_map_sum,
        middle_table_grad,
        tail_map_sum.T,
        tail_table_grad,
    )


def solution(mesh):
    return jax.shard_map(
        on_device,
        mesh=mesh,
        in_specs=(
            P("batch", "seq", None),
            P("batch", "seq"),
            P("batch", "seq", None),
            P("batch", "seq", None),
            P("batch", "seq"),
            P(),
            P(),
            P(),
            P(),
            P(),
            P(),
            P(),
            P(),
            P(),
            P(),
            P(),
            P(),
            P(),
            P(),
            P(),
            P(),
            P(),
            P("batch", None),
            P(),
            P(),
            P("batch", None),
            P(),
            P("batch", None),
        ),
        out_specs=(
            P("batch", "seq"),
            P("batch", "seq", None),
            P("batch"),
            P("batch"),
            P("batch", None),
            P("batch"),
            P("batch", None),
            P("batch", None),
            P("batch"),
            P("batch", None),
            P("batch"),
            P("batch"),
            P("batch"),
            P("batch", None),
            P("batch"),
            P("batch", None),
            P("batch"),
            P("batch"),
            P("batch"),
            P("batch", None),
            P("batch", None),
            P("batch", None),
            P("batch", None),
            P("batch", None),
            P("batch", None),
        ),
        check_vma=False,
    )
```

```python
import functools
import math

import jax
import jax.numpy as jnp
from jax import lax
from jax.experimental import pallas as pl
from jax.experimental.pallas import tpu as pltpu
from jax.sharding import PartitionSpec as P

HEADS = 16
HEAD_WORDS = 20000
MID_WORDS = 40000
TAIL_WORDS = 207735


NEG_FILL = -1e30
EPSILON = 1e-05
BLOCK = 256
SAFE = 1e30
VMEM_BYTES = 56 << 20
ONCE = dict(pipeline_mode=pl.Buffered(1))


def layer_norm(values, gain_vector, shift_vector):
    average = jnp.mean(values, -1, keepdims=True)
    centred = values - average
    spread = jnp.mean(centred * centred, -1, keepdims=True)
    return centred * lax.rsqrt(spread + EPSILON) * gain_vector + shift_vector


def norm_back(values, gain_vector, shift_vector, upstream):
    unused, pullback = jax.vjp(layer_norm, values, gain_vector, shift_vector)
    return pullback(upstream)


def gelu_back(before, upstream):
    unused, pullback = jax.vjp(jax.nn.gelu, before)
    return pullback(upstream)[0]


def product(former, latter):
    return jnp.dot(former, latter, preferred_element_type=jnp.float32)


def product_tn(former, latter):
    return lax.dot_general(
        former, latter, (((0,), (0,)), ((), ())), preferred_element_type=jnp.float32
    )


def product_nt(former, latter):
    return lax.dot_general(
        former, latter, (((1,), (1,)), ((), ())), preferred_element_type=jnp.float32
    )


def lowered(values):
    return values.astype(jnp.bfloat16)


def round_up(count, unit):
    return -(-count // unit) * unit


def thirds(values):
    high = lowered(values)
    rest = values - high.astype(jnp.float32)
    middle = lowered(rest)
    return [high, middle, lowered(rest - middle.astype(jnp.float32))]


def attend_kernel(start_ref, query_ref, key_ref, value_ref, out_ref):
    rows, keys = query_ref.shape[0], key_ref.shape[0]
    half = query_ref.shape[1] // 2
    query_pos = start_ref[0] + lax.broadcasted_iota(jnp.int32, (rows, keys), 0)
    allowed = lax.broadcasted_iota(jnp.int32, (rows, keys), 1) <= query_pos
    for part in range(2):
        cols = slice(part * half, part * half + half)
        scores = product_nt(query_ref[:, cols], key_ref[:, cols]) * half**-0.5
        scores = jnp.where(allowed, scores, NEG_FILL)
        weights = jnp.exp(scores - jnp.max(scores, 1, keepdims=True))
        weights = weights / jnp.sum(weights, 1, keepdims=True)
        out_ref[:, cols] = lowered(product(lowered(weights), value_ref[:, cols]))


def attend(start, queries, keys, values):
    rows, features = queries.shape
    width = 2 * features // HEADS
    own = pl.BlockSpec((rows, width), lambda i, s: (0, i))
    whole = pl.BlockSpec((keys.shape[0], width), lambda i, s: (0, i))
    return pl.pallas_call(
        attend_kernel,
        grid_spec=pltpu.PrefetchScalarGridSpec(
            num_scalar_prefetch=1,
            grid=(features // width,),
            in_specs=[own, whole, whole],
            out_specs=own,
        ),
        out_shape=jax.ShapeDtypeStruct((rows, features), jnp.bfloat16),
        compiler_params=pltpu.CompilerParams(vmem_limit_bytes=VMEM_BYTES),
        cost_estimate=pl.CostEstimate(
            flops=4 * rows * keys.shape[0] * features,
            bytes_accessed=4 * (rows + keys.shape[0]) * features,
            transcendentals=rows * keys.shape[0] * HEADS,
        ),
        name="attend",
    )(start, queries, keys, values)


def attend_back_kernel(
    start_ref, query_ref, key_ref, value_ref, up_ref, query_grad_ref, key_grad_ref, value_grad_ref
):
    rows, keys = query_ref.shape[0], key_ref.shape[0]
    half = query_ref.shape[1] // 2
    scale = half**-0.5
    query_pos = start_ref[0] + lax.broadcasted_iota(jnp.int32, (keys, rows), 1)
    allowed = lax.broadcasted_iota(jnp.int32, (keys, rows), 0) <= query_pos
    for part in range(2):
        cols = slice(part * half, part * half + half)
        query, key, value, up = (
            ref[:, cols] for ref in (query_ref, key_ref, value_ref, up_ref)
        )
        scores = jnp.where(allowed, product_nt(key, query) * scale, NEG_FILL)
        probs = jnp.exp(scores - jnp.max(scores, 0, keepdims=True))
        probs = probs / jnp.sum(probs, 0, keepdims=True)
        prob_grad = product_nt(value, up)
        delta = jnp.sum(probs * prob_grad, 0, keepdims=True)
        score_grad = lowered(probs * (prob_grad - delta))
        value_grad_ref[:, cols] = lowered(product(lowered(probs), up))
        key_grad_ref[:, cols] = lowered(product(score_grad, query) * scale)
        query_grad_ref[:, cols] = lowered(product_tn(score_grad, key) * scale)


def attend_back(start, queries, keys, values, upstream):
    rows, features = queries.shape
    count = keys.shape[0]
    width = 2 * features // HEADS
    own = pl.BlockSpec((rows, width), lambda i, s: (0, i))
    whole = pl.BlockSpec((count, width), lambda i, s: (0, i))
    return pl.pallas_call(
        attend_back_kernel,
        grid_spec=pltpu.PrefetchScalarGridSpec(
            num_scalar_prefetch=1,
            grid=(features // width,),
            in_specs=[own, whole, whole, own],
            out_specs=[own, whole, whole],
        ),
        out_shape=[
            jax.ShapeDtypeStruct((rows, features), jnp.bfloat16),
            jax.ShapeDtypeStruct((count, features), jnp.bfloat16),
            jax.ShapeDtypeStruct((count, features), jnp.bfloat16),
        ],
        compiler_params=pltpu.CompilerParams(vmem_limit_bytes=VMEM_BYTES),
        cost_estimate=pl.CostEstimate(
            flops=10 * rows * count * features,
            bytes_accessed=6 * (rows + count) * features,
            transcendentals=rows * count * HEADS,
        ),
        name="attend_back",
    )(start, queries, keys, values, upstream)


def pick_kernel(by_slot, index_ref, rows_ref, out_ref):
    count = rows_ref.shape[0]
    total = jnp.zeros(out_ref.shape, jnp.float32)
    base = pl.program_id(0) * BLOCK
    for at in range(0, count, BLOCK):
        if by_slot:
            place = base + lax.broadcasted_iota(jnp.int32, (BLOCK, BLOCK), 0)
            hit = index_ref[:, at : at + BLOCK] == place
        else:
            place = at + lax.broadcasted_iota(jnp.int32, (BLOCK, BLOCK), 1)
            hit = index_ref[...] == place
        onehot = lowered(jnp.where(hit, 1.0, 0.0))
        total = total + product(onehot, rows_ref[at : at + BLOCK, :])
    out_ref[...] = total.astype(out_ref.dtype)


def pick_rows(index, rows, out_count, by_slot, kind):
    count, width = rows.shape
    if by_slot:
        index = index.reshape(1, -1)
        index_spec = pl.BlockSpec(index.shape, lambda i: (0, 0))
    else:
        index = index.reshape(-1, 1)
        index_spec = pl.BlockSpec((BLOCK, 1), lambda i: (i, 0))
    return pl.pallas_call(
        functools.partial(pick_kernel, by_slot),
        grid=(out_count // BLOCK,),
        in_specs=[index_spec, pl.BlockSpec(rows.shape, lambda i: (0, 0), **ONCE)],
        out_specs=pl.BlockSpec((BLOCK, width), lambda i: (i, 0)),
        out_shape=jax.ShapeDtypeStruct((out_count, width), kind),
        compiler_params=pltpu.CompilerParams(vmem_limit_bytes=VMEM_BYTES),
        cost_estimate=pl.CostEstimate(
            flops=2 * out_count * count * max(width, 256),
            bytes_accessed=rows.size * 2 + out_count * width * 4,
            transcendentals=0,
        ),
        name="pick_rows",
    )(index, rows)


def band_kernel(chunk, per, words, sum_column, span_ref, rows_ref, table_ref, stat_ref, out_ref, mix_ref):
    step_id = pl.program_id(0)
    count, width = mix_ref.shape
    chunk_count = table_ref.shape[0] // chunk
    group_count = chunk_count // per
    active = (step_id >= span_ref[0]) & (step_id < span_ref[1])

    def put_stats(top, total):
        lane = lax.broadcasted_iota(jnp.int32, (count, 128), 1)
        both = jnp.where(lane == 0, top, jnp.where(lane == 1, total, 0.0))
        stat_ref[...] = both.T[:8, :]

    def logits_at(at, rows):
        return product_nt(rows, table_ref[pl.ds(at, chunk), :])

    def beyond(at, shape):
        return at + lax.broadcasted_iota(jnp.int32, shape, 1) >= words

    def run(rows, top):
        mix_ref[...] = jnp.zeros(mix_ref.shape, jnp.float32)

        def visit(group, total):
            for inner in range(per):
                at = (group * per + inner) * chunk
                checked = isinstance(at, int) and at + chunk > words
                if not isinstance(at, int):
                    at = pl.multiple_of(at, chunk)
                weights = jnp.exp(logits_at(at, rows) - top)
                if checked:
                    weights = jnp.where(beyond(at, weights.shape), 0.0, weights)
                if sum_column is None:
                    for lane in range(0, chunk, 128):
                        total = total + weights[:, lane : lane + 128]
                mix_ref[...] += product(lowered(weights), table_ref[pl.ds(at, chunk), :])
            return total

        lanes = jnp.zeros((count, 128), jnp.float32)
        lanes = visit(0, lanes) if group_count == 1 else lax.fori_loop(0, group_count, visit, lanes)
        if sum_column is None:
            return jnp.sum(lanes, 1, keepdims=True)
        return mix_ref[:, sum_column : sum_column + 1]

    @pl.when(active)
    def _():
        rows = rows_ref[...]
        first = product_nt(rows, table_ref[pl.ds(0, 128), :])
        top = jnp.max(first, 1, keepdims=True)
        total = run(rows, top)
        put_stats(top, total)

        @pl.when(jnp.logical_not(jnp.max(jnp.where(total < SAFE, 0.0, 1.0)) < 0.5))
        def _():
            def largest(index, top):
                at = pl.multiple_of(index * chunk, chunk)
                logits = logits_at(at, rows)
                if sum_column is None:
                    logits = jnp.where(beyond(at, logits.shape), NEG_FILL, logits)
                return jnp.maximum(top, jnp.max(logits, 1, keepdims=True))

            exact = lax.fori_loop(0, chunk_count, largest, jnp.full((count, 1), NEG_FILL))
            put_stats(exact, run(rows, exact))

        out_ref[...] = lowered(mix_ref[...])

    @pl.when(jnp.logical_not(active))
    def _():
        put_stats(jnp.full((count, 1), NEG_FILL), jnp.zeros((count, 1), jnp.float32))
        out_ref[...] = jnp.zeros(out_ref.shape, jnp.bfloat16)


def band_forward(span, rows, table, words, chunk, sum_column, share):
    count, width = rows.shape[0], table.shape[1]
    chunk_count = table.shape[0] // chunk
    per = chunk_count if chunk_count <= 4 else 4
    assert chunk_count % per == 0 and words >= 128
    return pl.pallas_call(
        functools.partial(band_kernel, chunk, per, words, sum_column),
        grid_spec=pltpu.PrefetchScalarGridSpec(
            num_scalar_prefetch=1,
            grid=(count // BLOCK,),
            in_specs=[
                pl.BlockSpec((BLOCK, width), lambda i, s: (i, 0)),
                pl.BlockSpec(table.shape, lambda i, s: (0, 0), **ONCE),
            ],
            out_specs=[
                pl.BlockSpec((8, BLOCK), lambda i, s: (0, i)),
                pl.BlockSpec((BLOCK, width), lambda i, s: (i, 0)),
            ],
            scratch_shapes=[pltpu.VMEM((BLOCK, width), jnp.float32)],
        ),
        out_shape=[
            jax.ShapeDtypeStruct((8, count), jnp.float32),
            jax.ShapeDtypeStruct((count, width), jnp.bfloat16),
        ],
        compiler_params=pltpu.CompilerParams(vmem_limit_bytes=VMEM_BYTES),
        cost_estimate=pl.CostEstimate(
            flops=int(share * 4 * count * table.shape[0] * max(width, 256)),
            bytes_accessed=table.size * 2 + count * width * 6,
            transcendentals=int(share * count * table.shape[0]),
        ),
        name="band_forward",
    )(span, rows, table)


def head_grad_kernel(chunk, lists, base_ref, table_ref, *refs):
    out_ref, sum_ref = refs[2 * lists :]
    words = table_ref.shape[0]
    base = base_ref[0] + pl.program_id(0) * words
    sum_ref[...] = jnp.zeros(sum_ref.shape, jnp.float32)
    for rows_ref, fact_ref in zip(refs[0 : 2 * lists : 2], refs[1 : 2 * lists : 2]):
        piece = min(rows_ref.shape[0], 1024)

        def visit(step, unused, rows_ref=rows_ref, fact_ref=fact_ref, piece=piece):
            at = pl.multiple_of(step * piece, piece)
            rows = rows_ref[pl.ds(at, piece), :]
            weight = fact_ref[0:1, pl.ds(at, piece)]
            total = fact_ref[1:2, pl.ds(at, piece)]
            ids = fact_ref[2:3, pl.ds(at, piece)].astype(jnp.int32)
            for start in range(0, words, chunk):
                probs = jnp.exp(product_nt(table_ref[start : start + chunk, :], rows) - total)
                word = base + start + lax.broadcasted_iota(jnp.int32, (chunk, 1), 0)
                grads = weight * (jnp.where(word == ids, 1.0, 0.0) - probs)
                sum_ref[start : start + chunk, :] += product(lowered(grads), rows)
            return unused

        lax.fori_loop(0, rows_ref.shape[0] // piece, visit, 0)
    out_ref[...] = lowered(sum_ref[...])


def head_grad(table, part, part_words, first_word, lists):
    width = table.shape[1]
    word_block = math.gcd(part_words, 640)
    steps = part_words // word_block
    chunk = word_block // 2 if word_block % 32 == 0 else word_block
    specs = []
    for rows, facts in lists:
        specs.append(pl.BlockSpec(rows.shape, lambda i, s: (0, 0), **ONCE))
        specs.append(pl.BlockSpec(facts.shape, lambda i, s: (0, 0), **ONCE))
    count = sum(rows.shape[0] for rows, facts in lists)
    scalars = jnp.stack([first_word + part * part_words, part * steps]).astype(jnp.int32)
    return pl.pallas_call(
        functools.partial(head_grad_kernel, chunk, len(lists)),
        grid_spec=pltpu.PrefetchScalarGridSpec(
            num_scalar_prefetch=1,
            grid=(steps,),
            in_specs=[pl.BlockSpec((word_block, width), lambda i, s: (s[1] + i, 0))] + specs,
            out_specs=pl.BlockSpec((word_block, width), lambda i, s: (i, 0)),
            scratch_shapes=[pltpu.VMEM((word_block, width), jnp.float32)],
        ),
        out_shape=jax.ShapeDtypeStruct((part_words, width), jnp.bfloat16),
        compiler_params=pltpu.CompilerParams(vmem_limit_bytes=VMEM_BYTES),
        cost_estimate=pl.CostEstimate(
            flops=4 * count * part_words * width,
            bytes_accessed=(count + part_words) * width * 2,
            transcendentals=count * part_words,
        ),
        name="head_grad",
    )(scalars, table, *[value for pair in lists for value in pair])


def band_grad_kernel(chunk, most, across, plan_ref, table_ref, rows_ref, fact_ref, out_ref, sum_ref):
    words = table_ref.shape[0]
    step_id = pl.program_id(0)
    base = plan_ref[most + 1] + step_id * words
    sum_ref[...] = jnp.zeros(sum_ref.shape, jnp.float32)

    def block_at(position):
        return pl.multiple_of(plan_ref[position] * BLOCK, BLOCK)

    def spread(starts):
        rows = [rows_ref[pl.ds(start, BLOCK), :] for start in starts]
        facts = [fact_ref[:, pl.ds(start, BLOCK)] for start in starts]
        rows = rows[0] if len(rows) == 1 else jnp.concatenate(rows, 0)
        facts = facts[0] if len(facts) == 1 else jnp.concatenate(facts, 1)
        weight, total = facts[0:1], facts[1:2]
        for start in range(0, words, chunk):
            probs = jnp.exp(product_nt(table_ref[start : start + chunk, :], rows) - total)
            sum_ref[start : start + chunk, :] -= product(lowered(weight * probs), rows)

    count = plan_ref[0]

    def pair(step, unused):
        spread([block_at(1 + 2 * step), block_at(2 + 2 * step)])
        return unused

    lax.fori_loop(0, count // 2, pair, 0)

    @pl.when(count % 2 == 1)
    def _():
        spread([block_at(count)])

    line = most + 2 + step_id * (most + 1)

    def hits(step, unused):
        at = block_at(line + 1 + step)
        rows = rows_ref[pl.ds(at, BLOCK), :]
        weight = fact_ref[0:1, pl.ds(at, BLOCK)]
        ids = fact_ref[2:3, pl.ds(at, BLOCK)].astype(jnp.int32)
        for start in range(0, words, chunk):
            word = base + start + lax.broadcasted_iota(jnp.int32, (chunk, 1), 0)
            chosen = lowered(jnp.where(word == ids, weight, 0.0))
            sum_ref[start : start + chunk, :] += product(chosen, rows)
        return unused

    lax.fori_loop(0, plan_ref[line], hits, 0)
    if across:
        out_ref[...] = sum_ref[...].T[: out_ref.shape[0], :].astype(out_ref.dtype)
    else:
        out_ref[...] = sum_ref[...].astype(out_ref.dtype)


def listed(flags):
    size = flags.shape[-1]
    order = jnp.cumsum(flags.astype(jnp.int32), -1)
    chosen = (order[..., None, :] == jnp.arange(1, size + 1)[:, None]) & flags[..., None, :]
    places = jnp.sum(jnp.where(chosen, jnp.arange(size), 0), -1)
    return jnp.concatenate([order[..., -1:], places], -1).astype(jnp.int32)


def band_grad(
    table, rows, facts, active, lowest, highest, part, part_words, first_word, chunk, result, across
):
    count, full = rows.shape[0], table.shape[1]
    word_block = chunk
    steps = part_words // word_block
    most = count // BLOCK
    first = first_word + part * part_words
    low = first + jnp.arange(steps, dtype=jnp.int32)[:, None] * word_block
    step_hits = active[None, :] & (lowest[None, :] < low + word_block) & (highest[None, :] >= low)
    plan = jnp.concatenate(
        [
            listed(active),
            first.reshape(1).astype(jnp.int32),
            listed(step_hits).reshape(-1),
            (part * steps).reshape(1).astype(jnp.int32),
        ]
    )
    last = plan.shape[0] - 1
    return pl.pallas_call(
        functools.partial(band_grad_kernel, chunk // 2 if chunk > 832 else chunk, most, across),
        grid_spec=pltpu.PrefetchScalarGridSpec(
            num_scalar_prefetch=1,
            grid=(steps,),
            in_specs=[
                pl.BlockSpec((word_block, full), lambda i, s: (s[last] + i, 0)),
                pl.BlockSpec((count, full), lambda i, s: (0, 0), **ONCE),
                pl.BlockSpec(facts.shape, lambda i, s: (0, 0), **ONCE),
            ],
            out_specs=(
                pl.BlockSpec((result.shape[0], word_block), lambda i, s: (0, i))
                if across
                else pl.BlockSpec((word_block, full), lambda i, s: (i, 0))
            ),
            scratch_shapes=[pltpu.VMEM((word_block, full), jnp.float32)],
        ),
        out_shape=result,
        compiler_params=pltpu.CompilerParams(vmem_limit_bytes=VMEM_BYTES),
        cost_estimate=pl.CostEstimate(
            flops=2 * count * part_words * 256,
            bytes_accessed=count * full * 2 + part_words * full * 4,
            transcendentals=count * part_words // 2,
        ),
        name="band_grad",
    )(plan, table, rows, facts)


def settle_kernel(
    member_ref,
    everyone_ref,
    fact_ref,
    head_mix_ref,
    middle_mix_ref,
    tail_mix_ref,
    head_hit_ref,
    middle_hit_ref,
    tail_hit_ref,
    term_ref,
    line_ref,
    slot_ref,
):
    step = pl.program_id(0)
    devices, _, slots = everyone_ref.shape
    tail_width = 64
    here = pl.ds(pl.multiple_of(step * BLOCK, BLOCK), BLOCK)

    def merged(read):
        lines = [read(device) for device in range(devices)]
        top = functools.reduce(jnp.maximum, [line[0] for line in lines])
        return top, sum(line[1] * jnp.exp(line[0] - top) for line in lines)

    head_top, head_sum = merged(
        lambda d: (everyone_ref[d, 0:1, here], everyone_ref[d, 1:2, here])
    )
    target = sum(everyone_ref[d, 2:3, here] for d in range(devices))
    slot_top, slot_sum = merged(lambda d: (everyone_ref[d, 3:4, :], everyone_ref[d, 4:5, :]))
    used = slot_sum > 0.0
    slot_total = jnp.where(used, slot_top + jnp.log(jnp.where(used, slot_sum, 1.0)), 0.0)
    member = member_ref[0]
    own_slot_top = jnp.where(used, everyone_ref[member, 3:4, :], 0.0)
    own_head_top = everyone_ref[member, 0:1, here]

    facts = fact_ref[...]
    slot, share, cotangent, first_cluster, second_cluster, band, word = (
        facts[index : index + 1] for index in range(7)
    )

    def as_columns(lines):
        square = jnp.concatenate(
            lines + [jnp.zeros((128 - len(lines), BLOCK), jnp.float32)], 0
        )
        return square.T

    def three(line):
        return [part.astype(jnp.float32) for part in thirds(line)]

    slot_column = as_columns([slot])[:, 0:1].astype(jnp.int32)
    hot = lowered(
        jnp.where(lax.broadcasted_iota(jnp.int32, (BLOCK, slots), 1) == slot_column, 1.0, 0.0)
    )
    lines = three(slot_total) + three(own_slot_top) + [jnp.zeros((10, slots), jnp.float32)]
    on_tokens = product_nt(lowered(jnp.concatenate(lines, 0)), hot)
    band_total = on_tokens[0:1] + on_tokens[1:2] + on_tokens[2:3]
    own_band_top = on_tokens[3:4] + on_tokens[4:5] + on_tokens[5:6]

    cluster_top = jnp.maximum(head_top, jnp.maximum(first_cluster, second_cluster))
    head_total = cluster_top + jnp.log(
        head_sum * jnp.exp(head_top - cluster_top)
        + jnp.exp(first_cluster - cluster_top)
        + jnp.exp(second_cluster - cluster_top)
    )
    in_head = band < 0.5
    cluster = jnp.where(band < 1.5, first_cluster, second_cluster)
    model_logp = target - head_total + jnp.where(in_head, 0.0, cluster - band_total)
    ratio = 0.25 * share * jnp.exp(-model_logp)
    weight = cotangent * 0.75 / (0.75 + ratio)
    head_scale = weight * jnp.exp(own_head_top - head_total)
    band_scale = weight * jnp.where(in_head, 0.0, jnp.exp(own_band_top - band_total))
    columns = as_columns([weight, head_scale, band_scale])
    weight_column, head_column, band_column = (columns[:, i : i + 1] for i in range(3))
    width = head_mix_ref.shape[1]
    term_ref[:, :width] = lowered(
        weight_column * head_hit_ref[...].astype(jnp.float32)
        - head_column * head_mix_ref[...].astype(jnp.float32)
    )
    narrow = tail_mix_ref.shape[1]
    kept = lax.broadcasted_iota(jnp.int32, (BLOCK, narrow), 1) < tail_width

    def widened(values):
        values = jnp.where(kept, values, 0.0)
        more = middle_mix_ref.shape[1] - narrow
        return jnp.concatenate([values, jnp.zeros((BLOCK, more), jnp.float32)], 1)

    band_mix = product(hot, middle_mix_ref[...]) + widened(product(hot, tail_mix_ref[...]))
    band_hit = middle_hit_ref[...].astype(jnp.float32) + widened(
        tail_hit_ref[...].astype(jnp.float32)
    )
    term_ref[:, width:] = lowered(weight_column * band_hit - band_column * band_mix)
    line_ref[...] = jnp.concatenate(
        [
            model_logp + jnp.log(0.75 + ratio),
            weight,
            head_total,
            word,
            jnp.zeros((4, BLOCK), jnp.float32),
        ],
        0,
    )

    @pl.when(step == 0)
    def _():
        slot_ref[...] = jnp.concatenate(
            [jnp.zeros((8, slots), jnp.float32), slot_total, jnp.zeros((7, slots), jnp.float32)], 0
        )

    sent = three(weight) + three(word) + [jnp.zeros((10, BLOCK), jnp.float32)]
    slot_ref[0:8, :] += product(lowered(jnp.concatenate(sent, 0)), hot)[0:8]


def settle(member, everyone, facts, head_mix, middle_mix, tail_mix, hits):
    count, width = head_mix.shape
    slots = middle_mix.shape[0]
    full = width + middle_mix.shape[1]

    def tokens(values):
        return pl.BlockSpec((BLOCK, values.shape[1]), lambda i, s: (i, 0))

    def whole(values):
        return pl.BlockSpec(values.shape, lambda i, s: (0,) * values.ndim, **ONCE)

    lines = pl.BlockSpec((8, BLOCK), lambda i, s: (0, i))
    return pl.pallas_call(
        settle_kernel,
        grid_spec=pltpu.PrefetchScalarGridSpec(
            num_scalar_prefetch=1,
            grid=(count // BLOCK,),
            in_specs=[whole(everyone), lines, tokens(head_mix), whole(middle_mix), whole(tail_mix)]
            + [tokens(hit) for hit in hits],
            out_specs=[
                pl.BlockSpec((BLOCK, full), lambda i, s: (i, 0)),
                lines,
                pl.BlockSpec((16, slots), lambda i, s: (0, 0)),
            ],
        ),
        out_shape=[
            jax.ShapeDtypeStruct((count, full), jnp.bfloat16),
            jax.ShapeDtypeStruct((8, count), jnp.float32),
            jax.ShapeDtypeStruct((16, slots), jnp.float32),
        ],
        compiler_params=pltpu.CompilerParams(vmem_limit_bytes=VMEM_BYTES),
        cost_estimate=pl.CostEstimate(
            flops=2 * count * slots * 1024,
            bytes_accessed=count * width * 12 + slots * full,
            transcendentals=slots * 64,
        ),
        name="settle",
    )(member.reshape(1).astype(jnp.int32), everyone, facts, head_mix, middle_mix, tail_mix, *hits)


def line_turns(value):
    size = lax.axis_size("seq")
    return [value] + [
        lax.ppermute(value, "seq", [(d, (d - k) % size) for d in range(size)])
        for k in range(1, size)
    ]


def line_step(before, behind, step):
    size = lax.axis_size("seq")
    return (
        lax.ppermute(before, "seq", [(d, d + 1) for d in range(step - 1, size - 1)]),
        lax.ppermute(behind, "seq", [(d, d - 1) for d in range(1, size - step + 1)]),
    )


def line_steps(value):
    found = [(value, value)]

    def advance(*others):
        step = len(found)
        if step == lax.axis_size("seq"):
            return others
        moved = line_step(*found[-1], step)
        moved, others = lax.optimization_barrier((moved, others))
        found.append(moved)
        return others

    return found, advance


def line_ordered(found, axis):
    size, place = lax.axis_size("seq"), lax.axis_index("seq")
    ordered = []
    for source in range(size):
        value = found[0][0]
        for step in range(1, size):
            if source + step < size:
                value = jnp.where(place == source + step, found[step][0], value)
            if source - step >= 0:
                value = jnp.where(place == source - step, found[step][1], value)
        ordered.append(value)
    return jnp.concatenate(ordered, axis)


def earlier_joined(value):
    size, place = lax.axis_size("seq"), lax.axis_index("seq")
    joined = jnp.zeros((size,) + value.shape, value.dtype)
    for step in range(size - 1, -1, -1):
        piece = value
        if step:
            piece = lax.ppermute(value, "seq", [(d, d + step) for d in range(size - step)])
        joined = lax.dynamic_update_index_in_dim(joined, piece, jnp.maximum(place - step, 0), 0)
    return joined.reshape((-1,) + value.shape[1:])


def in_order(pieces):
    size, place = lax.axis_size("seq"), lax.axis_index("seq")
    joined = jnp.zeros((size,) + pieces[0].shape, pieces[0].dtype)
    for k, piece in enumerate(pieces):
        joined = lax.dynamic_update_index_in_dim(joined, piece, lax.rem(place + k, size), 0)
    return joined.reshape((-1,) + pieces[0].shape[1:])


def line_scatter(values, behind=True):
    size, place = lax.axis_size("seq"), lax.axis_index("seq")
    parts = values.reshape((size, -1) + values.shape[1:])

    def part(index):
        return lax.dynamic_index_in_dim(parts, lax.rem(index, size), 0, False)

    total = part(place).astype(jnp.float32)
    for k in range(1, size):
        pairs = [(d, (d - k) % size) for d in range(0 if behind else k, size)]
        total = total + lax.ppermute(part(place + size - k), "seq", pairs).astype(jnp.float32)
    return total


def turn_kernel(rows_ref, out_ref):
    out_ref[...] = rows_ref[...].astype(jnp.float32).T.astype(out_ref.dtype)


def turned(rows, kind):
    return pl.pallas_call(
        turn_kernel, out_shape=jax.ShapeDtypeStruct(rows.shape[::-1], kind), name="turned"
    )(rows)


def word_pad(rows, biggest, splits):
    chunk = min(biggest, round_up(rows, 128))
    chunks = -(-rows // chunk)
    if chunks > 4:
        chunks = round_up(chunks, 4)
    return chunk, chunks * chunk


def on_device(
    inputs,
    targets,
    neighbours,
    neighbour_scores,
    loglik_grad,
    first_gain,
    first_shift,
    query_weight,
    query_bias,
    key_weight,
    value_weight,
    value_bias,
    out_weight,
    out_bias,
    second_gain,
    second_shift,
    inner_weight,
    inner_bias,
    outer_weight,
    outer_bias,
    final_gain,
    final_shift,
    head_table,
    cluster_weight,
    middle_map,
    middle_table,
    tail_map,
    tail_table,
):
    nb = lax.axis_size("batch")
    nz = lax.axis_size("seq")
    member = lax.axis_index("batch")
    place = lax.axis_index("seq")
    tokens = inputs[0]
    own_ids = targets[0]
    token_count, feature_count = tokens.shape
    group_count = token_count * nb
    slot_count = group_count + BLOCK
    query_start = (place * token_count).reshape(1)

    normed_low = lowered(layer_norm(tokens, first_gain, first_shift))
    normed_all = earlier_joined(normed_low)
    top_score = jnp.max(neighbour_scores[0], -1, keepdims=True)
    exponent = jnp.exp(neighbour_scores[0] - top_score)
    knn_prob = jnp.sum(jnp.where(neighbours[0] == 0, exponent, 0.0), -1) / jnp.sum(exponent, -1)
    early = jnp.stack([own_ids.astype(jnp.float32), knn_prob, loglik_grad[0]])
    early = lax.all_gather(early, "batch", axis=1, tiled=True)
    all_ids = early[0].astype(jnp.int32)
    all_knn, all_up = early[1], early[2]
    in_head = all_ids < HEAD_WORDS
    in_middle = (all_ids >= HEAD_WORDS) & (all_ids < HEAD_WORDS + MID_WORDS)
    in_tail = all_ids >= HEAD_WORDS + MID_WORDS
    order = jnp.arange(group_count, dtype=jnp.int32)
    ahead = (all_ids[None, :] < all_ids[:, None]) | (
        (all_ids[None, :] == all_ids[:, None]) & (order[None, :] < order[:, None])
    )
    rank = jnp.sum(ahead.astype(jnp.int32), -1)
    head_size = jnp.sum(in_head.astype(jnp.int32))
    middle_size = jnp.sum(in_middle.astype(jnp.int32))
    tail_size = group_count - head_size - middle_size
    middle_blocks = (middle_size + BLOCK - 1) // BLOCK
    tail_blocks = (tail_size + BLOCK - 1) // BLOCK
    slot = jnp.where(
        in_head,
        -1,
        rank - head_size + jnp.where(in_tail, middle_blocks * BLOCK - middle_size, 0),
    )
    zero_span = jnp.zeros((1,), jnp.int32)
    head_span = jnp.array([0, group_count // BLOCK], jnp.int32)
    middle_span = jnp.stack([0 * middle_blocks, middle_blocks]).astype(jnp.int32)
    tail_span = jnp.stack([middle_blocks, middle_blocks + tail_blocks]).astype(jnp.int32)
    slot_order = jnp.arange(slot_count, dtype=jnp.int32)
    slot_middle = slot_order < middle_size
    slot_tail = (slot_order >= middle_blocks * BLOCK) & (
        slot_order < middle_blocks * BLOCK + tail_size
    )
    slot_used = slot_middle | slot_tail
    band_id = all_ids - jnp.where(in_tail, HEAD_WORDS + MID_WORDS, HEAD_WORDS)

    tables = (head_table, middle_table, tail_table)
    sizes = tuple(table.shape[0] for table in tables)
    head_chunk, head_padded = word_pad(sizes[0], 1280, nz)
    middle_chunk, middle_padded = word_pad(sizes[1], 1280, nz)
    tail_chunk, tail_padded = word_pad(sizes[2], 1664, nz)
    tail_width = tail_table.shape[1]
    head_pad = jnp.pad(head_table, ((0, head_padded - sizes[0]), (0, 0)))
    middle_pad = jnp.pad(middle_table, ((0, middle_padded - sizes[1]), (0, 0)))
    tail_word = jnp.arange(tail_padded, dtype=jnp.int32)
    tail_bias = jnp.where(tail_word < jnp.minimum(TAIL_WORDS - member * sizes[2], sizes[2]), 0.0, NEG_FILL)
    tail_pad = jnp.concatenate(
        [
            jnp.pad(tail_table.T, ((0, 0), (0, tail_padded - sizes[2]))),
            jnp.ones((1, tail_padded), jnp.bfloat16),
            lowered(tail_bias)[None, :],
            jnp.zeros((126 - tail_width, tail_padded), jnp.bfloat16),
        ],
        0,
    ).T
    locals_ = (
        all_ids - member * sizes[0],
        all_ids - HEAD_WORDS - member * sizes[1],
        all_ids - HEAD_WORDS - MID_WORDS - member * sizes[2],
    )
    owned = tuple(
        inside & (local >= 0) & (local < size)
        for inside, local, size in zip((in_head, in_middle, in_tail), locals_, sizes)
    )
    hit_rows = tuple(
        jnp.where(
            own[:, None],
            jnp.take(table, jnp.clip(local, 0, size - 1), axis=0, mode="clip"),
            jnp.bfloat16(0),
        )
        for own, table, local, size in zip(owned, (head_pad, middle_pad, tail_pad), locals_, sizes)
    )

    queries = lowered(product(normed_low, query_weight) + query_bias)
    key_rows = lowered(product(normed_all, key_weight))
    value_rows = lowered(product(normed_all, value_weight) + value_bias)
    attended_low = attend(query_start, queries, key_rows, value_rows)
    mixed = tokens + product(attended_low, out_weight) + out_bias
    second_low = lowered(layer_norm(mixed, second_gain, second_shift))
    before = product(second_low, inner_weight) + inner_bias
    hidden_low = lowered(jax.nn.gelu(before))
    final = mixed + product(hidden_low, outer_weight) + outer_bias
    state_low = lowered(layer_norm(final, final_gain, final_shift))
    all_states = lax.all_gather(state_low, "batch", axis=0, tiled=True)
    split = 2 * nz * group_count * feature_count <= 24 << 20
    if split:
        block_states = lax.all_gather(state_low, "seq", axis=0, tiled=True)
    all_states, head_pad, middle_pad, tail_pad, tail_hits, slot, early = lax.optimization_barrier(
        (all_states, head_pad, middle_pad, tail_pad, hit_rows[2], slot, early)
    )
    hit_rows = hit_rows[:2] + (tail_hits,)

    middle_width = middle_map.shape[1]
    maps = jnp.pad(jnp.concatenate([middle_map, tail_map], 1), ((0, 0), (0, 128 - tail_width)))
    one_column = (jnp.arange(middle_width + 128) == middle_width + tail_width + 1).astype(jnp.float32)
    band_low = lowered(product(all_states, maps) + one_column)
    middle_low, tail_low = band_low[:, :middle_width], band_low[:, middle_width:]
    cluster_lines = product_nt(
        jnp.pad(cluster_weight.T, ((0, 6), (0, 0))), all_states
    )
    slot_full = pick_rows(slot, band_low, slot_count, True, jnp.bfloat16)
    first_tail = middle_blocks * BLOCK
    in_tail_slot = slot_order >= first_tail
    slot_low = jnp.where(
        in_tail_slot[:, None],
        jnp.pad(slot_full[:, middle_width:], ((0, 0), (0, middle_width - 128))),
        slot_full[:, :middle_width],
    )
    if split:
        piece = slot_count // nb
        slot_piece = lax.dynamic_slice_in_dim(slot_low, member * piece, piece, 0)
        other_slots = jnp.concatenate(line_turns(slot_piece)[1:], 0)
        slot_low, block_states, hit_rows = lax.optimization_barrier(
            (slot_low, block_states, hit_rows)
        )
        other_states = lax.dynamic_slice_in_dim(
            jnp.concatenate([block_states, block_states], 0),
            (place + 1) * token_count,
            (nz - 1) * token_count,
            0,
        )
        other_states = lax.all_gather(other_states, "batch", axis=0, tiled=True)
    tail_stats, tail_mix = band_forward(
        tail_span, slot_low, tail_pad, tail_padded, tail_chunk, tail_width, 0.5
    )
    middle_stats, middle_mix = band_forward(
        middle_span, slot_low, middle_pad, sizes[1], middle_chunk, None, 0.25
    )
    head_stats, head_mix = band_forward(
        head_span, all_states, head_pad, sizes[0], head_chunk, None, 1.0
    )
    inner_lane = jnp.arange(128) < tail_width
    target_part = (
        jnp.sum(hit_rows[0].astype(jnp.float32) * all_states.astype(jnp.float32), -1)
        + jnp.sum(hit_rows[1].astype(jnp.float32) * middle_low.astype(jnp.float32), -1)
        + jnp.sum(
            jnp.where(inner_lane, hit_rows[2].astype(jnp.float32), 0.0)
            * tail_low.astype(jnp.float32),
            -1,
        )
    )
    slot_stats = jnp.where(in_tail_slot[None, :], tail_stats[:2], middle_stats[:2])
    extra = ((0, 0), (0, BLOCK))
    stats = jnp.concatenate(
        [
            jnp.pad(jnp.concatenate([head_stats[:2], target_part[None]], 0), extra),
            slot_stats,
            jnp.zeros((3, slot_count), jnp.float32),
        ],
        0,
    )
    if split:
        stats, other_states, other_slots = lax.optimization_barrier(
            (stats, other_states, other_slots)
        )
        other_slots = lax.all_gather(other_slots, "batch", axis=0, tiled=True)
    everyone = lax.all_gather(stats, "batch")

    token_facts = jnp.concatenate(
        [
            slot.astype(jnp.float32)[None],
            early[1:3],
            cluster_lines[:2],
            jnp.where(in_head, 0.0, jnp.where(in_middle, 1.0, 2.0))[None],
            early[0:1],
            jnp.zeros((1, group_count), jnp.float32),
        ],
        0,
    )
    terms, lines, slot_lines = settle(
        member, everyone, token_facts, head_mix, middle_mix, tail_mix, hit_rows
    )
    own_terms = lax.psum_scatter(terms, "batch", scatter_dimension=0, tiled=True).astype(jnp.float32)

    def own_part(values):
        return lax.dynamic_slice_in_dim(values, member * token_count, token_count, 0)

    loglik = own_part(lines[0])

    kind = jnp.where(slot_middle, 1.0, jnp.where(slot_tail, 2.0, 0.0))
    slot_facts = jnp.stack(
        [
            jnp.sum(slot_lines[0:3], 0),
            slot_lines[8],
            jnp.sum(slot_lines[3:6], 0),
            kind,
        ]
    )
    head_facts = jnp.concatenate([lines[1:4], jnp.zeros((1, group_count), jnp.float32)], 0)
    if split:
        other_slots = (
            other_slots.reshape(nb, nz - 1, piece, middle_width)
            .transpose(1, 0, 2, 3)
            .reshape(-1, middle_width)
        )
        rows_all = jnp.concatenate([slot_low, other_slots], 0)
        fact_pieces = line_turns(jnp.concatenate([slot_facts, head_facts], 1))
        facts = jnp.concatenate([value[:, :slot_count] for value in fact_pieces], 1)
        other_facts = (
            jnp.stack([value[:, slot_count:] for value in fact_pieces[1:]], 1)
            .reshape(4, nz - 1, nb, token_count)
            .transpose(0, 2, 1, 3)
            .reshape(4, -1)
        )
        lists = [(all_states, head_facts), (other_states, other_facts)]
        part, parts = place, nz
    else:
        rows_all, facts, lists = slot_low, slot_facts, [(all_states, head_facts)]
        part, parts = 0 * place, 1
    head_part = head_grad(head_pad, part, head_padded // parts, member * sizes[0], lists)
    block_facts = facts[2:4].reshape(2, -1, BLOCK)
    block_kind = jnp.max(block_facts[1], -1)
    filled = block_facts[1] > 0
    lowest = jnp.min(jnp.where(filled, block_facts[0], 1e9), -1).astype(jnp.int32)
    highest = jnp.max(jnp.where(filled, block_facts[0], -1e9), -1).astype(jnp.int32)
    facts = jnp.concatenate(
        [facts[:2], jnp.where(facts[3:4] > 0, facts[2:3], -1e9), jnp.zeros_like(facts[:1])], 0
    )
    tail_part = band_grad(
        tail_pad,
        rows_all,
        facts,
        block_kind == 2,
        lowest,
        highest,
        part,
        tail_padded // parts,
        HEAD_WORDS + MID_WORDS + member * sizes[2],
        math.gcd(tail_padded // parts, tail_chunk),
        jax.ShapeDtypeStruct((tail_width, tail_padded // parts), jnp.bfloat16),
        True,
    )
    if split:
        head_found, head_advance = line_steps(head_part)
        own_terms, tail_part = head_advance(own_terms, tail_part)
        tail_found, tail_advance = line_steps(tail_part)
    else:
        own_terms, tail_part = lax.optimization_barrier((own_terms, tail_part))

    own_middle = own_part(in_middle)
    own_tail = own_part(in_tail)
    own_lines = lax.dynamic_slice_in_dim(lines, member * token_count, token_count, 1)
    own_weights, own_total = own_lines[1], own_lines[2]
    own_clusters = product(state_low, cluster_weight)
    band_state = own_terms[:, feature_count:]
    middle_state = lowered(jnp.where(own_middle[:, None], band_state, 0.0))
    tail_state = lowered(jnp.where(own_tail[:, None], band_state[:, :tail_width], 0.0))
    cluster_hit = jnp.stack([own_middle, own_tail], -1).astype(jnp.float32)
    cluster_grad = own_weights[:, None] * (
        cluster_hit - jnp.exp(own_clusters - own_total[:, None])
    )
    state_grad = (
        own_terms[:, :feature_count]
        + product_nt(middle_state, middle_map)
        + product_nt(tail_state, tail_map)
        + product_nt(cluster_grad, cluster_weight.astype(jnp.float32))
    )
    middle_map_grad = product_tn(state_low, middle_state)
    tail_map_rows = product_tn(tail_state, state_low)
    cluster_rows = product_tn(cluster_grad, state_low.astype(jnp.float32))
    final_grad, final_gain_grad, final_shift_grad = norm_back(
        final, final_gain, final_shift, state_grad
    )
    final_low = lowered(final_grad)
    outer_weight_grad = product_tn(hidden_low, final_low)
    outer_bias_grad = jnp.sum(final_grad, 0)
    outer_part = lax.psum_scatter(
        lowered(outer_weight_grad), "batch", scatter_dimension=0, tiled=True
    )
    before_grad = lowered(gelu_back(before, product_nt(final_low, outer_weight)))
    inner_weight_grad = product_tn(second_low, before_grad)
    inner_bias_grad = jnp.sum(before_grad.astype(jnp.float32), 0)
    inner_part = lax.psum_scatter(
        lowered(inner_weight_grad), "batch", scatter_dimension=0, tiled=True
    )
    second_in_grad, second_gain_grad, second_shift_grad = norm_back(
        mixed, second_gain, second_shift, product_nt(before_grad, inner_weight)
    )
    mixed_grad = final_grad + second_in_grad
    mixed_low = lowered(mixed_grad)
    out_weight_grad = product_tn(attended_low, mixed_low)
    out_bias_grad = jnp.sum(mixed_grad, 0)
    attended_grad = lowered(product_nt(mixed_low, out_weight))
    if split:
        (attended_grad,) = head_advance(attended_grad)
    query_low, key_low, value_low = attend_back(
        query_start, queries, key_rows, value_rows, attended_grad
    )
    if split:
        for unused in range(nz - 3):
            query_low, key_low, value_low = head_advance(query_low, key_low, value_low)
        query_low, key_low, value_low = tail_advance(query_low, key_low, value_low)
    query_weight_grad = product_tn(normed_low, query_low)
    key_weight_grad = product_tn(normed_all, key_low)
    value_weight_grad = product_tn(normed_all, value_low)
    query_bias_grad = jnp.sum(query_low.astype(jnp.float32), 0)
    value_bias_grad = jnp.sum(value_low.astype(jnp.float32), 0)
    spread = product_nt(key_low, key_weight) + product_nt(value_low, value_weight)
    query_spread = product_nt(query_low, query_weight)
    first_shift_grad = jnp.sum(spread, 0) + jnp.sum(query_spread, 0)
    all_centred = (normed_all.astype(jnp.float32) - first_shift) / first_gain
    own_average = jnp.mean(tokens, -1, keepdims=True)
    own_spread = jnp.mean((tokens - own_average) ** 2, -1, keepdims=True)
    own_centred = (tokens - own_average) * lax.rsqrt(own_spread + EPSILON)
    first_gain_grad = jnp.sum(all_centred * spread, 0) + jnp.sum(own_centred * query_spread, 0)
    bias_rows = inner_bias_grad.shape[0] // feature_count
    inner_bias_rows = (
        inner_bias_grad.reshape(nb, bias_rows, -1).transpose(1, 0, 2).reshape(bias_rows, -1)
    )
    vectors = [
        first_gain_grad,
        first_shift_grad,
        query_bias_grad,
        value_bias_grad,
        out_bias_grad,
        second_gain_grad,
        second_shift_grad,
        outer_bias_grad,
        final_gain_grad,
        final_shift_grad,
    ]
    rows = [tail_map_rows, cluster_rows, inner_bias_rows] + [value[None] for value in vectors]
    edges = [0]
    for row in rows:
        edges.append(edges[-1] + row.shape[0])
    row_count = round_up(edges[-1], 128)
    rows.append(jnp.zeros((row_count - edges[-1], feature_count), jnp.float32))
    columns = [
        query_weight_grad,
        key_weight_grad,
        value_weight_grad,
        out_weight_grad,
        middle_map_grad,
        turned(jnp.concatenate(rows, 0), jnp.bfloat16),
    ]
    rest = jnp.concatenate([lowered(column) for column in columns], 1)
    spread_low = lowered(spread)
    rest, facts, spread_low = lax.optimization_barrier((rest, facts, spread_low))
    if split:
        rest, facts, spread_low, inner_part = tail_advance(rest, facts, spread_low, inner_part)
    rest_part = lax.psum_scatter(rest, "batch", scatter_dimension=0, tiled=True)
    inner_low = lowered(line_scatter(inner_part))
    spread_sum = line_scatter(spread_low, False)
    middle_result = jax.ShapeDtypeStruct(
        (sizes[1], middle_width) if split else (middle_padded, middle_width),
        jnp.float32 if split else jnp.bfloat16,
    )
    middle_part = band_grad(
        middle_pad,
        rows_all,
        facts,
        block_kind == 1,
        lowest,
        highest,
        0 * place,
        middle_padded,
        HEAD_WORDS + member * sizes[1],
        middle_chunk,
        middle_result,
        False,
    )
    if split:
        for unused in range(nz - 3):
            (middle_part,) = tail_advance(middle_part)
    middle_part, inner_low, spread_sum, outer_part = lax.optimization_barrier(
        (middle_part, inner_low, spread_sum, outer_part)
    )
    inner_pieces = line_turns(inner_low)
    outer_low = lowered(line_scatter(outer_part))
    rest_part, inner_pieces, outer_low = lax.optimization_barrier(
        (rest_part, inner_pieces, outer_low)
    )
    if split:
        middle_table_grad = middle_part
        head_table_grad = line_ordered(head_found, 0)
        tail_sum = line_ordered(tail_found, 1)
    else:
        middle_table_grad = lax.psum(middle_part, "seq")[: sizes[1]].astype(jnp.float32)
        head_table_grad = lax.psum(head_part, "seq")
        tail_sum = lax.psum(tail_part, "seq")
    head_table_grad = head_table_grad[: sizes[0]].astype(jnp.float32)
    tail_table_grad = tail_sum[:, : sizes[2]].astype(jnp.float32).T
    normed_grad = query_spread + spread_sum
    first_in_grad, unused, unused = norm_back(tokens, first_gain, first_shift, normed_grad)
    input_grad = mixed_grad + first_in_grad
    inner_sum = in_order(inner_pieces).astype(jnp.float32)
    outer_sum = in_order(line_turns(outer_low)).astype(jnp.float32)
    rest_low = lax.psum(rest_part, "seq")
    rest_sum = rest_low[:, : 4 * feature_count + middle_width].astype(jnp.float32)
    cut = [rest_sum[:, i * feature_count : (i + 1) * feature_count] for i in range(4)]
    middle_map_sum = rest_sum[:, 4 * feature_count : 4 * feature_count + middle_width]
    row_sum = turned(rest_low[:, 4 * feature_count + middle_width :], jnp.float32)
    tail_map_sum, cluster_sum, inner_bias_sum = (
        row_sum[low:high] for low, high in zip(edges[:3], edges[1:4])
    )
    lines = [row_sum[index] for index in range(edges[3], edges[3] + len(vectors))]
    return (
        loglik.reshape(1, token_count),
        input_grad.reshape(1, token_count, feature_count),
        lines[0],
        lines[1],
        cut[0],
        lines[2],
        cut[1],
        cut[2],
        lines[3],
        cut[3],
        lines[4],
        lines[5],
        lines[6],
        inner_sum,
        inner_bias_sum.reshape(-1),
        outer_sum,
        lines[7],
        lines[8],
        lines[9],
        head_table_grad,
        cluster_sum.T,
        middle_map_sum,
        middle_table_grad,
        tail_map_sum.T,
        tail_table_grad,
    )


def solution(mesh):
    return jax.shard_map(
        on_device,
        mesh=mesh,
        in_specs=(
            P("batch", "seq", None),
            P("batch", "seq"),
            P("batch", "seq", None),
            P("batch", "seq", None),
            P("batch", "seq"),
            P(),
            P(),
            P(),
            P(),
            P(),
            P(),
            P(),
            P(),
            P(),
            P(),
            P(),
            P(),
            P(),
            P(),
            P(),
            P(),
            P(),
            P("batch", None),
            P(),
            P(),
            P("batch", None),
            P(),
            P("batch", None),
        ),
        out_specs=(
            P("batch", "seq"),
            P("batch", "seq", None),
            P("batch"),
            P("batch"),
            P("batch", None),
            P("batch"),
            P("batch", None),
            P("batch", None),
            P("batch"),
            P("batch", None),
            P("batch"),
            P("batch"),
            P("batch"),
            P("batch", None),
            P("batch"),
            P("batch", None),
            P("batch"),
            P("batch"),
            P("batch"),
            P("batch", None),
            P("batch", None),
            P("batch", None),
            P("batch", None),
            P("batch", None),
            P("batch", None),
        ),
        check_vma=False,
    )
```

```python
import functools
import math

import jax
import jax.numpy as jnp
from jax import lax
from jax.experimental import pallas as pl
from jax.experimental.pallas import tpu as pltpu
from jax.sharding import PartitionSpec as P

HEADS = 16
HEAD_WORDS = 20000
MID_WORDS = 40000
TAIL_WORDS = 207735


NEG_FILL = -1e30
EPSILON = 1e-05
BLOCK = 256
SAFE = 1e30
VMEM_BYTES = 56 << 20
ONCE = dict(pipeline_mode=pl.Buffered(1))


def layer_norm(values, gain_vector, shift_vector):
    average = jnp.mean(values, -1, keepdims=True)
    centred = values - average
    spread = jnp.mean(centred * centred, -1, keepdims=True)
    return centred * lax.rsqrt(spread + EPSILON) * gain_vector + shift_vector


def norm_back(values, gain_vector, shift_vector, upstream):
    unused, pullback = jax.vjp(layer_norm, values, gain_vector, shift_vector)
    return pullback(upstream)


def gelu_back(before, upstream):
    unused, pullback = jax.vjp(jax.nn.gelu, before)
    return pullback(upstream)[0]


def product(former, latter):
    return jnp.dot(former, latter, preferred_element_type=jnp.float32)


def product_tn(former, latter):
    return lax.dot_general(
        former, latter, (((0,), (0,)), ((), ())), preferred_element_type=jnp.float32
    )


def product_nt(former, latter):
    return lax.dot_general(
        former, latter, (((1,), (1,)), ((), ())), preferred_element_type=jnp.float32
    )


def lowered(values):
    return values.astype(jnp.bfloat16)


def round_up(count, unit):
    return -(-count // unit) * unit


def thirds(values):
    high = lowered(values)
    rest = values - high.astype(jnp.float32)
    middle = lowered(rest)
    return [high, middle, lowered(rest - middle.astype(jnp.float32))]


def attend_kernel(start_ref, query_ref, key_ref, value_ref, out_ref):
    rows, keys = query_ref.shape[0], key_ref.shape[0]
    half = query_ref.shape[1] // 2
    query_pos = start_ref[0] + lax.broadcasted_iota(jnp.int32, (rows, keys), 0)
    allowed = lax.broadcasted_iota(jnp.int32, (rows, keys), 1) <= query_pos
    for part in range(2):
        cols = slice(part * half, part * half + half)
        scores = product_nt(query_ref[:, cols], key_ref[:, cols]) * half**-0.5
        scores = jnp.where(allowed, scores, NEG_FILL)
        weights = jnp.exp(scores - jnp.max(scores, 1, keepdims=True))
        weights = weights / jnp.sum(weights, 1, keepdims=True)
        out_ref[:, cols] = lowered(product(lowered(weights), value_ref[:, cols]))


def attend(start, queries, keys, values):
    rows, features = queries.shape
    width = 2 * features // HEADS
    own = pl.BlockSpec((rows, width), lambda i, s: (0, i))
    whole = pl.BlockSpec((keys.shape[0], width), lambda i, s: (0, i))
    return pl.pallas_call(
        attend_kernel,
        grid_spec=pltpu.PrefetchScalarGridSpec(
            num_scalar_prefetch=1,
            grid=(features // width,),
            in_specs=[own, whole, whole],
            out_specs=own,
        ),
        out_shape=jax.ShapeDtypeStruct((rows, features), jnp.bfloat16),
        compiler_params=pltpu.CompilerParams(vmem_limit_bytes=VMEM_BYTES),
        cost_estimate=pl.CostEstimate(
            flops=4 * rows * keys.shape[0] * features,
            bytes_accessed=4 * (rows + keys.shape[0]) * features,
            transcendentals=rows * keys.shape[0] * HEADS,
        ),
        name="attend",
    )(start, queries, keys, values)


def attend_back_kernel(
    start_ref, query_ref, key_ref, value_ref, up_ref, query_grad_ref, key_grad_ref, value_grad_ref
):
    rows, keys = query_ref.shape[0], key_ref.shape[0]
    half = query_ref.shape[1] // 2
    scale = half**-0.5
    query_pos = start_ref[0] + lax.broadcasted_iota(jnp.int32, (keys, rows), 1)
    allowed = lax.broadcasted_iota(jnp.int32, (keys, rows), 0) <= query_pos
    for part in range(2):
        cols = slice(part * half, part * half + half)
        query, key, value, up = (
            ref[:, cols] for ref in (query_ref, key_ref, value_ref, up_ref)
        )
        scores = jnp.where(allowed, product_nt(key, query) * scale, NEG_FILL)
        probs = jnp.exp(scores - jnp.max(scores, 0, keepdims=True))
        probs = probs / jnp.sum(probs, 0, keepdims=True)
        prob_grad = product_nt(value, up)
        delta = jnp.sum(probs * prob_grad, 0, keepdims=True)
        score_grad = lowered(probs * (prob_grad - delta))
        value_grad_ref[:, cols] = lowered(product(lowered(probs), up))
        key_grad_ref[:, cols] = lowered(product(score_grad, query) * scale)
        query_grad_ref[:, cols] = lowered(product_tn(score_grad, key) * scale)


def attend_back(start, queries, keys, values, upstream):
    rows, features = queries.shape
    count = keys.shape[0]
    width = 2 * features // HEADS
    own = pl.BlockSpec((rows, width), lambda i, s: (0, i))
    whole = pl.BlockSpec((count, width), lambda i, s: (0, i))
    return pl.pallas_call(
        attend_back_kernel,
        grid_spec=pltpu.PrefetchScalarGridSpec(
            num_scalar_prefetch=1,
            grid=(features // width,),
            in_specs=[own, whole, whole, own],
            out_specs=[own, whole, whole],
        ),
        out_shape=[
            jax.ShapeDtypeStruct((rows, features), jnp.bfloat16),
            jax.ShapeDtypeStruct((count, features), jnp.bfloat16),
            jax.ShapeDtypeStruct((count, features), jnp.bfloat16),
        ],
        compiler_params=pltpu.CompilerParams(vmem_limit_bytes=VMEM_BYTES),
        cost_estimate=pl.CostEstimate(
            flops=10 * rows * count * features,
            bytes_accessed=6 * (rows + count) * features,
            transcendentals=rows * count * HEADS,
        ),
        name="attend_back",
    )(start, queries, keys, values, upstream)


def pick_kernel(by_slot, index_ref, rows_ref, out_ref):
    count = rows_ref.shape[0]
    total = jnp.zeros(out_ref.shape, jnp.float32)
    base = pl.program_id(0) * BLOCK
    for at in range(0, count, BLOCK):
        if by_slot:
            place = base + lax.broadcasted_iota(jnp.int32, (BLOCK, BLOCK), 0)
            hit = index_ref[:, at : at + BLOCK] == place
        else:
            place = at + lax.broadcasted_iota(jnp.int32, (BLOCK, BLOCK), 1)
            hit = index_ref[...] == place
        onehot = lowered(jnp.where(hit, 1.0, 0.0))
        total = total + product(onehot, rows_ref[at : at + BLOCK, :])
    out_ref[...] = total.astype(out_ref.dtype)


def pick_rows(index, rows, out_count, by_slot, kind):
    count, width = rows.shape
    if by_slot:
        index = index.reshape(1, -1)
        index_spec = pl.BlockSpec(index.shape, lambda i: (0, 0))
    else:
        index = index.reshape(-1, 1)
        index_spec = pl.BlockSpec((BLOCK, 1), lambda i: (i, 0))
    return pl.pallas_call(
        functools.partial(pick_kernel, by_slot),
        grid=(out_count // BLOCK,),
        in_specs=[index_spec, pl.BlockSpec(rows.shape, lambda i: (0, 0), **ONCE)],
        out_specs=pl.BlockSpec((BLOCK, width), lambda i: (i, 0)),
        out_shape=jax.ShapeDtypeStruct((out_count, width), kind),
        compiler_params=pltpu.CompilerParams(vmem_limit_bytes=VMEM_BYTES),
        cost_estimate=pl.CostEstimate(
            flops=2 * out_count * count * max(width, 256),
            bytes_accessed=rows.size * 2 + out_count * width * 4,
            transcendentals=0,
        ),
        name="pick_rows",
    )(index, rows)


def band_kernel(chunk, per, words, sum_column, span_ref, rows_ref, table_ref, stat_ref, out_ref, mix_ref):
    step_id = pl.program_id(0)
    count, width = mix_ref.shape
    chunk_count = table_ref.shape[0] // chunk
    group_count = chunk_count // per
    active = (step_id >= span_ref[0]) & (step_id < span_ref[1])

    def put_stats(top, total):
        lane = lax.broadcasted_iota(jnp.int32, (count, 128), 1)
        both = jnp.where(lane == 0, top, jnp.where(lane == 1, total, 0.0))
        stat_ref[...] = both.T[:8, :]

    def logits_at(at, rows):
        return product_nt(rows, table_ref[pl.ds(at, chunk), :])

    def beyond(at, shape):
        return at + lax.broadcasted_iota(jnp.int32, shape, 1) >= words

    def run(rows, top):
        mix_ref[...] = jnp.zeros(mix_ref.shape, jnp.float32)

        def visit(group, total):
            for inner in range(per):
                at = (group * per + inner) * chunk
                checked = isinstance(at, int) and at + chunk > words
                if not isinstance(at, int):
                    at = pl.multiple_of(at, chunk)
                weights = jnp.exp(logits_at(at, rows) - top)
                if checked:
                    weights = jnp.where(beyond(at, weights.shape), 0.0, weights)
                if sum_column is None:
                    for lane in range(0, chunk, 128):
                        total = total + weights[:, lane : lane + 128]
                mix_ref[...] += product(lowered(weights), table_ref[pl.ds(at, chunk), :])
            return total

        lanes = jnp.zeros((count, 128), jnp.float32)
        lanes = visit(0, lanes) if group_count == 1 else lax.fori_loop(0, group_count, visit, lanes)
        if sum_column is None:
            return jnp.sum(lanes, 1, keepdims=True)
        return mix_ref[:, sum_column : sum_column + 1]

    @pl.when(active)
    def _():
        rows = rows_ref[...]
        first = product_nt(rows, table_ref[pl.ds(0, 128), :])
        top = jnp.max(first, 1, keepdims=True)
        total = run(rows, top)
        put_stats(top, total)

        @pl.when(jnp.logical_not(jnp.max(jnp.where(total < SAFE, 0.0, 1.0)) < 0.5))
        def _():
            def largest(index, top):
                at = pl.multiple_of(index * chunk, chunk)
                logits = logits_at(at, rows)
                if sum_column is None:
                    logits = jnp.where(beyond(at, logits.shape), NEG_FILL, logits)
                return jnp.maximum(top, jnp.max(logits, 1, keepdims=True))

            exact = lax.fori_loop(0, chunk_count, largest, jnp.full((count, 1), NEG_FILL))
            put_stats(exact, run(rows, exact))

        out_ref[...] = lowered(mix_ref[...])

    @pl.when(jnp.logical_not(active))
    def _():
        put_stats(jnp.full((count, 1), NEG_FILL), jnp.zeros((count, 1), jnp.float32))
        out_ref[...] = jnp.zeros(out_ref.shape, jnp.bfloat16)


def band_forward(span, rows, table, words, chunk, sum_column, share):
    count, width = rows.shape[0], table.shape[1]
    chunk_count = table.shape[0] // chunk
    per = chunk_count if chunk_count <= 4 else 4
    assert chunk_count % per == 0 and words >= 128
    return pl.pallas_call(
        functools.partial(band_kernel, chunk, per, words, sum_column),
        grid_spec=pltpu.PrefetchScalarGridSpec(
            num_scalar_prefetch=1,
            grid=(count // BLOCK,),
            in_specs=[
                pl.BlockSpec((BLOCK, width), lambda i, s: (i, 0)),
                pl.BlockSpec(table.shape, lambda i, s: (0, 0), **ONCE),
            ],
            out_specs=[
                pl.BlockSpec((8, BLOCK), lambda i, s: (0, i)),
                pl.BlockSpec((BLOCK, width), lambda i, s: (i, 0)),
            ],
            scratch_shapes=[pltpu.VMEM((BLOCK, width), jnp.float32)],
        ),
        out_shape=[
            jax.ShapeDtypeStruct((8, count), jnp.float32),
            jax.ShapeDtypeStruct((count, width), jnp.bfloat16),
        ],
        compiler_params=pltpu.CompilerParams(vmem_limit_bytes=VMEM_BYTES),
        cost_estimate=pl.CostEstimate(
            flops=int(share * 4 * count * table.shape[0] * max(width, 256)),
            bytes_accessed=table.size * 2 + count * width * 6,
            transcendentals=int(share * count * table.shape[0]),
        ),
        name="band_forward",
    )(span, rows, table)


def head_grad_kernel(chunk, lists, base_ref, table_ref, *refs):
    out_ref, sum_ref = refs[2 * lists :]
    words = table_ref.shape[0]
    base = base_ref[0] + pl.program_id(0) * words
    sum_ref[...] = jnp.zeros(sum_ref.shape, jnp.float32)
    for rows_ref, fact_ref in zip(refs[0 : 2 * lists : 2], refs[1 : 2 * lists : 2]):
        piece = min(rows_ref.shape[0], 1024)

        def visit(step, unused, rows_ref=rows_ref, fact_ref=fact_ref, piece=piece):
            at = pl.multiple_of(step * piece, piece)
            rows = rows_ref[pl.ds(at, piece), :]
            weight = fact_ref[0:1, pl.ds(at, piece)]
            total = fact_ref[1:2, pl.ds(at, piece)]
            ids = fact_ref[2:3, pl.ds(at, piece)].astype(jnp.int32)
            for start in range(0, words, chunk):
                probs = jnp.exp(product_nt(table_ref[start : start + chunk, :], rows) - total)
                word = base + start + lax.broadcasted_iota(jnp.int32, (chunk, 1), 0)
                grads = weight * (jnp.where(word == ids, 1.0, 0.0) - probs)
                sum_ref[start : start + chunk, :] += product(lowered(grads), rows)
            return unused

        lax.fori_loop(0, rows_ref.shape[0] // piece, visit, 0)
    out_ref[...] = lowered(sum_ref[...])


def head_grad(table, part, part_words, first_word, lists):
    width = table.shape[1]
    word_block = math.gcd(part_words, 640)
    steps = part_words // word_block
    chunk = word_block // 2 if word_block % 32 == 0 else word_block
    specs = []
    for rows, facts in lists:
        specs.append(pl.BlockSpec(rows.shape, lambda i, s: (0, 0), **ONCE))
        specs.append(pl.BlockSpec(facts.shape, lambda i, s: (0, 0), **ONCE))
    count = sum(rows.shape[0] for rows, facts in lists)
    scalars = jnp.stack([first_word + part * part_words, part * steps]).astype(jnp.int32)
    return pl.pallas_call(
        functools.partial(head_grad_kernel, chunk, len(lists)),
        grid_spec=pltpu.PrefetchScalarGridSpec(
            num_scalar_prefetch=1,
            grid=(steps,),
            in_specs=[pl.BlockSpec((word_block, width), lambda i, s: (s[1] + i, 0))] + specs,
            out_specs=pl.BlockSpec((word_block, width), lambda i, s: (i, 0)),
            scratch_shapes=[pltpu.VMEM((word_block, width), jnp.float32)],
        ),
        out_shape=jax.ShapeDtypeStruct((part_words, width), jnp.bfloat16),
        compiler_params=pltpu.CompilerParams(vmem_limit_bytes=VMEM_BYTES),
        cost_estimate=pl.CostEstimate(
            flops=4 * count * part_words * width,
            bytes_accessed=(count + part_words) * width * 2,
            transcendentals=count * part_words,
        ),
        name="head_grad",
    )(scalars, table, *[value for pair in lists for value in pair])


def band_grad_kernel(chunk, most, across, plan_ref, table_ref, rows_ref, fact_ref, out_ref, sum_ref):
    words = table_ref.shape[0]
    step_id = pl.program_id(0)
    base = plan_ref[most + 1] + step_id * words
    sum_ref[...] = jnp.zeros(sum_ref.shape, jnp.float32)

    def block_at(position):
        return pl.multiple_of(plan_ref[position] * BLOCK, BLOCK)

    def spread(starts):
        rows = [rows_ref[pl.ds(start, BLOCK), :] for start in starts]
        facts = [fact_ref[:, pl.ds(start, BLOCK)] for start in starts]
        rows = rows[0] if len(rows) == 1 else jnp.concatenate(rows, 0)
        facts = facts[0] if len(facts) == 1 else jnp.concatenate(facts, 1)
        weight, total = facts[0:1], facts[1:2]
        for start in range(0, words, chunk):
            probs = jnp.exp(product_nt(table_ref[start : start + chunk, :], rows) - total)
            sum_ref[start : start + chunk, :] -= product(lowered(weight * probs), rows)

    count = plan_ref[0]

    def pair(step, unused):
        spread([block_at(1 + 2 * step), block_at(2 + 2 * step)])
        return unused

    lax.fori_loop(0, count // 2, pair, 0)

    @pl.when(count % 2 == 1)
    def _():
        spread([block_at(count)])

    line = most + 2 + step_id * (most + 1)

    def hits(step, unused):
        at = block_at(line + 1 + step)
        rows = rows_ref[pl.ds(at, BLOCK), :]
        weight = fact_ref[0:1, pl.ds(at, BLOCK)]
        ids = fact_ref[2:3, pl.ds(at, BLOCK)].astype(jnp.int32)
        for start in range(0, words, chunk):
            word = base + start + lax.broadcasted_iota(jnp.int32, (chunk, 1), 0)
            chosen = lowered(jnp.where(word == ids, weight, 0.0))
            sum_ref[start : start + chunk, :] += product(chosen, rows)
        return unused

    lax.fori_loop(0, plan_ref[line], hits, 0)
    if across:
        out_ref[...] = sum_ref[...].T[: out_ref.shape[0], :].astype(out_ref.dtype)
    else:
        out_ref[...] = sum_ref[...].astype(out_ref.dtype)


def listed(flags):
    size = flags.shape[-1]
    order = jnp.cumsum(flags.astype(jnp.int32), -1)
    chosen = (order[..., None, :] == jnp.arange(1, size + 1)[:, None]) & flags[..., None, :]
    places = jnp.sum(jnp.where(chosen, jnp.arange(size), 0), -1)
    return jnp.concatenate([order[..., -1:], places], -1).astype(jnp.int32)


def band_grad(
    table, rows, facts, active, lowest, highest, part, part_words, first_word, chunk, result, across
):
    count, full = rows.shape[0], table.shape[1]
    word_block = chunk
    steps = part_words // word_block
    most = count // BLOCK
    first = first_word + part * part_words
    low = first + jnp.arange(steps, dtype=jnp.int32)[:, None] * word_block
    step_hits = active[None, :] & (lowest[None, :] < low + word_block) & (highest[None, :] >= low)
    plan = jnp.concatenate(
        [
            listed(active),
            first.reshape(1).astype(jnp.int32),
            listed(step_hits).reshape(-1),
            (part * steps).reshape(1).astype(jnp.int32),
        ]
    )
    last = plan.shape[0] - 1
    return pl.pallas_call(
        functools.partial(band_grad_kernel, chunk // 2 if chunk > 832 else chunk, most, across),
        grid_spec=pltpu.PrefetchScalarGridSpec(
            num_scalar_prefetch=1,
            grid=(steps,),
            in_specs=[
                pl.BlockSpec((word_block, full), lambda i, s: (s[last] + i, 0)),
                pl.BlockSpec((count, full), lambda i, s: (0, 0), **ONCE),
                pl.BlockSpec(facts.shape, lambda i, s: (0, 0), **ONCE),
            ],
            out_specs=(
                pl.BlockSpec((result.shape[0], word_block), lambda i, s: (0, i))
                if across
                else pl.BlockSpec((word_block, full), lambda i, s: (i, 0))
            ),
            scratch_shapes=[pltpu.VMEM((word_block, full), jnp.float32)],
        ),
        out_shape=result,
        compiler_params=pltpu.CompilerParams(vmem_limit_bytes=VMEM_BYTES),
        cost_estimate=pl.CostEstimate(
            flops=2 * count * part_words * 256,
            bytes_accessed=count * full * 2 + part_words * full * 4,
            transcendentals=count * part_words // 2,
        ),
        name="band_grad",
    )(plan, table, rows, facts)


def settle_kernel(
    member_ref,
    everyone_ref,
    fact_ref,
    head_mix_ref,
    middle_mix_ref,
    tail_mix_ref,
    head_hit_ref,
    middle_hit_ref,
    tail_hit_ref,
    term_ref,
    line_ref,
    slot_ref,
):
    step = pl.program_id(0)
    devices, _, slots = everyone_ref.shape
    tail_width = 64
    here = pl.ds(pl.multiple_of(step * BLOCK, BLOCK), BLOCK)

    def merged(read):
        lines = [read(device) for device in range(devices)]
        top = functools.reduce(jnp.maximum, [line[0] for line in lines])
        return top, sum(line[1] * jnp.exp(line[0] - top) for line in lines)

    head_top, head_sum = merged(
        lambda d: (everyone_ref[d, 0:1, here], everyone_ref[d, 1:2, here])
    )
    target = sum(everyone_ref[d, 2:3, here] for d in range(devices))
    slot_top, slot_sum = merged(lambda d: (everyone_ref[d, 3:4, :], everyone_ref[d, 4:5, :]))
    used = slot_sum > 0.0
    slot_total = jnp.where(used, slot_top + jnp.log(jnp.where(used, slot_sum, 1.0)), 0.0)
    member = member_ref[0]
    own_slot_top = jnp.where(used, everyone_ref[member, 3:4, :], 0.0)
    own_head_top = everyone_ref[member, 0:1, here]

    facts = fact_ref[...]
    slot, share, cotangent, first_cluster, second_cluster, band, word = (
        facts[index : index + 1] for index in range(7)
    )

    def as_columns(lines):
        square = jnp.concatenate(
            lines + [jnp.zeros((128 - len(lines), BLOCK), jnp.float32)], 0
        )
        return square.T

    def three(line):
        return [part.astype(jnp.float32) for part in thirds(line)]

    slot_column = as_columns([slot])[:, 0:1].astype(jnp.int32)
    hot = lowered(
        jnp.where(lax.broadcasted_iota(jnp.int32, (BLOCK, slots), 1) == slot_column, 1.0, 0.0)
    )
    lines = three(slot_total) + three(own_slot_top) + [jnp.zeros((10, slots), jnp.float32)]
    on_tokens = product_nt(lowered(jnp.concatenate(lines, 0)), hot)
    band_total = on_tokens[0:1] + on_tokens[1:2] + on_tokens[2:3]
    own_band_top = on_tokens[3:4] + on_tokens[4:5] + on_tokens[5:6]

    cluster_top = jnp.maximum(head_top, jnp.maximum(first_cluster, second_cluster))
    head_total = cluster_top + jnp.log(
        head_sum * jnp.exp(head_top - cluster_top)
        + jnp.exp(first_cluster - cluster_top)
        + jnp.exp(second_cluster - cluster_top)
    )
    in_head = band < 0.5
    cluster = jnp.where(band < 1.5, first_cluster, second_cluster)
    model_logp = target - head_total + jnp.where(in_head, 0.0, cluster - band_total)
    ratio = 0.25 * share * jnp.exp(-model_logp)
    weight = cotangent * 0.75 / (0.75 + ratio)
    head_scale = weight * jnp.exp(own_head_top - head_total)
    band_scale = weight * jnp.where(in_head, 0.0, jnp.exp(own_band_top - band_total))
    columns = as_columns([weight, head_scale, band_scale])
    weight_column, head_column, band_column = (columns[:, i : i + 1] for i in range(3))
    width = head_mix_ref.shape[1]
    term_ref[:, :width] = lowered(
        weight_column * head_hit_ref[...].astype(jnp.float32)
        - head_column * head_mix_ref[...].astype(jnp.float32)
    )
    narrow = tail_mix_ref.shape[1]
    kept = lax.broadcasted_iota(jnp.int32, (BLOCK, narrow), 1) < tail_width

    def widened(values):
        values = jnp.where(kept, values, 0.0)
        more = middle_mix_ref.shape[1] - narrow
        return jnp.concatenate([values, jnp.zeros((BLOCK, more), jnp.float32)], 1)

    band_mix = product(hot, middle_mix_ref[...]) + widened(product(hot, tail_mix_ref[...]))
    band_hit = middle_hit_ref[...].astype(jnp.float32) + widened(
        tail_hit_ref[...].astype(jnp.float32)
    )
    term_ref[:, width:] = lowered(weight_column * band_hit - band_column * band_mix)
    line_ref[...] = jnp.concatenate(
        [
            model_logp + jnp.log(0.75 + ratio),
            weight,
            head_total,
            word,
            jnp.zeros((4, BLOCK), jnp.float32),
        ],
        0,
    )

    @pl.when(step == 0)
    def _():
        slot_ref[...] = jnp.concatenate(
            [jnp.zeros((8, slots), jnp.float32), slot_total, jnp.zeros((7, slots), jnp.float32)], 0
        )

    sent = three(weight) + three(word) + [jnp.zeros((10, BLOCK), jnp.float32)]
    slot_ref[0:8, :] += product(lowered(jnp.concatenate(sent, 0)), hot)[0:8]


def settle(member, everyone, facts, head_mix, middle_mix, tail_mix, hits):
    count, width = head_mix.shape
    slots = middle_mix.shape[0]
    full = width + middle_mix.shape[1]

    def tokens(values):
        return pl.BlockSpec((BLOCK, values.shape[1]), lambda i, s: (i, 0))

    def whole(values):
        return pl.BlockSpec(values.shape, lambda i, s: (0,) * values.ndim, **ONCE)

    lines = pl.BlockSpec((8, BLOCK), lambda i, s: (0, i))
    return pl.pallas_call(
        settle_kernel,
        grid_spec=pltpu.PrefetchScalarGridSpec(
            num_scalar_prefetch=1,
            grid=(count // BLOCK,),
            in_specs=[whole(everyone), lines, tokens(head_mix), whole(middle_mix), whole(tail_mix)]
            + [tokens(hit) for hit in hits],
            out_specs=[
                pl.BlockSpec((BLOCK, full), lambda i, s: (i, 0)),
                lines,
                pl.BlockSpec((16, slots), lambda i, s: (0, 0)),
            ],
        ),
        out_shape=[
            jax.ShapeDtypeStruct((count, full), jnp.bfloat16),
            jax.ShapeDtypeStruct((8, count), jnp.float32),
            jax.ShapeDtypeStruct((16, slots), jnp.float32),
        ],
        compiler_params=pltpu.CompilerParams(vmem_limit_bytes=VMEM_BYTES),
        cost_estimate=pl.CostEstimate(
            flops=2 * count * slots * 1024,
            bytes_accessed=count * width * 12 + slots * full,
            transcendentals=slots * 64,
        ),
        name="settle",
    )(member.reshape(1).astype(jnp.int32), everyone, facts, head_mix, middle_mix, tail_mix, *hits)


def line_turns(value):
    size = lax.axis_size("seq")
    return [value] + [
        lax.ppermute(value, "seq", [(d, (d - k) % size) for d in range(size)])
        for k in range(1, size)
    ]


def line_step(before, behind, step):
    size = lax.axis_size("seq")
    return (
        lax.ppermute(before, "seq", [(d, d + 1) for d in range(step - 1, size - 1)]),
        lax.ppermute(behind, "seq", [(d, d - 1) for d in range(1, size - step + 1)]),
    )


def line_steps(value):
    found = [(value, value)]

    def advance(*others):
        step = len(found)
        if step == lax.axis_size("seq"):
            return others
        moved = line_step(*found[-1], step)
        moved, others = lax.optimization_barrier((moved, others))
        found.append(moved)
        return others

    return found, advance


def line_ordered(found):
    size, place = lax.axis_size("seq"), lax.axis_index("seq")
    ordered = []
    for source in range(size):
        value = found[0][0]
        for step in range(1, size):
            if source + step < size:
                value = jnp.where(place == source + step, found[step][0], value)
            if source - step >= 0:
                value = jnp.where(place == source - step, found[step][1], value)
        ordered.append(value)
    return ordered


def earlier_joined(value):
    size, place = lax.axis_size("seq"), lax.axis_index("seq")
    joined = jnp.zeros((size,) + value.shape, value.dtype)
    for step in range(size - 1, -1, -1):
        piece = value
        if step:
            piece = lax.ppermute(value, "seq", [(d, d + step) for d in range(size - step)])
        joined = lax.dynamic_update_index_in_dim(joined, piece, jnp.maximum(place - step, 0), 0)
    return joined.reshape((-1,) + value.shape[1:])


def in_order(pieces):
    size, place = lax.axis_size("seq"), lax.axis_index("seq")
    joined = jnp.zeros((size,) + pieces[0].shape, pieces[0].dtype)
    for k, piece in enumerate(pieces):
        joined = lax.dynamic_update_index_in_dim(joined, piece, lax.rem(place + k, size), 0)
    return joined.reshape((-1,) + pieces[0].shape[1:])


def line_scatter(values, behind=True):
    size, place = lax.axis_size("seq"), lax.axis_index("seq")
    parts = values.reshape((size, -1) + values.shape[1:])

    def part(index):
        return lax.dynamic_index_in_dim(parts, lax.rem(index, size), 0, False)

    total = part(place).astype(jnp.float32)
    for k in range(1, size):
        pairs = [(d, (d - k) % size) for d in range(0 if behind else k, size)]
        total = total + lax.ppermute(part(place + size - k), "seq", pairs).astype(jnp.float32)
    return total


def turn_kernel(rows_ref, out_ref):
    out_ref[...] = rows_ref[...].astype(jnp.float32).T.astype(out_ref.dtype)


def turned(rows, kind):
    return pl.pallas_call(
        turn_kernel, out_shape=jax.ShapeDtypeStruct(rows.shape[::-1], kind), name="turned"
    )(rows)


def word_pad(rows, biggest, splits):
    chunk = min(biggest, round_up(rows, 128))
    chunks = -(-rows // chunk)
    if chunks > 4:
        chunks = round_up(chunks, 4)
    return chunk, chunks * chunk


def on_device(
    inputs,
    targets,
    neighbours,
    neighbour_scores,
    loglik_grad,
    first_gain,
    first_shift,
    query_weight,
    query_bias,
    key_weight,
    value_weight,
    value_bias,
    out_weight,
    out_bias,
    second_gain,
    second_shift,
    inner_weight,
    inner_bias,
    outer_weight,
    outer_bias,
    final_gain,
    final_shift,
    head_table,
    cluster_weight,
    middle_map,
    middle_table,
    tail_map,
    tail_table,
):
    nb = lax.axis_size("batch")
    nz = lax.axis_size("seq")
    member = lax.axis_index("batch")
    place = lax.axis_index("seq")
    tokens = inputs[0]
    own_ids = targets[0]
    token_count, feature_count = tokens.shape
    group_count = token_count * nb
    slot_count = group_count + BLOCK
    query_start = (place * token_count).reshape(1)

    normed_low = lowered(layer_norm(tokens, first_gain, first_shift))
    normed_all = earlier_joined(normed_low)
    top_score = jnp.max(neighbour_scores[0], -1, keepdims=True)
    exponent = jnp.exp(neighbour_scores[0] - top_score)
    knn_prob = jnp.sum(jnp.where(neighbours[0] == 0, exponent, 0.0), -1) / jnp.sum(exponent, -1)
    early = jnp.stack([own_ids.astype(jnp.float32), knn_prob, loglik_grad[0]])
    early = lax.all_gather(early, "batch", axis=1, tiled=True)
    all_ids = early[0].astype(jnp.int32)
    all_knn, all_up = early[1], early[2]
    in_head = all_ids < HEAD_WORDS
    in_middle = (all_ids >= HEAD_WORDS) & (all_ids < HEAD_WORDS + MID_WORDS)
    in_tail = all_ids >= HEAD_WORDS + MID_WORDS
    order = jnp.arange(group_count, dtype=jnp.int32)
    ahead = (all_ids[None, :] < all_ids[:, None]) | (
        (all_ids[None, :] == all_ids[:, None]) & (order[None, :] < order[:, None])
    )
    rank = jnp.sum(ahead.astype(jnp.int32), -1)
    head_size = jnp.sum(in_head.astype(jnp.int32))
    middle_size = jnp.sum(in_middle.astype(jnp.int32))
    tail_size = group_count - head_size - middle_size
    middle_blocks = (middle_size + BLOCK - 1) // BLOCK
    tail_blocks = (tail_size + BLOCK - 1) // BLOCK
    slot = jnp.where(
        in_head,
        -1,
        rank - head_size + jnp.where(in_tail, middle_blocks * BLOCK - middle_size, 0),
    )
    zero_span = jnp.zeros((1,), jnp.int32)
    head_span = jnp.array([0, group_count // BLOCK], jnp.int32)
    middle_span = jnp.stack([0 * middle_blocks, middle_blocks]).astype(jnp.int32)
    tail_span = jnp.stack([middle_blocks, middle_blocks + tail_blocks]).astype(jnp.int32)
    slot_order = jnp.arange(slot_count, dtype=jnp.int32)
    slot_middle = slot_order < middle_size
    slot_tail = (slot_order >= middle_blocks * BLOCK) & (
        slot_order < middle_blocks * BLOCK + tail_size
    )
    slot_used = slot_middle | slot_tail
    band_id = all_ids - jnp.where(in_tail, HEAD_WORDS + MID_WORDS, HEAD_WORDS)

    tables = (head_table, middle_table, tail_table)
    sizes = tuple(table.shape[0] for table in tables)
    head_chunk, head_padded = word_pad(sizes[0], 1280, nz)
    middle_chunk, middle_padded = word_pad(sizes[1], 1280, nz)
    tail_chunk, tail_padded = word_pad(sizes[2], 1664, nz)
    tail_width = tail_table.shape[1]
    head_pad = jnp.pad(head_table, ((0, head_padded - sizes[0]), (0, 0)))
    middle_pad = jnp.pad(middle_table, ((0, middle_padded - sizes[1]), (0, 0)))
    tail_word = jnp.arange(tail_padded, dtype=jnp.int32)
    tail_bias = jnp.where(tail_word < jnp.minimum(TAIL_WORDS - member * sizes[2], sizes[2]), 0.0, NEG_FILL)
    tail_pad = jnp.concatenate(
        [
            jnp.pad(tail_table.T, ((0, 0), (0, tail_padded - sizes[2]))),
            jnp.ones((1, tail_padded), jnp.bfloat16),
            lowered(tail_bias)[None, :],
            jnp.zeros((126 - tail_width, tail_padded), jnp.bfloat16),
        ],
        0,
    ).T
    locals_ = (
        all_ids - member * sizes[0],
        all_ids - HEAD_WORDS - member * sizes[1],
        all_ids - HEAD_WORDS - MID_WORDS - member * sizes[2],
    )
    owned = tuple(
        inside & (local >= 0) & (local < size)
        for inside, local, size in zip((in_head, in_middle, in_tail), locals_, sizes)
    )
    hit_rows = tuple(
        jnp.where(
            own[:, None],
            jnp.take(table, jnp.clip(local, 0, size - 1), axis=0, mode="clip"),
            jnp.bfloat16(0),
        )
        for own, table, local, size in zip(owned, (head_pad, middle_pad, tail_pad), locals_, sizes)
    )

    queries = lowered(product(normed_low, query_weight) + query_bias)
    key_rows = lowered(product(normed_all, key_weight))
    value_rows = lowered(product(normed_all, value_weight) + value_bias)
    attended_low = attend(query_start, queries, key_rows, value_rows)
    mixed = tokens + product(attended_low, out_weight) + out_bias
    second_low = lowered(layer_norm(mixed, second_gain, second_shift))
    before = product(second_low, inner_weight) + inner_bias
    hidden_low = lowered(jax.nn.gelu(before))
    final = mixed + product(hidden_low, outer_weight) + outer_bias
    state_low = lowered(layer_norm(final, final_gain, final_shift))
    all_states = lax.all_gather(state_low, "batch", axis=0, tiled=True)
    split = 2 * nz * group_count * feature_count <= 24 << 20
    if split:
        block_states = lax.all_gather(state_low, "seq", axis=0, tiled=True)
    all_states, head_pad, middle_pad, tail_pad, tail_hits, slot, early = lax.optimization_barrier(
        (all_states, head_pad, middle_pad, tail_pad, hit_rows[2], slot, early)
    )
    hit_rows = hit_rows[:2] + (tail_hits,)

    middle_width = middle_map.shape[1]
    maps = jnp.pad(jnp.concatenate([middle_map, tail_map], 1), ((0, 0), (0, 128 - tail_width)))
    one_column = (jnp.arange(middle_width + 128) == middle_width + tail_width + 1).astype(jnp.float32)
    band_low = lowered(product(all_states, maps) + one_column)
    middle_low, tail_low = band_low[:, :middle_width], band_low[:, middle_width:]
    cluster_lines = product_nt(
        jnp.pad(cluster_weight.T, ((0, 6), (0, 0))), all_states
    )
    slot_full = pick_rows(slot, band_low, slot_count, True, jnp.bfloat16)
    first_tail = middle_blocks * BLOCK
    in_tail_slot = slot_order >= first_tail
    slot_low = jnp.where(
        in_tail_slot[:, None],
        jnp.pad(slot_full[:, middle_width:], ((0, 0), (0, middle_width - 128))),
        slot_full[:, :middle_width],
    )
    if split:
        piece = slot_count // nb
        slot_piece = lax.dynamic_slice_in_dim(slot_low, member * piece, piece, 0)
        other_slots = jnp.concatenate(line_turns(slot_piece)[1:], 0)
    head_stats, head_mix = band_forward(
        head_span, all_states, head_pad, sizes[0], head_chunk, None, 1.0
    )
    if split:
        slot_low, block_states, hit_rows, head_stats = lax.optimization_barrier(
            (slot_low, block_states, hit_rows, head_stats)
        )
        other_states = lax.dynamic_slice_in_dim(
            jnp.concatenate([block_states, block_states], 0),
            (place + 1) * token_count,
            (nz - 1) * token_count,
            0,
        )
        other_states = lax.all_gather(other_states, "batch", axis=0, tiled=True)
    tail_stats, tail_mix = band_forward(
        tail_span, slot_low, tail_pad, tail_padded, tail_chunk, tail_width, 0.5
    )
    middle_stats, middle_mix = band_forward(
        middle_span, slot_low, middle_pad, sizes[1], middle_chunk, None, 0.25
    )
    inner_lane = jnp.arange(128) < tail_width
    target_part = (
        jnp.sum(hit_rows[0].astype(jnp.float32) * all_states.astype(jnp.float32), -1)
        + jnp.sum(hit_rows[1].astype(jnp.float32) * middle_low.astype(jnp.float32), -1)
        + jnp.sum(
            jnp.where(inner_lane, hit_rows[2].astype(jnp.float32), 0.0)
            * tail_low.astype(jnp.float32),
            -1,
        )
    )
    slot_stats = jnp.where(in_tail_slot[None, :], tail_stats[:2], middle_stats[:2])
    extra = ((0, 0), (0, BLOCK))
    stats = jnp.concatenate(
        [
            jnp.pad(jnp.concatenate([head_stats[:2], target_part[None]], 0), extra),
            slot_stats,
            jnp.zeros((3, slot_count), jnp.float32),
        ],
        0,
    )
    if split:
        stats, other_states, other_slots = lax.optimization_barrier(
            (stats, other_states, other_slots)
        )
        other_slots = lax.all_gather(other_slots, "batch", axis=0, tiled=True)
    everyone = lax.all_gather(stats, "batch")

    token_facts = jnp.concatenate(
        [
            slot.astype(jnp.float32)[None],
            early[1:3],
            cluster_lines[:2],
            jnp.where(in_head, 0.0, jnp.where(in_middle, 1.0, 2.0))[None],
            early[0:1],
            jnp.zeros((1, group_count), jnp.float32),
        ],
        0,
    )
    terms, lines, slot_lines = settle(
        member, everyone, token_facts, head_mix, middle_mix, tail_mix, hit_rows
    )
    own_terms = lax.psum_scatter(terms, "batch", scatter_dimension=0, tiled=True).astype(jnp.float32)

    def own_part(values):
        return lax.dynamic_slice_in_dim(values, member * token_count, token_count, 0)

    loglik = own_part(lines[0])

    kind = jnp.where(slot_middle, 1.0, jnp.where(slot_tail, 2.0, 0.0))
    slot_facts = jnp.stack(
        [
            jnp.sum(slot_lines[0:3], 0),
            slot_lines[8],
            jnp.sum(slot_lines[3:6], 0),
            kind,
        ]
    )
    head_facts = jnp.concatenate([lines[1:4], jnp.zeros((1, group_count), jnp.float32)], 0)
    if split:
        other_slots = (
            other_slots.reshape(nb, nz - 1, piece, middle_width)
            .transpose(1, 0, 2, 3)
            .reshape(-1, middle_width)
        )
        rows_all = jnp.concatenate([slot_low, other_slots], 0)
        fact_pieces = line_turns(jnp.concatenate([slot_facts, head_facts], 1))
        facts = jnp.concatenate([value[:, :slot_count] for value in fact_pieces], 1)
        other_facts = (
            jnp.stack([value[:, slot_count:] for value in fact_pieces[1:]], 1)
            .reshape(4, nz - 1, nb, token_count)
            .transpose(0, 2, 1, 3)
            .reshape(4, -1)
        )
        lists = [(all_states, head_facts), (other_states, other_facts)]
        part, parts = place, nz
    else:
        rows_all, facts, lists = slot_low, slot_facts, [(all_states, head_facts)]
        part, parts = 0 * place, 1
    head_part = head_grad(head_pad, part, head_padded // parts, member * sizes[0], lists)
    block_facts = facts[2:4].reshape(2, -1, BLOCK)
    block_kind = jnp.max(block_facts[1], -1)
    filled = block_facts[1] > 0
    lowest = jnp.min(jnp.where(filled, block_facts[0], 1e9), -1).astype(jnp.int32)
    highest = jnp.max(jnp.where(filled, block_facts[0], -1e9), -1).astype(jnp.int32)
    facts = jnp.concatenate(
        [facts[:2], jnp.where(facts[3:4] > 0, facts[2:3], -1e9), jnp.zeros_like(facts[:1])], 0
    )
    def tail_gradient(part, parts):
        return band_grad(
            tail_pad,
            rows_all,
            facts,
            block_kind == 2,
            lowest,
            highest,
            part,
            tail_padded // parts,
            HEAD_WORDS + MID_WORDS + member * sizes[2],
            math.gcd(tail_padded // parts, tail_chunk),
            jax.ShapeDtypeStruct((tail_width, tail_padded // parts), jnp.bfloat16),
            True,
        )

    first_tail = tail_gradient(2 * part, 2 * parts)
    if split:
        head_found, head_advance = line_steps(head_part)
        first_tail, facts = head_advance(first_tail, facts)
        first_found, first_advance = line_steps(first_tail)
        second_tail = tail_gradient(2 * part + 1, 2 * parts)
        second_tail, own_terms = head_advance(second_tail, own_terms)
        second_tail, own_terms = first_advance(second_tail, own_terms)
        second_found, second_advance = line_steps(second_tail)
    else:
        second_tail = tail_gradient(2 * part + 1, 2 * parts)
        own_terms, first_tail, second_tail = lax.optimization_barrier(
            (own_terms, first_tail, second_tail)
        )

    own_middle = own_part(in_middle)
    own_tail = own_part(in_tail)
    own_lines = lax.dynamic_slice_in_dim(lines, member * token_count, token_count, 1)
    own_weights, own_total = own_lines[1], own_lines[2]
    own_clusters = product(state_low, cluster_weight)
    band_state = own_terms[:, feature_count:]
    middle_state = lowered(jnp.where(own_middle[:, None], band_state, 0.0))
    tail_state = lowered(jnp.where(own_tail[:, None], band_state[:, :tail_width], 0.0))
    cluster_hit = jnp.stack([own_middle, own_tail], -1).astype(jnp.float32)
    cluster_grad = own_weights[:, None] * (
        cluster_hit - jnp.exp(own_clusters - own_total[:, None])
    )
    state_grad = (
        own_terms[:, :feature_count]
        + product_nt(middle_state, middle_map)
        + product_nt(tail_state, tail_map)
        + product_nt(cluster_grad, cluster_weight.astype(jnp.float32))
    )
    middle_map_grad = product_tn(state_low, middle_state)
    tail_map_rows = product_tn(tail_state, state_low)
    cluster_rows = product_tn(cluster_grad, state_low.astype(jnp.float32))
    final_grad, final_gain_grad, final_shift_grad = norm_back(
        final, final_gain, final_shift, state_grad
    )
    final_low = lowered(final_grad)
    outer_weight_grad = product_tn(hidden_low, final_low)
    outer_bias_grad = jnp.sum(final_grad, 0)
    outer_part = lax.psum_scatter(
        lowered(outer_weight_grad), "batch", scatter_dimension=0, tiled=True
    )
    before_grad = lowered(gelu_back(before, product_nt(final_low, outer_weight)))
    inner_weight_grad = product_tn(second_low, before_grad)
    inner_bias_grad = jnp.sum(before_grad.astype(jnp.float32), 0)
    inner_part = lax.psum_scatter(
        lowered(inner_weight_grad), "batch", scatter_dimension=0, tiled=True
    )
    second_in_grad, second_gain_grad, second_shift_grad = norm_back(
        mixed, second_gain, second_shift, product_nt(before_grad, inner_weight)
    )
    mixed_grad = final_grad + second_in_grad
    mixed_low = lowered(mixed_grad)
    out_weight_grad = product_tn(attended_low, mixed_low)
    out_bias_grad = jnp.sum(mixed_grad, 0)
    attended_grad = lowered(product_nt(mixed_low, out_weight))
    if split:
        for unused in range(nz - 3):
            (attended_grad,) = head_advance(attended_grad)
        (attended_grad,) = second_advance(attended_grad)
    query_low, key_low, value_low = attend_back(
        query_start, queries, key_rows, value_rows, attended_grad
    )
    if split:
        query_low, key_low, value_low = first_advance(query_low, key_low, value_low)
        query_low, key_low, value_low = second_advance(query_low, key_low, value_low)
    query_weight_grad = product_tn(normed_low, query_low)
    key_weight_grad = product_tn(normed_all, key_low)
    value_weight_grad = product_tn(normed_all, value_low)
    query_bias_grad = jnp.sum(query_low.astype(jnp.float32), 0)
    value_bias_grad = jnp.sum(value_low.astype(jnp.float32), 0)
    spread = product_nt(key_low, key_weight) + product_nt(value_low, value_weight)
    query_spread = product_nt(query_low, query_weight)
    first_shift_grad = jnp.sum(spread, 0) + jnp.sum(query_spread, 0)
    all_centred = (normed_all.astype(jnp.float32) - first_shift) / first_gain
    own_average = jnp.mean(tokens, -1, keepdims=True)
    own_spread = jnp.mean((tokens - own_average) ** 2, -1, keepdims=True)
    own_centred = (tokens - own_average) * lax.rsqrt(own_spread + EPSILON)
    first_gain_grad = jnp.sum(all_centred * spread, 0) + jnp.sum(own_centred * query_spread, 0)
    bias_rows = inner_bias_grad.shape[0] // feature_count
    inner_bias_rows = (
        inner_bias_grad.reshape(nb, bias_rows, -1).transpose(1, 0, 2).reshape(bias_rows, -1)
    )
    vectors = [
        first_gain_grad,
        first_shift_grad,
        query_bias_grad,
        value_bias_grad,
        out_bias_grad,
        second_gain_grad,
        second_shift_grad,
        outer_bias_grad,
        final_gain_grad,
        final_shift_grad,
    ]
    rows = [tail_map_rows, cluster_rows, inner_bias_rows] + [value[None] for value in vectors]
    edges = [0]
    for row in rows:
        edges.append(edges[-1] + row.shape[0])
    row_count = round_up(edges[-1], 128)
    rows.append(jnp.zeros((row_count - edges[-1], feature_count), jnp.float32))
    columns = [
        query_weight_grad,
        key_weight_grad,
        value_weight_grad,
        out_weight_grad,
        middle_map_grad,
        turned(jnp.concatenate(rows, 0), jnp.bfloat16),
    ]
    rest = jnp.concatenate([lowered(column) for column in columns], 1)
    spread_low = lowered(spread)
    inner_low = lowered(line_scatter(inner_part))
    rest, facts, spread_low, inner_low = lax.optimization_barrier(
        (rest, facts, spread_low, inner_low)
    )
    if split:
        for unused in range(nz - 3):
            rest, facts, spread_low = first_advance(rest, facts, spread_low)
            rest, facts, spread_low = second_advance(rest, facts, spread_low)
    rest_part = lax.psum_scatter(rest, "batch", scatter_dimension=0, tiled=True)
    inner_pieces = line_turns(inner_low)
    spread_sum = line_scatter(spread_low, False)
    middle_result = jax.ShapeDtypeStruct(
        (sizes[1], middle_width) if split else (middle_padded, middle_width),
        jnp.float32 if split else jnp.bfloat16,
    )
    middle_part = band_grad(
        middle_pad,
        rows_all,
        facts,
        block_kind == 1,
        lowest,
        highest,
        0 * place,
        middle_padded,
        HEAD_WORDS + member * sizes[1],
        middle_chunk,
        middle_result,
        False,
    )
    middle_part, inner_pieces, spread_sum, outer_part = lax.optimization_barrier(
        (middle_part, inner_pieces, spread_sum, outer_part)
    )
    outer_low = lowered(line_scatter(outer_part))
    rest_part, outer_low = lax.optimization_barrier((rest_part, outer_low))
    if split:
        middle_table_grad = middle_part
        head_table_grad = jnp.concatenate(line_ordered(head_found), 0)
        pairs = zip(line_ordered(first_found), line_ordered(second_found))
        tail_sum = jnp.concatenate([value for pair in pairs for value in pair], 1)
    else:
        middle_table_grad = lax.psum(middle_part, "seq")[: sizes[1]].astype(jnp.float32)
        head_table_grad = lax.psum(head_part, "seq")
        tail_sum = lax.psum(jnp.concatenate([first_tail, second_tail], 1), "seq")
    head_table_grad = head_table_grad[: sizes[0]].astype(jnp.float32)
    tail_table_grad = tail_sum[:, : sizes[2]].astype(jnp.float32).T
    normed_grad = query_spread + spread_sum
    first_in_grad, unused, unused = norm_back(tokens, first_gain, first_shift, normed_grad)
    input_grad = mixed_grad + first_in_grad
    inner_sum = in_order(inner_pieces).astype(jnp.float32)
    outer_sum = in_order(line_turns(outer_low)).astype(jnp.float32)
    rest_low = lax.psum(rest_part, "seq")
    rest_sum = rest_low[:, : 4 * feature_count + middle_width].astype(jnp.float32)
    cut = [rest_sum[:, i * feature_count : (i + 1) * feature_count] for i in range(4)]
    middle_map_sum = rest_sum[:, 4 * feature_count : 4 * feature_count + middle_width]
    row_sum = turned(rest_low[:, 4 * feature_count + middle_width :], jnp.float32)
    tail_map_sum, cluster_sum, inner_bias_sum = (
        row_sum[low:high] for low, high in zip(edges[:3], edges[1:4])
    )
    lines = [row_sum[index] for index in range(edges[3], edges[3] + len(vectors))]
    return (
        loglik.reshape(1, token_count),
        input_grad.reshape(1, token_count, feature_count),
        lines[0],
        lines[1],
        cut[0],
        lines[2],
        cut[1],
        cut[2],
        lines[3],
        cut[3],
        lines[4],
        lines[5],
        lines[6],
        inner_sum,
        inner_bias_sum.reshape(-1),
        outer_sum,
        lines[7],
        lines[8],
        lines[9],
        head_table_grad,
        cluster_sum.T,
        middle_map_sum,
        middle_table_grad,
        tail_map_sum.T,
        tail_table_grad,
    )


def solution(mesh):
    return jax.shard_map(
        on_device,
        mesh=mesh,
        in_specs=(
            P("batch", "seq", None),
            P("batch", "seq"),
            P("batch", "seq", None),
            P("batch", "seq", None),
            P("batch", "seq"),
            P(),
            P(),
            P(),
            P(),
            P(),
            P(),
            P(),
            P(),
            P(),
            P(),
            P(),
            P(),
            P(),
            P(),
            P(),
            P(),
            P(),
            P("batch", None),
            P(),
            P(),
            P("batch", None),
            P(),
            P("batch", None),
        ),
        out_specs=(
            P("batch", "seq"),
            P("batch", "seq", None),
            P("batch"),
            P("batch"),
            P("batch", None),
            P("batch"),
            P("batch", None),
            P("batch", None),
            P("batch"),
            P("batch", None),
            P("batch"),
            P("batch"),
            P("batch"),
            P("batch", None),
            P("batch"),
            P("batch", None),
            P("batch"),
            P("batch"),
            P("batch"),
            P("batch", None),
            P("batch", None),
            P("batch", None),
            P("batch", None),
            P("batch", None),
            P("batch", None),
        ),
        check_vma=False,
    )
```

```python
import functools
import math

import jax
import jax.numpy as jnp
from jax import lax
from jax.experimental import pallas as pl
from jax.experimental.pallas import tpu as pltpu
from jax.sharding import PartitionSpec as P

HEADS = 16
HEAD_WORDS = 20000
MID_WORDS = 40000
TAIL_WORDS = 207735


NEG_FILL = -1e30
EPSILON = 1e-05
BLOCK = 256
SAFE = 1e30
VMEM_BYTES = 56 << 20
ONCE = dict(pipeline_mode=pl.Buffered(1))


def layer_norm(values, gain_vector, shift_vector):
    average = jnp.mean(values, -1, keepdims=True)
    centred = values - average
    spread = jnp.mean(centred * centred, -1, keepdims=True)
    return centred * lax.rsqrt(spread + EPSILON) * gain_vector + shift_vector


def norm_back(values, gain_vector, shift_vector, upstream):
    unused, pullback = jax.vjp(layer_norm, values, gain_vector, shift_vector)
    return pullback(upstream)


def gelu_back(before, upstream):
    unused, pullback = jax.vjp(jax.nn.gelu, before)
    return pullback(upstream)[0]


def product(former, latter):
    return jnp.dot(former, latter, preferred_element_type=jnp.float32)


def product_tn(former, latter):
    return lax.dot_general(
        former, latter, (((0,), (0,)), ((), ())), preferred_element_type=jnp.float32
    )


def product_nt(former, latter):
    return lax.dot_general(
        former, latter, (((1,), (1,)), ((), ())), preferred_element_type=jnp.float32
    )


def lowered(values):
    return values.astype(jnp.bfloat16)


def round_up(count, unit):
    return -(-count // unit) * unit


def thirds(values):
    high = lowered(values)
    rest = values - high.astype(jnp.float32)
    middle = lowered(rest)
    return [high, middle, lowered(rest - middle.astype(jnp.float32))]


def attend_kernel(start_ref, query_ref, key_ref, value_ref, out_ref):
    rows, keys = query_ref.shape[0], key_ref.shape[0]
    half = query_ref.shape[1] // 2
    query_pos = start_ref[0] + lax.broadcasted_iota(jnp.int32, (rows, keys), 0)
    allowed = lax.broadcasted_iota(jnp.int32, (rows, keys), 1) <= query_pos
    for part in range(2):
        cols = slice(part * half, part * half + half)
        scores = product_nt(query_ref[:, cols], key_ref[:, cols]) * half**-0.5
        scores = jnp.where(allowed, scores, NEG_FILL)
        weights = jnp.exp(scores - jnp.max(scores, 1, keepdims=True))
        weights = weights / jnp.sum(weights, 1, keepdims=True)
        out_ref[:, cols] = lowered(product(lowered(weights), value_ref[:, cols]))


def attend(start, queries, keys, values):
    rows, features = queries.shape
    width = 2 * features // HEADS
    own = pl.BlockSpec((rows, width), lambda i, s: (0, i))
    whole = pl.BlockSpec((keys.shape[0], width), lambda i, s: (0, i))
    return pl.pallas_call(
        attend_kernel,
        grid_spec=pltpu.PrefetchScalarGridSpec(
            num_scalar_prefetch=1,
            grid=(features // width,),
            in_specs=[own, whole, whole],
            out_specs=own,
        ),
        out_shape=jax.ShapeDtypeStruct((rows, features), jnp.bfloat16),
        compiler_params=pltpu.CompilerParams(vmem_limit_bytes=VMEM_BYTES),
        cost_estimate=pl.CostEstimate(
            flops=4 * rows * keys.shape[0] * features,
            bytes_accessed=4 * (rows + keys.shape[0]) * features,
            transcendentals=rows * keys.shape[0] * HEADS,
        ),
        name="attend",
    )(start, queries, keys, values)


def attend_back_kernel(
    start_ref, query_ref, key_ref, value_ref, up_ref, query_grad_ref, key_grad_ref, value_grad_ref
):
    rows, keys = query_ref.shape[0], key_ref.shape[0]
    half = query_ref.shape[1] // 2
    scale = half**-0.5
    query_pos = start_ref[0] + lax.broadcasted_iota(jnp.int32, (keys, rows), 1)
    allowed = lax.broadcasted_iota(jnp.int32, (keys, rows), 0) <= query_pos
    for part in range(2):
        cols = slice(part * half, part * half + half)
        query, key, value, up = (
            ref[:, cols] for ref in (query_ref, key_ref, value_ref, up_ref)
        )
        scores = jnp.where(allowed, product_nt(key, query) * scale, NEG_FILL)
        probs = jnp.exp(scores - jnp.max(scores, 0, keepdims=True))
        probs = probs / jnp.sum(probs, 0, keepdims=True)
        prob_grad = product_nt(value, up)
        delta = jnp.sum(probs * prob_grad, 0, keepdims=True)
        score_grad = lowered(probs * (prob_grad - delta))
        value_grad_ref[:, cols] = lowered(product(lowered(probs), up))
        key_grad_ref[:, cols] = lowered(product(score_grad, query) * scale)
        query_grad_ref[:, cols] = lowered(product_tn(score_grad, key) * scale)


def attend_back(start, queries, keys, values, upstream):
    rows, features = queries.shape
    count = keys.shape[0]
    width = 2 * features // HEADS
    own = pl.BlockSpec((rows, width), lambda i, s: (0, i))
    whole = pl.BlockSpec((count, width), lambda i, s: (0, i))
    return pl.pallas_call(
        attend_back_kernel,
        grid_spec=pltpu.PrefetchScalarGridSpec(
            num_scalar_prefetch=1,
            grid=(features // width,),
            in_specs=[own, whole, whole, own],
            out_specs=[own, whole, whole],
        ),
        out_shape=[
            jax.ShapeDtypeStruct((rows, features), jnp.bfloat16),
            jax.ShapeDtypeStruct((count, features), jnp.bfloat16),
            jax.ShapeDtypeStruct((count, features), jnp.bfloat16),
        ],
        compiler_params=pltpu.CompilerParams(vmem_limit_bytes=VMEM_BYTES),
        cost_estimate=pl.CostEstimate(
            flops=10 * rows * count * features,
            bytes_accessed=6 * (rows + count) * features,
            transcendentals=rows * count * HEADS,
        ),
        name="attend_back",
    )(start, queries, keys, values, upstream)


def pick_kernel(by_slot, index_ref, rows_ref, out_ref):
    count = rows_ref.shape[0]
    total = jnp.zeros(out_ref.shape, jnp.float32)
    base = pl.program_id(0) * BLOCK
    for at in range(0, count, BLOCK):
        if by_slot:
            place = base + lax.broadcasted_iota(jnp.int32, (BLOCK, BLOCK), 0)
            hit = index_ref[:, at : at + BLOCK] == place
        else:
            place = at + lax.broadcasted_iota(jnp.int32, (BLOCK, BLOCK), 1)
            hit = index_ref[...] == place
        onehot = lowered(jnp.where(hit, 1.0, 0.0))
        total = total + product(onehot, rows_ref[at : at + BLOCK, :])
    out_ref[...] = total.astype(out_ref.dtype)


def pick_rows(index, rows, out_count, by_slot, kind):
    count, width = rows.shape
    if by_slot:
        index = index.reshape(1, -1)
        index_spec = pl.BlockSpec(index.shape, lambda i: (0, 0))
    else:
        index = index.reshape(-1, 1)
        index_spec = pl.BlockSpec((BLOCK, 1), lambda i: (i, 0))
    return pl.pallas_call(
        functools.partial(pick_kernel, by_slot),
        grid=(out_count // BLOCK,),
        in_specs=[index_spec, pl.BlockSpec(rows.shape, lambda i: (0, 0), **ONCE)],
        out_specs=pl.BlockSpec((BLOCK, width), lambda i: (i, 0)),
        out_shape=jax.ShapeDtypeStruct((out_count, width), kind),
        compiler_params=pltpu.CompilerParams(vmem_limit_bytes=VMEM_BYTES),
        cost_estimate=pl.CostEstimate(
            flops=2 * out_count * count * max(width, 256),
            bytes_accessed=rows.size * 2 + out_count * width * 4,
            transcendentals=0,
        ),
        name="pick_rows",
    )(index, rows)


def band_kernel(chunk, per, words, sum_column, span_ref, rows_ref, table_ref, stat_ref, out_ref, mix_ref):
    step_id = pl.program_id(0)
    count, width = mix_ref.shape
    chunk_count = table_ref.shape[0] // chunk
    group_count = chunk_count // per
    active = (step_id >= span_ref[0]) & (step_id < span_ref[1])

    def put_stats(top, total):
        lane = lax.broadcasted_iota(jnp.int32, (count, 128), 1)
        both = jnp.where(lane == 0, top, jnp.where(lane == 1, total, 0.0))
        stat_ref[...] = both.T[:8, :]

    def logits_at(at, rows):
        return product_nt(rows, table_ref[pl.ds(at, chunk), :])

    def beyond(at, shape):
        return at + lax.broadcasted_iota(jnp.int32, shape, 1) >= words

    def run(rows, top):
        mix_ref[...] = jnp.zeros(mix_ref.shape, jnp.float32)

        def visit(group, total):
            for inner in range(per):
                at = (group * per + inner) * chunk
                checked = isinstance(at, int) and at + chunk > words
                if not isinstance(at, int):
                    at = pl.multiple_of(at, chunk)
                weights = jnp.exp(logits_at(at, rows) - top)
                if checked:
                    weights = jnp.where(beyond(at, weights.shape), 0.0, weights)
                if sum_column is None:
                    for lane in range(0, chunk, 128):
                        total = total + weights[:, lane : lane + 128]
                mix_ref[...] += product(lowered(weights), table_ref[pl.ds(at, chunk), :])
            return total

        lanes = jnp.zeros((count, 128), jnp.float32)
        lanes = visit(0, lanes) if group_count == 1 else lax.fori_loop(0, group_count, visit, lanes)
        if sum_column is None:
            return jnp.sum(lanes, 1, keepdims=True)
        return mix_ref[:, sum_column : sum_column + 1]

    @pl.when(active)
    def _():
        rows = rows_ref[...]
        first = product_nt(rows, table_ref[pl.ds(0, 128), :])
        top = jnp.max(first, 1, keepdims=True)
        total = run(rows, top)
        put_stats(top, total)

        @pl.when(jnp.logical_not(jnp.max(jnp.where(total < SAFE, 0.0, 1.0)) < 0.5))
        def _():
            def largest(index, top):
                at = pl.multiple_of(index * chunk, chunk)
                logits = logits_at(at, rows)
                if sum_column is None:
                    logits = jnp.where(beyond(at, logits.shape), NEG_FILL, logits)
                return jnp.maximum(top, jnp.max(logits, 1, keepdims=True))

            exact = lax.fori_loop(0, chunk_count, largest, jnp.full((count, 1), NEG_FILL))
            put_stats(exact, run(rows, exact))

        out_ref[...] = lowered(mix_ref[...])

    @pl.when(jnp.logical_not(active))
    def _():
        put_stats(jnp.full((count, 1), NEG_FILL), jnp.zeros((count, 1), jnp.float32))
        out_ref[...] = jnp.zeros(out_ref.shape, jnp.bfloat16)


def band_forward(span, rows, table, words, chunk, sum_column, share):
    count, width = rows.shape[0], table.shape[1]
    chunk_count = table.shape[0] // chunk
    per = chunk_count if chunk_count <= 4 else 4
    assert chunk_count % per == 0 and words >= 128
    return pl.pallas_call(
        functools.partial(band_kernel, chunk, per, words, sum_column),
        grid_spec=pltpu.PrefetchScalarGridSpec(
            num_scalar_prefetch=1,
            grid=(count // BLOCK,),
            in_specs=[
                pl.BlockSpec((BLOCK, width), lambda i, s: (i, 0)),
                pl.BlockSpec(table.shape, lambda i, s: (0, 0), **ONCE),
            ],
            out_specs=[
                pl.BlockSpec((8, BLOCK), lambda i, s: (0, i)),
                pl.BlockSpec((BLOCK, width), lambda i, s: (i, 0)),
            ],
            scratch_shapes=[pltpu.VMEM((BLOCK, width), jnp.float32)],
        ),
        out_shape=[
            jax.ShapeDtypeStruct((8, count), jnp.float32),
            jax.ShapeDtypeStruct((count, width), jnp.bfloat16),
        ],
        compiler_params=pltpu.CompilerParams(vmem_limit_bytes=VMEM_BYTES),
        cost_estimate=pl.CostEstimate(
            flops=int(share * 4 * count * table.shape[0] * max(width, 256)),
            bytes_accessed=table.size * 2 + count * width * 6,
            transcendentals=int(share * count * table.shape[0]),
        ),
        name="band_forward",
    )(span, rows, table)


def head_grad_kernel(chunk, lists, base_ref, table_ref, *refs):
    out_ref, sum_ref = refs[2 * lists :]
    words = table_ref.shape[0]
    base = base_ref[0] + pl.program_id(0) * words
    sum_ref[...] = jnp.zeros(sum_ref.shape, jnp.float32)
    for rows_ref, fact_ref in zip(refs[0 : 2 * lists : 2], refs[1 : 2 * lists : 2]):
        piece = min(rows_ref.shape[0], 1024)

        def visit(step, unused, rows_ref=rows_ref, fact_ref=fact_ref, piece=piece):
            at = pl.multiple_of(step * piece, piece)
            rows = rows_ref[pl.ds(at, piece), :]
            weight = fact_ref[0:1, pl.ds(at, piece)]
            total = fact_ref[1:2, pl.ds(at, piece)]
            ids = fact_ref[2:3, pl.ds(at, piece)].astype(jnp.int32)
            for start in range(0, words, chunk):
                probs = jnp.exp(product_nt(table_ref[start : start + chunk, :], rows) - total)
                word = base + start + lax.broadcasted_iota(jnp.int32, (chunk, 1), 0)
                grads = weight * (jnp.where(word == ids, 1.0, 0.0) - probs)
                sum_ref[start : start + chunk, :] += product(lowered(grads), rows)
            return unused

        lax.fori_loop(0, rows_ref.shape[0] // piece, visit, 0)
    out_ref[...] = lowered(sum_ref[...])


def head_grad(table, part, part_words, first_word, lists):
    width = table.shape[1]
    word_block = math.gcd(part_words, 640)
    steps = part_words // word_block
    chunk = word_block // 2 if word_block % 32 == 0 else word_block
    specs = []
    for rows, facts in lists:
        specs.append(pl.BlockSpec(rows.shape, lambda i, s: (0, 0), **ONCE))
        specs.append(pl.BlockSpec(facts.shape, lambda i, s: (0, 0), **ONCE))
    count = sum(rows.shape[0] for rows, facts in lists)
    scalars = jnp.stack([first_word + part * part_words, part * steps]).astype(jnp.int32)
    return pl.pallas_call(
        functools.partial(head_grad_kernel, chunk, len(lists)),
        grid_spec=pltpu.PrefetchScalarGridSpec(
            num_scalar_prefetch=1,
            grid=(steps,),
            in_specs=[pl.BlockSpec((word_block, width), lambda i, s: (s[1] + i, 0))] + specs,
            out_specs=pl.BlockSpec((word_block, width), lambda i, s: (i, 0)),
            scratch_shapes=[pltpu.VMEM((word_block, width), jnp.float32)],
        ),
        out_shape=jax.ShapeDtypeStruct((part_words, width), jnp.bfloat16),
        compiler_params=pltpu.CompilerParams(vmem_limit_bytes=VMEM_BYTES),
        cost_estimate=pl.CostEstimate(
            flops=4 * count * part_words * width,
            bytes_accessed=(count + part_words) * width * 2,
            transcendentals=count * part_words,
        ),
        name="head_grad",
    )(scalars, table, *[value for pair in lists for value in pair])


def band_grad_kernel(chunk, most, across, plan_ref, table_ref, rows_ref, fact_ref, out_ref, sum_ref):
    words = table_ref.shape[0]
    step_id = pl.program_id(0)
    base = plan_ref[most + 1] + step_id * words
    sum_ref[...] = jnp.zeros(sum_ref.shape, jnp.float32)

    def block_at(position):
        return pl.multiple_of(plan_ref[position] * BLOCK, BLOCK)

    def spread(starts):
        rows = [rows_ref[pl.ds(start, BLOCK), :] for start in starts]
        facts = [fact_ref[:, pl.ds(start, BLOCK)] for start in starts]
        rows = rows[0] if len(rows) == 1 else jnp.concatenate(rows, 0)
        facts = facts[0] if len(facts) == 1 else jnp.concatenate(facts, 1)
        weight, total = facts[0:1], facts[1:2]
        for start in range(0, words, chunk):
            probs = jnp.exp(product_nt(table_ref[start : start + chunk, :], rows) - total)
            sum_ref[start : start + chunk, :] -= product(lowered(weight * probs), rows)

    count = plan_ref[0]

    def pair(step, unused):
        spread([block_at(1 + 2 * step), block_at(2 + 2 * step)])
        return unused

    lax.fori_loop(0, count // 2, pair, 0)

    @pl.when(count % 2 == 1)
    def _():
        spread([block_at(count)])

    line = most + 2 + step_id * (most + 1)

    def hits(step, unused):
        at = block_at(line + 1 + step)
        rows = rows_ref[pl.ds(at, BLOCK), :]
        weight = fact_ref[0:1, pl.ds(at, BLOCK)]
        ids = fact_ref[2:3, pl.ds(at, BLOCK)].astype(jnp.int32)
        for start in range(0, words, chunk):
            word = base + start + lax.broadcasted_iota(jnp.int32, (chunk, 1), 0)
            chosen = lowered(jnp.where(word == ids, weight, 0.0))
            sum_ref[start : start + chunk, :] += product(chosen, rows)
        return unused

    lax.fori_loop(0, plan_ref[line], hits, 0)
    if across:
        out_ref[...] = sum_ref[...].T[: out_ref.shape[0], :].astype(out_ref.dtype)
    else:
        out_ref[...] = sum_ref[...].astype(out_ref.dtype)


def listed(flags):
    size = flags.shape[-1]
    order = jnp.cumsum(flags.astype(jnp.int32), -1)
    chosen = (order[..., None, :] == jnp.arange(1, size + 1)[:, None]) & flags[..., None, :]
    places = jnp.sum(jnp.where(chosen, jnp.arange(size), 0), -1)
    return jnp.concatenate([order[..., -1:], places], -1).astype(jnp.int32)


def band_grad(
    table, rows, facts, active, lowest, highest, part, part_words, first_word, chunk, result, across
):
    count, full = rows.shape[0], table.shape[1]
    word_block = chunk
    steps = part_words // word_block
    most = count // BLOCK
    first = first_word + part * part_words
    low = first + jnp.arange(steps, dtype=jnp.int32)[:, None] * word_block
    step_hits = active[None, :] & (lowest[None, :] < low + word_block) & (highest[None, :] >= low)
    plan = jnp.concatenate(
        [
            listed(active),
            first.reshape(1).astype(jnp.int32),
            listed(step_hits).reshape(-1),
            (part * steps).reshape(1).astype(jnp.int32),
        ]
    )
    last = plan.shape[0] - 1
    return pl.pallas_call(
        functools.partial(band_grad_kernel, chunk // 2 if chunk > 832 else chunk, most, across),
        grid_spec=pltpu.PrefetchScalarGridSpec(
            num_scalar_prefetch=1,
            grid=(steps,),
            in_specs=[
                pl.BlockSpec((word_block, full), lambda i, s: (s[last] + i, 0)),
                pl.BlockSpec((count, full), lambda i, s: (0, 0), **ONCE),
                pl.BlockSpec(facts.shape, lambda i, s: (0, 0), **ONCE),
            ],
            out_specs=(
                pl.BlockSpec((result.shape[0], word_block), lambda i, s: (0, i))
                if across
                else pl.BlockSpec((word_block, full), lambda i, s: (i, 0))
            ),
            scratch_shapes=[pltpu.VMEM((word_block, full), jnp.float32)],
        ),
        out_shape=result,
        compiler_params=pltpu.CompilerParams(vmem_limit_bytes=VMEM_BYTES),
        cost_estimate=pl.CostEstimate(
            flops=2 * count * part_words * 256,
            bytes_accessed=count * full * 2 + part_words * full * 4,
            transcendentals=count * part_words // 2,
        ),
        name="band_grad",
    )(plan, table, rows, facts)


def settle_kernel(
    member_ref,
    everyone_ref,
    fact_ref,
    head_mix_ref,
    middle_mix_ref,
    tail_mix_ref,
    head_hit_ref,
    middle_hit_ref,
    tail_hit_ref,
    term_ref,
    line_ref,
    slot_ref,
):
    step = pl.program_id(0)
    devices, _, slots = everyone_ref.shape
    tail_width = 64
    here = pl.ds(pl.multiple_of(step * BLOCK, BLOCK), BLOCK)

    def merged(read):
        lines = [read(device) for device in range(devices)]
        top = functools.reduce(jnp.maximum, [line[0] for line in lines])
        return top, sum(line[1] * jnp.exp(line[0] - top) for line in lines)

    head_top, head_sum = merged(
        lambda d: (everyone_ref[d, 0:1, here], everyone_ref[d, 1:2, here])
    )
    target = sum(everyone_ref[d, 2:3, here] for d in range(devices))
    slot_top, slot_sum = merged(lambda d: (everyone_ref[d, 3:4, :], everyone_ref[d, 4:5, :]))
    used = slot_sum > 0.0
    slot_total = jnp.where(used, slot_top + jnp.log(jnp.where(used, slot_sum, 1.0)), 0.0)
    member = member_ref[0]
    own_slot_top = jnp.where(used, everyone_ref[member, 3:4, :], 0.0)
    own_head_top = everyone_ref[member, 0:1, here]

    facts = fact_ref[...]
    slot, share, cotangent, first_cluster, second_cluster, band, word = (
        facts[index : index + 1] for index in range(7)
    )

    def as_columns(lines):
        square = jnp.concatenate(
            lines + [jnp.zeros((128 - len(lines), BLOCK), jnp.float32)], 0
        )
        return square.T

    def three(line):
        return [part.astype(jnp.float32) for part in thirds(line)]

    slot_column = as_columns([slot])[:, 0:1].astype(jnp.int32)
    hot = lowered(
        jnp.where(lax.broadcasted_iota(jnp.int32, (BLOCK, slots), 1) == slot_column, 1.0, 0.0)
    )
    lines = three(slot_total) + three(own_slot_top) + [jnp.zeros((10, slots), jnp.float32)]
    on_tokens = product_nt(lowered(jnp.concatenate(lines, 0)), hot)
    band_total = on_tokens[0:1] + on_tokens[1:2] + on_tokens[2:3]
    own_band_top = on_tokens[3:4] + on_tokens[4:5] + on_tokens[5:6]

    cluster_top = jnp.maximum(head_top, jnp.maximum(first_cluster, second_cluster))
    head_total = cluster_top + jnp.log(
        head_sum * jnp.exp(head_top - cluster_top)
        + jnp.exp(first_cluster - cluster_top)
        + jnp.exp(second_cluster - cluster_top)
    )
    in_head = band < 0.5
    cluster = jnp.where(band < 1.5, first_cluster, second_cluster)
    model_logp = target - head_total + jnp.where(in_head, 0.0, cluster - band_total)
    ratio = 0.25 * share * jnp.exp(-model_logp)
    weight = cotangent * 0.75 / (0.75 + ratio)
    head_scale = weight * jnp.exp(own_head_top - head_total)
    band_scale = weight * jnp.where(in_head, 0.0, jnp.exp(own_band_top - band_total))
    columns = as_columns([weight, head_scale, band_scale])
    weight_column, head_column, band_column = (columns[:, i : i + 1] for i in range(3))
    width = head_mix_ref.shape[1]
    term_ref[:, :width] = lowered(
        weight_column * head_hit_ref[...].astype(jnp.float32)
        - head_column * head_mix_ref[...].astype(jnp.float32)
    )
    narrow = tail_mix_ref.shape[1]
    kept = lax.broadcasted_iota(jnp.int32, (BLOCK, narrow), 1) < tail_width

    def widened(values):
        values = jnp.where(kept, values, 0.0)
        more = middle_mix_ref.shape[1] - narrow
        return jnp.concatenate([values, jnp.zeros((BLOCK, more), jnp.float32)], 1)

    band_mix = product(hot, middle_mix_ref[...]) + widened(product(hot, tail_mix_ref[...]))
    band_hit = middle_hit_ref[...].astype(jnp.float32) + widened(
        tail_hit_ref[...].astype(jnp.float32)
    )
    term_ref[:, width:] = lowered(weight_column * band_hit - band_column * band_mix)
    line_ref[...] = jnp.concatenate(
        [
            model_logp + jnp.log(0.75 + ratio),
            weight,
            head_total,
            word,
            jnp.zeros((4, BLOCK), jnp.float32),
        ],
        0,
    )

    @pl.when(step == 0)
    def _():
        slot_ref[...] = jnp.concatenate(
            [jnp.zeros((8, slots), jnp.float32), slot_total, jnp.zeros((7, slots), jnp.float32)], 0
        )

    sent = three(weight) + three(word) + [jnp.zeros((10, BLOCK), jnp.float32)]
    slot_ref[0:8, :] += product(lowered(jnp.concatenate(sent, 0)), hot)[0:8]


def settle(member, everyone, facts, head_mix, middle_mix, tail_mix, hits):
    count, width = head_mix.shape
    slots = middle_mix.shape[0]
    full = width + middle_mix.shape[1]

    def tokens(values):
        return pl.BlockSpec((BLOCK, values.shape[1]), lambda i, s: (i, 0))

    def whole(values):
        return pl.BlockSpec(values.shape, lambda i, s: (0,) * values.ndim, **ONCE)

    lines = pl.BlockSpec((8, BLOCK), lambda i, s: (0, i))
    return pl.pallas_call(
        settle_kernel,
        grid_spec=pltpu.PrefetchScalarGridSpec(
            num_scalar_prefetch=1,
            grid=(count // BLOCK,),
            in_specs=[whole(everyone), lines, tokens(head_mix), whole(middle_mix), whole(tail_mix)]
            + [tokens(hit) for hit in hits],
            out_specs=[
                pl.BlockSpec((BLOCK, full), lambda i, s: (i, 0)),
                lines,
                pl.BlockSpec((16, slots), lambda i, s: (0, 0)),
            ],
        ),
        out_shape=[
            jax.ShapeDtypeStruct((count, full), jnp.bfloat16),
            jax.ShapeDtypeStruct((8, count), jnp.float32),
            jax.ShapeDtypeStruct((16, slots), jnp.float32),
        ],
        compiler_params=pltpu.CompilerParams(vmem_limit_bytes=VMEM_BYTES),
        cost_estimate=pl.CostEstimate(
            flops=2 * count * slots * 1024,
            bytes_accessed=count * width * 12 + slots * full,
            transcendentals=slots * 64,
        ),
        name="settle",
    )(member.reshape(1).astype(jnp.int32), everyone, facts, head_mix, middle_mix, tail_mix, *hits)


def line_turns(value):
    size = lax.axis_size("seq")
    return [value] + [
        lax.ppermute(value, "seq", [(d, (d - k) % size) for d in range(size)])
        for k in range(1, size)
    ]


def line_step(before, behind, step):
    size = lax.axis_size("seq")
    return (
        lax.ppermute(before, "seq", [(d, d + 1) for d in range(step - 1, size - 1)]),
        lax.ppermute(behind, "seq", [(d, d - 1) for d in range(1, size - step + 1)]),
    )


def line_steps(value):
    found = [(value, value)]

    def advance(*others):
        step = len(found)
        if step == lax.axis_size("seq"):
            return others
        moved = line_step(*found[-1], step)
        moved, others = lax.optimization_barrier((moved, others))
        found.append(moved)
        return others

    return found, advance


def line_ordered(found):
    size, place = lax.axis_size("seq"), lax.axis_index("seq")
    ordered = []
    for source in range(size):
        value = found[0][0]
        for step in range(1, size):
            if source + step < size:
                value = jnp.where(place == source + step, found[step][0], value)
            if source - step >= 0:
                value = jnp.where(place == source - step, found[step][1], value)
        ordered.append(value)
    return ordered


def earlier_joined(value):
    size, place = lax.axis_size("seq"), lax.axis_index("seq")
    joined = jnp.zeros((size,) + value.shape, value.dtype)
    for step in range(size - 1, -1, -1):
        piece = value
        if step:
            piece = lax.ppermute(value, "seq", [(d, d + step) for d in range(size - step)])
        joined = lax.dynamic_update_index_in_dim(joined, piece, jnp.maximum(place - step, 0), 0)
    return joined.reshape((-1,) + value.shape[1:])


def in_order(pieces):
    size, place = lax.axis_size("seq"), lax.axis_index("seq")
    joined = jnp.zeros((size,) + pieces[0].shape, pieces[0].dtype)
    for k, piece in enumerate(pieces):
        joined = lax.dynamic_update_index_in_dim(joined, piece, lax.rem(place + k, size), 0)
    return joined.reshape((-1,) + pieces[0].shape[1:])


def line_scatter(values, behind=True):
    size, place = lax.axis_size("seq"), lax.axis_index("seq")
    parts = values.reshape((size, -1) + values.shape[1:])

    def part(index):
        return lax.dynamic_index_in_dim(parts, lax.rem(index, size), 0, False)

    total = part(place).astype(jnp.float32)
    for k in range(1, size):
        pairs = [(d, (d - k) % size) for d in range(0 if behind else k, size)]
        total = total + lax.ppermute(part(place + size - k), "seq", pairs).astype(jnp.float32)
    return total


def turn_kernel(rows_ref, out_ref):
    out_ref[...] = rows_ref[...].astype(jnp.float32).T.astype(out_ref.dtype)


def turned(rows, kind):
    return pl.pallas_call(
        turn_kernel, out_shape=jax.ShapeDtypeStruct(rows.shape[::-1], kind), name="turned"
    )(rows)


def word_pad(rows, biggest, splits):
    chunk = min(biggest, round_up(rows, 128))
    chunks = -(-rows // chunk)
    if chunks > 4:
        chunks = round_up(chunks, 4)
    return chunk, chunks * chunk


def on_device(
    inputs,
    targets,
    neighbours,
    neighbour_scores,
    loglik_grad,
    first_gain,
    first_shift,
    query_weight,
    query_bias,
    key_weight,
    value_weight,
    value_bias,
    out_weight,
    out_bias,
    second_gain,
    second_shift,
    inner_weight,
    inner_bias,
    outer_weight,
    outer_bias,
    final_gain,
    final_shift,
    head_table,
    cluster_weight,
    middle_map,
    middle_table,
    tail_map,
    tail_table,
):
    nb = lax.axis_size("batch")
    nz = lax.axis_size("seq")
    member = lax.axis_index("batch")
    place = lax.axis_index("seq")
    tokens = inputs[0]
    own_ids = targets[0]
    token_count, feature_count = tokens.shape
    group_count = token_count * nb
    slot_count = group_count + BLOCK
    query_start = (place * token_count).reshape(1)

    normed_low = lowered(layer_norm(tokens, first_gain, first_shift))
    normed_all = earlier_joined(normed_low)
    top_score = jnp.max(neighbour_scores[0], -1, keepdims=True)
    exponent = jnp.exp(neighbour_scores[0] - top_score)
    knn_prob = jnp.sum(jnp.where(neighbours[0] == 0, exponent, 0.0), -1) / jnp.sum(exponent, -1)
    early = jnp.stack([own_ids.astype(jnp.float32), knn_prob, loglik_grad[0]])
    early = lax.all_gather(early, "batch", axis=1, tiled=True)
    all_ids = early[0].astype(jnp.int32)
    all_knn, all_up = early[1], early[2]
    in_head = all_ids < HEAD_WORDS
    in_middle = (all_ids >= HEAD_WORDS) & (all_ids < HEAD_WORDS + MID_WORDS)
    in_tail = all_ids >= HEAD_WORDS + MID_WORDS
    order = jnp.arange(group_count, dtype=jnp.int32)
    ahead = (all_ids[None, :] < all_ids[:, None]) | (
        (all_ids[None, :] == all_ids[:, None]) & (order[None, :] < order[:, None])
    )
    rank = jnp.sum(ahead.astype(jnp.int32), -1)
    head_size = jnp.sum(in_head.astype(jnp.int32))
    middle_size = jnp.sum(in_middle.astype(jnp.int32))
    tail_size = group_count - head_size - middle_size
    middle_blocks = (middle_size + BLOCK - 1) // BLOCK
    tail_blocks = (tail_size + BLOCK - 1) // BLOCK
    slot = jnp.where(
        in_head,
        -1,
        rank - head_size + jnp.where(in_tail, middle_blocks * BLOCK - middle_size, 0),
    )
    zero_span = jnp.zeros((1,), jnp.int32)
    head_span = jnp.array([0, group_count // BLOCK], jnp.int32)
    middle_span = jnp.stack([0 * middle_blocks, middle_blocks]).astype(jnp.int32)
    tail_span = jnp.stack([middle_blocks, middle_blocks + tail_blocks]).astype(jnp.int32)
    slot_order = jnp.arange(slot_count, dtype=jnp.int32)
    slot_middle = slot_order < middle_size
    slot_tail = (slot_order >= middle_blocks * BLOCK) & (
        slot_order < middle_blocks * BLOCK + tail_size
    )
    slot_used = slot_middle | slot_tail
    band_id = all_ids - jnp.where(in_tail, HEAD_WORDS + MID_WORDS, HEAD_WORDS)

    tables = (head_table, middle_table, tail_table)
    sizes = tuple(table.shape[0] for table in tables)
    head_chunk, head_padded = word_pad(sizes[0], 1280, nz)
    middle_chunk, middle_padded = word_pad(sizes[1], 1280, nz)
    tail_chunk, tail_padded = word_pad(sizes[2], 1664, nz)
    tail_width = tail_table.shape[1]
    head_pad = jnp.pad(head_table, ((0, head_padded - sizes[0]), (0, 0)))
    middle_pad = jnp.pad(middle_table, ((0, middle_padded - sizes[1]), (0, 0)))
    tail_word = jnp.arange(tail_padded, dtype=jnp.int32)
    tail_bias = jnp.where(tail_word < jnp.minimum(TAIL_WORDS - member * sizes[2], sizes[2]), 0.0, NEG_FILL)
    tail_pad = jnp.concatenate(
        [
            jnp.pad(tail_table.T, ((0, 0), (0, tail_padded - sizes[2]))),
            jnp.ones((1, tail_padded), jnp.bfloat16),
            lowered(tail_bias)[None, :],
            jnp.zeros((126 - tail_width, tail_padded), jnp.bfloat16),
        ],
        0,
    ).T
    locals_ = (
        all_ids - member * sizes[0],
        all_ids - HEAD_WORDS - member * sizes[1],
        all_ids - HEAD_WORDS - MID_WORDS - member * sizes[2],
    )
    owned = tuple(
        inside & (local >= 0) & (local < size)
        for inside, local, size in zip((in_head, in_middle, in_tail), locals_, sizes)
    )
    hit_rows = tuple(
        jnp.where(
            own[:, None],
            jnp.take(table, jnp.clip(local, 0, size - 1), axis=0, mode="clip"),
            jnp.bfloat16(0),
        )
        for own, table, local, size in zip(owned, (head_pad, middle_pad, tail_pad), locals_, sizes)
    )

    queries = lowered(product(normed_low, query_weight) + query_bias)
    normed_all, head_pad, middle_pad, tail_pad, slot = lax.optimization_barrier(
        (normed_all, head_pad, middle_pad, tail_pad, slot)
    )
    key_rows = lowered(product(normed_all, key_weight))
    value_rows = lowered(product(normed_all, value_weight) + value_bias)
    attended_low = attend(query_start, queries, key_rows, value_rows)
    mixed = tokens + product(attended_low, out_weight) + out_bias
    second_low = lowered(layer_norm(mixed, second_gain, second_shift))
    before = product(second_low, inner_weight) + inner_bias
    hidden_low = lowered(jax.nn.gelu(before))
    final = mixed + product(hidden_low, outer_weight) + outer_bias
    state_low = lowered(layer_norm(final, final_gain, final_shift))
    all_states = lax.all_gather(state_low, "batch", axis=0, tiled=True)
    split = 2 * nz * group_count * feature_count <= 24 << 20
    if split:
        block_states = lax.all_gather(state_low, "seq", axis=0, tiled=True)
    all_states, tail_hits, early = lax.optimization_barrier((all_states, hit_rows[2], early))
    hit_rows = hit_rows[:2] + (tail_hits,)

    middle_width = middle_map.shape[1]
    maps = jnp.pad(jnp.concatenate([middle_map, tail_map], 1), ((0, 0), (0, 128 - tail_width)))
    one_column = (jnp.arange(middle_width + 128) == middle_width + tail_width + 1).astype(jnp.float32)
    band_low = lowered(product(all_states, maps) + one_column)
    middle_low, tail_low = band_low[:, :middle_width], band_low[:, middle_width:]
    cluster_lines = product_nt(
        jnp.pad(cluster_weight.T, ((0, 6), (0, 0))), all_states
    )
    slot_full = pick_rows(slot, band_low, slot_count, True, jnp.bfloat16)
    first_tail = middle_blocks * BLOCK
    in_tail_slot = slot_order >= first_tail
    slot_low = jnp.where(
        in_tail_slot[:, None],
        jnp.pad(slot_full[:, middle_width:], ((0, 0), (0, middle_width - 128))),
        slot_full[:, :middle_width],
    )
    if split:
        piece = slot_count // nb
        slot_piece = lax.dynamic_slice_in_dim(slot_low, member * piece, piece, 0)
        other_slots = jnp.concatenate(line_turns(slot_piece)[1:], 0)
    head_stats, head_mix = band_forward(
        head_span, all_states, head_pad, sizes[0], head_chunk, None, 1.0
    )
    if split:
        slot_low, block_states, hit_rows, head_stats = lax.optimization_barrier(
            (slot_low, block_states, hit_rows, head_stats)
        )
        other_states = lax.dynamic_slice_in_dim(
            jnp.concatenate([block_states, block_states], 0),
            (place + 1) * token_count,
            (nz - 1) * token_count,
            0,
        )
        other_states = lax.all_gather(other_states, "batch", axis=0, tiled=True)
    tail_stats, tail_mix = band_forward(
        tail_span, slot_low, tail_pad, tail_padded, tail_chunk, tail_width, 0.5
    )
    middle_stats, middle_mix = band_forward(
        middle_span, slot_low, middle_pad, sizes[1], middle_chunk, None, 0.25
    )
    inner_lane = jnp.arange(128) < tail_width
    target_part = (
        jnp.sum(hit_rows[0].astype(jnp.float32) * all_states.astype(jnp.float32), -1)
        + jnp.sum(hit_rows[1].astype(jnp.float32) * middle_low.astype(jnp.float32), -1)
        + jnp.sum(
            jnp.where(inner_lane, hit_rows[2].astype(jnp.float32), 0.0)
            * tail_low.astype(jnp.float32),
            -1,
        )
    )
    slot_stats = jnp.where(in_tail_slot[None, :], tail_stats[:2], middle_stats[:2])
    extra = ((0, 0), (0, BLOCK))
    stats = jnp.concatenate(
        [
            jnp.pad(jnp.concatenate([head_stats[:2], target_part[None]], 0), extra),
            slot_stats,
            jnp.zeros((3, slot_count), jnp.float32),
        ],
        0,
    )
    if split:
        stats, other_states, other_slots = lax.optimization_barrier(
            (stats, other_states, other_slots)
        )
        other_slots = lax.all_gather(other_slots, "batch", axis=0, tiled=True)
    everyone = lax.all_gather(stats, "batch")

    token_facts = jnp.concatenate(
        [
            slot.astype(jnp.float32)[None],
            early[1:3],
            cluster_lines[:2],
            jnp.where(in_head, 0.0, jnp.where(in_middle, 1.0, 2.0))[None],
            early[0:1],
            jnp.zeros((1, group_count), jnp.float32),
        ],
        0,
    )
    terms, lines, slot_lines = settle(
        member, everyone, token_facts, head_mix, middle_mix, tail_mix, hit_rows
    )
    own_terms = lax.psum_scatter(terms, "batch", scatter_dimension=0, tiled=True).astype(jnp.float32)

    def own_part(values):
        return lax.dynamic_slice_in_dim(values, member * token_count, token_count, 0)

    loglik = own_part(lines[0])

    kind = jnp.where(slot_middle, 1.0, jnp.where(slot_tail, 2.0, 0.0))
    slot_facts = jnp.stack(
        [
            jnp.sum(slot_lines[0:3], 0),
            slot_lines[8],
            jnp.sum(slot_lines[3:6], 0),
            kind,
        ]
    )
    head_facts = jnp.concatenate([lines[1:4], jnp.zeros((1, group_count), jnp.float32)], 0)
    if split:
        other_slots = (
            other_slots.reshape(nb, nz - 1, piece, middle_width)
            .transpose(1, 0, 2, 3)
            .reshape(-1, middle_width)
        )
        rows_all = jnp.concatenate([slot_low, other_slots], 0)
        fact_pieces = line_turns(jnp.concatenate([slot_facts, head_facts], 1))
        facts = jnp.concatenate([value[:, :slot_count] for value in fact_pieces], 1)
        other_facts = (
            jnp.stack([value[:, slot_count:] for value in fact_pieces[1:]], 1)
            .reshape(4, nz - 1, nb, token_count)
            .transpose(0, 2, 1, 3)
            .reshape(4, -1)
        )
        lists = [(all_states, head_facts), (other_states, other_facts)]
        part, parts = place, nz
    else:
        rows_all, facts, lists = slot_low, slot_facts, [(all_states, head_facts)]
        part, parts = 0 * place, 1
    head_part = head_grad(head_pad, part, head_padded // parts, member * sizes[0], lists)
    block_facts = facts[2:4].reshape(2, -1, BLOCK)
    block_kind = jnp.max(block_facts[1], -1)
    filled = block_facts[1] > 0
    lowest = jnp.min(jnp.where(filled, block_facts[0], 1e9), -1).astype(jnp.int32)
    highest = jnp.max(jnp.where(filled, block_facts[0], -1e9), -1).astype(jnp.int32)
    facts = jnp.concatenate(
        [facts[:2], jnp.where(facts[3:4] > 0, facts[2:3], -1e9), jnp.zeros_like(facts[:1])], 0
    )
    def tail_gradient(part, parts):
        return band_grad(
            tail_pad,
            rows_all,
            facts,
            block_kind == 2,
            lowest,
            highest,
            part,
            tail_padded // parts,
            HEAD_WORDS + MID_WORDS + member * sizes[2],
            math.gcd(tail_padded // parts, tail_chunk),
            jax.ShapeDtypeStruct((tail_width, tail_padded // parts), jnp.bfloat16),
            True,
        )

    first_tail = tail_gradient(2 * part, 2 * parts)
    if split:
        head_found, head_advance = line_steps(head_part)
        first_tail, facts = head_advance(first_tail, facts)
        first_found, first_advance = line_steps(first_tail)
        second_tail = tail_gradient(2 * part + 1, 2 * parts)
        second_tail, own_terms = head_advance(second_tail, own_terms)
        second_tail, own_terms = first_advance(second_tail, own_terms)
        second_found, second_advance = line_steps(second_tail)
    else:
        second_tail = tail_gradient(2 * part + 1, 2 * parts)
        own_terms, first_tail, second_tail = lax.optimization_barrier(
            (own_terms, first_tail, second_tail)
        )

    own_middle = own_part(in_middle)
    own_tail = own_part(in_tail)
    own_lines = lax.dynamic_slice_in_dim(lines, member * token_count, token_count, 1)
    own_weights, own_total = own_lines[1], own_lines[2]
    own_clusters = product(state_low, cluster_weight)
    band_state = own_terms[:, feature_count:]
    middle_state = lowered(jnp.where(own_middle[:, None], band_state, 0.0))
    tail_state = lowered(jnp.where(own_tail[:, None], band_state[:, :tail_width], 0.0))
    cluster_hit = jnp.stack([own_middle, own_tail], -1).astype(jnp.float32)
    cluster_grad = own_weights[:, None] * (
        cluster_hit - jnp.exp(own_clusters - own_total[:, None])
    )
    state_grad = (
        own_terms[:, :feature_count]
        + product_nt(middle_state, middle_map)
        + product_nt(tail_state, tail_map)
        + product_nt(cluster_grad, cluster_weight.astype(jnp.float32))
    )
    middle_map_grad = product_tn(state_low, middle_state)
    tail_map_rows = product_tn(tail_state, state_low)
    cluster_rows = product_tn(cluster_grad, state_low.astype(jnp.float32))
    final_grad, final_gain_grad, final_shift_grad = norm_back(
        final, final_gain, final_shift, state_grad
    )
    final_low = lowered(final_grad)
    outer_weight_grad = product_tn(hidden_low, final_low)
    outer_bias_grad = jnp.sum(final_grad, 0)
    outer_part = lax.psum_scatter(
        lowered(outer_weight_grad), "batch", scatter_dimension=0, tiled=True
    )
    before_grad = lowered(gelu_back(before, product_nt(final_low, outer_weight)))
    inner_weight_grad = product_tn(second_low, before_grad)
    inner_bias_grad = jnp.sum(before_grad.astype(jnp.float32), 0)
    inner_part = lax.psum_scatter(
        lowered(inner_weight_grad), "batch", scatter_dimension=0, tiled=True
    )
    second_in_grad, second_gain_grad, second_shift_grad = norm_back(
        mixed, second_gain, second_shift, product_nt(before_grad, inner_weight)
    )
    mixed_grad = final_grad + second_in_grad
    mixed_low = lowered(mixed_grad)
    out_weight_grad = product_tn(attended_low, mixed_low)
    out_bias_grad = jnp.sum(mixed_grad, 0)
    attended_grad = lowered(product_nt(mixed_low, out_weight))
    if split:
        for unused in range(nz - 3):
            (attended_grad,) = head_advance(attended_grad)
        (attended_grad,) = second_advance(attended_grad)
    query_low, key_low, value_low = attend_back(
        query_start, queries, key_rows, value_rows, attended_grad
    )
    if split:
        query_low, key_low, value_low = first_advance(query_low, key_low, value_low)
        query_low, key_low, value_low = second_advance(query_low, key_low, value_low)
    query_weight_grad = product_tn(normed_low, query_low)
    key_weight_grad = product_tn(normed_all, key_low)
    value_weight_grad = product_tn(normed_all, value_low)
    query_bias_grad = jnp.sum(query_low.astype(jnp.float32), 0)
    value_bias_grad = jnp.sum(value_low.astype(jnp.float32), 0)
    spread = product_nt(key_low, key_weight) + product_nt(value_low, value_weight)
    query_spread = product_nt(query_low, query_weight)
    first_shift_grad = jnp.sum(spread, 0) + jnp.sum(query_spread, 0)
    all_centred = (normed_all.astype(jnp.float32) - first_shift) / first_gain
    own_average = jnp.mean(tokens, -1, keepdims=True)
    own_spread = jnp.mean((tokens - own_average) ** 2, -1, keepdims=True)
    own_centred = (tokens - own_average) * lax.rsqrt(own_spread + EPSILON)
    first_gain_grad = jnp.sum(all_centred * spread, 0) + jnp.sum(own_centred * query_spread, 0)
    bias_rows = inner_bias_grad.shape[0] // feature_count
    inner_bias_rows = (
        inner_bias_grad.reshape(nb, bias_rows, -1).transpose(1, 0, 2).reshape(bias_rows, -1)
    )
    vectors = [
        first_gain_grad,
        first_shift_grad,
        query_bias_grad,
        value_bias_grad,
        out_bias_grad,
        second_gain_grad,
        second_shift_grad,
        outer_bias_grad,
        final_gain_grad,
        final_shift_grad,
    ]
    rows = [tail_map_rows, cluster_rows, inner_bias_rows] + [value[None] for value in vectors]
    edges = [0]
    for row in rows:
        edges.append(edges[-1] + row.shape[0])
    row_count = round_up(edges[-1], 128)
    rows.append(jnp.zeros((row_count - edges[-1], feature_count), jnp.float32))
    columns = [
        query_weight_grad,
        key_weight_grad,
        value_weight_grad,
        out_weight_grad,
        middle_map_grad,
        turned(jnp.concatenate(rows, 0), jnp.bfloat16),
    ]
    rest = jnp.concatenate([lowered(column) for column in columns], 1)
    spread_low = lowered(spread)
    rest, facts, spread_low, inner_part = lax.optimization_barrier(
        (rest, facts, spread_low, inner_part)
    )
    rest_part = lax.psum_scatter(rest, "batch", scatter_dimension=0, tiled=True)
    inner_low = lowered(line_scatter(inner_part))
    spread_sum = line_scatter(spread_low, False)
    middle_result = jax.ShapeDtypeStruct(
        (sizes[1], middle_width) if split else (middle_padded, middle_width),
        jnp.float32 if split else jnp.bfloat16,
    )
    middle_part = band_grad(
        middle_pad,
        rows_all,
        facts,
        block_kind == 1,
        lowest,
        highest,
        0 * place,
        middle_padded,
        HEAD_WORDS + member * sizes[1],
        middle_chunk,
        middle_result,
        False,
    )
    if split:
        for unused in range(nz - 3):
            (rest_part,) = first_advance(rest_part)
            (rest_part,) = second_advance(rest_part)
    rest_part, middle_part, inner_low, spread_sum, outer_part = lax.optimization_barrier(
        (rest_part, middle_part, inner_low, spread_sum, outer_part)
    )
    inner_pieces = line_turns(inner_low)
    outer_low = lowered(line_scatter(outer_part))
    if split:
        middle_table_grad = middle_part
        head_table_grad = jnp.concatenate(line_ordered(head_found), 0)
        pairs = zip(line_ordered(first_found), line_ordered(second_found))
        tail_sum = jnp.concatenate([value for pair in pairs for value in pair], 1)
    else:
        middle_table_grad = lax.psum(middle_part, "seq")[: sizes[1]].astype(jnp.float32)
        head_table_grad = lax.psum(head_part, "seq")
        tail_sum = lax.psum(jnp.concatenate([first_tail, second_tail], 1), "seq")
    head_table_grad = head_table_grad[: sizes[0]].astype(jnp.float32)
    tail_table_grad = tail_sum[:, : sizes[2]].astype(jnp.float32).T
    normed_grad = query_spread + spread_sum
    first_in_grad, unused, unused = norm_back(tokens, first_gain, first_shift, normed_grad)
    input_grad = mixed_grad + first_in_grad
    inner_sum = in_order(inner_pieces).astype(jnp.float32)
    outer_sum = in_order(line_turns(outer_low)).astype(jnp.float32)
    rest_low = lax.psum(rest_part, "seq")
    rest_sum = rest_low[:, : 4 * feature_count + middle_width].astype(jnp.float32)
    cut = [rest_sum[:, i * feature_count : (i + 1) * feature_count] for i in range(4)]
    middle_map_sum = rest_sum[:, 4 * feature_count : 4 * feature_count + middle_width]
    row_sum = turned(rest_low[:, 4 * feature_count + middle_width :], jnp.float32)
    tail_map_sum, cluster_sum, inner_bias_sum = (
        row_sum[low:high] for low, high in zip(edges[:3], edges[1:4])
    )
    lines = [row_sum[index] for index in range(edges[3], edges[3] + len(vectors))]
    return (
        loglik.reshape(1, token_count),
        input_grad.reshape(1, token_count, feature_count),
        lines[0],
        lines[1],
        cut[0],
        lines[2],
        cut[1],
        cut[2],
        lines[3],
        cut[3],
        lines[4],
        lines[5],
        lines[6],
        inner_sum,
        inner_bias_sum.reshape(-1),
        outer_sum,
        lines[7],
        lines[8],
        lines[9],
        head_table_grad,
        cluster_sum.T,
        middle_map_sum,
        middle_table_grad,
        tail_map_sum.T,
        tail_table_grad,
    )


def solution(mesh):
    return jax.shard_map(
        on_device,
        mesh=mesh,
        in_specs=(
            P("batch", "seq", None),
            P("batch", "seq"),
            P("batch", "seq", None),
            P("batch", "seq", None),
            P("batch", "seq"),
            P(),
            P(),
            P(),
            P(),
            P(),
            P(),
            P(),
            P(),
            P(),
            P(),
            P(),
            P(),
            P(),
            P(),
            P(),
            P(),
            P(),
            P("batch", None),
            P(),
            P(),
            P("batch", None),
            P(),
            P("batch", None),
        ),
        out_specs=(
            P("batch", "seq"),
            P("batch", "seq", None),
            P("batch"),
            P("batch"),
            P("batch", None),
            P("batch"),
            P("batch", None),
            P("batch", None),
            P("batch"),
            P("batch", None),
            P("batch"),
            P("batch"),
            P("batch"),
            P("batch", None),
            P("batch"),
            P("batch", None),
            P("batch"),
            P("batch"),
            P("batch"),
            P("batch", None),
            P("batch", None),
            P("batch", None),
            P("batch", None),
            P("batch", None),
            P("batch", None),
        ),
        check_vma=False,
    )
```

```python
import functools
import math

import jax
import jax.numpy as jnp
from jax import lax
from jax.experimental import pallas as pl
from jax.experimental.pallas import tpu as pltpu
from jax.sharding import PartitionSpec as P

HEADS = 16
HEAD_WORDS = 20000
MID_WORDS = 40000
TAIL_WORDS = 207735


NEG_FILL = -1e30
EPSILON = 1e-05
BLOCK = 256
SAFE = 1e30
VMEM_BYTES = 56 << 20
ONCE = dict(pipeline_mode=pl.Buffered(1))


def layer_norm(values, gain_vector, shift_vector):
    average = jnp.mean(values, -1, keepdims=True)
    centred = values - average
    spread = jnp.mean(centred * centred, -1, keepdims=True)
    return centred * lax.rsqrt(spread + EPSILON) * gain_vector + shift_vector


def norm_back(values, gain_vector, shift_vector, upstream):
    unused, pullback = jax.vjp(layer_norm, values, gain_vector, shift_vector)
    return pullback(upstream)


def gelu_back(before, upstream):
    unused, pullback = jax.vjp(jax.nn.gelu, before)
    return pullback(upstream)[0]


def product(former, latter):
    return jnp.dot(former, latter, preferred_element_type=jnp.float32)


def product_tn(former, latter):
    return lax.dot_general(
        former, latter, (((0,), (0,)), ((), ())), preferred_element_type=jnp.float32
    )


def product_nt(former, latter):
    return lax.dot_general(
        former, latter, (((1,), (1,)), ((), ())), preferred_element_type=jnp.float32
    )


def lowered(values):
    return values.astype(jnp.bfloat16)


def round_up(count, unit):
    return -(-count // unit) * unit


def thirds(values):
    high = lowered(values)
    rest = values - high.astype(jnp.float32)
    middle = lowered(rest)
    return [high, middle, lowered(rest - middle.astype(jnp.float32))]


def attend_kernel(start_ref, query_ref, key_ref, value_ref, out_ref):
    rows, keys = query_ref.shape[0], key_ref.shape[0]
    half = query_ref.shape[1] // 2
    query_pos = start_ref[0] + lax.broadcasted_iota(jnp.int32, (rows, keys), 0)
    allowed = lax.broadcasted_iota(jnp.int32, (rows, keys), 1) <= query_pos
    for part in range(2):
        cols = slice(part * half, part * half + half)
        scores = product_nt(query_ref[:, cols], key_ref[:, cols]) * half**-0.5
        scores = jnp.where(allowed, scores, NEG_FILL)
        weights = jnp.exp(scores - jnp.max(scores, 1, keepdims=True))
        weights = weights / jnp.sum(weights, 1, keepdims=True)
        out_ref[:, cols] = lowered(product(lowered(weights), value_ref[:, cols]))


def attend(start, queries, keys, values):
    rows, features = queries.shape
    width = 2 * features // HEADS
    own = pl.BlockSpec((rows, width), lambda i, s: (0, i))
    whole = pl.BlockSpec((keys.shape[0], width), lambda i, s: (0, i))
    return pl.pallas_call(
        attend_kernel,
        grid_spec=pltpu.PrefetchScalarGridSpec(
            num_scalar_prefetch=1,
            grid=(features // width,),
            in_specs=[own, whole, whole],
            out_specs=own,
        ),
        out_shape=jax.ShapeDtypeStruct((rows, features), jnp.bfloat16),
        compiler_params=pltpu.CompilerParams(vmem_limit_bytes=VMEM_BYTES),
        cost_estimate=pl.CostEstimate(
            flops=4 * rows * keys.shape[0] * features,
            bytes_accessed=4 * (rows + keys.shape[0]) * features,
            transcendentals=rows * keys.shape[0] * HEADS,
        ),
        name="attend",
    )(start, queries, keys, values)


def attend_back_kernel(
    start_ref, query_ref, key_ref, value_ref, up_ref, query_grad_ref, key_grad_ref, value_grad_ref
):
    rows, keys = query_ref.shape[0], key_ref.shape[0]
    half = query_ref.shape[1] // 2
    scale = half**-0.5
    query_pos = start_ref[0] + lax.broadcasted_iota(jnp.int32, (keys, rows), 1)
    allowed = lax.broadcasted_iota(jnp.int32, (keys, rows), 0) <= query_pos
    for part in range(2):
        cols = slice(part * half, part * half + half)
        query, key, value, up = (
            ref[:, cols] for ref in (query_ref, key_ref, value_ref, up_ref)
        )
        scores = jnp.where(allowed, product_nt(key, query) * scale, NEG_FILL)
        probs = jnp.exp(scores - jnp.max(scores, 0, keepdims=True))
        probs = probs / jnp.sum(probs, 0, keepdims=True)
        prob_grad = product_nt(value, up)
        delta = jnp.sum(probs * prob_grad, 0, keepdims=True)
        score_grad = lowered(probs * (prob_grad - delta))
        value_grad_ref[:, cols] = lowered(product(lowered(probs), up))
        key_grad_ref[:, cols] = lowered(product(score_grad, query) * scale)
        query_grad_ref[:, cols] = lowered(product_tn(score_grad, key) * scale)


def attend_back(start, queries, keys, values, upstream):
    rows, features = queries.shape
    count = keys.shape[0]
    width = 2 * features // HEADS
    own = pl.BlockSpec((rows, width), lambda i, s: (0, i))
    whole = pl.BlockSpec((count, width), lambda i, s: (0, i))
    return pl.pallas_call(
        attend_back_kernel,
        grid_spec=pltpu.PrefetchScalarGridSpec(
            num_scalar_prefetch=1,
            grid=(features // width,),
            in_specs=[own, whole, whole, own],
            out_specs=[own, whole, whole],
        ),
        out_shape=[
            jax.ShapeDtypeStruct((rows, features), jnp.bfloat16),
            jax.ShapeDtypeStruct((count, features), jnp.bfloat16),
            jax.ShapeDtypeStruct((count, features), jnp.bfloat16),
        ],
        compiler_params=pltpu.CompilerParams(vmem_limit_bytes=VMEM_BYTES),
        cost_estimate=pl.CostEstimate(
            flops=10 * rows * count * features,
            bytes_accessed=6 * (rows + count) * features,
            transcendentals=rows * count * HEADS,
        ),
        name="attend_back",
    )(start, queries, keys, values, upstream)


def pick_kernel(by_slot, index_ref, rows_ref, out_ref):
    count = rows_ref.shape[0]
    total = jnp.zeros(out_ref.shape, jnp.float32)
    base = pl.program_id(0) * BLOCK
    for at in range(0, count, BLOCK):
        if by_slot:
            place = base + lax.broadcasted_iota(jnp.int32, (BLOCK, BLOCK), 0)
            hit = index_ref[:, at : at + BLOCK] == place
        else:
            place = at + lax.broadcasted_iota(jnp.int32, (BLOCK, BLOCK), 1)
            hit = index_ref[...] == place
        onehot = lowered(jnp.where(hit, 1.0, 0.0))
        total = total + product(onehot, rows_ref[at : at + BLOCK, :])
    out_ref[...] = total.astype(out_ref.dtype)


def pick_rows(index, rows, out_count, by_slot, kind):
    count, width = rows.shape
    if by_slot:
        index = index.reshape(1, -1)
        index_spec = pl.BlockSpec(index.shape, lambda i: (0, 0))
    else:
        index = index.reshape(-1, 1)
        index_spec = pl.BlockSpec((BLOCK, 1), lambda i: (i, 0))
    return pl.pallas_call(
        functools.partial(pick_kernel, by_slot),
        grid=(out_count // BLOCK,),
        in_specs=[index_spec, pl.BlockSpec(rows.shape, lambda i: (0, 0), **ONCE)],
        out_specs=pl.BlockSpec((BLOCK, width), lambda i: (i, 0)),
        out_shape=jax.ShapeDtypeStruct((out_count, width), kind),
        compiler_params=pltpu.CompilerParams(vmem_limit_bytes=VMEM_BYTES),
        cost_estimate=pl.CostEstimate(
            flops=2 * out_count * count * max(width, 256),
            bytes_accessed=rows.size * 2 + out_count * width * 4,
            transcendentals=0,
        ),
        name="pick_rows",
    )(index, rows)


def band_kernel(chunk, per, words, sum_column, span_ref, rows_ref, table_ref, stat_ref, out_ref, mix_ref):
    step_id = pl.program_id(0)
    count, width = mix_ref.shape
    chunk_count = table_ref.shape[0] // chunk
    group_count = chunk_count // per
    active = (step_id >= span_ref[0]) & (step_id < span_ref[1])

    def put_stats(top, total):
        lane = lax.broadcasted_iota(jnp.int32, (count, 128), 1)
        both = jnp.where(lane == 0, top, jnp.where(lane == 1, total, 0.0))
        stat_ref[...] = both.T[:8, :]

    def logits_at(at, rows):
        return product_nt(rows, table_ref[pl.ds(at, chunk), :])

    def beyond(at, shape):
        return at + lax.broadcasted_iota(jnp.int32, shape, 1) >= words

    def run(rows, top):
        mix_ref[...] = jnp.zeros(mix_ref.shape, jnp.float32)

        def visit(group, total):
            for inner in range(per):
                at = (group * per + inner) * chunk
                checked = isinstance(at, int) and at + chunk > words
                if not isinstance(at, int):
                    at = pl.multiple_of(at, chunk)
                weights = jnp.exp(logits_at(at, rows) - top)
                if checked:
                    weights = jnp.where(beyond(at, weights.shape), 0.0, weights)
                if sum_column is None:
                    for lane in range(0, chunk, 128):
                        total = total + weights[:, lane : lane + 128]
                mix_ref[...] += product(lowered(weights), table_ref[pl.ds(at, chunk), :])
            return total

        lanes = jnp.zeros((count, 128), jnp.float32)
        lanes = visit(0, lanes) if group_count == 1 else lax.fori_loop(0, group_count, visit, lanes)
        if sum_column is None:
            return jnp.sum(lanes, 1, keepdims=True)
        return mix_ref[:, sum_column : sum_column + 1]

    @pl.when(active)
    def _():
        rows = rows_ref[...]
        first = product_nt(rows, table_ref[pl.ds(0, 128), :])
        top = jnp.max(first, 1, keepdims=True)
        total = run(rows, top)
        put_stats(top, total)

        @pl.when(jnp.logical_not(jnp.max(jnp.where(total < SAFE, 0.0, 1.0)) < 0.5))
        def _():
            def largest(index, top):
                at = pl.multiple_of(index * chunk, chunk)
                logits = logits_at(at, rows)
                if sum_column is None:
                    logits = jnp.where(beyond(at, logits.shape), NEG_FILL, logits)
                return jnp.maximum(top, jnp.max(logits, 1, keepdims=True))

            exact = lax.fori_loop(0, chunk_count, largest, jnp.full((count, 1), NEG_FILL))
            put_stats(exact, run(rows, exact))

        out_ref[...] = lowered(mix_ref[...])

    @pl.when(jnp.logical_not(active))
    def _():
        put_stats(jnp.full((count, 1), NEG_FILL), jnp.zeros((count, 1), jnp.float32))
        out_ref[...] = jnp.zeros(out_ref.shape, jnp.bfloat16)


def band_forward(span, rows, table, words, chunk, sum_column, share):
    count, width = rows.shape[0], table.shape[1]
    chunk_count = table.shape[0] // chunk
    per = chunk_count if chunk_count <= 4 else 4
    assert chunk_count % per == 0 and words >= 128
    return pl.pallas_call(
        functools.partial(band_kernel, chunk, per, words, sum_column),
        grid_spec=pltpu.PrefetchScalarGridSpec(
            num_scalar_prefetch=1,
            grid=(count // BLOCK,),
            in_specs=[
                pl.BlockSpec((BLOCK, width), lambda i, s: (i, 0)),
                pl.BlockSpec(table.shape, lambda i, s: (0, 0), **ONCE),
            ],
            out_specs=[
                pl.BlockSpec((8, BLOCK), lambda i, s: (0, i)),
                pl.BlockSpec((BLOCK, width), lambda i, s: (i, 0)),
            ],
            scratch_shapes=[pltpu.VMEM((BLOCK, width), jnp.float32)],
        ),
        out_shape=[
            jax.ShapeDtypeStruct((8, count), jnp.float32),
            jax.ShapeDtypeStruct((count, width), jnp.bfloat16),
        ],
        compiler_params=pltpu.CompilerParams(vmem_limit_bytes=VMEM_BYTES),
        cost_estimate=pl.CostEstimate(
            flops=int(share * 4 * count * table.shape[0] * max(width, 256)),
            bytes_accessed=table.size * 2 + count * width * 6,
            transcendentals=int(share * count * table.shape[0]),
        ),
        name="band_forward",
    )(span, rows, table)


def head_grad_kernel(chunk, lists, base_ref, table_ref, *refs):
    out_ref, sum_ref = refs[2 * lists :]
    words = table_ref.shape[0]
    base = base_ref[0] + pl.program_id(0) * words
    sum_ref[...] = jnp.zeros(sum_ref.shape, jnp.float32)
    for rows_ref, fact_ref in zip(refs[0 : 2 * lists : 2], refs[1 : 2 * lists : 2]):
        piece = min(rows_ref.shape[0], 1024)

        def visit(step, unused, rows_ref=rows_ref, fact_ref=fact_ref, piece=piece):
            at = pl.multiple_of(step * piece, piece)
            rows = rows_ref[pl.ds(at, piece), :]
            weight = fact_ref[0:1, pl.ds(at, piece)]
            total = fact_ref[1:2, pl.ds(at, piece)]
            ids = fact_ref[2:3, pl.ds(at, piece)].astype(jnp.int32)
            for start in range(0, words, chunk):
                probs = jnp.exp(product_nt(table_ref[start : start + chunk, :], rows) - total)
                word = base + start + lax.broadcasted_iota(jnp.int32, (chunk, 1), 0)
                grads = weight * (jnp.where(word == ids, 1.0, 0.0) - probs)
                sum_ref[start : start + chunk, :] += product(lowered(grads), rows)
            return unused

        lax.fori_loop(0, rows_ref.shape[0] // piece, visit, 0)
    out_ref[...] = lowered(sum_ref[...])


def head_grad(table, part, part_words, first_word, lists):
    width = table.shape[1]
    word_block = math.gcd(part_words, 640)
    steps = part_words // word_block
    chunk = word_block // 2 if word_block % 32 == 0 else word_block
    specs = []
    for rows, facts in lists:
        specs.append(pl.BlockSpec(rows.shape, lambda i, s: (0, 0), **ONCE))
        specs.append(pl.BlockSpec(facts.shape, lambda i, s: (0, 0), **ONCE))
    count = sum(rows.shape[0] for rows, facts in lists)
    scalars = jnp.stack([first_word + part * part_words, part * steps]).astype(jnp.int32)
    return pl.pallas_call(
        functools.partial(head_grad_kernel, chunk, len(lists)),
        grid_spec=pltpu.PrefetchScalarGridSpec(
            num_scalar_prefetch=1,
            grid=(steps,),
            in_specs=[pl.BlockSpec((word_block, width), lambda i, s: (s[1] + i, 0))] + specs,
            out_specs=pl.BlockSpec((word_block, width), lambda i, s: (i, 0)),
            scratch_shapes=[pltpu.VMEM((word_block, width), jnp.float32)],
        ),
        out_shape=jax.ShapeDtypeStruct((part_words, width), jnp.bfloat16),
        compiler_params=pltpu.CompilerParams(vmem_limit_bytes=VMEM_BYTES),
        cost_estimate=pl.CostEstimate(
            flops=4 * count * part_words * width,
            bytes_accessed=(count + part_words) * width * 2,
            transcendentals=count * part_words,
        ),
        name="head_grad",
    )(scalars, table, *[value for pair in lists for value in pair])


def band_grad_kernel(chunk, most, across, plan_ref, table_ref, rows_ref, fact_ref, out_ref, sum_ref):
    words = table_ref.shape[0]
    step_id = pl.program_id(0)
    base = plan_ref[most + 1] + step_id * words
    sum_ref[...] = jnp.zeros(sum_ref.shape, jnp.float32)

    def block_at(position):
        return pl.multiple_of(plan_ref[position] * BLOCK, BLOCK)

    def spread(starts):
        rows = [rows_ref[pl.ds(start, BLOCK), :] for start in starts]
        facts = [fact_ref[:, pl.ds(start, BLOCK)] for start in starts]
        rows = rows[0] if len(rows) == 1 else jnp.concatenate(rows, 0)
        facts = facts[0] if len(facts) == 1 else jnp.concatenate(facts, 1)
        weight, total = facts[0:1], facts[1:2]
        for start in range(0, words, chunk):
            probs = jnp.exp(product_nt(table_ref[start : start + chunk, :], rows) - total)
            sum_ref[start : start + chunk, :] -= product(lowered(weight * probs), rows)

    count = plan_ref[0]

    def pair(step, unused):
        spread([block_at(1 + 2 * step), block_at(2 + 2 * step)])
        return unused

    lax.fori_loop(0, count // 2, pair, 0)

    @pl.when(count % 2 == 1)
    def _():
        spread([block_at(count)])

    line = most + 2 + step_id * (most + 1)

    def hits(step, unused):
        at = block_at(line + 1 + step)
        rows = rows_ref[pl.ds(at, BLOCK), :]
        weight = fact_ref[0:1, pl.ds(at, BLOCK)]
        ids = fact_ref[2:3, pl.ds(at, BLOCK)].astype(jnp.int32)
        for start in range(0, words, chunk):
            word = base + start + lax.broadcasted_iota(jnp.int32, (chunk, 1), 0)
            chosen = lowered(jnp.where(word == ids, weight, 0.0))
            sum_ref[start : start + chunk, :] += product(chosen, rows)
        return unused

    lax.fori_loop(0, plan_ref[line], hits, 0)
    if across:
        out_ref[...] = sum_ref[...].T[: out_ref.shape[0], :].astype(out_ref.dtype)
    else:
        out_ref[...] = sum_ref[...].astype(out_ref.dtype)


def listed(flags):
    size = flags.shape[-1]
    order = jnp.cumsum(flags.astype(jnp.int32), -1)
    chosen = (order[..., None, :] == jnp.arange(1, size + 1)[:, None]) & flags[..., None, :]
    places = jnp.sum(jnp.where(chosen, jnp.arange(size), 0), -1)
    return jnp.concatenate([order[..., -1:], places], -1).astype(jnp.int32)


def band_grad(
    table, rows, facts, active, lowest, highest, part, part_words, first_word, chunk, result, across
):
    count, full = rows.shape[0], table.shape[1]
    word_block = chunk
    steps = part_words // word_block
    most = count // BLOCK
    first = first_word + part * part_words
    low = first + jnp.arange(steps, dtype=jnp.int32)[:, None] * word_block
    step_hits = active[None, :] & (lowest[None, :] < low + word_block) & (highest[None, :] >= low)
    plan = jnp.concatenate(
        [
            listed(active),
            first.reshape(1).astype(jnp.int32),
            listed(step_hits).reshape(-1),
            (part * steps).reshape(1).astype(jnp.int32),
        ]
    )
    last = plan.shape[0] - 1
    return pl.pallas_call(
        functools.partial(band_grad_kernel, chunk // 2 if chunk > 832 else chunk, most, across),
        grid_spec=pltpu.PrefetchScalarGridSpec(
            num_scalar_prefetch=1,
            grid=(steps,),
            in_specs=[
                pl.BlockSpec((word_block, full), lambda i, s: (s[last] + i, 0)),
                pl.BlockSpec((count, full), lambda i, s: (0, 0), **ONCE),
                pl.BlockSpec(facts.shape, lambda i, s: (0, 0), **ONCE),
            ],
            out_specs=(
                pl.BlockSpec((result.shape[0], word_block), lambda i, s: (0, i))
                if across
                else pl.BlockSpec((word_block, full), lambda i, s: (i, 0))
            ),
            scratch_shapes=[pltpu.VMEM((word_block, full), jnp.float32)],
        ),
        out_shape=result,
        compiler_params=pltpu.CompilerParams(vmem_limit_bytes=VMEM_BYTES),
        cost_estimate=pl.CostEstimate(
            flops=2 * count * part_words * 256,
            bytes_accessed=count * full * 2 + part_words * full * 4,
            transcendentals=count * part_words // 2,
        ),
        name="band_grad",
    )(plan, table, rows, facts)


def settle_kernel(
    member_ref,
    everyone_ref,
    fact_ref,
    head_mix_ref,
    middle_mix_ref,
    tail_mix_ref,
    head_hit_ref,
    middle_hit_ref,
    tail_hit_ref,
    term_ref,
    line_ref,
    slot_ref,
):
    step = pl.program_id(0)
    devices, _, slots = everyone_ref.shape
    tail_width = 64
    here = pl.ds(pl.multiple_of(step * BLOCK, BLOCK), BLOCK)

    def merged(read):
        lines = [read(device) for device in range(devices)]
        top = functools.reduce(jnp.maximum, [line[0] for line in lines])
        return top, sum(line[1] * jnp.exp(line[0] - top) for line in lines)

    head_top, head_sum = merged(
        lambda d: (everyone_ref[d, 0:1, here], everyone_ref[d, 1:2, here])
    )
    target = sum(everyone_ref[d, 2:3, here] for d in range(devices))
    slot_top, slot_sum = merged(lambda d: (everyone_ref[d, 3:4, :], everyone_ref[d, 4:5, :]))
    used = slot_sum > 0.0
    slot_total = jnp.where(used, slot_top + jnp.log(jnp.where(used, slot_sum, 1.0)), 0.0)
    member = member_ref[0]
    own_slot_top = jnp.where(used, everyone_ref[member, 3:4, :], 0.0)
    own_head_top = everyone_ref[member, 0:1, here]

    facts = fact_ref[...]
    slot, share, cotangent, first_cluster, second_cluster, band, word = (
        facts[index : index + 1] for index in range(7)
    )

    def as_columns(lines):
        square = jnp.concatenate(
            lines + [jnp.zeros((128 - len(lines), BLOCK), jnp.float32)], 0
        )
        return square.T

    def three(line):
        return [part.astype(jnp.float32) for part in thirds(line)]

    slot_column = as_columns([slot])[:, 0:1].astype(jnp.int32)
    hot = lowered(
        jnp.where(lax.broadcasted_iota(jnp.int32, (BLOCK, slots), 1) == slot_column, 1.0, 0.0)
    )
    lines = three(slot_total) + three(own_slot_top) + [jnp.zeros((10, slots), jnp.float32)]
    on_tokens = product_nt(lowered(jnp.concatenate(lines, 0)), hot)
    band_total = on_tokens[0:1] + on_tokens[1:2] + on_tokens[2:3]
    own_band_top = on_tokens[3:4] + on_tokens[4:5] + on_tokens[5:6]

    cluster_top = jnp.maximum(head_top, jnp.maximum(first_cluster, second_cluster))
    head_total = cluster_top + jnp.log(
        head_sum * jnp.exp(head_top - cluster_top)
        + jnp.exp(first_cluster - cluster_top)
        + jnp.exp(second_cluster - cluster_top)
    )
    in_head = band < 0.5
    cluster = jnp.where(band < 1.5, first_cluster, second_cluster)
    model_logp = target - head_total + jnp.where(in_head, 0.0, cluster - band_total)
    ratio = 0.25 * share * jnp.exp(-model_logp)
    weight = cotangent * 0.75 / (0.75 + ratio)
    head_scale = weight * jnp.exp(own_head_top - head_total)
    band_scale = weight * jnp.where(in_head, 0.0, jnp.exp(own_band_top - band_total))
    columns = as_columns([weight, head_scale, band_scale])
    weight_column, head_column, band_column = (columns[:, i : i + 1] for i in range(3))
    width = head_mix_ref.shape[1]
    term_ref[:, :width] = lowered(
        weight_column * head_hit_ref[...].astype(jnp.float32)
        - head_column * head_mix_ref[...].astype(jnp.float32)
    )
    narrow = tail_mix_ref.shape[1]
    kept = lax.broadcasted_iota(jnp.int32, (BLOCK, narrow), 1) < tail_width

    def widened(values):
        values = jnp.where(kept, values, 0.0)
        more = middle_mix_ref.shape[1] - narrow
        return jnp.concatenate([values, jnp.zeros((BLOCK, more), jnp.float32)], 1)

    band_mix = product(hot, middle_mix_ref[...]) + widened(product(hot, tail_mix_ref[...]))
    band_hit = middle_hit_ref[...].astype(jnp.float32) + widened(
        tail_hit_ref[...].astype(jnp.float32)
    )
    term_ref[:, width:] = lowered(weight_column * band_hit - band_column * band_mix)
    line_ref[...] = jnp.concatenate(
        [
            model_logp + jnp.log(0.75 + ratio),
            weight,
            head_total,
            word,
            jnp.zeros((4, BLOCK), jnp.float32),
        ],
        0,
    )

    @pl.when(step == 0)
    def _():
        slot_ref[...] = jnp.concatenate(
            [jnp.zeros((8, slots), jnp.float32), slot_total, jnp.zeros((7, slots), jnp.float32)], 0
        )

    sent = three(weight) + three(word) + [jnp.zeros((10, BLOCK), jnp.float32)]
    slot_ref[0:8, :] += product(lowered(jnp.concatenate(sent, 0)), hot)[0:8]


def settle(member, everyone, facts, head_mix, middle_mix, tail_mix, hits):
    count, width = head_mix.shape
    slots = middle_mix.shape[0]
    full = width + middle_mix.shape[1]

    def tokens(values):
        return pl.BlockSpec((BLOCK, values.shape[1]), lambda i, s: (i, 0))

    def whole(values):
        return pl.BlockSpec(values.shape, lambda i, s: (0,) * values.ndim, **ONCE)

    lines = pl.BlockSpec((8, BLOCK), lambda i, s: (0, i))
    return pl.pallas_call(
        settle_kernel,
        grid_spec=pltpu.PrefetchScalarGridSpec(
            num_scalar_prefetch=1,
            grid=(count // BLOCK,),
            in_specs=[whole(everyone), lines, tokens(head_mix), whole(middle_mix), whole(tail_mix)]
            + [tokens(hit) for hit in hits],
            out_specs=[
                pl.BlockSpec((BLOCK, full), lambda i, s: (i, 0)),
                lines,
                pl.BlockSpec((16, slots), lambda i, s: (0, 0)),
            ],
        ),
        out_shape=[
            jax.ShapeDtypeStruct((count, full), jnp.bfloat16),
            jax.ShapeDtypeStruct((8, count), jnp.float32),
            jax.ShapeDtypeStruct((16, slots), jnp.float32),
        ],
        compiler_params=pltpu.CompilerParams(vmem_limit_bytes=VMEM_BYTES),
        cost_estimate=pl.CostEstimate(
            flops=2 * count * slots * 1024,
            bytes_accessed=count * width * 12 + slots * full,
            transcendentals=slots * 64,
        ),
        name="settle",
    )(member.reshape(1).astype(jnp.int32), everyone, facts, head_mix, middle_mix, tail_mix, *hits)


def line_turns(value):
    size = lax.axis_size("seq")
    return [value] + [
        lax.ppermute(value, "seq", [(d, (d - k) % size) for d in range(size)])
        for k in range(1, size)
    ]


def line_step(before, behind, step):
    size = lax.axis_size("seq")
    return (
        lax.ppermute(before, "seq", [(d, d + 1) for d in range(step - 1, size - 1)]),
        lax.ppermute(behind, "seq", [(d, d - 1) for d in range(1, size - step + 1)]),
    )


def line_steps(value):
    found = [(value, value)]

    def advance(*others):
        step = len(found)
        if step == lax.axis_size("seq"):
            return others
        moved = line_step(*found[-1], step)
        moved, others = lax.optimization_barrier((moved, others))
        found.append(moved)
        return others

    return found, advance


def line_ordered(found):
    size, place = lax.axis_size("seq"), lax.axis_index("seq")
    ordered = []
    for source in range(size):
        value = found[0][0]
        for step in range(1, size):
            if source + step < size:
                value = jnp.where(place == source + step, found[step][0], value)
            if source - step >= 0:
                value = jnp.where(place == source - step, found[step][1], value)
        ordered.append(value)
    return ordered


def earlier_joined(value):
    size, place = lax.axis_size("seq"), lax.axis_index("seq")
    joined = jnp.zeros((size,) + value.shape, value.dtype)
    for step in range(size - 1, -1, -1):
        piece = value
        if step:
            piece = lax.ppermute(value, "seq", [(d, d + step) for d in range(size - step)])
        joined = lax.dynamic_update_index_in_dim(joined, piece, jnp.maximum(place - step, 0), 0)
    return joined.reshape((-1,) + value.shape[1:])


def in_order(pieces):
    size, place = lax.axis_size("seq"), lax.axis_index("seq")
    joined = jnp.zeros((size,) + pieces[0].shape, pieces[0].dtype)
    for k, piece in enumerate(pieces):
        joined = lax.dynamic_update_index_in_dim(joined, piece, lax.rem(place + k, size), 0)
    return joined.reshape((-1,) + pieces[0].shape[1:])


def line_scatter(values, behind=True):
    size, place = lax.axis_size("seq"), lax.axis_index("seq")
    parts = values.reshape((size, -1) + values.shape[1:])

    def part(index):
        return lax.dynamic_index_in_dim(parts, lax.rem(index, size), 0, False)

    total = part(place).astype(jnp.float32)
    for k in range(1, size):
        pairs = [(d, (d - k) % size) for d in range(0 if behind else k, size)]
        total = total + lax.ppermute(part(place + size - k), "seq", pairs).astype(jnp.float32)
    return total


def turn_kernel(rows_ref, out_ref):
    out_ref[...] = rows_ref[...].astype(jnp.float32).T.astype(out_ref.dtype)


def turned(rows, kind):
    return pl.pallas_call(
        turn_kernel, out_shape=jax.ShapeDtypeStruct(rows.shape[::-1], kind), name="turned"
    )(rows)


def word_pad(rows, biggest, splits):
    chunk = min(biggest, round_up(rows, 128))
    chunks = -(-rows // chunk)
    if chunks > 4:
        chunks = round_up(chunks, 4)
    return chunk, chunks * chunk


def on_device(
    inputs,
    targets,
    neighbours,
    neighbour_scores,
    loglik_grad,
    first_gain,
    first_shift,
    query_weight,
    query_bias,
    key_weight,
    value_weight,
    value_bias,
    out_weight,
    out_bias,
    second_gain,
    second_shift,
    inner_weight,
    inner_bias,
    outer_weight,
    outer_bias,
    final_gain,
    final_shift,
    head_table,
    cluster_weight,
    middle_map,
    middle_table,
    tail_map,
    tail_table,
):
    nb = lax.axis_size("batch")
    nz = lax.axis_size("seq")
    member = lax.axis_index("batch")
    place = lax.axis_index("seq")
    tokens = inputs[0]
    own_ids = targets[0]
    token_count, feature_count = tokens.shape
    group_count = token_count * nb
    slot_count = group_count + BLOCK
    query_start = (place * token_count).reshape(1)

    normed_low = lowered(layer_norm(tokens, first_gain, first_shift))
    normed_all = earlier_joined(normed_low)
    top_score = jnp.max(neighbour_scores[0], -1, keepdims=True)
    exponent = jnp.exp(neighbour_scores[0] - top_score)
    knn_prob = jnp.sum(jnp.where(neighbours[0] == 0, exponent, 0.0), -1) / jnp.sum(exponent, -1)
    early = jnp.stack([own_ids.astype(jnp.float32), knn_prob, loglik_grad[0]])
    early = lax.all_gather(early, "batch", axis=1, tiled=True)
    all_ids = early[0].astype(jnp.int32)
    all_knn, all_up = early[1], early[2]
    in_head = all_ids < HEAD_WORDS
    in_middle = (all_ids >= HEAD_WORDS) & (all_ids < HEAD_WORDS + MID_WORDS)
    in_tail = all_ids >= HEAD_WORDS + MID_WORDS
    order = jnp.arange(group_count, dtype=jnp.int32)
    ahead = (all_ids[None, :] < all_ids[:, None]) | (
        (all_ids[None, :] == all_ids[:, None]) & (order[None, :] < order[:, None])
    )
    rank = jnp.sum(ahead.astype(jnp.int32), -1)
    head_size = jnp.sum(in_head.astype(jnp.int32))
    middle_size = jnp.sum(in_middle.astype(jnp.int32))
    tail_size = group_count - head_size - middle_size
    middle_blocks = (middle_size + BLOCK - 1) // BLOCK
    tail_blocks = (tail_size + BLOCK - 1) // BLOCK
    slot = jnp.where(
        in_head,
        -1,
        rank - head_size + jnp.where(in_tail, middle_blocks * BLOCK - middle_size, 0),
    )
    zero_span = jnp.zeros((1,), jnp.int32)
    head_span = jnp.array([0, group_count // BLOCK], jnp.int32)
    middle_span = jnp.stack([0 * middle_blocks, middle_blocks]).astype(jnp.int32)
    tail_span = jnp.stack([middle_blocks, middle_blocks + tail_blocks]).astype(jnp.int32)
    slot_order = jnp.arange(slot_count, dtype=jnp.int32)
    slot_middle = slot_order < middle_size
    slot_tail = (slot_order >= middle_blocks * BLOCK) & (
        slot_order < middle_blocks * BLOCK + tail_size
    )
    slot_used = slot_middle | slot_tail
    band_id = all_ids - jnp.where(in_tail, HEAD_WORDS + MID_WORDS, HEAD_WORDS)

    tables = (head_table, middle_table, tail_table)
    sizes = tuple(table.shape[0] for table in tables)
    head_chunk, head_padded = word_pad(sizes[0], 1280, nz)
    middle_chunk, middle_padded = word_pad(sizes[1], 1280, nz)
    tail_chunk, tail_padded = word_pad(sizes[2], 1664, nz)
    tail_width = tail_table.shape[1]
    head_pad = jnp.pad(head_table, ((0, head_padded - sizes[0]), (0, 0)))
    middle_pad = jnp.pad(middle_table, ((0, middle_padded - sizes[1]), (0, 0)))
    tail_word = jnp.arange(tail_padded, dtype=jnp.int32)
    tail_bias = jnp.where(tail_word < jnp.minimum(TAIL_WORDS - member * sizes[2], sizes[2]), 0.0, NEG_FILL)
    tail_pad = jnp.concatenate(
        [
            jnp.pad(tail_table.T, ((0, 0), (0, tail_padded - sizes[2]))),
            jnp.ones((1, tail_padded), jnp.bfloat16),
            lowered(tail_bias)[None, :],
            jnp.zeros((126 - tail_width, tail_padded), jnp.bfloat16),
        ],
        0,
    ).T
    locals_ = (
        all_ids - member * sizes[0],
        all_ids - HEAD_WORDS - member * sizes[1],
        all_ids - HEAD_WORDS - MID_WORDS - member * sizes[2],
    )
    owned = tuple(
        inside & (local >= 0) & (local < size)
        for inside, local, size in zip((in_head, in_middle, in_tail), locals_, sizes)
    )
    hit_rows = tuple(
        jnp.where(
            own[:, None],
            jnp.take(table, jnp.clip(local, 0, size - 1), axis=0, mode="clip"),
            jnp.bfloat16(0),
        )
        for own, table, local, size in zip(owned, (head_pad, middle_pad, tail_pad), locals_, sizes)
    )

    queries = lowered(product(normed_low, query_weight) + query_bias)
    key_rows = lowered(product(normed_all, key_weight))
    value_rows = lowered(product(normed_all, value_weight) + value_bias)
    attended_low = attend(query_start, queries, key_rows, value_rows)
    mixed = tokens + product(attended_low, out_weight) + out_bias
    second_low = lowered(layer_norm(mixed, second_gain, second_shift))
    before = product(second_low, inner_weight) + inner_bias
    hidden_low = lowered(jax.nn.gelu(before))
    final = mixed + product(hidden_low, outer_weight) + outer_bias
    state_low = lowered(layer_norm(final, final_gain, final_shift))
    all_states = lax.all_gather(state_low, "batch", axis=0, tiled=True)
    split = 2 * nz * group_count * feature_count <= 24 << 20
    if split:
        block_states = lax.all_gather(state_low, "seq", axis=0, tiled=True)
    all_states, head_pad, middle_pad, tail_pad, tail_hits, slot, early = lax.optimization_barrier(
        (all_states, head_pad, middle_pad, tail_pad, hit_rows[2], slot, early)
    )
    hit_rows = hit_rows[:2] + (tail_hits,)

    middle_width = middle_map.shape[1]
    maps = jnp.pad(jnp.concatenate([middle_map, tail_map], 1), ((0, 0), (0, 128 - tail_width)))
    one_column = (jnp.arange(middle_width + 128) == middle_width + tail_width + 1).astype(jnp.float32)
    band_low = lowered(product(all_states, maps) + one_column)
    middle_low, tail_low = band_low[:, :middle_width], band_low[:, middle_width:]
    cluster_lines = product_nt(
        jnp.pad(cluster_weight.T, ((0, 6), (0, 0))), all_states
    )
    slot_full = pick_rows(slot, band_low, slot_count, True, jnp.bfloat16)
    first_tail = middle_blocks * BLOCK
    in_tail_slot = slot_order >= first_tail
    slot_low = jnp.where(
        in_tail_slot[:, None],
        jnp.pad(slot_full[:, middle_width:], ((0, 0), (0, middle_width - 128))),
        slot_full[:, :middle_width],
    )
    if split:
        piece = slot_count // nb
        slot_piece = lax.dynamic_slice_in_dim(slot_low, member * piece, piece, 0)
        other_slots = jnp.concatenate(line_turns(slot_piece)[1:], 0)
    head_stats, head_mix = band_forward(
        head_span, all_states, head_pad, sizes[0], head_chunk, None, 1.0
    )
    if split:
        slot_low, block_states, hit_rows, head_stats = lax.optimization_barrier(
            (slot_low, block_states, hit_rows, head_stats)
        )
        other_states = lax.dynamic_slice_in_dim(
            jnp.concatenate([block_states, block_states], 0),
            (place + 1) * token_count,
            (nz - 1) * token_count,
            0,
        )
        other_states = lax.all_gather(other_states, "batch", axis=0, tiled=True)
    tail_stats, tail_mix = band_forward(
        tail_span, slot_low, tail_pad, tail_padded, tail_chunk, tail_width, 0.5
    )
    middle_stats, middle_mix = band_forward(
        middle_span, slot_low, middle_pad, sizes[1], middle_chunk, None, 0.25
    )
    inner_lane = jnp.arange(128) < tail_width
    target_part = (
        jnp.sum(hit_rows[0].astype(jnp.float32) * all_states.astype(jnp.float32), -1)
        + jnp.sum(hit_rows[1].astype(jnp.float32) * middle_low.astype(jnp.float32), -1)
        + jnp.sum(
            jnp.where(inner_lane, hit_rows[2].astype(jnp.float32), 0.0)
            * tail_low.astype(jnp.float32),
            -1,
        )
    )
    slot_stats = jnp.where(in_tail_slot[None, :], tail_stats[:2], middle_stats[:2])
    extra = ((0, 0), (0, BLOCK))
    stats = jnp.concatenate(
        [
            jnp.pad(jnp.concatenate([head_stats[:2], target_part[None]], 0), extra),
            slot_stats,
            jnp.zeros((3, slot_count), jnp.float32),
        ],
        0,
    )
    if split:
        stats, other_states, other_slots = lax.optimization_barrier(
            (stats, other_states, other_slots)
        )
        other_slots = lax.all_gather(other_slots, "batch", axis=0, tiled=True)
    everyone = lax.all_gather(stats, "batch")

    token_facts = jnp.concatenate(
        [
            slot.astype(jnp.float32)[None],
            early[1:3],
            cluster_lines[:2],
            jnp.where(in_head, 0.0, jnp.where(in_middle, 1.0, 2.0))[None],
            early[0:1],
            jnp.zeros((1, group_count), jnp.float32),
        ],
        0,
    )
    terms, lines, slot_lines = settle(
        member, everyone, token_facts, head_mix, middle_mix, tail_mix, hit_rows
    )
    own_terms = lax.psum_scatter(terms, "batch", scatter_dimension=0, tiled=True).astype(jnp.float32)

    def own_part(values):
        return lax.dynamic_slice_in_dim(values, member * token_count, token_count, 0)

    loglik = own_part(lines[0])

    kind = jnp.where(slot_middle, 1.0, jnp.where(slot_tail, 2.0, 0.0))
    slot_facts = jnp.stack(
        [
            jnp.sum(slot_lines[0:3], 0),
            slot_lines[8],
            jnp.sum(slot_lines[3:6], 0),
            kind,
        ]
    )
    head_facts = jnp.concatenate([lines[1:4], jnp.zeros((1, group_count), jnp.float32)], 0)
    if split:
        other_slots = (
            other_slots.reshape(nb, nz - 1, piece, middle_width)
            .transpose(1, 0, 2, 3)
            .reshape(-1, middle_width)
        )
        rows_all = jnp.concatenate([slot_low, other_slots], 0)
        fact_pieces = line_turns(jnp.concatenate([slot_facts, head_facts], 1))
        facts = jnp.concatenate([value[:, :slot_count] for value in fact_pieces], 1)
        other_facts = (
            jnp.stack([value[:, slot_count:] for value in fact_pieces[1:]], 1)
            .reshape(4, nz - 1, nb, token_count)
            .transpose(0, 2, 1, 3)
            .reshape(4, -1)
        )
        lists = [(all_states, head_facts), (other_states, other_facts)]
        part, parts = place, nz
    else:
        rows_all, facts, lists = slot_low, slot_facts, [(all_states, head_facts)]
        part, parts = 0 * place, 1
    head_part = head_grad(head_pad, part, head_padded // parts, member * sizes[0], lists)
    block_facts = facts[2:4].reshape(2, -1, BLOCK)
    block_kind = jnp.max(block_facts[1], -1)
    filled = block_facts[1] > 0
    lowest = jnp.min(jnp.where(filled, block_facts[0], 1e9), -1).astype(jnp.int32)
    highest = jnp.max(jnp.where(filled, block_facts[0], -1e9), -1).astype(jnp.int32)
    facts = jnp.concatenate(
        [facts[:2], jnp.where(facts[3:4] > 0, facts[2:3], -1e9), jnp.zeros_like(facts[:1])], 0
    )
    def tail_gradient(part, parts):
        return band_grad(
            tail_pad,
            rows_all,
            facts,
            block_kind == 2,
            lowest,
            highest,
            part,
            tail_padded // parts,
            HEAD_WORDS + MID_WORDS + member * sizes[2],
            math.gcd(tail_padded // parts, tail_chunk),
            jax.ShapeDtypeStruct((tail_width, tail_padded // parts), jnp.bfloat16),
            True,
        )

    first_tail = tail_gradient(2 * part, 2 * parts)
    if split:
        head_found, head_advance = line_steps(head_part)
        first_tail, facts = head_advance(first_tail, facts)
        first_found, first_advance = line_steps(first_tail)
        second_tail = tail_gradient(2 * part + 1, 2 * parts)
        second_tail, own_terms = head_advance(second_tail, own_terms)
        second_tail, own_terms = first_advance(second_tail, own_terms)
        second_found, second_advance = line_steps(second_tail)
    else:
        second_tail = tail_gradient(2 * part + 1, 2 * parts)
        own_terms, first_tail, second_tail = lax.optimization_barrier(
            (own_terms, first_tail, second_tail)
        )

    own_middle = own_part(in_middle)
    own_tail = own_part(in_tail)
    own_lines = lax.dynamic_slice_in_dim(lines, member * token_count, token_count, 1)
    own_weights, own_total = own_lines[1], own_lines[2]
    own_clusters = product(state_low, cluster_weight)
    band_state = own_terms[:, feature_count:]
    middle_state = lowered(jnp.where(own_middle[:, None], band_state, 0.0))
    tail_state = lowered(jnp.where(own_tail[:, None], band_state[:, :tail_width], 0.0))
    cluster_hit = jnp.stack([own_middle, own_tail], -1).astype(jnp.float32)
    cluster_grad = own_weights[:, None] * (
        cluster_hit - jnp.exp(own_clusters - own_total[:, None])
    )
    state_grad = (
        own_terms[:, :feature_count]
        + product_nt(middle_state, middle_map)
        + product_nt(tail_state, tail_map)
        + product_nt(cluster_grad, cluster_weight.astype(jnp.float32))
    )
    middle_map_grad = product_tn(state_low, middle_state)
    tail_map_rows = product_tn(tail_state, state_low)
    cluster_rows = product_tn(cluster_grad, state_low.astype(jnp.float32))
    final_grad, final_gain_grad, final_shift_grad = norm_back(
        final, final_gain, final_shift, state_grad
    )
    final_low = lowered(final_grad)
    outer_weight_grad = product_tn(hidden_low, final_low)
    outer_bias_grad = jnp.sum(final_grad, 0)
    outer_part = lax.psum_scatter(
        lowered(outer_weight_grad), "batch", scatter_dimension=0, tiled=True
    )
    before_grad = lowered(gelu_back(before, product_nt(final_low, outer_weight)))
    inner_weight_grad = product_tn(second_low, before_grad)
    inner_bias_grad = jnp.sum(before_grad.astype(jnp.float32), 0)
    inner_part = lax.psum_scatter(
        lowered(inner_weight_grad), "batch", scatter_dimension=0, tiled=True
    )
    second_in_grad, second_gain_grad, second_shift_grad = norm_back(
        mixed, second_gain, second_shift, product_nt(before_grad, inner_weight)
    )
    mixed_grad = final_grad + second_in_grad
    mixed_low = lowered(mixed_grad)
    out_weight_grad = product_tn(attended_low, mixed_low)
    out_bias_grad = jnp.sum(mixed_grad, 0)
    attended_grad = lowered(product_nt(mixed_low, out_weight))
    if split:
        for unused in range(nz - 3):
            (attended_grad,) = head_advance(attended_grad)
        (attended_grad,) = second_advance(attended_grad)
    query_low, key_low, value_low = attend_back(
        query_start, queries, key_rows, value_rows, attended_grad
    )
    if split:
        query_low, key_low, value_low = first_advance(query_low, key_low, value_low)
        query_low, key_low, value_low = second_advance(query_low, key_low, value_low)
    query_weight_grad = product_tn(normed_low, query_low)
    key_weight_grad = product_tn(normed_all, key_low)
    value_weight_grad = product_tn(normed_all, value_low)
    query_bias_grad = jnp.sum(query_low.astype(jnp.float32), 0)
    value_bias_grad = jnp.sum(value_low.astype(jnp.float32), 0)
    spread = product_nt(key_low, key_weight) + product_nt(value_low, value_weight)
    query_spread = product_nt(query_low, query_weight)
    first_shift_grad = jnp.sum(spread, 0) + jnp.sum(query_spread, 0)
    all_centred = (normed_all.astype(jnp.float32) - first_shift) / first_gain
    own_average = jnp.mean(tokens, -1, keepdims=True)
    own_spread = jnp.mean((tokens - own_average) ** 2, -1, keepdims=True)
    own_centred = (tokens - own_average) * lax.rsqrt(own_spread + EPSILON)
    first_gain_grad = jnp.sum(all_centred * spread, 0) + jnp.sum(own_centred * query_spread, 0)
    bias_rows = inner_bias_grad.shape[0] // feature_count
    inner_bias_rows = (
        inner_bias_grad.reshape(nb, bias_rows, -1).transpose(1, 0, 2).reshape(bias_rows, -1)
    )
    vectors = [
        first_gain_grad,
        first_shift_grad,
        query_bias_grad,
        value_bias_grad,
        out_bias_grad,
        second_gain_grad,
        second_shift_grad,
        outer_bias_grad,
        final_gain_grad,
        final_shift_grad,
    ]
    rows = [tail_map_rows, cluster_rows, inner_bias_rows] + [value[None] for value in vectors]
    edges = [0]
    for row in rows:
        edges.append(edges[-1] + row.shape[0])
    row_count = round_up(edges[-1], 128)
    rows.append(jnp.zeros((row_count - edges[-1], feature_count), jnp.float32))
    columns = [
        query_weight_grad,
        key_weight_grad,
        value_weight_grad,
        out_weight_grad,
        middle_map_grad,
        turned(jnp.concatenate(rows, 0), jnp.bfloat16),
    ]
    rest = jnp.concatenate([lowered(column) for column in columns], 1)
    spread_low = lowered(spread)
    rest, facts, spread_low, inner_part = lax.optimization_barrier(
        (rest, facts, spread_low, inner_part)
    )
    if split:
        for unused in range(nz - 3):
            rest, facts, spread_low, inner_part = first_advance(rest, facts, spread_low, inner_part)
            rest, facts, spread_low, inner_part = second_advance(
                rest, facts, spread_low, inner_part
            )
    rest_part = lax.psum_scatter(rest, "batch", scatter_dimension=0, tiled=True)
    inner_low = lowered(line_scatter(inner_part))
    spread_sum = line_scatter(spread_low, False)
    middle_result = jax.ShapeDtypeStruct(
        (sizes[1], middle_width) if split else (middle_padded, middle_width),
        jnp.float32 if split else jnp.bfloat16,
    )
    middle_part = band_grad(
        middle_pad,
        rows_all,
        facts,
        block_kind == 1,
        lowest,
        highest,
        0 * place,
        middle_padded,
        HEAD_WORDS + member * sizes[1],
        middle_chunk,
        middle_result,
        False,
    )
    middle_part, inner_low, outer_part = lax.optimization_barrier(
        (middle_part, inner_low, outer_part)
    )
    rest_part, spread_sum = lax.optimization_barrier((rest_part, spread_sum))
    inner_pieces = line_turns(inner_low)
    outer_low = lowered(line_scatter(outer_part))
    if split:
        middle_table_grad = middle_part
        head_table_grad = jnp.concatenate(line_ordered(head_found), 0)
        pairs = zip(line_ordered(first_found), line_ordered(second_found))
        tail_sum = jnp.concatenate([value for pair in pairs for value in pair], 1)
    else:
        middle_table_grad = lax.psum(middle_part, "seq")[: sizes[1]].astype(jnp.float32)
        head_table_grad = lax.psum(head_part, "seq")
        tail_sum = lax.psum(jnp.concatenate([first_tail, second_tail], 1), "seq")
    head_table_grad = head_table_grad[: sizes[0]].astype(jnp.float32)
    tail_table_grad = tail_sum[:, : sizes[2]].astype(jnp.float32).T
    normed_grad = query_spread + spread_sum
    first_in_grad, unused, unused = norm_back(tokens, first_gain, first_shift, normed_grad)
    input_grad = mixed_grad + first_in_grad
    inner_sum = in_order(inner_pieces).astype(jnp.float32)
    outer_sum = in_order(line_turns(outer_low)).astype(jnp.float32)
    rest_low = lax.psum(rest_part, "seq")
    rest_sum = rest_low[:, : 4 * feature_count + middle_width].astype(jnp.float32)
    cut = [rest_sum[:, i * feature_count : (i + 1) * feature_count] for i in range(4)]
    middle_map_sum = rest_sum[:, 4 * feature_count : 4 * feature_count + middle_width]
    row_sum = turned(rest_low[:, 4 * feature_count + middle_width :], jnp.float32)
    tail_map_sum, cluster_sum, inner_bias_sum = (
        row_sum[low:high] for low, high in zip(edges[:3], edges[1:4])
    )
    lines = [row_sum[index] for index in range(edges[3], edges[3] + len(vectors))]
    return (
        loglik.reshape(1, token_count),
        input_grad.reshape(1, token_count, feature_count),
        lines[0],
        lines[1],
        cut[0],
        lines[2],
        cut[1],
        cut[2],
        lines[3],
        cut[3],
        lines[4],
        lines[5],
        lines[6],
        inner_sum,
        inner_bias_sum.reshape(-1),
        outer_sum,
        lines[7],
        lines[8],
        lines[9],
        head_table_grad,
        cluster_sum.T,
        middle_map_sum,
        middle_table_grad,
        tail_map_sum.T,
        tail_table_grad,
    )


def solution(mesh):
    return jax.shard_map(
        on_device,
        mesh=mesh,
        in_specs=(
            P("batch", "seq", None),
            P("batch", "seq"),
            P("batch", "seq", None),
            P("batch", "seq", None),
            P("batch", "seq"),
            P(),
            P(),
            P(),
            P(),
            P(),
            P(),
            P(),
            P(),
            P(),
            P(),
            P(),
            P(),
            P(),
            P(),
            P(),
            P(),
            P(),
            P("batch", None),
            P(),
            P(),
            P("batch", None),
            P(),
            P("batch", None),
        ),
        out_specs=(
            P("batch", "seq"),
            P("batch", "seq", None),
            P("batch"),
            P("batch"),
            P("batch", None),
            P("batch"),
            P("batch", None),
            P("batch", None),
            P("batch"),
            P("batch", None),
            P("batch"),
            P("batch"),
            P("batch"),
            P("batch", None),
            P("batch"),
            P("batch", None),
            P("batch"),
            P("batch"),
            P("batch"),
            P("batch", None),
            P("batch", None),
            P("batch", None),
            P("batch", None),
            P("batch", None),
            P("batch", None),
        ),
        check_vma=False,
    )
```

```python
import functools
import math

import jax
import jax.numpy as jnp
from jax import lax
from jax.experimental import pallas as pl
from jax.experimental.pallas import tpu as pltpu
from jax.sharding import PartitionSpec as P

HEADS = 16
HEAD_WORDS = 20000
MID_WORDS = 40000
TAIL_WORDS = 207735


NEG_FILL = -1e30
EPSILON = 1e-05
BLOCK = 256
SAFE = 1e30
VMEM_BYTES = 56 << 20
ONCE = dict(pipeline_mode=pl.Buffered(1))


def layer_norm(values, gain_vector, shift_vector):
    average = jnp.mean(values, -1, keepdims=True)
    centred = values - average
    spread = jnp.mean(centred * centred, -1, keepdims=True)
    return centred * lax.rsqrt(spread + EPSILON) * gain_vector + shift_vector


def norm_back(values, gain_vector, shift_vector, upstream):
    unused, pullback = jax.vjp(layer_norm, values, gain_vector, shift_vector)
    return pullback(upstream)


def gelu_back(before, upstream):
    unused, pullback = jax.vjp(jax.nn.gelu, before)
    return pullback(upstream)[0]


def product(former, latter):
    return jnp.dot(former, latter, preferred_element_type=jnp.float32)


def product_tn(former, latter):
    return lax.dot_general(
        former, latter, (((0,), (0,)), ((), ())), preferred_element_type=jnp.float32
    )


def product_nt(former, latter):
    return lax.dot_general(
        former, latter, (((1,), (1,)), ((), ())), preferred_element_type=jnp.float32
    )


def lowered(values):
    return values.astype(jnp.bfloat16)


def round_up(count, unit):
    return -(-count // unit) * unit


def thirds(values):
    high = lowered(values)
    rest = values - high.astype(jnp.float32)
    middle = lowered(rest)
    return [high, middle, lowered(rest - middle.astype(jnp.float32))]


def attend_kernel(start_ref, query_ref, key_ref, value_ref, out_ref):
    rows, keys = query_ref.shape[0], key_ref.shape[0]
    half = query_ref.shape[1] // 2
    query_pos = start_ref[0] + lax.broadcasted_iota(jnp.int32, (rows, keys), 0)
    allowed = lax.broadcasted_iota(jnp.int32, (rows, keys), 1) <= query_pos
    for part in range(2):
        cols = slice(part * half, part * half + half)
        scores = product_nt(query_ref[:, cols], key_ref[:, cols]) * half**-0.5
        scores = jnp.where(allowed, scores, NEG_FILL)
        weights = jnp.exp(scores - jnp.max(scores, 1, keepdims=True))
        weights = weights / jnp.sum(weights, 1, keepdims=True)
        out_ref[:, cols] = lowered(product(lowered(weights), value_ref[:, cols]))


def attend(start, queries, keys, values):
    rows, features = queries.shape
    width = 2 * features // HEADS
    own = pl.BlockSpec((rows, width), lambda i, s: (0, i))
    whole = pl.BlockSpec((keys.shape[0], width), lambda i, s: (0, i))
    return pl.pallas_call(
        attend_kernel,
        grid_spec=pltpu.PrefetchScalarGridSpec(
            num_scalar_prefetch=1,
            grid=(features // width,),
            in_specs=[own, whole, whole],
            out_specs=own,
        ),
        out_shape=jax.ShapeDtypeStruct((rows, features), jnp.bfloat16),
        compiler_params=pltpu.CompilerParams(vmem_limit_bytes=VMEM_BYTES),
        cost_estimate=pl.CostEstimate(
            flops=4 * rows * keys.shape[0] * features,
            bytes_accessed=4 * (rows + keys.shape[0]) * features,
            transcendentals=rows * keys.shape[0] * HEADS,
        ),
        name="attend",
    )(start, queries, keys, values)


def attend_back_kernel(
    start_ref, query_ref, key_ref, value_ref, up_ref, query_grad_ref, key_grad_ref, value_grad_ref
):
    rows, keys = query_ref.shape[0], key_ref.shape[0]
    half = query_ref.shape[1] // 2
    scale = half**-0.5
    query_pos = start_ref[0] + lax.broadcasted_iota(jnp.int32, (keys, rows), 1)
    allowed = lax.broadcasted_iota(jnp.int32, (keys, rows), 0) <= query_pos
    for part in range(2):
        cols = slice(part * half, part * half + half)
        query, key, value, up = (
            ref[:, cols] for ref in (query_ref, key_ref, value_ref, up_ref)
        )
        scores = jnp.where(allowed, product_nt(key, query) * scale, NEG_FILL)
        probs = jnp.exp(scores - jnp.max(scores, 0, keepdims=True))
        probs = probs / jnp.sum(probs, 0, keepdims=True)
        prob_grad = product_nt(value, up)
        delta = jnp.sum(probs * prob_grad, 0, keepdims=True)
        score_grad = lowered(probs * (prob_grad - delta))
        value_grad_ref[:, cols] = lowered(product(lowered(probs), up))
        key_grad_ref[:, cols] = lowered(product(score_grad, query) * scale)
        query_grad_ref[:, cols] = lowered(product_tn(score_grad, key) * scale)


def attend_back(start, queries, keys, values, upstream):
    rows, features = queries.shape
    count = keys.shape[0]
    width = 2 * features // HEADS
    own = pl.BlockSpec((rows, width), lambda i, s: (0, i))
    whole = pl.BlockSpec((count, width), lambda i, s: (0, i))
    return pl.pallas_call(
        attend_back_kernel,
        grid_spec=pltpu.PrefetchScalarGridSpec(
            num_scalar_prefetch=1,
            grid=(features // width,),
            in_specs=[own, whole, whole, own],
            out_specs=[own, whole, whole],
        ),
        out_shape=[
            jax.ShapeDtypeStruct((rows, features), jnp.bfloat16),
            jax.ShapeDtypeStruct((count, features), jnp.bfloat16),
            jax.ShapeDtypeStruct((count, features), jnp.bfloat16),
        ],
        compiler_params=pltpu.CompilerParams(vmem_limit_bytes=VMEM_BYTES),
        cost_estimate=pl.CostEstimate(
            flops=10 * rows * count * features,
            bytes_accessed=6 * (rows + count) * features,
            transcendentals=rows * count * HEADS,
        ),
        name="attend_back",
    )(start, queries, keys, values, upstream)


def pick_kernel(by_slot, index_ref, rows_ref, out_ref):
    count = rows_ref.shape[0]
    total = jnp.zeros(out_ref.shape, jnp.float32)
    base = pl.program_id(0) * BLOCK
    for at in range(0, count, BLOCK):
        if by_slot:
            place = base + lax.broadcasted_iota(jnp.int32, (BLOCK, BLOCK), 0)
            hit = index_ref[:, at : at + BLOCK] == place
        else:
            place = at + lax.broadcasted_iota(jnp.int32, (BLOCK, BLOCK), 1)
            hit = index_ref[...] == place
        onehot = lowered(jnp.where(hit, 1.0, 0.0))
        total = total + product(onehot, rows_ref[at : at + BLOCK, :])
    out_ref[...] = total.astype(out_ref.dtype)


def pick_rows(index, rows, out_count, by_slot, kind):
    count, width = rows.shape
    if by_slot:
        index = index.reshape(1, -1)
        index_spec = pl.BlockSpec(index.shape, lambda i: (0, 0))
    else:
        index = index.reshape(-1, 1)
        index_spec = pl.BlockSpec((BLOCK, 1), lambda i: (i, 0))
    return pl.pallas_call(
        functools.partial(pick_kernel, by_slot),
        grid=(out_count // BLOCK,),
        in_specs=[index_spec, pl.BlockSpec(rows.shape, lambda i: (0, 0), **ONCE)],
        out_specs=pl.BlockSpec((BLOCK, width), lambda i: (i, 0)),
        out_shape=jax.ShapeDtypeStruct((out_count, width), kind),
        compiler_params=pltpu.CompilerParams(vmem_limit_bytes=VMEM_BYTES),
        cost_estimate=pl.CostEstimate(
            flops=2 * out_count * count * max(width, 256),
            bytes_accessed=rows.size * 2 + out_count * width * 4,
            transcendentals=0,
        ),
        name="pick_rows",
    )(index, rows)


def band_kernel(chunk, per, words, sum_column, span_ref, rows_ref, table_ref, stat_ref, out_ref, mix_ref):
    step_id = pl.program_id(0)
    count, width = mix_ref.shape
    chunk_count = table_ref.shape[0] // chunk
    group_count = chunk_count // per
    active = (step_id >= span_ref[0]) & (step_id < span_ref[1])

    def put_stats(top, total):
        lane = lax.broadcasted_iota(jnp.int32, (count, 128), 1)
        both = jnp.where(lane == 0, top, jnp.where(lane == 1, total, 0.0))
        stat_ref[...] = both.T[:8, :]

    def logits_at(at, rows):
        return product_nt(rows, table_ref[pl.ds(at, chunk), :])

    def beyond(at, shape):
        return at + lax.broadcasted_iota(jnp.int32, shape, 1) >= words

    def run(rows, top):
        mix_ref[...] = jnp.zeros(mix_ref.shape, jnp.float32)

        def visit(group, total):
            for inner in range(per):
                at = (group * per + inner) * chunk
                checked = isinstance(at, int) and at + chunk > words
                if not isinstance(at, int):
                    at = pl.multiple_of(at, chunk)
                weights = jnp.exp(logits_at(at, rows) - top)
                if checked:
                    weights = jnp.where(beyond(at, weights.shape), 0.0, weights)
                if sum_column is None:
                    for lane in range(0, chunk, 128):
                        total = total + weights[:, lane : lane + 128]
                mix_ref[...] += product(lowered(weights), table_ref[pl.ds(at, chunk), :])
            return total

        lanes = jnp.zeros((count, 128), jnp.float32)
        lanes = visit(0, lanes) if group_count == 1 else lax.fori_loop(0, group_count, visit, lanes)
        if sum_column is None:
            return jnp.sum(lanes, 1, keepdims=True)
        return mix_ref[:, sum_column : sum_column + 1]

    @pl.when(active)
    def _():
        rows = rows_ref[...]
        first = product_nt(rows, table_ref[pl.ds(0, 128), :])
        top = jnp.max(first, 1, keepdims=True)
        total = run(rows, top)
        put_stats(top, total)

        @pl.when(jnp.logical_not(jnp.max(jnp.where(total < SAFE, 0.0, 1.0)) < 0.5))
        def _():
            def largest(index, top):
                at = pl.multiple_of(index * chunk, chunk)
                logits = logits_at(at, rows)
                if sum_column is None:
                    logits = jnp.where(beyond(at, logits.shape), NEG_FILL, logits)
                return jnp.maximum(top, jnp.max(logits, 1, keepdims=True))

            exact = lax.fori_loop(0, chunk_count, largest, jnp.full((count, 1), NEG_FILL))
            put_stats(exact, run(rows, exact))

        out_ref[...] = lowered(mix_ref[...])

    @pl.when(jnp.logical_not(active))
    def _():
        put_stats(jnp.full((count, 1), NEG_FILL), jnp.zeros((count, 1), jnp.float32))
        out_ref[...] = jnp.zeros(out_ref.shape, jnp.bfloat16)


def band_forward(span, rows, table, words, chunk, sum_column, share):
    count, width = rows.shape[0], table.shape[1]
    chunk_count = table.shape[0] // chunk
    per = chunk_count if chunk_count <= 4 else 4
    assert chunk_count % per == 0 and words >= 128
    return pl.pallas_call(
        functools.partial(band_kernel, chunk, per, words, sum_column),
        grid_spec=pltpu.PrefetchScalarGridSpec(
            num_scalar_prefetch=1,
            grid=(count // BLOCK,),
            in_specs=[
                pl.BlockSpec((BLOCK, width), lambda i, s: (i, 0)),
                pl.BlockSpec(table.shape, lambda i, s: (0, 0), **ONCE),
            ],
            out_specs=[
                pl.BlockSpec((8, BLOCK), lambda i, s: (0, i)),
                pl.BlockSpec((BLOCK, width), lambda i, s: (i, 0)),
            ],
            scratch_shapes=[pltpu.VMEM((BLOCK, width), jnp.float32)],
        ),
        out_shape=[
            jax.ShapeDtypeStruct((8, count), jnp.float32),
            jax.ShapeDtypeStruct((count, width), jnp.bfloat16),
        ],
        compiler_params=pltpu.CompilerParams(vmem_limit_bytes=VMEM_BYTES),
        cost_estimate=pl.CostEstimate(
            flops=int(share * 4 * count * table.shape[0] * max(width, 256)),
            bytes_accessed=table.size * 2 + count * width * 6,
            transcendentals=int(share * count * table.shape[0]),
        ),
        name="band_forward",
    )(span, rows, table)


def head_grad_kernel(chunk, lists, base_ref, table_ref, *refs):
    out_ref, sum_ref = refs[2 * lists :]
    words = table_ref.shape[0]
    base = base_ref[0] + pl.program_id(0) * words
    sum_ref[...] = jnp.zeros(sum_ref.shape, jnp.float32)
    for rows_ref, fact_ref in zip(refs[0 : 2 * lists : 2], refs[1 : 2 * lists : 2]):
        piece = min(rows_ref.shape[0], 1024)

        def visit(step, unused, rows_ref=rows_ref, fact_ref=fact_ref, piece=piece):
            at = pl.multiple_of(step * piece, piece)
            rows = rows_ref[pl.ds(at, piece), :]
            weight = fact_ref[0:1, pl.ds(at, piece)]
            total = fact_ref[1:2, pl.ds(at, piece)]
            ids = fact_ref[2:3, pl.ds(at, piece)].astype(jnp.int32)
            for start in range(0, words, chunk):
                probs = jnp.exp(product_nt(table_ref[start : start + chunk, :], rows) - total)
                word = base + start + lax.broadcasted_iota(jnp.int32, (chunk, 1), 0)
                grads = weight * (jnp.where(word == ids, 1.0, 0.0) - probs)
                sum_ref[start : start + chunk, :] += product(lowered(grads), rows)
            return unused

        lax.fori_loop(0, rows_ref.shape[0] // piece, visit, 0)
    out_ref[...] = lowered(sum_ref[...])


def head_grad(table, part, part_words, first_word, lists):
    width = table.shape[1]
    word_block = math.gcd(part_words, 640)
    steps = part_words // word_block
    chunk = word_block // 2 if word_block % 32 == 0 else word_block
    specs = []
    for rows, facts in lists:
        specs.append(pl.BlockSpec(rows.shape, lambda i, s: (0, 0), **ONCE))
        specs.append(pl.BlockSpec(facts.shape, lambda i, s: (0, 0), **ONCE))
    count = sum(rows.shape[0] for rows, facts in lists)
    scalars = jnp.stack([first_word + part * part_words, part * steps]).astype(jnp.int32)
    return pl.pallas_call(
        functools.partial(head_grad_kernel, chunk, len(lists)),
        grid_spec=pltpu.PrefetchScalarGridSpec(
            num_scalar_prefetch=1,
            grid=(steps,),
            in_specs=[pl.BlockSpec((word_block, width), lambda i, s: (s[1] + i, 0))] + specs,
            out_specs=pl.BlockSpec((word_block, width), lambda i, s: (i, 0)),
            scratch_shapes=[pltpu.VMEM((word_block, width), jnp.float32)],
        ),
        out_shape=jax.ShapeDtypeStruct((part_words, width), jnp.bfloat16),
        compiler_params=pltpu.CompilerParams(vmem_limit_bytes=VMEM_BYTES),
        cost_estimate=pl.CostEstimate(
            flops=4 * count * part_words * width,
            bytes_accessed=(count + part_words) * width * 2,
            transcendentals=count * part_words,
        ),
        name="head_grad",
    )(scalars, table, *[value for pair in lists for value in pair])


def band_grad_kernel(chunk, most, across, plan_ref, table_ref, rows_ref, fact_ref, out_ref, sum_ref):
    words = table_ref.shape[0]
    step_id = pl.program_id(0)
    base = plan_ref[most + 1] + step_id * words
    sum_ref[...] = jnp.zeros(sum_ref.shape, jnp.float32)

    def block_at(position):
        return pl.multiple_of(plan_ref[position] * BLOCK, BLOCK)

    def spread(starts):
        rows = [rows_ref[pl.ds(start, BLOCK), :] for start in starts]
        facts = [fact_ref[:, pl.ds(start, BLOCK)] for start in starts]
        rows = rows[0] if len(rows) == 1 else jnp.concatenate(rows, 0)
        facts = facts[0] if len(facts) == 1 else jnp.concatenate(facts, 1)
        weight, total = facts[0:1], facts[1:2]
        for start in range(0, words, chunk):
            probs = jnp.exp(product_nt(table_ref[start : start + chunk, :], rows) - total)
            sum_ref[start : start + chunk, :] -= product(lowered(weight * probs), rows)

    count = plan_ref[0]

    def pair(step, unused):
        spread([block_at(1 + 2 * step), block_at(2 + 2 * step)])
        return unused

    lax.fori_loop(0, count // 2, pair, 0)

    @pl.when(count % 2 == 1)
    def _():
        spread([block_at(count)])

    line = most + 2 + step_id * (most + 1)

    def hits(step, unused):
        at = block_at(line + 1 + step)
        rows = rows_ref[pl.ds(at, BLOCK), :]
        weight = fact_ref[0:1, pl.ds(at, BLOCK)]
        ids = fact_ref[2:3, pl.ds(at, BLOCK)].astype(jnp.int32)
        for start in range(0, words, chunk):
            word = base + start + lax.broadcasted_iota(jnp.int32, (chunk, 1), 0)
            chosen = lowered(jnp.where(word == ids, weight, 0.0))
            sum_ref[start : start + chunk, :] += product(chosen, rows)
        return unused

    lax.fori_loop(0, plan_ref[line], hits, 0)
    if across:
        out_ref[...] = sum_ref[...].T[: out_ref.shape[0], :].astype(out_ref.dtype)
    else:
        out_ref[...] = sum_ref[...].astype(out_ref.dtype)


def listed(flags):
    size = flags.shape[-1]
    order = jnp.cumsum(flags.astype(jnp.int32), -1)
    chosen = (order[..., None, :] == jnp.arange(1, size + 1)[:, None]) & flags[..., None, :]
    places = jnp.sum(jnp.where(chosen, jnp.arange(size), 0), -1)
    return jnp.concatenate([order[..., -1:], places], -1).astype(jnp.int32)


def band_grad(
    table, rows, facts, active, lowest, highest, part, part_words, first_word, chunk, result, across
):
    count, full = rows.shape[0], table.shape[1]
    word_block = chunk
    steps = part_words // word_block
    most = count // BLOCK
    first = first_word + part * part_words
    low = first + jnp.arange(steps, dtype=jnp.int32)[:, None] * word_block
    step_hits = active[None, :] & (lowest[None, :] < low + word_block) & (highest[None, :] >= low)
    plan = jnp.concatenate(
        [
            listed(active),
            first.reshape(1).astype(jnp.int32),
            listed(step_hits).reshape(-1),
            (part * steps).reshape(1).astype(jnp.int32),
        ]
    )
    last = plan.shape[0] - 1
    return pl.pallas_call(
        functools.partial(band_grad_kernel, chunk // 2 if chunk > 832 else chunk, most, across),
        grid_spec=pltpu.PrefetchScalarGridSpec(
            num_scalar_prefetch=1,
            grid=(steps,),
            in_specs=[
                pl.BlockSpec((word_block, full), lambda i, s: (s[last] + i, 0)),
                pl.BlockSpec((count, full), lambda i, s: (0, 0), **ONCE),
                pl.BlockSpec(facts.shape, lambda i, s: (0, 0), **ONCE),
            ],
            out_specs=(
                pl.BlockSpec((result.shape[0], word_block), lambda i, s: (0, i))
                if across
                else pl.BlockSpec((word_block, full), lambda i, s: (i, 0))
            ),
            scratch_shapes=[pltpu.VMEM((word_block, full), jnp.float32)],
        ),
        out_shape=result,
        compiler_params=pltpu.CompilerParams(vmem_limit_bytes=VMEM_BYTES),
        cost_estimate=pl.CostEstimate(
            flops=2 * count * part_words * 256,
            bytes_accessed=count * full * 2 + part_words * full * 4,
            transcendentals=count * part_words // 2,
        ),
        name="band_grad",
    )(plan, table, rows, facts)


def settle_kernel(
    member_ref,
    everyone_ref,
    fact_ref,
    head_mix_ref,
    middle_mix_ref,
    tail_mix_ref,
    head_hit_ref,
    middle_hit_ref,
    tail_hit_ref,
    term_ref,
    line_ref,
    slot_ref,
):
    step = pl.program_id(0)
    devices, _, slots = everyone_ref.shape
    tail_width = 64
    here = pl.ds(pl.multiple_of(step * BLOCK, BLOCK), BLOCK)

    def merged(read):
        lines = [read(device) for device in range(devices)]
        top = functools.reduce(jnp.maximum, [line[0] for line in lines])
        return top, sum(line[1] * jnp.exp(line[0] - top) for line in lines)

    head_top, head_sum = merged(
        lambda d: (everyone_ref[d, 0:1, here], everyone_ref[d, 1:2, here])
    )
    target = sum(everyone_ref[d, 2:3, here] for d in range(devices))
    slot_top, slot_sum = merged(lambda d: (everyone_ref[d, 3:4, :], everyone_ref[d, 4:5, :]))
    used = slot_sum > 0.0
    slot_total = jnp.where(used, slot_top + jnp.log(jnp.where(used, slot_sum, 1.0)), 0.0)
    member = member_ref[0]
    own_slot_top = jnp.where(used, everyone_ref[member, 3:4, :], 0.0)
    own_head_top = everyone_ref[member, 0:1, here]

    facts = fact_ref[...]
    slot, share, cotangent, first_cluster, second_cluster, band, word = (
        facts[index : index + 1] for index in range(7)
    )

    def as_columns(lines):
        square = jnp.concatenate(
            lines + [jnp.zeros((128 - len(lines), BLOCK), jnp.float32)], 0
        )
        return square.T

    def three(line):
        return [part.astype(jnp.float32) for part in thirds(line)]

    slot_column = as_columns([slot])[:, 0:1].astype(jnp.int32)
    hot = lowered(
        jnp.where(lax.broadcasted_iota(jnp.int32, (BLOCK, slots), 1) == slot_column, 1.0, 0.0)
    )
    lines = three(slot_total) + three(own_slot_top) + [jnp.zeros((10, slots), jnp.float32)]
    on_tokens = product_nt(lowered(jnp.concatenate(lines, 0)), hot)
    band_total = on_tokens[0:1] + on_tokens[1:2] + on_tokens[2:3]
    own_band_top = on_tokens[3:4] + on_tokens[4:5] + on_tokens[5:6]

    cluster_top = jnp.maximum(head_top, jnp.maximum(first_cluster, second_cluster))
    head_total = cluster_top + jnp.log(
        head_sum * jnp.exp(head_top - cluster_top)
        + jnp.exp(first_cluster - cluster_top)
        + jnp.exp(second_cluster - cluster_top)
    )
    in_head = band < 0.5
    cluster = jnp.where(band < 1.5, first_cluster, second_cluster)
    model_logp = target - head_total + jnp.where(in_head, 0.0, cluster - band_total)
    ratio = 0.25 * share * jnp.exp(-model_logp)
    weight = cotangent * 0.75 / (0.75 + ratio)
    head_scale = weight * jnp.exp(own_head_top - head_total)
    band_scale = weight * jnp.where(in_head, 0.0, jnp.exp(own_band_top - band_total))
    columns = as_columns([weight, head_scale, band_scale])
    weight_column, head_column, band_column = (columns[:, i : i + 1] for i in range(3))
    width = head_mix_ref.shape[1]
    term_ref[:, :width] = lowered(
        weight_column * head_hit_ref[...].astype(jnp.float32)
        - head_column * head_mix_ref[...].astype(jnp.float32)
    )
    narrow = tail_mix_ref.shape[1]
    kept = lax.broadcasted_iota(jnp.int32, (BLOCK, narrow), 1) < tail_width

    def widened(values):
        values = jnp.where(kept, values, 0.0)
        more = middle_mix_ref.shape[1] - narrow
        return jnp.concatenate([values, jnp.zeros((BLOCK, more), jnp.float32)], 1)

    band_mix = product(hot, middle_mix_ref[...]) + widened(product(hot, tail_mix_ref[...]))
    band_hit = middle_hit_ref[...].astype(jnp.float32) + widened(
        tail_hit_ref[...].astype(jnp.float32)
    )
    term_ref[:, width:] = lowered(weight_column * band_hit - band_column * band_mix)
    line_ref[...] = jnp.concatenate(
        [
            model_logp + jnp.log(0.75 + ratio),
            weight,
            head_total,
            word,
            jnp.zeros((4, BLOCK), jnp.float32),
        ],
        0,
    )

    @pl.when(step == 0)
    def _():
        slot_ref[...] = jnp.concatenate(
            [jnp.zeros((8, slots), jnp.float32), slot_total, jnp.zeros((7, slots), jnp.float32)], 0
        )

    sent = three(weight) + three(word) + [jnp.zeros((10, BLOCK), jnp.float32)]
    slot_ref[0:8, :] += product(lowered(jnp.concatenate(sent, 0)), hot)[0:8]


def settle(member, everyone, facts, head_mix, middle_mix, tail_mix, hits):
    count, width = head_mix.shape
    slots = middle_mix.shape[0]
    full = width + middle_mix.shape[1]

    def tokens(values):
        return pl.BlockSpec((BLOCK, values.shape[1]), lambda i, s: (i, 0))

    def whole(values):
        return pl.BlockSpec(values.shape, lambda i, s: (0,) * values.ndim, **ONCE)

    lines = pl.BlockSpec((8, BLOCK), lambda i, s: (0, i))
    return pl.pallas_call(
        settle_kernel,
        grid_spec=pltpu.PrefetchScalarGridSpec(
            num_scalar_prefetch=1,
            grid=(count // BLOCK,),
            in_specs=[whole(everyone), lines, tokens(head_mix), whole(middle_mix), whole(tail_mix)]
            + [tokens(hit) for hit in hits],
            out_specs=[
                pl.BlockSpec((BLOCK, full), lambda i, s: (i, 0)),
                lines,
                pl.BlockSpec((16, slots), lambda i, s: (0, 0)),
            ],
        ),
        out_shape=[
            jax.ShapeDtypeStruct((count, full), jnp.bfloat16),
            jax.ShapeDtypeStruct((8, count), jnp.float32),
            jax.ShapeDtypeStruct((16, slots), jnp.float32),
        ],
        compiler_params=pltpu.CompilerParams(vmem_limit_bytes=VMEM_BYTES),
        cost_estimate=pl.CostEstimate(
            flops=2 * count * slots * 1024,
            bytes_accessed=count * width * 12 + slots * full,
            transcendentals=slots * 64,
        ),
        name="settle",
    )(member.reshape(1).astype(jnp.int32), everyone, facts, head_mix, middle_mix, tail_mix, *hits)


def line_turns(value):
    size = lax.axis_size("seq")
    return [value] + [
        lax.ppermute(value, "seq", [(d, (d - k) % size) for d in range(size)])
        for k in range(1, size)
    ]


def line_step(before, behind, step):
    size = lax.axis_size("seq")
    return (
        lax.ppermute(before, "seq", [(d, d + 1) for d in range(step - 1, size - 1)]),
        lax.ppermute(behind, "seq", [(d, d - 1) for d in range(1, size - step + 1)]),
    )


def line_steps(value):
    found = [(value, value)]

    def advance(*others):
        step = len(found)
        if step == lax.axis_size("seq"):
            return others
        moved = line_step(*found[-1], step)
        moved, others = lax.optimization_barrier((moved, others))
        found.append(moved)
        return others

    return found, advance


def line_ordered(found):
    size, place = lax.axis_size("seq"), lax.axis_index("seq")
    ordered = []
    for source in range(size):
        value = found[0][0]
        for step in range(1, size):
            if source + step < size:
                value = jnp.where(place == source + step, found[step][0], value)
            if source - step >= 0:
                value = jnp.where(place == source - step, found[step][1], value)
        ordered.append(value)
    return ordered


def earlier_joined(value):
    size, place = lax.axis_size("seq"), lax.axis_index("seq")
    joined = jnp.zeros((size,) + value.shape, value.dtype)
    for step in range(size - 1, -1, -1):
        piece = value
        if step:
            piece = lax.ppermute(value, "seq", [(d, d + step) for d in range(size - step)])
        joined = lax.dynamic_update_index_in_dim(joined, piece, jnp.maximum(place - step, 0), 0)
    return joined.reshape((-1,) + value.shape[1:])


def in_order(pieces):
    size, place = lax.axis_size("seq"), lax.axis_index("seq")
    joined = jnp.zeros((size,) + pieces[0].shape, pieces[0].dtype)
    for k, piece in enumerate(pieces):
        joined = lax.dynamic_update_index_in_dim(joined, piece, lax.rem(place + k, size), 0)
    return joined.reshape((-1,) + pieces[0].shape[1:])


def line_scatter(values, behind=True):
    size, place = lax.axis_size("seq"), lax.axis_index("seq")
    parts = values.reshape((size, -1) + values.shape[1:])

    def part(index):
        return lax.dynamic_index_in_dim(parts, lax.rem(index, size), 0, False)

    total = part(place).astype(jnp.float32)
    for k in range(1, size):
        pairs = [(d, (d - k) % size) for d in range(0 if behind else k, size)]
        total = total + lax.ppermute(part(place + size - k), "seq", pairs).astype(jnp.float32)
    return total


def turn_kernel(rows_ref, out_ref):
    out_ref[...] = rows_ref[...].astype(jnp.float32).T.astype(out_ref.dtype)


def turned(rows, kind):
    return pl.pallas_call(
        turn_kernel, out_shape=jax.ShapeDtypeStruct(rows.shape[::-1], kind), name="turned"
    )(rows)


def word_pad(rows, biggest, splits):
    chunk = min(biggest, round_up(rows, 128))
    chunks = -(-rows // chunk)
    if chunks > 4:
        chunks = round_up(chunks, 4)
    return chunk, chunks * chunk


def on_device(
    inputs,
    targets,
    neighbours,
    neighbour_scores,
    loglik_grad,
    first_gain,
    first_shift,
    query_weight,
    query_bias,
    key_weight,
    value_weight,
    value_bias,
    out_weight,
    out_bias,
    second_gain,
    second_shift,
    inner_weight,
    inner_bias,
    outer_weight,
    outer_bias,
    final_gain,
    final_shift,
    head_table,
    cluster_weight,
    middle_map,
    middle_table,
    tail_map,
    tail_table,
):
    nb = lax.axis_size("batch")
    nz = lax.axis_size("seq")
    member = lax.axis_index("batch")
    place = lax.axis_index("seq")
    tokens = inputs[0]
    own_ids = targets[0]
    token_count, feature_count = tokens.shape
    group_count = token_count * nb
    slot_count = group_count + BLOCK
    query_start = (place * token_count).reshape(1)

    normed_low = lowered(layer_norm(tokens, first_gain, first_shift))
    normed_all = earlier_joined(normed_low)
    top_score = jnp.max(neighbour_scores[0], -1, keepdims=True)
    exponent = jnp.exp(neighbour_scores[0] - top_score)
    knn_prob = jnp.sum(jnp.where(neighbours[0] == 0, exponent, 0.0), -1) / jnp.sum(exponent, -1)
    early = jnp.stack([own_ids.astype(jnp.float32), knn_prob, loglik_grad[0]])
    early = lax.all_gather(early, "batch", axis=1, tiled=True)
    all_ids = early[0].astype(jnp.int32)
    all_knn, all_up = early[1], early[2]
    in_head = all_ids < HEAD_WORDS
    in_middle = (all_ids >= HEAD_WORDS) & (all_ids < HEAD_WORDS + MID_WORDS)
    in_tail = all_ids >= HEAD_WORDS + MID_WORDS
    order = jnp.arange(group_count, dtype=jnp.int32)
    ahead = (all_ids[None, :] < all_ids[:, None]) | (
        (all_ids[None, :] == all_ids[:, None]) & (order[None, :] < order[:, None])
    )
    rank = jnp.sum(ahead.astype(jnp.int32), -1)
    head_size = jnp.sum(in_head.astype(jnp.int32))
    middle_size = jnp.sum(in_middle.astype(jnp.int32))
    tail_size = group_count - head_size - middle_size
    middle_blocks = (middle_size + BLOCK - 1) // BLOCK
    tail_blocks = (tail_size + BLOCK - 1) // BLOCK
    slot = jnp.where(
        in_head,
        -1,
        rank - head_size + jnp.where(in_tail, middle_blocks * BLOCK - middle_size, 0),
    )
    zero_span = jnp.zeros((1,), jnp.int32)
    head_span = jnp.array([0, group_count // BLOCK], jnp.int32)
    middle_span = jnp.stack([0 * middle_blocks, middle_blocks]).astype(jnp.int32)
    tail_span = jnp.stack([middle_blocks, middle_blocks + tail_blocks]).astype(jnp.int32)
    slot_order = jnp.arange(slot_count, dtype=jnp.int32)
    slot_middle = slot_order < middle_size
    slot_tail = (slot_order >= middle_blocks * BLOCK) & (
        slot_order < middle_blocks * BLOCK + tail_size
    )
    slot_used = slot_middle | slot_tail
    band_id = all_ids - jnp.where(in_tail, HEAD_WORDS + MID_WORDS, HEAD_WORDS)

    tables = (head_table, middle_table, tail_table)
    sizes = tuple(table.shape[0] for table in tables)
    head_chunk, head_padded = word_pad(sizes[0], 1280, nz)
    middle_chunk, middle_padded = word_pad(sizes[1], 1280, nz)
    tail_chunk, tail_padded = word_pad(sizes[2], 1664, nz)
    tail_width = tail_table.shape[1]
    head_pad = jnp.pad(head_table, ((0, head_padded - sizes[0]), (0, 0)))
    middle_pad = jnp.pad(middle_table, ((0, middle_padded - sizes[1]), (0, 0)))
    tail_word = jnp.arange(tail_padded, dtype=jnp.int32)
    tail_bias = jnp.where(tail_word < jnp.minimum(TAIL_WORDS - member * sizes[2], sizes[2]), 0.0, NEG_FILL)
    tail_pad = jnp.concatenate(
        [
            jnp.pad(tail_table.T, ((0, 0), (0, tail_padded - sizes[2]))),
            jnp.ones((1, tail_padded), jnp.bfloat16),
            lowered(tail_bias)[None, :],
            jnp.zeros((126 - tail_width, tail_padded), jnp.bfloat16),
        ],
        0,
    ).T
    locals_ = (
        all_ids - member * sizes[0],
        all_ids - HEAD_WORDS - member * sizes[1],
        all_ids - HEAD_WORDS - MID_WORDS - member * sizes[2],
    )
    owned = tuple(
        inside & (local >= 0) & (local < size)
        for inside, local, size in zip((in_head, in_middle, in_tail), locals_, sizes)
    )
    hit_rows = tuple(
        jnp.where(
            own[:, None],
            jnp.take(table, jnp.clip(local, 0, size - 1), axis=0, mode="clip"),
            jnp.bfloat16(0),
        )
        for own, table, local, size in zip(owned, (head_pad, middle_pad, tail_pad), locals_, sizes)
    )

    queries = lowered(product(normed_low, query_weight) + query_bias)
    key_rows = lowered(product(normed_all, key_weight))
    value_rows = lowered(product(normed_all, value_weight) + value_bias)
    attended_low = attend(query_start, queries, key_rows, value_rows)
    mixed = tokens + product(attended_low, out_weight) + out_bias
    second_low = lowered(layer_norm(mixed, second_gain, second_shift))
    before = product(second_low, inner_weight) + inner_bias
    hidden_low = lowered(jax.nn.gelu(before))
    final = mixed + product(hidden_low, outer_weight) + outer_bias
    state_low = lowered(layer_norm(final, final_gain, final_shift))
    all_states = lax.all_gather(state_low, "batch", axis=0, tiled=True)
    split = 2 * nz * group_count * feature_count <= 24 << 20
    if split:
        block_states = lax.all_gather(state_low, "seq", axis=0, tiled=True)
    all_states, head_pad, middle_pad, tail_pad, tail_hits, slot, early = lax.optimization_barrier(
        (all_states, head_pad, middle_pad, tail_pad, hit_rows[2], slot, early)
    )
    hit_rows = hit_rows[:2] + (tail_hits,)

    middle_width = middle_map.shape[1]
    maps = jnp.pad(jnp.concatenate([middle_map, tail_map], 1), ((0, 0), (0, 128 - tail_width)))
    one_column = (jnp.arange(middle_width + 128) == middle_width + tail_width + 1).astype(jnp.float32)
    band_low = lowered(product(all_states, maps) + one_column)
    middle_low, tail_low = band_low[:, :middle_width], band_low[:, middle_width:]
    cluster_lines = product_nt(
        jnp.pad(cluster_weight.T, ((0, 6), (0, 0))), all_states
    )
    slot_full = pick_rows(slot, band_low, slot_count, True, jnp.bfloat16)
    first_tail = middle_blocks * BLOCK
    in_tail_slot = slot_order >= first_tail
    slot_low = jnp.where(
        in_tail_slot[:, None],
        jnp.pad(slot_full[:, middle_width:], ((0, 0), (0, middle_width - 128))),
        slot_full[:, :middle_width],
    )
    if split:
        piece = slot_count // nb
        slot_piece = lax.dynamic_slice_in_dim(slot_low, member * piece, piece, 0)
        other_slots = jnp.concatenate(line_turns(slot_piece)[1:], 0)
    head_stats, head_mix = band_forward(
        head_span, all_states, head_pad, sizes[0], head_chunk, None, 1.0
    )
    if split:
        slot_low, block_states, hit_rows, head_stats = lax.optimization_barrier(
            (slot_low, block_states, hit_rows, head_stats)
        )
        other_states = lax.dynamic_slice_in_dim(
            jnp.concatenate([block_states, block_states], 0),
            (place + 1) * token_count,
            (nz - 1) * token_count,
            0,
        )
        other_states = lax.all_gather(other_states, "batch", axis=0, tiled=True)
    tail_stats, tail_mix = band_forward(
        tail_span, slot_low, tail_pad, tail_padded, tail_chunk, tail_width, 0.5
    )
    middle_stats, middle_mix = band_forward(
        middle_span, slot_low, middle_pad, sizes[1], middle_chunk, None, 0.25
    )
    inner_lane = jnp.arange(128) < tail_width
    target_part = (
        jnp.sum(hit_rows[0].astype(jnp.float32) * all_states.astype(jnp.float32), -1)
        + jnp.sum(hit_rows[1].astype(jnp.float32) * middle_low.astype(jnp.float32), -1)
        + jnp.sum(
            jnp.where(inner_lane, hit_rows[2].astype(jnp.float32), 0.0)
            * tail_low.astype(jnp.float32),
            -1,
        )
    )
    slot_stats = jnp.where(in_tail_slot[None, :], tail_stats[:2], middle_stats[:2])
    extra = ((0, 0), (0, BLOCK))
    stats = jnp.concatenate(
        [
            jnp.pad(jnp.concatenate([head_stats[:2], target_part[None]], 0), extra),
            slot_stats,
            jnp.zeros((3, slot_count), jnp.float32),
        ],
        0,
    )
    if split:
        stats, other_states, other_slots = lax.optimization_barrier(
            (stats, other_states, other_slots)
        )
        other_slots = lax.all_gather(other_slots, "batch", axis=0, tiled=True)
    everyone = lax.all_gather(stats, "batch")

    token_facts = jnp.concatenate(
        [
            slot.astype(jnp.float32)[None],
            early[1:3],
            cluster_lines[:2],
            jnp.where(in_head, 0.0, jnp.where(in_middle, 1.0, 2.0))[None],
            early[0:1],
            jnp.zeros((1, group_count), jnp.float32),
        ],
        0,
    )
    terms, lines, slot_lines = settle(
        member, everyone, token_facts, head_mix, middle_mix, tail_mix, hit_rows
    )
    own_terms = lax.psum_scatter(terms, "batch", scatter_dimension=0, tiled=True).astype(jnp.float32)

    def own_part(values):
        return lax.dynamic_slice_in_dim(values, member * token_count, token_count, 0)

    loglik = own_part(lines[0])

    kind = jnp.where(slot_middle, 1.0, jnp.where(slot_tail, 2.0, 0.0))
    slot_facts = jnp.stack(
        [
            jnp.sum(slot_lines[0:3], 0),
            slot_lines[8],
            jnp.sum(slot_lines[3:6], 0),
            kind,
        ]
    )
    head_facts = jnp.concatenate([lines[1:4], jnp.zeros((1, group_count), jnp.float32)], 0)
    if split:
        other_slots = (
            other_slots.reshape(nb, nz - 1, piece, middle_width)
            .transpose(1, 0, 2, 3)
            .reshape(-1, middle_width)
        )
        rows_all = jnp.concatenate([slot_low, other_slots], 0)
        fact_pieces = line_turns(jnp.concatenate([slot_facts, head_facts], 1))
        facts = jnp.concatenate([value[:, :slot_count] for value in fact_pieces], 1)
        other_facts = (
            jnp.stack([value[:, slot_count:] for value in fact_pieces[1:]], 1)
            .reshape(4, nz - 1, nb, token_count)
            .transpose(0, 2, 1, 3)
            .reshape(4, -1)
        )
        lists = [(all_states, head_facts), (other_states, other_facts)]
        part, parts = place, nz
    else:
        rows_all, facts, lists = slot_low, slot_facts, [(all_states, head_facts)]
        part, parts = 0 * place, 1
    head_part = head_grad(head_pad, part, head_padded // parts, member * sizes[0], lists)
    block_facts = facts[2:4].reshape(2, -1, BLOCK)
    block_kind = jnp.max(block_facts[1], -1)
    filled = block_facts[1] > 0
    lowest = jnp.min(jnp.where(filled, block_facts[0], 1e9), -1).astype(jnp.int32)
    highest = jnp.max(jnp.where(filled, block_facts[0], -1e9), -1).astype(jnp.int32)
    facts = jnp.concatenate(
        [facts[:2], jnp.where(facts[3:4] > 0, facts[2:3], -1e9), jnp.zeros_like(facts[:1])], 0
    )
    def tail_gradient(part, parts):
        return band_grad(
            tail_pad,
            rows_all,
            facts,
            block_kind == 2,
            lowest,
            highest,
            part,
            tail_padded // parts,
            HEAD_WORDS + MID_WORDS + member * sizes[2],
            math.gcd(tail_padded // parts, tail_chunk),
            jax.ShapeDtypeStruct((tail_width, tail_padded // parts), jnp.bfloat16),
            True,
        )

    first_tail = tail_gradient(2 * part, 2 * parts)
    if split:
        head_found, head_advance = line_steps(head_part)
        first_tail, facts = head_advance(first_tail, facts)
        first_found, first_advance = line_steps(first_tail)
        second_tail = tail_gradient(2 * part + 1, 2 * parts)
        second_tail, own_terms = head_advance(second_tail, own_terms)
        second_tail, own_terms = first_advance(second_tail, own_terms)
        second_found, second_advance = line_steps(second_tail)
    else:
        second_tail = tail_gradient(2 * part + 1, 2 * parts)
        own_terms, first_tail, second_tail = lax.optimization_barrier(
            (own_terms, first_tail, second_tail)
        )

    own_middle = own_part(in_middle)
    own_tail = own_part(in_tail)
    own_lines = lax.dynamic_slice_in_dim(lines, member * token_count, token_count, 1)
    own_weights, own_total = own_lines[1], own_lines[2]
    own_clusters = product(state_low, cluster_weight)
    band_state = own_terms[:, feature_count:]
    middle_state = lowered(jnp.where(own_middle[:, None], band_state, 0.0))
    tail_state = lowered(jnp.where(own_tail[:, None], band_state[:, :tail_width], 0.0))
    cluster_hit = jnp.stack([own_middle, own_tail], -1).astype(jnp.float32)
    cluster_grad = own_weights[:, None] * (
        cluster_hit - jnp.exp(own_clusters - own_total[:, None])
    )
    state_grad = (
        own_terms[:, :feature_count]
        + product_nt(middle_state, middle_map)
        + product_nt(tail_state, tail_map)
        + product_nt(cluster_grad, cluster_weight.astype(jnp.float32))
    )
    middle_map_grad = product_tn(state_low, middle_state)
    tail_map_rows = product_tn(tail_state, state_low)
    cluster_rows = product_tn(cluster_grad, state_low.astype(jnp.float32))
    final_grad, final_gain_grad, final_shift_grad = norm_back(
        final, final_gain, final_shift, state_grad
    )
    final_low = lowered(final_grad)
    outer_weight_grad = product_tn(hidden_low, final_low)
    outer_bias_grad = jnp.sum(final_grad, 0)
    outer_part = lax.psum_scatter(
        lowered(outer_weight_grad), "batch", scatter_dimension=0, tiled=True
    )
    before_grad = lowered(gelu_back(before, product_nt(final_low, outer_weight)))
    inner_weight_grad = product_tn(second_low, before_grad)
    inner_bias_grad = jnp.sum(before_grad.astype(jnp.float32), 0)
    inner_part = lax.psum_scatter(
        lowered(inner_weight_grad), "batch", scatter_dimension=0, tiled=True
    )
    second_in_grad, second_gain_grad, second_shift_grad = norm_back(
        mixed, second_gain, second_shift, product_nt(before_grad, inner_weight)
    )
    mixed_grad = final_grad + second_in_grad
    mixed_low = lowered(mixed_grad)
    out_weight_grad = product_tn(attended_low, mixed_low)
    out_bias_grad = jnp.sum(mixed_grad, 0)
    attended_grad = lowered(product_nt(mixed_low, out_weight))
    if split:
        for unused in range(nz - 3):
            (attended_grad,) = head_advance(attended_grad)
        (attended_grad,) = second_advance(attended_grad)
    query_low, key_low, value_low = attend_back(
        query_start, queries, key_rows, value_rows, attended_grad
    )
    if split:
        query_low, key_low, value_low = first_advance(query_low, key_low, value_low)
        query_low, key_low, value_low = second_advance(query_low, key_low, value_low)
    query_weight_grad = product_tn(normed_low, query_low)
    key_weight_grad = product_tn(normed_all, key_low)
    value_weight_grad = product_tn(normed_all, value_low)
    query_bias_grad = jnp.sum(query_low.astype(jnp.float32), 0)
    value_bias_grad = jnp.sum(value_low.astype(jnp.float32), 0)
    spread = product_nt(key_low, key_weight) + product_nt(value_low, value_weight)
    query_spread = product_nt(query_low, query_weight)
    first_shift_grad = jnp.sum(spread, 0) + jnp.sum(query_spread, 0)
    all_centred = (normed_all.astype(jnp.float32) - first_shift) / first_gain
    own_average = jnp.mean(tokens, -1, keepdims=True)
    own_spread = jnp.mean((tokens - own_average) ** 2, -1, keepdims=True)
    own_centred = (tokens - own_average) * lax.rsqrt(own_spread + EPSILON)
    first_gain_grad = jnp.sum(all_centred * spread, 0) + jnp.sum(own_centred * query_spread, 0)
    bias_rows = inner_bias_grad.shape[0] // feature_count
    inner_bias_rows = (
        inner_bias_grad.reshape(nb, bias_rows, -1).transpose(1, 0, 2).reshape(bias_rows, -1)
    )
    vectors = [
        first_gain_grad,
        first_shift_grad,
        query_bias_grad,
        value_bias_grad,
        out_bias_grad,
        second_gain_grad,
        second_shift_grad,
        outer_bias_grad,
        final_gain_grad,
        final_shift_grad,
    ]
    rows = [tail_map_rows, cluster_rows, inner_bias_rows] + [value[None] for value in vectors]
    edges = [0]
    for row in rows:
        edges.append(edges[-1] + row.shape[0])
    row_count = round_up(edges[-1], 128)
    rows.append(jnp.zeros((row_count - edges[-1], feature_count), jnp.float32))
    columns = [
        query_weight_grad,
        key_weight_grad,
        value_weight_grad,
        out_weight_grad,
        middle_map_grad,
        turned(jnp.concatenate(rows, 0), jnp.bfloat16),
    ]
    rest = jnp.concatenate([lowered(column) for column in columns], 1)
    spread_low = lowered(spread)
    rest, facts, spread_low, inner_part = lax.optimization_barrier(
        (rest, facts, spread_low, inner_part)
    )
    if split:
        for unused in range(nz - 3):
            rest, facts, spread_low, inner_part = first_advance(rest, facts, spread_low, inner_part)
            rest, facts, spread_low, inner_part = second_advance(
                rest, facts, spread_low, inner_part
            )
    rest_part = lax.psum_scatter(rest, "batch", scatter_dimension=0, tiled=True)
    inner_low = lowered(line_scatter(inner_part))
    spread_sum = line_scatter(spread_low, False)
    middle_result = jax.ShapeDtypeStruct(
        (sizes[1], middle_width) if split else (middle_padded, middle_width),
        jnp.float32 if split else jnp.bfloat16,
    )
    middle_part = band_grad(
        middle_pad,
        rows_all,
        facts,
        block_kind == 1,
        lowest,
        highest,
        0 * place,
        middle_padded,
        HEAD_WORDS + member * sizes[1],
        middle_chunk,
        middle_result,
        False,
    )
    middle_part, inner_low, outer_part = lax.optimization_barrier(
        (middle_part, inner_low, outer_part)
    )
    rest_part, spread_sum = lax.optimization_barrier((rest_part, spread_sum))
    rest_low = lax.psum(rest_part, "seq")
    inner_pieces = line_turns(inner_low)
    outer_low = lowered(line_scatter(outer_part))
    rest_low, inner_pieces, outer_low = lax.optimization_barrier(
        (rest_low, inner_pieces, outer_low)
    )
    if split:
        middle_table_grad = middle_part
        head_table_grad = jnp.concatenate(line_ordered(head_found), 0)
        pairs = zip(line_ordered(first_found), line_ordered(second_found))
        tail_sum = jnp.concatenate([value for pair in pairs for value in pair], 1)
    else:
        middle_table_grad = lax.psum(middle_part, "seq")[: sizes[1]].astype(jnp.float32)
        head_table_grad = lax.psum(head_part, "seq")
        tail_sum = lax.psum(jnp.concatenate([first_tail, second_tail], 1), "seq")
    head_table_grad = head_table_grad[: sizes[0]].astype(jnp.float32)
    tail_table_grad = tail_sum[:, : sizes[2]].astype(jnp.float32).T
    normed_grad = query_spread + spread_sum
    first_in_grad, unused, unused = norm_back(tokens, first_gain, first_shift, normed_grad)
    input_grad = mixed_grad + first_in_grad
    inner_sum = in_order(inner_pieces).astype(jnp.float32)
    outer_sum = in_order(line_turns(outer_low)).astype(jnp.float32)
    rest_sum = rest_low[:, : 4 * feature_count + middle_width].astype(jnp.float32)
    cut = [rest_sum[:, i * feature_count : (i + 1) * feature_count] for i in range(4)]
    middle_map_sum = rest_sum[:, 4 * feature_count : 4 * feature_count + middle_width]
    row_sum = turned(rest_low[:, 4 * feature_count + middle_width :], jnp.float32)
    tail_map_sum, cluster_sum, inner_bias_sum = (
        row_sum[low:high] for low, high in zip(edges[:3], edges[1:4])
    )
    lines = [row_sum[index] for index in range(edges[3], edges[3] + len(vectors))]
    return (
        loglik.reshape(1, token_count),
        input_grad.reshape(1, token_count, feature_count),
        lines[0],
        lines[1],
        cut[0],
        lines[2],
        cut[1],
        cut[2],
        lines[3],
        cut[3],
        lines[4],
        lines[5],
        lines[6],
        inner_sum,
        inner_bias_sum.reshape(-1),
        outer_sum,
        lines[7],
        lines[8],
        lines[9],
        head_table_grad,
        cluster_sum.T,
        middle_map_sum,
        middle_table_grad,
        tail_map_sum.T,
        tail_table_grad,
    )


def solution(mesh):
    return jax.shard_map(
        on_device,
        mesh=mesh,
        in_specs=(
            P("batch", "seq", None),
            P("batch", "seq"),
            P("batch", "seq", None),
            P("batch", "seq", None),
            P("batch", "seq"),
            P(),
            P(),
            P(),
            P(),
            P(),
            P(),
            P(),
            P(),
            P(),
            P(),
            P(),
            P(),
            P(),
            P(),
            P(),
            P(),
            P(),
            P("batch", None),
            P(),
            P(),
            P("batch", None),
            P(),
            P("batch", None),
        ),
        out_specs=(
            P("batch", "seq"),
            P("batch", "seq", None),
            P("batch"),
            P("batch"),
            P("batch", None),
            P("batch"),
            P("batch", None),
            P("batch", None),
            P("batch"),
            P("batch", None),
            P("batch"),
            P("batch"),
            P("batch"),
            P("batch", None),
            P("batch"),
            P("batch", None),
            P("batch"),
            P("batch"),
            P("batch"),
            P("batch", None),
            P("batch", None),
            P("batch", None),
            P("batch", None),
            P("batch", None),
            P("batch", None),
        ),
        check_vma=False,
    )
```
